32 devices in a mesh: seq: 32 (over z, y, x, core).
Axes of the slice: x: 2, y: 2, z: 4, core: 2. Of those that a mesh axis runs over, the one named last changes fastest.
Arguments:
- tokens: bfloat16 [16384, 640], P('seq'), may hold values from -6 to 6
- segment_ids: int32 [16384], replicated, may hold values from 0 to 15, never falling along the last dimension, each value on 1 to 2048 neighbouring positions
- w_query: bfloat16 [640, 1024], P('seq'), may hold values from -0.25 to 0.25
- w_key: bfloat16 [640, 256], P('seq'), may hold values from -0.25 to 0.25
- w_value: bfloat16 [640, 256], P('seq'), may hold values from -0.25 to 0.25
- w_output: bfloat16 [1024, 640], P(None, 'seq'), may hold values from -0.1875 to 0.1875
- w_gate: bfloat16 [640, 2048], P('seq'), may hold values from -0.25 to 0.25
- w_up: bfloat16 [640, 2048], P('seq'), may hold values from -0.25 to 0.25
- w_down: bfloat16 [2048, 640], P(None, 'seq'), may hold values from -0.125 to 0.125
- norm_gains: bfloat16 [4, 640], P(None, 'seq'), may hold values from 0.5 to 1.5
- qk_gains: bfloat16 [512], P('seq'), may hold values from 0.5 to 1.5
- cotangent: bfloat16 [16384, 640], P('seq'), may hold values from -6 to 6
Outputs:
- mixed: bfloat16 [16384, 640], P('seq')
- input_grad: float32 [16384, 640], P('seq')
- grad_query: float32 [640, 1024], P('seq')
- grad_key: float32 [640, 256], P('seq')
- grad_value: float32 [640, 256], P('seq')
- grad_output: float32 [1024, 640], P(None, 'seq')
- grad_gate: float32 [640, 2048], P('seq')
- grad_up: float32 [640, 2048], P('seq')
- grad_down: float32 [2048, 640], P(None, 'seq')
- grad_norm_gains: float32 [4, 640], P(None, 'seq')
- grad_qk_gains: float32 [512], P('seq')
The draws below stay inside these ranges and needn't reach their ends.
Inputs may be any that keep to these rules, and one draw needn't show every extreme that they name: `segment_ids`: never falls along the row; every document has 1 to 2048 tokens, one exactly 2048.
All inputs are finite; a program needn't handle non-finite values.
Results may differ from the reference program's by a relative error of at most 0.017.
Values may be sent and summed in bfloat16 or wider, within the bound.
No kernel may reach another device: no remote copies, remote signals or barrier semaphores. Data moves between devices by JAX's collectives and lax.ppermute only.
A program may use at most 128 MiB of HBM per device.

```python
import math
import jax
import jax.numpy as jnp
import numpy as np
from jax import lax

D = 640
H = 4
HD = 256
FF = 2048
WINDOW = 512
TOKENS = 16384


def block_levels(key, shape, shards, smallest, high):
    factor_of, own = 1.0, jax.random.fold_in(key, 6)
    for position, shards_of in shards:
        heights = jnp.exp(jax.random.uniform(jax.random.fold_in(own, position), (shards_of,), jnp.float32, smallest / len(shards), high / len(shards)))
        factor_of = factor_of * jnp.repeat(heights, shape[position] // shards_of).reshape([-1 if axis == position else 1 for axis in range(len(shape))])
    return factor_of


def length_profile(amount, total, limit, skew):
    weights = [(1 << 20) // math.isqrt(grade ** skew) + 1 for grade in range(2, amount + 1)]
    surplus, given = total - limit - (amount - 1), [1] * (amount - 1)
    while surplus > 0:
        candidates = [i for i in range(amount - 1) if given[i] < limit]
        whole, left = sum([weights[i] for i in candidates]), surplus
        for i in candidates:
            addition = min(limit - given[i], max(1, left * weights[i] // whole), surplus)
            given[i] = given[i] + addition
            surplus = surplus - addition
    return np.array([limit] + given)


def ragged_sizes(rng, amount, total, most, lean):
    if amount == 2:
        one = jax.random.randint(rng, (), max(1, total - most), min(most, total - 1) + 1)
        return jnp.stack([one, total - one])
    sizes = jnp.asarray(length_profile(amount, total, most, lean), jnp.int32)
    twos = (amount - 1) // 2
    donor, receiver = sizes[1:1 + 2 * twos:2], sizes[2:2 + 2 * twos:2]
    margin = jnp.minimum(donor - 1, most - receiver)
    passed = jax.random.randint(jax.random.fold_in(rng, 1), (twos,), 0, 1 << 20) % (margin + 1)
    sizes = sizes.at[1:1 + 2 * twos:2].set(donor - passed).at[2:2 + 2 * twos:2].set(receiver + passed)
    return sizes[jax.random.permutation(jax.random.fold_in(rng, 2), amount)]


def centred(rng, extent, scale, most, pieces=(), kind=jnp.bfloat16):
    values = jax.random.normal(rng, extent, jnp.float32) * scale
    if len(pieces) > 0:
        values = block_levels(rng, extent, pieces, -0.22, 0.18) * values
    return jnp.clip(values, min=-most, max=most).astype(kind)


def setup_inputs(seed: int = 0) -> dict:
    seeds = jax.random.split(jax.random.key(seed), 13)
    tokens = centred(seeds[0], (TOKENS, D), 1.0, 6.0, ((0, 32),))
    segment_ids = jnp.searchsorted(jnp.cumsum(ragged_sizes(seeds[1], TOKENS // (2 * WINDOW), TOKENS, 4 * WINDOW, 1)), jnp.arange(TOKENS), side="right").astype(jnp.int32)
    w_query = centred(seeds[2], (D, H * HD), D ** -0.5, 0.25, ((0, 32),))
    w_key = centred(seeds[3], (D, HD), D ** -0.5, 0.25, ((0, 32),))
    w_value = centred(seeds[4], (D, HD), D ** -0.5, 0.25, ((0, 32),))
    w_output = centred(seeds[5], (H * HD, D), (H * HD) ** -0.5, 0.1875, ((1, 32),))
    w_gate = centred(seeds[6], (D, FF), D ** -0.5, 0.25, ((0, 32),))
    w_up = centred(seeds[7], (D, FF), D ** -0.5, 0.25, ((0, 32),))
    w_down = centred(seeds[8], (FF, D), FF ** -0.5, 0.125, ((1, 32),))
    norm_gains = jnp.clip(1.0 + 0.1 * jax.random.normal(seeds[9], (4, D), jnp.float32), 0.5, 1.5).astype(jnp.bfloat16)
    qk_gains = jnp.clip(1.0 + 0.1 * jax.random.normal(seeds[10], (2 * HD,), jnp.float32), 0.5, 1.5).astype(jnp.bfloat16)
    cotangent = centred(seeds[11], (TOKENS, D), 1.0, 6.0, ((0, 32),))
    return dict(tokens=tokens, segment_ids=segment_ids, w_query=w_query, w_key=w_key, w_value=w_value, w_output=w_output, w_gate=w_gate, w_up=w_up, w_down=w_down, norm_gains=norm_gains, qk_gains=qk_gains, cotangent=cotangent)


epsilon = 1e-06
highest = lax.Precision.HIGHEST

@jax.custom_vjp
def low(v):
    return lax.optimization_barrier(v.astype(jnp.bfloat16)).astype(jnp.float32)

@jax.custom_vjp
def low_back(v):
    return v

def low_keep(v):
    return (low(v), None)

def low_pass(kept, grad):
    return (grad,)

def back_keep(v):
    return (v, None)

def back_low(kept, grad):
    return (low(grad),)
low.defvjp(low_keep, low_pass)
low_back.defvjp(back_keep, back_low)

def rms_gain(values, gain):
    return values * lax.rsqrt(lax.optimization_barrier(jnp.mean(values * values, axis=-1, keepdims=True)) + epsilon) * gain

def rope_tables(positions, width):
    half_width = width // 2
    freqs = 10000.0 ** (-2.0 * jnp.arange(half_width, dtype=jnp.float32) / width)
    angles = positions.astype(jnp.float32)[:, None] * freqs[None, :]
    return (jnp.cos(angles), jnp.sin(angles))

def rotate(values, cosine, sine):
    half_width = values.shape[-1] // 2
    first = values[..., :half_width]
    second = values[..., half_width:]
    return jnp.concatenate([first * cosine - second * sine, second * cosine + first * sine], axis=-1)

def layer_forward(inputs, w_query, w_key, w_value, w_output, w_gate, w_up, w_down, norm_gain, qk_gain, segment_ids, cosine, sine):
    hidden = low(rms_gain(inputs, norm_gain[0]))
    query_raw = low_back(jnp.dot(hidden, w_query, precision=highest)).reshape(TOKENS, H, HD)
    key_raw = low_back(jnp.dot(hidden, w_key, precision=highest))
    value_rows = low(low_back(jnp.dot(hidden, w_value, precision=highest)))
    query_rows = low(rotate(rms_gain(query_raw, qk_gain[:HD]), cosine[:, None, :], sine[:, None, :]))
    key_rows = low(rotate(rms_gain(key_raw, qk_gain[HD:]), cosine, sine))
    key_padded = jnp.concatenate([jnp.zeros((WINDOW, HD), jnp.float32), key_rows], axis=0)
    value_padded = jnp.concatenate([jnp.zeros((WINDOW, HD), jnp.float32), value_rows], axis=0)
    segment_padded = jnp.concatenate([jnp.full((WINDOW,), -1, jnp.int32), segment_ids])

    def attend_block(block_index):
        begin = block_index * WINDOW
        query_block = lax.dynamic_slice_in_dim(query_rows, begin, WINDOW, 0)
        key_block = lax.dynamic_slice_in_dim(key_padded, begin, 2 * WINDOW, 0)
        value_block = lax.dynamic_slice_in_dim(value_padded, begin, 2 * WINDOW, 0)
        query_segment = lax.dynamic_slice_in_dim(segment_ids, begin, WINDOW, 0)
        key_segment = lax.dynamic_slice_in_dim(segment_padded, begin, 2 * WINDOW, 0)
        distance = (jnp.arange(WINDOW, dtype=jnp.int32) + WINDOW)[:, None] - jnp.arange(2 * WINDOW, dtype=jnp.int32)[None, :]
        allowed = (query_segment[:, None] == key_segment[None, :]) & (distance >= 0) & (distance < WINDOW)
        scores = low_back(jnp.einsum('qhd,kd->hqk', query_block, key_block, precision=highest) / math.sqrt(HD))
        scores = jnp.where(allowed[None], scores, -1e+30)
        row_top = lax.optimization_barrier(jnp.max(scores, axis=-1, keepdims=True))
        weights = jnp.exp(scores - row_top)
        probs = low(weights / lax.optimization_barrier(jnp.sum(weights, axis=-1, keepdims=True)))
        attended_block = jnp.einsum('hqk,kd->qhd', probs, value_block, precision=highest)
        return attended_block.reshape(WINDOW, H * HD)
    attended = lax.map(jax.checkpoint(attend_block), jnp.arange(TOKENS // WINDOW, dtype=jnp.int32)).reshape(TOKENS, H * HD)
    attended = low(low_back(attended))
    attn_out = low_back(jnp.dot(attended, w_output, precision=highest))
    middle = inputs + rms_gain(attn_out, norm_gain[1])
    block_rows = min(4096, TOKENS)

    def feed_block(rows_in):
        normed = low(rms_gain(rows_in, norm_gain[2]))
        gate_raw = low_back(jnp.dot(normed, w_gate, precision=highest))
        up_raw = low_back(jnp.dot(normed, w_up, precision=highest))
        product = low(jax.nn.gelu(gate_raw, approximate=True) * up_raw)
        branch = low_back(jnp.dot(product, w_down, precision=highest))
        return rows_in + rms_gain(branch, norm_gain[3])
    result = lax.map(jax.checkpoint(feed_block), middle.reshape(TOKENS // block_rows, block_rows, D))
    return result.reshape(TOKENS, D)

def reference(tokens, segment_ids, w_query, w_key, w_value, w_output, w_gate, w_up, w_down, norm_gains, qk_gains, cotangent):
    starts = jnp.searchsorted(segment_ids, segment_ids, side='left').astype(jnp.int32)
    positions = jnp.arange(TOKENS, dtype=jnp.int32) - starts
    cosine, sine = rope_tables(positions, HD)

    def forward(inputs, wq_f, wk_f, wv_f, wo_f, wg_f, wu_f, wd_f, gains_f, qkg_f):
        return layer_forward(inputs, wq_f, wk_f, wv_f, wo_f, wg_f, wu_f, wd_f, gains_f, qkg_f, segment_ids, cosine, sine)
    floats = [array.astype(jnp.float32) for array in (tokens, w_query, w_key, w_value, w_output, w_gate, w_up, w_down, norm_gains, qk_gains)]
    result, pullback = jax.vjp(forward, *floats)
    grads = pullback(cotangent.astype(jnp.float32))
    return (result.astype(jnp.bfloat16), grads[0], grads[1], grads[2], grads[3], grads[4], grads[5], grads[6], grads[7], grads[8], grads[9])
```

```python
import math

import jax
import jax.numpy as jnp
from jax import lax
from jax.sharding import PartitionSpec as P

H = 4
HD = 256
WINDOW = 512
LONGEST = 2048
EXTRA = 128

epsilon = 1e-06
bf16 = jnp.bfloat16
f32 = jnp.float32


def masks_of(n, core):
    bits = [1 << i for i in range(n.bit_length() - 1)]
    pair = [bits[1], bits[3] if len(bits) > 6 else bits[2]]
    rest = [b for b in bits[1:] if b not in pair]
    if core:
        rest, pair = rest[::-1], pair[::-1]
    return rest + pair + [1]


def exchange(x, n, step):
    masks = [masks_of(n, c)[step] for c in (0, 1)]
    return lax.ppermute(x, "seq", [(i, i ^ masks[i & 1]) for i in range(n)])


def slot_devices(n, me):
    half = n // 2
    slot = jnp.arange(half, dtype=jnp.int32)

    def offsets(core):
        total = jnp.zeros((half,), jnp.int32)
        for k, m in enumerate(masks_of(n, core)[:-1]):
            total = total + ((slot >> k) & 1) * m
        return total

    even, odd = offsets(0), offsets(1)
    core = me & 1
    mine = jnp.where(core == 0, even, odd)
    other = jnp.where(core == 0, odd, even)
    return jnp.concatenate([me ^ mine, me ^ 1 ^ other])


def gather_rows(shard, n):
    steps = n.bit_length() - 1
    block = shard
    for k in range(steps):
        block = jnp.concatenate([block, exchange(block, n, k)], axis=0)
    return block


def scatter_rows(partial, n):
    steps = n.bit_length() - 1
    total = partial
    for k in reversed(range(steps)):
        half = total.shape[0] // 2
        got = exchange(total[half:].astype(bf16), n, k)
        total = total[:half].astype(f32) + got.astype(f32)
    return total


def rms_gain(values, gain):
    return values * lax.rsqrt(jnp.mean(values * values, axis=-1, keepdims=True) + epsilon) * gain


def rotate(values, cosine, sine):
    half_width = values.shape[-1] // 2
    first = values[..., :half_width]
    second = values[..., half_width:]
    return jnp.concatenate(
        [first * cosine - second * sine, second * cosine + first * sine], axis=-1
    )


def nn(left, right):
    return jnp.dot(left, right, preferred_element_type=f32)


def tn(left, right):
    return lax.dot_general(left, right, (((0,), (0,)), ((), ())), preferred_element_type=f32)


def nt(left, right):
    return lax.dot_general(left, right, (((1,), (1,)), ((), ())), preferred_element_type=f32)


def gelu_product(gate_raw, up_raw):
    return jax.nn.gelu(gate_raw, approximate=True) * up_raw


def on_device(
    tokens,
    segment_ids,
    w_query,
    w_key,
    w_value,
    w_output,
    w_gate,
    w_up,
    w_down,
    norm_gains,
    qk_gains,
    cotangent,
):
    n = lax.axis_size("seq")
    me = lax.axis_index("seq")
    rows = tokens.shape[0]
    width = tokens.shape[1]
    shard = w_query.shape[0]
    qk_shard = qk_gains.shape[0]
    root_scale = math.sqrt(HD)

    extra = jnp.zeros((shard, EXTRA), bf16)
    extra = extra.at[:, :4].set(norm_gains.T)
    extra = extra.at[:qk_shard, 4].set(qk_gains)
    full_a = gather_rows(jnp.concatenate([w_query, w_key, w_value, extra], axis=1), n)
    full_b = gather_rows(jnp.concatenate([w_output.T, w_gate, w_up], axis=1), n)
    full_c = gather_rows(w_down.T, n)
    w_q = full_a[:, :1024]
    w_k = full_a[:, 1024:1280]
    w_v = full_a[:, 1280:1536]
    gains_col = full_a[:, 1536:]
    w_o = full_b[:, :1024]
    w_g = full_b[:, 1024:3072]
    w_u = full_b[:, 3072:]
    w_d = full_c

    device = slot_devices(n, me)
    place = (device[:, None] * shard + jnp.arange(shard, dtype=jnp.int32)[None, :]).reshape(-1)
    order = (jnp.arange(width, dtype=jnp.int32)[:, None] == place[None, :]).astype(bf16)
    inner = jnp.arange(shard, dtype=jnp.int32)
    qk_place = jnp.where(inner < qk_shard, device[:, None] * qk_shard + inner, -1).reshape(-1)
    qk_order = (qk_place[:, None] == jnp.arange(2 * HD, dtype=jnp.int32)[None, :]).astype(bf16)

    gain_float = gains_col[:, :4].astype(f32).T
    qk_float = tn(gains_col[:, 4:5], qk_order)[0]

    inputs = nn(tokens, order)
    local_segment = lax.dynamic_slice_in_dim(segment_ids, me * rows, rows)
    padded = jnp.concatenate([jnp.full((LONGEST,), -1, jnp.int32), segment_ids])
    nearby = lax.dynamic_slice_in_dim(padded, me * rows, rows + LONGEST)
    ahead = (jnp.arange(rows) + LONGEST)[:, None] > jnp.arange(rows + LONGEST)[None, :]
    positions = jnp.sum(
        ((local_segment[:, None] == nearby[None, :]) & ahead).astype(jnp.int32), axis=1
    )
    freqs = 10000.0 ** (-2.0 * jnp.arange(HD // 2, dtype=f32) / HD)
    angles = positions.astype(f32)[:, None] * freqs[None, :]
    cosine, sine = jnp.cos(angles), jnp.sin(angles)

    hidden_f, hidden_pull = jax.vjp(rms_gain, inputs, gain_float[0])
    hidden = hidden_f.astype(bf16)
    query_raw = nn(hidden, w_q)
    key_raw = nn(hidden, w_k)
    value_raw = nn(hidden, w_v)

    def shape_qk(query_in, key_in, gain_query, gain_key):
        query_out = rotate(
            rms_gain(query_in.reshape(rows, H, HD), gain_query),
            cosine[:, None, :],
            sine[:, None, :],
        )
        key_out = rotate(rms_gain(key_in, gain_key), cosine, sine)
        return (query_out, key_out)

    (query_f, key_f), qk_pull = jax.vjp(shape_qk, query_raw, key_raw, qk_float[:HD], qk_float[HD:])
    query_rows = query_f.astype(bf16)
    own_pairs = jnp.concatenate([key_f.astype(bf16), value_raw.astype(bf16)], axis=1)
    behind = lax.ppermute(own_pairs, "seq", [(i, i + 1) for i in range(n - 1)])
    all_pairs = jnp.concatenate([behind, own_pairs], axis=0)
    key_rows = all_pairs[:, :HD]
    value_rows = all_pairs[:, HD:]
    key_segment = nearby[LONGEST - rows :]
    distance = (jnp.arange(rows) + rows)[:, None] - jnp.arange(2 * rows)[None, :]
    allowed = (
        (local_segment[:, None] == key_segment[None, :]) & (distance >= 0) & (distance < WINDOW)
    )

    def masked_scores():
        raw_scores = (
            jnp.einsum("qhd,kd->hqk", query_rows, key_rows, preferred_element_type=f32)
            / root_scale
        )
        return jnp.where(allowed[None], raw_scores, -1e30)

    scores = masked_scores()
    row_top = jnp.max(scores, axis=-1, keepdims=True)
    weights = jnp.exp(scores - row_top)
    row_total = jnp.sum(weights, axis=-1, keepdims=True)
    log_total = row_top + jnp.log(row_total)
    probs_low = (weights / row_total).astype(bf16)
    attended = jnp.einsum("hqk,kd->qhd", probs_low, value_rows, preferred_element_type=f32)
    attended_low = attended.reshape(rows, H * HD).astype(bf16)
    attn_raw = nt(attended_low, w_o)
    post_attn, post_attn_pull = jax.vjp(rms_gain, attn_raw, gain_float[1])
    middle = inputs + post_attn
    normed_f, normed_pull = jax.vjp(rms_gain, middle, gain_float[2])
    normed = normed_f.astype(bf16)
    gate_raw = nn(normed, w_g)
    up_raw = nn(normed, w_u)
    product_f, product_pull = jax.vjp(gelu_product, gate_raw, up_raw)
    product = product_f.astype(bf16)
    branch = nt(product, w_d)
    post_ffn, post_ffn_pull = jax.vjp(rms_gain, branch, gain_float[3])
    mixed = nt((middle + post_ffn).astype(bf16), order).astype(bf16)

    out_grad = nn(cotangent, order)
    branch_grad, gain_grad3 = post_ffn_pull(out_grad)
    branch_low = branch_grad.astype(bf16)
    sum_c = scatter_rows(tn(branch_low, product), n)
    product_grad = nn(branch_low, w_d)
    gate_grad, up_grad = product_pull(product_grad)
    gate_low = gate_grad.astype(bf16)
    up_low = up_grad.astype(bf16)
    sum_b = scatter_rows(jnp.concatenate([tn(normed, gate_low), tn(normed, up_low)], axis=1), n)
    normed_grad = nt(gate_low, w_g) + nt(up_low, w_u)
    middle_part, gain_grad2 = normed_pull(normed_grad)
    middle_grad = out_grad + middle_part
    attn_grad, gain_grad1 = post_attn_pull(middle_grad)
    attn_low = attn_grad.astype(bf16)
    output_wgrad = tn(attn_low, attended_low)
    attended_grad = nn(attn_low, w_o).astype(bf16).reshape(rows, H, HD)
    probs = jnp.exp(masked_scores() - log_total)
    probs_again = probs.astype(bf16)
    probs_grad = jnp.einsum("qhd,kd->hqk", attended_grad, value_rows, preferred_element_type=f32)
    row_delta = jnp.sum(probs * probs_grad, axis=-1, keepdims=True)
    scores_grad = (probs * (probs_grad - row_delta)).astype(bf16)
    query_grad = (
        jnp.einsum("hqk,kd->qhd", scores_grad, key_rows, preferred_element_type=f32) / root_scale
    )
    keys_grad = (
        jnp.einsum("hqk,qhd->kd", scores_grad, query_rows, preferred_element_type=f32) / root_scale
    )
    values_grad = jnp.einsum("hqk,qhd->kd", probs_again, attended_grad, preferred_element_type=f32)
    pairs_grad = jnp.concatenate([keys_grad, values_grad], axis=1)
    own_grad = pairs_grad[rows:] + lax.ppermute(
        pairs_grad[:rows].astype(bf16), "seq", [(i + 1, i) for i in range(n - 1)]
    ).astype(f32)
    key_grad_f = own_grad[:, :HD]
    value_low = own_grad[:, HD:].astype(bf16)
    query_raw_grad, key_raw_grad, gain_grad_query, gain_grad_key = qk_pull((query_grad, key_grad_f))
    query_low = query_raw_grad.astype(bf16)
    key_low = key_raw_grad.astype(bf16)
    hidden_grad = nt(query_low, w_q) + nt(key_low, w_k) + nt(value_low, w_v)
    input_part, gain_grad0 = hidden_pull(hidden_grad)
    input_grad = lax.dot_general(
        middle_grad + input_part,
        order.astype(f32),
        (((1,), (1,)), ((), ())),
        precision=lax.Precision.HIGHEST,
    )
    qk_grad = jnp.concatenate([gain_grad_query, gain_grad_key])
    qk_col = jnp.sum(jnp.where(qk_order > 0, qk_grad[None, :], 0.0), axis=1)
    gains_grad = jnp.stack(
        [gain_grad0, gain_grad1, gain_grad2, gain_grad3, qk_col]
        + [jnp.zeros((width,), f32)] * (EXTRA - 5),
        axis=1,
    )
    sum_a = scatter_rows(
        jnp.concatenate(
            [
                output_wgrad,
                tn(hidden, query_low),
                tn(hidden, key_low),
                tn(hidden, value_low),
                gains_grad,
            ],
            axis=1,
        ),
        n,
    )
    return (
        mixed,
        input_grad,
        sum_a[:, 1024:2048],
        sum_a[:, 2048:2304],
        sum_a[:, 2304:2560],
        sum_a[:, :1024].T,
        sum_b[:, :2048],
        sum_b[:, 2048:],
        sum_c.T,
        sum_a[:, 2560:2564].T,
        sum_a[:qk_shard, 2564],
    )


def solution(mesh):
    return jax.shard_map(
        on_device,
        mesh=mesh,
        in_specs=(
            P("seq", None),
            P(),
            P("seq", None),
            P("seq", None),
            P("seq", None),
            P(None, "seq"),
            P("seq", None),
            P("seq", None),
            P(None, "seq"),
            P(None, "seq"),
            P("seq"),
            P("seq", None),
        ),
        out_specs=(
            P("seq", None),
            P("seq", None),
            P("seq", None),
            P("seq", None),
            P("seq", None),
            P(None, "seq"),
            P("seq", None),
            P("seq", None),
            P(None, "seq"),
            P(None, "seq"),
            P("seq"),
        ),
        check_vma=False,
    )
```

```python
import functools

import jax
import jax.numpy as jnp
import numpy as np
from jax import lax
from jax.experimental import pallas as pl
from jax.experimental.pallas import tpu as pltpu
from jax.sharding import PartitionSpec as P

H = 4
HD = 256
WINDOW = 512
LONGEST = 2048
EXTRA = 128
FF_CHUNK = 512
BLOCK = 128
REACH = BLOCK + WINDOW
MIB = 1024 * 1024

epsilon = 1e-06
bf16 = jnp.bfloat16
f32 = jnp.float32


def far_masks(n):
    bits = [1 << i for i in range(n.bit_length() - 1)]
    near = near_pair(n)
    rest = [b for b in bits[1:] if b not in near]
    mixes = [0]
    for b in rest:
        mixes = mixes + [m | b for m in mixes]
    return mixes[1:]


def near_pair(n):
    return (2, 8) if n > 64 else (2, 4)


def to_partner(x, n, masks):
    return lax.ppermute(x, "seq", [(i, i ^ masks[i & 1]) for i in range(n)])


def row_table(n, shard):
    first, second = near_pair(n)
    far = [0] + far_masks(n)
    main = whole_tiles(shard)
    inner = [(f, r) for f in far for r in range(main)] + [
        (f, r) for f in far for r in range(main, shard)
    ]

    def offsets(a, b):
        return [m ^ f for m in (0, a, b, a | b) for f, _ in inner]

    even, odd = offsets(first, second), offsets(second, first)
    return (
        np.array(even + [1 ^ m for m in odd], np.int32),
        np.array(odd + [1 ^ m for m in even], np.int32),
        np.array([r for _, r in inner] * 8, np.int32),
    )


def nn(left, right):
    return jnp.dot(left, right, preferred_element_type=f32)


def tn(left, right):
    return lax.dot_general(left, right, (((0,), (0,)), ((), ())), preferred_element_type=f32)


def nt(left, right):
    return lax.dot_general(left, right, (((1,), (1,)), ((), ())), preferred_element_type=f32)


def inverse_rms(values):
    return lax.rsqrt(jnp.mean(values * values, axis=-1, keepdims=True) + epsilon)


def rms_back(values, gain, grad):
    scale = inverse_rms(values)
    hat = values * scale
    inner = grad * gain
    mean = jnp.mean(inner * hat, axis=-1, keepdims=True)
    return scale * (inner - hat * mean), jnp.sum(grad * hat, axis=0, keepdims=True)


def rotate(values, cosine, sine):
    half = values.shape[-1] // 2
    a, b = values[:, :half], values[:, half:]
    return jnp.concatenate([a * cosine - b * sine, b * cosine + a * sine], axis=-1)


def rotate_back(values, cosine, sine):
    half = values.shape[-1] // 2
    a, b = values[:, :half], values[:, half:]
    return jnp.concatenate([a * cosine + b * sine, b * cosine - a * sine], axis=-1)


def call(kernel, outs, args, us, scratch=(), after=(), room=12):
    given, extra = len(args), len(after)

    def body(*refs):
        kernel(*refs[:given], *refs[given + extra :])

    return pl.pallas_call(
        body,
        in_specs=[pl.BlockSpec(memory_space=pltpu.VMEM)] * given
        + [pl.BlockSpec(memory_space=pl.ANY)] * extra,
        out_specs=[pl.BlockSpec(memory_space=pltpu.VMEM)] * len(outs),
        out_shape=outs,
        scratch_shapes=scratch,
        compiler_params=pltpu.CompilerParams(vmem_limit_bytes=room * MIB),
        cost_estimate=pl.CostEstimate(
            flops=int(us * 10**9), bytes_accessed=int(us * 10**6), transcendentals=0
        ),
    )(*args, *after)


def shaped(shape, dtype):
    return jax.ShapeDtypeStruct(shape, dtype)


def join_rows(parts, cols=slice(None)):
    return jnp.concatenate([p[:, cols] for p in parts], axis=0)


def whole_tiles(rows):
    return rows // 16 * 16


def tiles_of(rows, cols):
    return rows == 20 and cols % 512 == 0


def to_tiles(values):
    quarter = values.shape[1] // 4
    rest = [values[16:, k * quarter : (k + 1) * quarter] for k in range(4)]
    return jnp.concatenate([values[:16], jnp.concatenate(rest, axis=0)], axis=1)


def tile_kernel(*refs):
    half = len(refs) // 2
    for source, out in zip(refs[:half], refs[half:]):
        values = source[...].astype(f32)
        out[...] = (to_tiles(values) if tiles_of(*values.shape) else values).astype(bf16)


def travel_shape(rows, cols):
    return (16, cols * 5 // 4) if tiles_of(rows, cols) else (rows, cols)


def pack_kernel(count, cols, *refs):
    pieces, forward = refs[:count], refs[count : (len(refs) - 1 + count) // 2]
    out, copies = refs[len(pieces) + len(forward)], refs[len(pieces) + len(forward) + 1 :]
    rows = out.shape[0] // count
    main = whole_tiles(rows)
    for i, piece in enumerate(pieces):
        if main:
            out[i * main : (i + 1) * main] = piece[:main, :cols]
    if tiles_of(rows, cols):
        quarter = cols // 4
        rest = [piece[:, cols:].astype(f32) for piece in pieces]
        for k in range(4):
            out[main * count :, k * quarter : (k + 1) * quarter] = jnp.concatenate(
                [r[4 * k : 4 * k + 4] for r in rest], axis=0
            ).astype(bf16)
    elif rows > main:
        rest = [piece[main:].astype(f32) for piece in pieces]
        out[main * count :] = jnp.concatenate(rest, axis=0).astype(bf16)
    for source, target in zip(forward, copies):
        target[...] = source[...]


def pack(pieces, rows, cols, forward=(), after=()):
    count = len(pieces)
    outs = [shaped((rows * count, cols), bf16)] + [shaped(f.shape, f.dtype) for f in forward]
    return call(
        functools.partial(pack_kernel, count, cols), outs, [*pieces, *forward], us=1, after=after
    )


def far_pieces(shard, n):
    return [shard] + [to_partner(shard, n, (m, m)) for m in far_masks(n)]


def near_pieces(own, n, direct=False):
    first, second = near_pair(n)
    a = to_partner(own, n, (first, second))
    b = to_partner(own, n, (second, first))
    ab = to_partner(own, n, (first | second,) * 2) if direct else to_partner(a, n, (second, first))
    return [own, a, b, ab]


def both_cores(pieces, n):
    return [*pieces, *[to_partner(p, n, (1, 1)) for p in pieces]]


def fold_kernel(mine, got, *outs):
    rows = outs[0].shape[0]
    for i, out in enumerate(outs):
        part = pl.ds(i * rows, rows)
        out[...] = (mine[part].astype(f32) + got[part].astype(f32)).astype(bf16)


def fold(mine, got, parts, after=()):
    rows, cols = mine.shape
    outs = [shaped((rows // parts, cols), bf16)] * parts
    return call(fold_kernel, outs, [mine, got], us=1, after=after)


def split_kernel(count, *refs):
    given, outs = refs[:-count], refs[-count:]
    total = given[0][...].astype(f32)
    for got in given[1:]:
        total = total + got[...].astype(f32)
    rows = total.shape[0] // count
    main = whole_tiles(rows)
    rest, done = rows - main, main * count
    for i, out in enumerate(outs):
        parts = []
        if main:
            parts.append(total[i * main : (i + 1) * main])
        if rest:
            parts.append(total[done + i * rest : done + (i + 1) * rest])
        values = jnp.concatenate(parts, axis=0)
        out[...] = (to_tiles(values) if tiles_of(*values.shape) else values).astype(bf16)


def split(given, count, after=()):
    rows, cols = given[0].shape
    outs = [shaped(travel_shape(rows // count, cols), bf16)] * count
    return call(functools.partial(split_kernel, count), outs, given, us=1.5, after=after)


def core_sum(top, send, n, parts, after=()):
    return fold(top, to_partner(send, n, (1, 1)), parts, after)


def near_sum_direct(pieces, n, after=()):
    first, second = near_pair(n)
    own, a, b, ab = pieces
    got = [
        to_partner(a, n, (first, second)),
        to_partner(b, n, (second, first)),
        to_partner(ab, n, (first | second,) * 2),
    ]
    return split([own, *got], len(far_masks(n)) + 1, after)


def near_sum_first(halves, n, after=()):
    first, second = near_pair(n)
    keep, send = halves
    return fold(keep, to_partner(send, n, (second, first)), 2, after)


def near_sum_second(halves, n, after=()):
    first, second = near_pair(n)
    keep, send = halves
    return split([keep, to_partner(send, n, (first, second))], len(far_masks(n)) + 1, after)


def far_sum_kernel(count, bounds, *refs):
    given, outs = refs[:count], refs[count:]
    total = given[0][...].astype(f32)
    for got in given[1:]:
        total = total + got[...].astype(f32)
    rows = outs[0].shape[0]
    cols = bounds[-1]
    if tiles_of(rows, cols):
        quarter = cols // 4
        rest = [total[4 * k : 4 * k + 4, cols:] for k in range(4)]
        total = jnp.concatenate(
            [total[:, :cols], jnp.concatenate(rest, axis=1)], axis=0
        )
    for out, begin, end in zip(outs, bounds[:-1], bounds[1:]):
        out[...] = total[:, begin:end]


def far_sum(pieces, n, rows, bounds, after=()):
    got = [to_partner(p, n, (m, m)) for p, m in zip(pieces[1:], far_masks(n))]
    outs = [shaped((rows, e - b), f32) for b, e in zip(bounds[:-1], bounds[1:])]
    return call(
        functools.partial(far_sum_kernel, len(pieces), bounds), outs, [pieces[0], *got], us=1,
        after=after,
    )


def attend_kernel(x, qk_order, cosine, sine, seg_q, seg_k, *refs):
    pieces = refs[:8]
    hidden, q_raw, k_raw, q_out, k_out, v_out, probs, o, gains, qk_gain = refs[8:]
    rows = q_raw.shape[0]
    w_q = join_rows(pieces, slice(0, 1024))
    w_kv = join_rows(pieces, slice(1024, 1536))
    gain_rows = join_rows(pieces, slice(1536, 1664)).astype(f32).T[:8]
    gains[...] = gain_rows
    gain_qk = nn(gain_rows.astype(bf16), qk_order[...])
    qk_gain[...] = gain_qk
    gain_q, gain_k = gain_qk[4:5, :HD], gain_qk[4:5, HD:]
    for c in range(2 * rows // 256):
        part = pl.ds(c * 256, 256)
        xs = x[part].astype(f32)
        hs = (xs * inverse_rms(xs) * gain_rows[0:1]).astype(bf16)
        hidden[part] = hs
        cs, sn = cosine[part], sine[part]
        kv = nn(hs, w_kv)
        raw = kv[:, :HD]
        k_raw[part] = raw
        k_out[part] = rotate(raw * inverse_rms(raw) * gain_k, cs, sn).astype(bf16)
        v_out[part] = kv[:, HD:].astype(bf16)
        if c * 256 >= rows:
            own = pl.ds(c * 256 - rows, 256)
            qs = nn(hs, w_q)
            q_raw[own] = qs
            for h in range(H):
                raw = qs[:, h * HD : (h + 1) * HD]
                q_out[own, h * HD : (h + 1) * HD] = rotate(
                    raw * inverse_rms(raw) * gain_q, cs, sn
                ).astype(bf16)
    for b in range(rows // BLOCK):
        mine = pl.ds(b * BLOCK, BLOCK)
        reach = pl.ds(b * BLOCK, REACH)
        q_rows = q_out[mine] * bf16(1.0 / 16.0)
        q_stack = jnp.concatenate([q_rows[:, h * HD : (h + 1) * HD] for h in range(H)], axis=0)
        scores = nt(q_stack, k_out[reach])
        i = lax.broadcasted_iota(jnp.int32, (BLOCK, REACH), 0)
        j = lax.broadcasted_iota(jnp.int32, (BLOCK, REACH), 1)
        allowed = (j > i) & (j <= i + WINDOW) & (seg_q[mine] == seg_k[b])
        allowed = jnp.concatenate([allowed.astype(f32)] * H, axis=0)
        weights = jnp.exp(scores) * allowed
        total = jnp.sum(weights, axis=-1, keepdims=True)
        p = (weights * (1.0 / total)).astype(bf16)
        probs[b] = p
        out = nn(p, v_out[reach])
        for h in range(H):
            o[mine, h * HD : (h + 1) * HD] = out[h * BLOCK : (h + 1) * BLOCK].astype(bf16)


def attend(x, pieces, qk_order, cosine, sine, seg_q, seg_k, after):
    rows = x.shape[0] // 2
    width = x.shape[1]
    return call(
        attend_kernel,
        [
            shaped((2 * rows, width), bf16),
            shaped((rows, H * HD), f32),
            shaped((2 * rows, HD), f32),
            shaped((rows, H * HD), bf16),
            shaped((2 * rows, HD), bf16),
            shaped((2 * rows, HD), bf16),
            shaped((rows // BLOCK, H * BLOCK, REACH), bf16),
            shaped((rows, H * HD), bf16),
            shaped((8, width), f32),
            shaped((8, 2 * HD), f32),
        ],
        [x, qk_order, cosine, sine, seg_q, seg_k, *pieces],
        us=8,
        after=after,
    )


def gelu_parts(g):
    c0, c1 = 0.7978845608028654, 0.044715
    square = g * g
    t = jnp.tanh(c0 * g * (1.0 + c1 * square))
    value = 0.5 * g * (1.0 + t)
    slope = 0.5 * (1.0 + t) + 0.5 * g * (1.0 - t * t) * c0 * (1.0 + 3.0 * c1 * square)
    return value, slope


def feed_kernel(o, x, gains, *refs):
    pieces = refs[:8]
    a_out, middle, normed, product, by_gate, by_up = refs[8:]
    rows, ff = product.shape
    w_o = join_rows(pieces, slice(0, H * HD))
    for c in range(rows // 256):
        part = pl.ds(c * 256, 256)
        a = nt(o[part], w_o)
        a_out[part] = a
        x1 = x[rows + c * 256 : rows + (c + 1) * 256].astype(f32) + a * inverse_rms(a) * gains[1:2]
        middle[part] = x1
        normed[part] = (x1 * inverse_rms(x1) * gains[2:3]).astype(bf16)
    for j in range(ff // FF_CHUNK):
        cols = slice(j * FF_CHUNK, (j + 1) * FF_CHUNK)
        w_g = join_rows(pieces, slice(H * HD + cols.start, H * HD + cols.stop))
        w_u = join_rows(pieces, slice(H * HD + ff + cols.start, H * HD + ff + cols.stop))
        for c in range(rows // 256):
            part = pl.ds(c * 256, 256)
            h2 = normed[part]
            g = nn(h2, w_g)
            u = nn(h2, w_u)
            value, slope = gelu_parts(g)
            product[part, cols] = (value * u).astype(bf16)
            by_gate[part, cols] = (slope * u).astype(bf16)
            by_up[part, cols] = value.astype(bf16)


def feed(o, pieces, x, gains, after):
    rows, width = o.shape[0], x.shape[1]
    ff = (pieces[0].shape[1] - H * HD) // 2
    return call(
        feed_kernel,
        [
            shaped((rows, width), f32),
            shaped((rows, width), f32),
            shaped((rows, width), bf16),
            shaped((rows, ff), bf16),
            shaped((rows, ff), bf16),
            shaped((rows, ff), bf16),
        ],
        [o, x, gains, *pieces],
        us=6,
        after=after,
    )


def turn_kernel(product, middle, dy, gains, order, *refs):
    pieces = refs[:8]
    mixed, low, gain_grad, grad_top, grad_send = refs[8:]
    half, ff = grad_top.shape
    w_d = join_rows(pieces)
    total = jnp.zeros((1, dy.shape[1]), f32)
    for c in range(dy.shape[0] // 256):
        part = pl.ds(c * 256, 256)
        f = nt(product[part], w_d)
        grad = dy[part].astype(f32)
        y = middle[part] + f * inverse_rms(f) * gains[3:4]
        mixed[part] = nt(y.astype(bf16), order[...]).astype(bf16)
        df, dgain = rms_back(f, gains[3:4], grad)
        low[part] = df.astype(bf16)
        total = total + dgain
    gain_grad[...] = jnp.broadcast_to(total, gain_grad.shape)
    for j in range(ff // FF_CHUNK):
        cols = slice(j * FF_CHUNK, (j + 1) * FF_CHUNK)
        grad = tn(low[...], product[:, cols]).astype(bf16)
        grad_top[:, cols] = grad[:half]
        grad_send[:, cols] = grad[half:]


def turn(product, pieces, middle, dy, gains, order):
    rows, width = middle.shape
    half, ff = width // 2, product.shape[1]
    return call(
        turn_kernel,
        [
            shaped((rows, width), bf16),
            shaped((rows, width), bf16),
            shaped((8, width), f32),
            shaped((half, ff), bf16),
            shaped((half, ff), bf16),
        ],
        [product, middle, dy, gains, order, *pieces],
        us=6,
    )


def feed_back_kernel(low, by_gate, by_up, normed, *refs):
    pieces = refs[:8]
    gate_low, up_low, top, send = refs[8:]
    half = top.shape[0]
    rows, ff = gate_low.shape
    for j in range(ff // FF_CHUNK):
        cols = slice(j * FF_CHUNK, (j + 1) * FF_CHUNK)
        w_d = join_rows(pieces, cols)
        for c in range(rows // 256):
            part = pl.ds(c * 256, 256)
            dm = nn(low[part], w_d)
            gate_low[part, cols] = (dm * by_gate[part, cols].astype(f32)).astype(bf16)
            up_low[part, cols] = (dm * by_up[part, cols].astype(f32)).astype(bf16)
        for source, shift in ((gate_low, 0), (up_low, ff)):
            grad = tn(normed[...], source[:, cols]).astype(bf16)
            out = slice(shift + cols.start, shift + cols.stop)
            top[:, out] = grad[:half]
            send[:, out] = grad[half:]


def feed_back(low, pieces, by_gate, by_up, normed):
    rows, width = low.shape
    half, ff = width // 2, by_gate.shape[1]
    return call(
        feed_back_kernel,
        [shaped((rows, ff), bf16)] * 2 + [shaped((half, 2 * ff), bf16)] * 2,
        [low, by_gate, by_up, normed, *pieces],
        us=7,
    )


def middle_back_kernel(gate_low, up_low, middle, a, dy, gains, *refs):
    pieces = refs[:8]
    dx1, gain_grad, attn_low, do = refs[8:]
    rows, ff = gate_low.shape
    w_o = join_rows(pieces, slice(0, H * HD))
    w_g = join_rows(pieces, slice(H * HD, H * HD + ff))
    w_u = join_rows(pieces, slice(H * HD + ff, H * HD + 2 * ff))
    sum1 = jnp.zeros((1, dy.shape[1]), f32)
    sum2 = jnp.zeros((1, dy.shape[1]), f32)
    for c in range(rows // 256):
        part = pl.ds(c * 256, 256)
        grad = nt(gate_low[part], w_g) + nt(up_low[part], w_u)
        back, dgain2 = rms_back(middle[part], gains[2:3], grad)
        dx = dy[part].astype(f32) + back
        dx1[part] = dx
        da, dgain1 = rms_back(a[part], gains[1:2], dx)
        low = da.astype(bf16)
        attn_low[part] = low
        do[part] = nn(low, w_o).astype(bf16)
        sum1, sum2 = sum1 + dgain1, sum2 + dgain2
    gain_grad[...] = jnp.concatenate([sum1, sum2, jnp.zeros((6, dy.shape[1]), f32)], axis=0)


def middle_back(gate_low, up_low, pieces, middle, a, dy, gains, after):
    rows, width = middle.shape
    return call(
        middle_back_kernel,
        [
            shaped((rows, width), f32),
            shaped((8, width), f32),
            shaped((rows, width), bf16),
            shaped((rows, H * HD), bf16),
        ],
        [gate_low, up_low, middle, a, dy, gains, *pieces],
        us=6,
        after=after,
        room=16,
    )


def attend_back_kernel(
    probs, do, q, k, v, q_raw, k_raw, cosine, sine, qk_gain, hidden, x, o, attn_low,
    qk_order, gain3, gain12, *refs
):
    pieces = refs[:8]
    top, send, dh, dk, dv, dq_low, dkv_low = refs[8:]
    rows = q_raw.shape[0]
    half = top.shape[0]
    dk[...] = jnp.zeros_like(dk)
    dv[...] = jnp.zeros_like(dv)
    gain_q, gain_k = qk_gain[4:5, :HD], qk_gain[4:5, HD:]
    sum_q = jnp.zeros((1, HD), f32)
    for b in range(rows // BLOCK):
        mine = pl.ds(b * BLOCK, BLOCK)
        reach = pl.ds(b * BLOCK, REACH)
        keys, values = k[reach], v[reach]
        do_rows, q_rows = do[mine], q[mine]
        do_stack = jnp.concatenate([do_rows[:, h * HD : (h + 1) * HD] for h in range(H)], axis=0)
        q_stack = jnp.concatenate([q_rows[:, h * HD : (h + 1) * HD] for h in range(H)], axis=0)
        p_low = probs[b]
        p = p_low.astype(f32)
        t = p * nt(do_stack, values)
        ds = (t - p * jnp.sum(t, axis=-1, keepdims=True)).astype(bf16)
        dk[reach] += tn(ds, q_stack)
        dv[reach] += tn(p_low, do_stack)
        dq = nn(ds, keys) * (1.0 / 16.0)
        own = pl.ds(rows + b * BLOCK, BLOCK)
        cs, sn = cosine[own], sine[own]
        for h in range(H):
            grad = rotate_back(dq[h * BLOCK : (h + 1) * BLOCK], cs, sn)
            back, dgain = rms_back(q_raw[mine, h * HD : (h + 1) * HD], gain_q, grad)
            dq_low[mine, h * HD : (h + 1) * HD] = back.astype(bf16)
            sum_q = sum_q + dgain
    sum_k = jnp.zeros((1, HD), f32)
    for c in range(2 * rows // 256):
        part = pl.ds(c * 256, 256)
        grad = rotate_back(dk[part] * (1.0 / 16.0), cosine[part], sine[part])
        back, dgain = rms_back(k_raw[part], gain_k, grad)
        dkv_low[part, :HD] = back.astype(bf16)
        dkv_low[part, HD:] = dv[part].astype(bf16)
        sum_k = sum_k + dgain
    gq = tn(hidden[rows:], dq_low[...]).astype(bf16)
    top[:, :1024] = gq[:half]
    send[:, :1024] = gq[half:]
    gkv = tn(hidden[...], dkv_low[...]).astype(bf16)
    top[:, 1024:1536] = gkv[:half]
    send[:, 1024:1536] = gkv[half:]
    w_q = join_rows(pieces, slice(0, 1024))
    w_kv = join_rows(pieces, slice(1024, 1536))
    sum0 = jnp.zeros((1, x.shape[1]), f32)
    for c in range(2 * rows // 256):
        part = pl.ds(c * 256, 256)
        grad = nt(dkv_low[part], w_kv)
        if c * 256 >= rows:
            grad = grad + nt(dq_low[c * 256 - rows : c * 256 - rows + 256], w_q)
        dh[part] = grad
        xs = x[part].astype(f32)
        sum0 = sum0 + jnp.sum(grad * (xs * inverse_rms(xs)), axis=0, keepdims=True)
    qk = jnp.concatenate([sum_q, sum_k], axis=1)
    qk = jnp.broadcast_to(qk, (8, 2 * HD)).astype(bf16)
    qk_spread = nt(qk, qk_order[...])
    rows_of = jnp.concatenate(
        [
            sum0, gain12[0:1], gain12[1:2], gain3[0:1], qk_spread[0:1],
            jnp.zeros((EXTRA - 5, x.shape[1]), f32),
        ],
        axis=0,
    )
    cols_of = rows_of.T.astype(bf16)
    top[:, 1536:1664] = cols_of[:half]
    send[:, 1536:1664] = cols_of[half:]
    go = tn(attn_low[...], o[...]).astype(bf16)
    top[:, 1664:] = go[:half]
    send[:, 1664:] = go[half:]


def attend_back(
    probs, do, q, k, v, q_raw, k_raw, cosine, sine, qk_gain, hidden, x, o, attn_low,
    qk_order, gain3, gain12, pieces, after,
):
    rows = q.shape[0]
    width = x.shape[1]
    grads = (width // 2, pieces[0].shape[1] + H * HD)
    return call(
        attend_back_kernel,
        [shaped(grads, bf16)] * 2 + [shaped((2 * rows, width), f32)],
        [
            probs, do, q, k, v, q_raw, k_raw, cosine, sine, qk_gain, hidden, x, o, attn_low,
            qk_order, gain3, gain12, *pieces,
        ],
        us=12,
        scratch=[
            pltpu.VMEM((2 * rows, HD), f32),
            pltpu.VMEM((2 * rows, HD), f32),
            pltpu.VMEM((rows, H * HD), bf16),
            pltpu.VMEM((2 * rows, 2 * HD), bf16),
        ],
        after=after,
        room=16,
    )


def input_back_kernel(dh, x, gains, dx1, order, own, before):
    rows = dx1.shape[0]
    table = order[...]
    for c in range(2 * rows // 256):
        part = pl.ds(c * 256, 256)
        back, _ = rms_back(x[part].astype(f32), gains[0:1], dh[part])
        if c * 256 < rows:
            before[part] = nt(back.astype(bf16), table).astype(bf16)
        else:
            mine = pl.ds(c * 256 - rows, 256)
            rest = back + dx1[mine]
            total = jnp.zeros_like(rest)
            for _ in range(3):
                piece = rest.astype(bf16)
                rest = rest - piece.astype(f32)
                total = total + nt(piece, table)
            own[mine] = total


def input_back(dh, x, gains, dx1, order, after=()):
    rows, width = dx1.shape
    return call(
        input_back_kernel,
        [shaped((rows, width), f32), shaped((rows, width), bf16)],
        [dh, x, gains, dx1, order],
        us=2,
        after=after,
    )


def on_device(
    tokens,
    segment_ids,
    w_query,
    w_key,
    w_value,
    w_output,
    w_gate,
    w_up,
    w_down,
    norm_gains,
    qk_gains,
    cotangent,
):
    n = lax.axis_size("seq")
    me = lax.axis_index("seq")
    rows, width = tokens.shape
    shard = w_query.shape[0]
    qk_shard = qk_gains.shape[0]

    extra = jnp.concatenate(
        [
            norm_gains.T,
            jnp.pad(qk_gains, (0, shard - qk_shard))[:, None],
            jnp.zeros((shard, EXTRA - 5), bf16),
        ],
        axis=1,
    )
    shard_a = jnp.concatenate([w_query, w_key, w_value, extra], axis=1)
    shard_b = jnp.concatenate([w_output.T, w_gate, w_up], axis=1)
    shard_c = w_down.T

    even, odd, inner = row_table(n, shard)
    device = me ^ jnp.where(me & 1 == 0, jnp.asarray(even), jnp.asarray(odd))
    place = device * shard + inner
    order = (jnp.arange(width, dtype=jnp.int32)[:, None] == place[None, :]).astype(bf16)
    qk_place = jnp.where(inner < qk_shard, device * qk_shard + inner, -1)
    qk_order = (qk_place[:, None] == jnp.arange(2 * HD, dtype=jnp.int32)[None, :]).astype(bf16)

    padded = jnp.concatenate([jnp.full((LONGEST + rows,), -1, jnp.int32), segment_ids])
    nearby = lax.dynamic_slice_in_dim(padded, me * rows, 2 * rows + LONGEST)
    keys_segment = nearby[LONGEST:]
    ahead = (jnp.arange(2 * rows) + LONGEST)[:, None] > jnp.arange(2 * rows + LONGEST)[None, :]
    positions = jnp.sum(
        ((keys_segment[:, None] == nearby[None, :]) & ahead).astype(jnp.int32), axis=1
    )
    freqs = 10000.0 ** (-2.0 * jnp.arange(HD // 2, dtype=f32) / HD)
    angles = positions.astype(f32)[:, None] * freqs[None, :]
    cosine, sine = jnp.cos(angles), jnp.sin(angles)
    seg_q = keys_segment[rows:, None]
    seg_k = jnp.stack(
        [keys_segment[b * BLOCK : b * BLOCK + REACH] for b in range(rows // BLOCK)]
    )[:, None, :]

    tokens_before = lax.ppermute(tokens, "seq", [(i, i + 1) for i in range(n - 1)])
    travel_b, travel_c = call(
        tile_kernel,
        [shaped(travel_shape(*w.shape), bf16) for w in (shard_b, shard_c)],
        [shard_b, shard_c],
        us=1,
    )
    own_a, travel_b = pack(
        far_pieces(shard_a, n), *shard_a.shape, [travel_b], after=(seg_q, seg_k, qk_order)
    )
    weights_a = both_cores(near_pieces(own_a, n, direct=True), n)
    x = nn(jnp.concatenate([tokens_before, tokens], axis=0), order).astype(bf16)
    dy = nn(cotangent, order).astype(bf16)
    own_b, travel_c = pack(
        far_pieces(travel_b, n), *shard_b.shape, [travel_c],
        after=(x, dy, cosine, sine, *weights_a[1:]),
    )
    weights_b = both_cores(near_pieces(own_b, n), n)
    hidden, q_raw, k_raw, q, k, v, probs, o, gains, qk_gain = attend(
        x, weights_a, qk_order, cosine, sine, seg_q, seg_k, after=(own_b,)
    )
    (own_c,) = pack(far_pieces(travel_c, n), *shard_c.shape, after=(o, weights_b[1]))
    weights_c = both_cores(near_pieces(own_c, n, direct=True), n)
    a, middle, normed, product, by_gate, by_up = feed(
        o, weights_b, x, gains, after=weights_c[1:4]
    )
    mixed, low, gain3, gd_top, gd_send = turn(product, weights_c, middle, dy, gains, order)
    gate_low, up_low, gf_top, gf_send = feed_back(low, weights_c, by_gate, by_up, normed)
    sum_d = core_sum(gd_top, gd_send, n, 4, after=(gate_low,))
    sum_f = core_sum(gf_top, gf_send, n, 2, after=sum_d[:1])
    dx1, gain12, attn_low, do = middle_back(
        gate_low, up_low, weights_b, middle, a, dy, gains, after=sum_f[:1]
    )
    sum_d = near_sum_direct(sum_d, n, after=(do,))
    sum_f = near_sum_first(sum_f, n, after=sum_d[:1])
    ga_top, ga_send, dh = attend_back(
        probs, do, q, k, v, q_raw, k_raw, cosine, sine, qk_gain, hidden, x, o, attn_low,
        qk_order, gain3, gain12, weights_a, after=sum_f[:1],
    )
    (sum_d,) = far_sum(sum_d, n, shard, (0, gd_top.shape[1]), after=(dh,))
    sum_a = core_sum(ga_top, ga_send, n, 4, after=(sum_d,))
    sum_f = near_sum_second(sum_f, n, after=sum_a[:1])
    own, before = input_back(dh, x, gains, dx1, order, after=sum_f[:1])
    behind = lax.ppermute(before, "seq", [(i + 1, i) for i in range(n - 1)])
    sum_a = near_sum_direct(sum_a, n, after=(own,))
    half = gf_top.shape[1] // 2
    sum_g, sum_u = far_sum(sum_f, n, shard, (0, half, 2 * half), after=sum_a[:1])
    input_grad = own + behind.astype(f32)
    sum_q, sum_k, sum_v, sum_n, sum_o = far_sum(sum_a, n, shard, (0, 1024, 1280, 1536, 1664, 2688))
    return (
        mixed,
        input_grad,
        sum_q,
        sum_k,
        sum_v,
        sum_o.T,
        sum_g,
        sum_u,
        sum_d.T,
        sum_n[:, :4].T,
        sum_n[:qk_shard, 4],
    )


def solution(mesh):
    return jax.shard_map(
        on_device,
        mesh=mesh,
        in_specs=(
            P("seq", None),
            P(),
            P("seq", None),
            P("seq", None),
            P("seq", None),
            P(None, "seq"),
            P("seq", None),
            P("seq", None),
            P(None, "seq"),
            P(None, "seq"),
            P("seq"),
            P("seq", None),
        ),
        out_specs=(
            P("seq", None),
            P("seq", None),
            P("seq", None),
            P("seq", None),
            P("seq", None),
            P(None, "seq"),
            P("seq", None),
            P("seq", None),
            P(None, "seq"),
            P(None, "seq"),
            P("seq"),
        ),
        check_vma=False,
    )
```

```python
import functools

import jax
import jax.numpy as jnp
import numpy as np
from jax import lax
from jax.experimental import pallas as pl
from jax.experimental.pallas import tpu as pltpu
from jax.sharding import PartitionSpec as P

H = 4
HD = 256
WINDOW = 512
LONGEST = 2048
EXTRA = 128
FF_CHUNK = 512
BLOCK = 128
REACH = BLOCK + WINDOW
MIB = 1024 * 1024

epsilon = 1e-06
bf16 = jnp.bfloat16
f32 = jnp.float32


def far_bits(n):
    bits = [1 << i for i in range(n.bit_length() - 1)]
    rest = [b for b in bits[1:] if b not in near_pair(n)]
    return rest, rest[::-1]


def far_slots(bits):
    slots = [0]
    for b in bits:
        slots = slots + [s | b for s in slots]
    return slots


def near_pair(n):
    return (2, 8) if n > 64 else (2, 4)


def to_partner(x, n, masks):
    return lax.ppermute(x, "seq", [(i, i ^ masks[i & 1]) for i in range(n)])


def row_table(n, shard):
    first, second = near_pair(n)
    main = whole_tiles(shard)
    count = n // 8
    inner = [(i, r) for i in range(count) for r in range(main)]
    inner += [(i, r) for i in range(count) for r in range(main, shard)]

    def offsets(a, b, bits):
        far = far_slots(bits)
        return [m ^ far[i] for m in (0, a, b, a | b) for i, _ in inner]

    even_bits, odd_bits = far_bits(n)
    even, odd = offsets(first, second, even_bits), offsets(second, first, odd_bits)
    return (
        np.array(even + [1 ^ m for m in odd], np.int32),
        np.array(odd + [1 ^ m for m in even], np.int32),
        np.array([r for _, r in inner] * 8, np.int32),
    )


def nn(left, right):
    return jnp.dot(left, right, preferred_element_type=f32)


def tn(left, right):
    return lax.dot_general(left, right, (((0,), (0,)), ((), ())), preferred_element_type=f32)


def nt(left, right):
    return lax.dot_general(left, right, (((1,), (1,)), ((), ())), preferred_element_type=f32)


def inverse_rms(values):
    return lax.rsqrt(jnp.mean(values * values, axis=-1, keepdims=True) + epsilon)


def rms_back(values, gain, grad):
    scale = inverse_rms(values)
    hat = values * scale
    inner = grad * gain
    mean = jnp.mean(inner * hat, axis=-1, keepdims=True)
    return scale * (inner - hat * mean), jnp.sum(grad * hat, axis=0, keepdims=True)


def rotate(values, cosine, sine):
    half = values.shape[-1] // 2
    a, b = values[:, :half], values[:, half:]
    return jnp.concatenate([a * cosine - b * sine, b * cosine + a * sine], axis=-1)


def rotate_back(values, cosine, sine):
    half = values.shape[-1] // 2
    a, b = values[:, :half], values[:, half:]
    return jnp.concatenate([a * cosine + b * sine, b * cosine - a * sine], axis=-1)


def call(kernel, outs, args, us, scratch=(), after=(), room=12):
    given, extra = len(args), len(after)

    def body(*refs):
        kernel(*refs[:given], *refs[given + extra :])

    return pl.pallas_call(
        body,
        in_specs=[pl.BlockSpec(memory_space=pltpu.VMEM)] * given
        + [pl.BlockSpec(memory_space=pl.ANY)] * extra,
        out_specs=[pl.BlockSpec(memory_space=pltpu.VMEM)] * len(outs),
        out_shape=outs,
        scratch_shapes=scratch,
        compiler_params=pltpu.CompilerParams(vmem_limit_bytes=room * MIB),
        cost_estimate=pl.CostEstimate(
            flops=int(us * 10**9), bytes_accessed=int(us * 10**6), transcendentals=0
        ),
    )(*args, *after)


def shaped(shape, dtype):
    return jax.ShapeDtypeStruct(shape, dtype)


def join_rows(parts, cols=slice(None)):
    return jnp.concatenate([p[:, cols] for p in parts], axis=0)


def whole_tiles(rows):
    return rows // 16 * 16


def padded(cols):
    return -(-cols // 512) * 512


def in_tiles(rows):
    return rows == 20


def travel_shape(rows, cols):
    return (16, padded(cols) * 5 // 4) if in_tiles(rows) else (rows, cols)


def to_tiles(values):
    rows, cols = values.shape
    if not in_tiles(rows):
        return values
    wide = padded(cols)
    if wide > cols:
        values = jnp.concatenate([values, jnp.zeros((rows, wide - cols), f32)], axis=1)
    quarter = wide // 4
    rest = [values[16:, k * quarter : (k + 1) * quarter] for k in range(4)]
    return jnp.concatenate([values[:16], jnp.concatenate(rest, axis=0)], axis=1)


def tile_kernel(*refs):
    half = len(refs) // 2
    for source, out in zip(refs[:half], refs[half:]):
        out[...] = to_tiles(source[...].astype(f32)).astype(bf16)


def stack_kernel(*refs):
    count = len(refs) // 3
    for i in range(count):
        a, b, out = refs[2 * i], refs[2 * i + 1], refs[2 * count + i]
        rows = a.shape[0]
        if rows % 16 == 0:
            out[:rows] = a[...]
            out[rows:] = b[...]
        else:
            both = [a[...].astype(f32), b[...].astype(f32)]
            out[...] = jnp.concatenate(both, axis=0).astype(bf16)


def stack(*pairs, after=()):
    outs = [shaped((2 * a.shape[0], a.shape[1]), bf16) for a, _ in pairs]
    return call(stack_kernel, outs, [x for pair in pairs for x in pair], us=0.5, after=after)


def pack_kernel(pieces, blocks, out):
    count = len(pieces)
    share, cols = out.shape[0] // blocks, out.shape[1]
    rows = share // count
    main = whole_tiles(rows)
    height, wide = travel_shape(rows, cols)
    quarter = padded(cols) // 4
    for block in range(blocks):
        at = block * share
        starts = [(ref, begin + block * height) for ref, begin in pieces]
        if main:
            for i, (ref, begin) in enumerate(starts):
                out[at + i * main : at + (i + 1) * main] = ref[begin : begin + main, :cols]
        at = at + main * count
        if in_tiles(rows):
            rest = [ref[begin : begin + 16, 4 * quarter :].astype(f32) for ref, begin in starts]
            for k in range(4):
                end = min((k + 1) * quarter, cols)
                part = jnp.concatenate([r[4 * k : 4 * k + 4] for r in rest], axis=0)
                out[at : at + 4 * count, k * quarter : end] = part[:, : end - k * quarter].astype(
                    bf16
                )
        elif rows > main:
            rest = [
                ref[...].astype(f32)[begin + main : begin + rows] for ref, begin in starts
            ]
            out[at : at + (rows - main) * count] = jnp.concatenate(rest, axis=0).astype(bf16)


def pack(arrays, rows, cols, blocks, n, parts=1, after=()):
    count = n // 8
    height = travel_shape(rows, cols)[0] * blocks
    held = count // len(arrays)
    total = rows * count * blocks

    def kernel(*refs):
        given = refs[: len(arrays)]
        pieces = [(ref, h * height) for ref in given for h in range(held)]
        if parts == 1:
            pack_kernel(pieces, blocks, refs[-1])
        else:
            for block, out in enumerate(refs[len(arrays) :]):
                shift = block * height // blocks
                pack_kernel([(ref, at + shift) for ref, at in pieces], 1, out)

    outs = [shaped((total // parts, cols), bf16)] * parts
    return call(kernel, outs, arrays, us=1, after=after)


def far_step(block, n, step):
    even, odd = far_bits(n)
    return to_partner(block, n, (even[step], odd[step]))


def far_direct(block, n):
    even, odd = far_bits(n)
    slots = zip(far_slots(even)[1:], far_slots(odd)[1:])
    return [block] + [to_partner(block, n, masks) for masks in slots]


def start_kernel(a, b, given, out, copy):
    stack_kernel(a, b, out)
    copy[...] = given[...]


def hold_kernel(*refs):
    half = len(refs) // 2
    for value, out in zip(refs[:half], refs[half:]):
        out[...] = value[...]


def hold(*values, after):
    return call(hold_kernel, [shaped(v.shape, v.dtype) for v in values], values, 0.2, after=after)


def far_gather(blocks, n, joins):
    steps = len(far_bits(n)[0])
    for k in range(steps - 1):
        got = [far_step(b, n, k) for b in blocks]
        blocks = stack(*zip(blocks, got), after=joins[k] if k < len(joins) else ())
    return [(b, far_step(b, n, steps - 1)) for b in blocks]


def to_first(x, n):
    first, second = near_pair(n)
    return to_partner(x, n, (first, second))


def to_second(x, n):
    first, second = near_pair(n)
    return to_partner(x, n, (second, first))


def to_core(pieces, n):
    return [to_partner(p, n, (1, 1)) for p in pieces]


def fold_kernel(count, *refs):
    given, outs = refs[:count], refs[count:]
    mine, got = given[0], given[1:]
    rows = outs[0].shape[0]
    height = got[0].shape[0]
    if rows % 16 == 0 and height % rows == 0:
        per = height // rows
        for i, out in enumerate(outs):
            other = got[i // per][(i % per) * rows : (i % per + 1) * rows]
            part = mine[i * rows : (i + 1) * rows]
            out[...] = (part.astype(f32) + other.astype(f32)).astype(bf16)
    else:
        total = mine[...].astype(f32)
        total = total + jnp.concatenate([g[...].astype(f32) for g in got], axis=0)
        for i, out in enumerate(outs):
            out[...] = total[i * rows : (i + 1) * rows].astype(bf16)


def fold(mine, got, after=()):
    rows, cols = mine.shape
    outs = [shaped((rows // 2, cols), bf16)] * 2
    kernel = functools.partial(fold_kernel, 1 + len(got))
    return call(kernel, outs, [mine, *got], us=0.7, after=after)


def wide_fold_kernel(mine, *refs):
    got, (keep, send) = refs[:-2], refs[-2:]
    rows = got[0].shape[0]
    per = keep.shape[0] // rows
    for i, other in enumerate(got):
        out = keep if i < per else send
        at = (i % per) * rows
        part = mine[i * rows : (i + 1) * rows].astype(f32)
        out[at : at + rows] = (part + other[...].astype(f32)).astype(bf16)


def core_sum(top, sends, n, after=()):
    rows, cols = top.shape
    outs = [shaped((rows // 2, cols), bf16)] * 2
    return call(wide_fold_kernel, outs, [top, *to_core(sends, n)], us=0.7, after=after)


def core_sum_by_far(top, sends, n, after=()):
    rows, cols = top.shape
    count, blocks = n // 8, len(sends)
    shard = rows // blocks // count
    main = whole_tiles(shard)
    rest, done = shard - main, main * count
    height, wide = travel_shape(shard, cols)

    def kernel(mine, *refs):
        got, (keep, send) = refs[:-2], refs[-2:]
        share = rows // blocks
        tiles = []
        for block in range(blocks):
            total = mine[block * share : (block + 1) * share].astype(f32) + got[block][...].astype(
                f32
            )
            for i in range(count):
                parts = []
                if main:
                    parts.append(total[i * main : (i + 1) * main])
                if rest:
                    parts.append(total[done + i * rest : done + (i + 1) * rest])
                tiles.append((i, block, to_tiles(jnp.concatenate(parts, axis=0))))
        tiles = [t for _, _, t in sorted(tiles, key=lambda item: item[:2])]
        half = len(tiles) // 2
        keep[...] = jnp.concatenate(tiles[:half], axis=0).astype(bf16)
        send[...] = jnp.concatenate(tiles[half:], axis=0).astype(bf16)

    outs = [shaped((count // 2 * blocks * height, wide), bf16)] * 2
    return call(kernel, outs, [top, *to_core(sends, n)], us=1.5, after=after)


def far_fold(halves, n, step, after=()):
    keep, send = halves
    return fold(keep, [far_step(send, n, step)], after)


def near_sum_last(halves, n, shard, cuts, after=()):
    keep, send = halves
    outs = [shaped((shard, e - b), f32) for b, e in zip(cuts[:-1], cuts[1:])]
    return call(
        functools.partial(far_sum_kernel, cuts), outs, [keep, to_first(send, n)], us=1, after=after
    )


def near_sum_first(halves, n, after=()):
    keep, send = halves
    return fold(keep, [to_second(send, n)], after)


def split_kernel(count, mine, got, keep, send):
    total = mine[...].astype(f32) + got[...].astype(f32)
    rows = total.shape[0] // count
    main = whole_tiles(rows)
    rest, done = rows - main, main * count
    slots = []
    for i in range(count):
        parts = []
        if main:
            parts.append(total[i * main : (i + 1) * main])
        if rest:
            parts.append(total[done + i * rest : done + (i + 1) * rest])
        slots.append(to_tiles(jnp.concatenate(parts, axis=0)))
    keep[...] = jnp.concatenate(slots[: count // 2], axis=0).astype(bf16)
    send[...] = jnp.concatenate(slots[count // 2 :], axis=0).astype(bf16)


def near_sum_second(halves, n, after=()):
    keep, send = halves
    rows, cols = keep.shape
    count = n // 8
    height, wide = travel_shape(rows // count, cols)
    outs = [shaped((count // 2 * height, wide), bf16)] * 2
    return call(
        functools.partial(split_kernel, count), outs, [keep, to_first(send, n)], us=1, after=after
    )


def far_sum_first(halves, n, after=()):
    keep, send = halves
    for k in reversed(range(1, len(far_bits(n)[0]))):
        keep, send = fold(keep, [far_step(send, n, k)], after)
        after = ()
    return keep, send


def far_sum_kernel(cuts, mine, got, *outs):
    total = mine[...].astype(f32) + got[...].astype(f32)
    rows = outs[0].shape[0]
    if in_tiles(rows):
        wide = padded(cuts[-1])
        rest = [total[4 * k : 4 * k + 4, wide:] for k in range(4)]
        total = jnp.concatenate([total[:, :wide], jnp.concatenate(rest, axis=1)], axis=0)
    for out, begin, end in zip(outs, cuts[:-1], cuts[1:]):
        out[...] = total[:, begin:end]


def far_sum_last(halves, n, shard, cuts, after=()):
    keep, send = halves
    outs = [shaped((shard, e - b), f32) for b, e in zip(cuts[:-1], cuts[1:])]
    return call(
        functools.partial(far_sum_kernel, cuts), outs, [keep, far_step(send, n, 0)], us=1,
        after=after,
    )


def attend_kernel(x, qk_order, cosine, sine, seg_q, seg_k, *refs):
    pieces = refs[:-10]
    hidden, q_raw, k_raw, q_out, k_out, v_out, probs, o, gains, qk_gain = refs[-10:]
    rows = q_raw.shape[0]
    w_q = join_rows(pieces, slice(0, 1024))
    w_kv = join_rows(pieces, slice(1024, 1536))
    gain_rows = join_rows(pieces, slice(1536, 1664)).astype(f32).T[:8]
    gains[...] = gain_rows
    gain_qk = nn(gain_rows.astype(bf16), qk_order[...])
    qk_gain[...] = gain_qk
    gain_q, gain_k = gain_qk[4:5, :HD], gain_qk[4:5, HD:]
    for c in range(2 * rows // 256):
        part = pl.ds(c * 256, 256)
        xs = x[part].astype(f32)
        hs = (xs * inverse_rms(xs) * gain_rows[0:1]).astype(bf16)
        hidden[part] = hs
        cs, sn = cosine[part], sine[part]
        kv = nn(hs, w_kv)
        raw = kv[:, :HD]
        k_raw[part] = raw
        k_out[part] = rotate(raw * inverse_rms(raw) * gain_k, cs, sn).astype(bf16)
        v_out[part] = kv[:, HD:].astype(bf16)
        if c * 256 >= rows:
            own = pl.ds(c * 256 - rows, 256)
            qs = nn(hs, w_q)
            q_raw[own] = qs
            for h in range(H):
                raw = qs[:, h * HD : (h + 1) * HD]
                q_out[own, h * HD : (h + 1) * HD] = rotate(
                    raw * inverse_rms(raw) * gain_q, cs, sn
                ).astype(bf16)
    for b in range(rows // BLOCK):
        mine = pl.ds(b * BLOCK, BLOCK)
        reach = pl.ds(b * BLOCK, REACH)
        q_rows = q_out[mine] * bf16(1.0 / 16.0)
        q_stack = jnp.concatenate([q_rows[:, h * HD : (h + 1) * HD] for h in range(H)], axis=0)
        scores = nt(q_stack, k_out[reach])
        i = lax.broadcasted_iota(jnp.int32, (BLOCK, REACH), 0)
        j = lax.broadcasted_iota(jnp.int32, (BLOCK, REACH), 1)
        allowed = (j > i) & (j <= i + WINDOW) & (seg_q[mine] == seg_k[b])
        allowed = jnp.concatenate([allowed.astype(f32)] * H, axis=0)
        weights = jnp.exp(scores) * allowed
        total = jnp.sum(weights, axis=-1, keepdims=True)
        p = (weights * (1.0 / total)).astype(bf16)
        probs[b] = p
        out = nn(p, v_out[reach])
        for h in range(H):
            o[mine, h * HD : (h + 1) * HD] = out[h * BLOCK : (h + 1) * BLOCK].astype(bf16)


def attend(x, pieces, qk_order, cosine, sine, seg_q, seg_k, after):
    rows = x.shape[0] // 2
    width = x.shape[1]
    return call(
        attend_kernel,
        [
            shaped((2 * rows, width), bf16),
            shaped((rows, H * HD), f32),
            shaped((2 * rows, HD), f32),
            shaped((rows, H * HD), bf16),
            shaped((2 * rows, HD), bf16),
            shaped((2 * rows, HD), bf16),
            shaped((rows // BLOCK, H * BLOCK, REACH), bf16),
            shaped((rows, H * HD), bf16),
            shaped((8, width), f32),
            shaped((8, 2 * HD), f32),
        ],
        [x, qk_order, cosine, sine, seg_q, seg_k, *pieces],
        us=8,
        after=after,
    )


def gelu_parts(g):
    c0, c1 = 0.7978845608028654, 0.044715
    square = g * g
    t = jnp.tanh(c0 * g * (1.0 + c1 * square))
    value = 0.5 * g * (1.0 + t)
    slope = 0.5 * (1.0 + t) + 0.5 * g * (1.0 - t * t) * c0 * (1.0 + 3.0 * c1 * square)
    return value, slope


def feed_kernel(o, x, gains, *refs):
    pieces = refs[:-6]
    a_out, middle, normed, product, by_gate, by_up = refs[-6:]
    rows, ff = product.shape
    w_o = join_rows(pieces, slice(0, H * HD))
    for c in range(rows // 256):
        part = pl.ds(c * 256, 256)
        a = nt(o[part], w_o)
        a_out[part] = a
        x1 = x[rows + c * 256 : rows + (c + 1) * 256].astype(f32) + a * inverse_rms(a) * gains[1:2]
        middle[part] = x1
        normed[part] = (x1 * inverse_rms(x1) * gains[2:3]).astype(bf16)
    for j in range(ff // FF_CHUNK):
        cols = slice(j * FF_CHUNK, (j + 1) * FF_CHUNK)
        w_g = join_rows(pieces, slice(H * HD + cols.start, H * HD + cols.stop))
        w_u = join_rows(pieces, slice(H * HD + ff + cols.start, H * HD + ff + cols.stop))
        for c in range(rows // 256):
            part = pl.ds(c * 256, 256)
            h2 = normed[part]
            g = nn(h2, w_g)
            u = nn(h2, w_u)
            value, slope = gelu_parts(g)
            product[part, cols] = (value * u).astype(bf16)
            by_gate[part, cols] = (slope * u).astype(bf16)
            by_up[part, cols] = value.astype(bf16)


def feed(o, pieces, x, gains, after):
    rows, width = o.shape[0], x.shape[1]
    ff = (pieces[0].shape[1] - H * HD) // 2
    return call(
        feed_kernel,
        [
            shaped((rows, width), f32),
            shaped((rows, width), f32),
            shaped((rows, width), bf16),
            shaped((rows, ff), bf16),
            shaped((rows, ff), bf16),
            shaped((rows, ff), bf16),
        ],
        [o, x, gains, *pieces],
        us=6,
        after=after,
    )


def put_grad(grads, cols, values):
    top, *sends = grads
    half = top.shape[0]
    top[:, cols] = values[:half]
    part = half // len(sends)
    for i, send in enumerate(sends):
        send[:, cols] = values[half + i * part : half + (i + 1) * part]


def grad_shapes(width, cols):
    return [shaped((width // 2, cols), bf16)] + [shaped((width // 8, cols), bf16)] * 4


def turn_kernel(product, middle, dy, gains, order, *refs):
    pieces, (mixed, low, gain_grad, *grads) = refs[:-8], refs[-8:]
    ff = product.shape[1]
    w_d = join_rows(pieces)
    total = jnp.zeros((1, dy.shape[1]), f32)
    for c in range(dy.shape[0] // 256):
        part = pl.ds(c * 256, 256)
        f = nt(product[part], w_d)
        grad = dy[part].astype(f32)
        y = middle[part] + f * inverse_rms(f) * gains[3:4]
        mixed[part] = nt(y.astype(bf16), order[...]).astype(bf16)
        df, dgain = rms_back(f, gains[3:4], grad)
        low[part] = df.astype(bf16)
        total = total + dgain
    gain_grad[...] = jnp.broadcast_to(total, gain_grad.shape)
    for j in range(ff // FF_CHUNK):
        cols = slice(j * FF_CHUNK, (j + 1) * FF_CHUNK)
        grad = tn(low[...], product[:, cols]).astype(bf16)
        put_grad(grads, cols, grad)


def turn(product, pieces, middle, dy, gains, order):
    rows, width = middle.shape
    return call(
        turn_kernel,
        [
            shaped((rows, width), bf16),
            shaped((rows, width), bf16),
            shaped((8, width), f32),
            *grad_shapes(width, product.shape[1]),
        ],
        [product, middle, dy, gains, order, *pieces],
        us=6,
    )


def feed_back_kernel(low, by_gate, by_up, normed, *refs):
    pieces, (gate_low, up_low, *grads) = refs[:-7], refs[-7:]
    rows, ff = gate_low.shape
    for j in range(ff // FF_CHUNK):
        cols = slice(j * FF_CHUNK, (j + 1) * FF_CHUNK)
        w_d = join_rows(pieces, cols)
        for c in range(rows // 256):
            part = pl.ds(c * 256, 256)
            dm = nn(low[part], w_d)
            gate_low[part, cols] = (dm * by_gate[part, cols].astype(f32)).astype(bf16)
            up_low[part, cols] = (dm * by_up[part, cols].astype(f32)).astype(bf16)
        for source, shift in ((gate_low, 0), (up_low, ff)):
            grad = tn(normed[...], source[:, cols]).astype(bf16)
            put_grad(grads, slice(shift + cols.start, shift + cols.stop), grad)


def feed_back(low, pieces, by_gate, by_up, normed):
    rows, width = low.shape
    ff = by_gate.shape[1]
    return call(
        feed_back_kernel,
        [shaped((rows, ff), bf16)] * 2 + grad_shapes(width, 2 * ff),
        [low, by_gate, by_up, normed, *pieces],
        us=7,
    )


def middle_back_kernel(gate_low, up_low, middle, a, dy, gains, *refs):
    pieces = refs[:-4]
    dx1, gain_grad, attn_low, do = refs[-4:]
    rows, ff = gate_low.shape
    w_o = join_rows(pieces, slice(0, H * HD))
    w_g = join_rows(pieces, slice(H * HD, H * HD + ff))
    w_u = join_rows(pieces, slice(H * HD + ff, H * HD + 2 * ff))
    sum1 = jnp.zeros((1, dy.shape[1]), f32)
    sum2 = jnp.zeros((1, dy.shape[1]), f32)
    for c in range(rows // 256):
        part = pl.ds(c * 256, 256)
        grad = nt(gate_low[part], w_g) + nt(up_low[part], w_u)
        back, dgain2 = rms_back(middle[part], gains[2:3], grad)
        dx = dy[part].astype(f32) + back
        dx1[part] = dx
        da, dgain1 = rms_back(a[part], gains[1:2], dx)
        low = da.astype(bf16)
        attn_low[part] = low
        do[part] = nn(low, w_o).astype(bf16)
        sum1, sum2 = sum1 + dgain1, sum2 + dgain2
    gain_grad[...] = jnp.concatenate([sum1, sum2, jnp.zeros((6, dy.shape[1]), f32)], axis=0)


def middle_back(gate_low, up_low, pieces, middle, a, dy, gains, after):
    rows, width = middle.shape
    return call(
        middle_back_kernel,
        [
            shaped((rows, width), f32),
            shaped((8, width), f32),
            shaped((rows, width), bf16),
            shaped((rows, H * HD), bf16),
        ],
        [gate_low, up_low, middle, a, dy, gains, *pieces],
        us=6,
        after=after,
        room=16,
    )


def attend_back_kernel(
    probs, do, q, k, v, q_raw, k_raw, cosine, sine, qk_gain, dq_low, dkv_low, qk_grad, dk, dv
):
    rows = q_raw.shape[0]
    dk[...] = jnp.zeros_like(dk)
    dv[...] = jnp.zeros_like(dv)
    gain_q, gain_k = qk_gain[4:5, :HD], qk_gain[4:5, HD:]
    sum_q = jnp.zeros((1, HD), f32)
    for b in range(rows // BLOCK):
        mine = pl.ds(b * BLOCK, BLOCK)
        reach = pl.ds(b * BLOCK, REACH)
        keys, values = k[reach], v[reach]
        do_rows, q_rows = do[mine], q[mine]
        do_stack = jnp.concatenate([do_rows[:, h * HD : (h + 1) * HD] for h in range(H)], axis=0)
        q_stack = jnp.concatenate([q_rows[:, h * HD : (h + 1) * HD] for h in range(H)], axis=0)
        p_low = probs[b]
        p = p_low.astype(f32)
        t = p * nt(do_stack, values)
        ds = (t - p * jnp.sum(t, axis=-1, keepdims=True)).astype(bf16)
        dk[reach] += tn(ds, q_stack)
        dv[reach] += tn(p_low, do_stack)
        dq = nn(ds, keys) * (1.0 / 16.0)
        own = pl.ds(rows + b * BLOCK, BLOCK)
        cs, sn = cosine[own], sine[own]
        for h in range(H):
            grad = rotate_back(dq[h * BLOCK : (h + 1) * BLOCK], cs, sn)
            back, dgain = rms_back(q_raw[mine, h * HD : (h + 1) * HD], gain_q, grad)
            dq_low[mine, h * HD : (h + 1) * HD] = back.astype(bf16)
            sum_q = sum_q + dgain
    sum_k = jnp.zeros((1, HD), f32)
    for c in range(2 * rows // 256):
        part = pl.ds(c * 256, 256)
        grad = rotate_back(dk[part] * (1.0 / 16.0), cosine[part], sine[part])
        back, dgain = rms_back(k_raw[part], gain_k, grad)
        dkv_low[part, :HD] = back.astype(bf16)
        dkv_low[part, HD:] = dv[part].astype(bf16)
        sum_k = sum_k + dgain
    qk_grad[...] = jnp.broadcast_to(jnp.concatenate([sum_q, sum_k], axis=1), qk_grad.shape)


def attend_back(probs, do, q, k, v, q_raw, k_raw, cosine, sine, qk_gain, after):
    rows = q.shape[0]
    return call(
        attend_back_kernel,
        [
            shaped((rows, H * HD), bf16), shaped((2 * rows, 2 * HD), bf16),
            shaped((8, 2 * HD), f32),
        ],
        [probs, do, q, k, v, q_raw, k_raw, cosine, sine, qk_gain],
        us=6,
        scratch=[pltpu.VMEM((2 * rows, HD), f32), pltpu.VMEM((2 * rows, HD), f32)],
        after=after,
    )


def project_back_kernel(
    dq_low, dkv_low, qk_grad, hidden, x, o, attn_low, qk_order, gain3, gain12, *refs
):
    pieces, (dh, *grads) = refs[:-6], refs[-6:]
    rows = dq_low.shape[0]
    put_grad(grads, slice(0, 1024), tn(hidden[rows:], dq_low[...]).astype(bf16))
    put_grad(grads, slice(1024, 1536), tn(hidden[...], dkv_low[...]).astype(bf16))
    w_q = join_rows(pieces, slice(0, 1024))
    w_kv = join_rows(pieces, slice(1024, 1536))
    sum0 = jnp.zeros((1, x.shape[1]), f32)
    for c in range(2 * rows // 256):
        part = pl.ds(c * 256, 256)
        grad = nt(dkv_low[part], w_kv)
        if c * 256 >= rows:
            grad = grad + nt(dq_low[c * 256 - rows : c * 256 - rows + 256], w_q)
        dh[part] = grad
        xs = x[part].astype(f32)
        sum0 = sum0 + jnp.sum(grad * (xs * inverse_rms(xs)), axis=0, keepdims=True)
    qk_spread = nt(qk_grad[...].astype(bf16), qk_order[...])
    rows_of = jnp.concatenate(
        [
            sum0, gain12[0:1], gain12[1:2], gain3[0:1], qk_spread[0:1],
            jnp.zeros((EXTRA - 5, x.shape[1]), f32),
        ],
        axis=0,
    )
    put_grad(grads, slice(1536, 1664), rows_of.T.astype(bf16))
    put_grad(grads, slice(1664, 2688), tn(attn_low[...], o[...]).astype(bf16))


def project_back(
    dq_low, dkv_low, qk_grad, hidden, x, o, attn_low, qk_order, gain3, gain12, pieces, after
):
    rows, width = o.shape[0], x.shape[1]
    return call(
        project_back_kernel,
        [shaped((2 * rows, width), f32), *grad_shapes(width, pieces[0].shape[1] + H * HD)],
        [dq_low, dkv_low, qk_grad, hidden, x, o, attn_low, qk_order, gain3, gain12, *pieces],
        us=4,
        after=after,
    )


def input_back_kernel(dh, x, gains, dx1, order, own, before):
    rows = dx1.shape[0]
    table = order[...]
    for c in range(2 * rows // 256):
        part = pl.ds(c * 256, 256)
        back, _ = rms_back(x[part].astype(f32), gains[0:1], dh[part])
        if c * 256 < rows:
            before[part] = nt(back.astype(bf16), table).astype(bf16)
        else:
            mine = pl.ds(c * 256 - rows, 256)
            rest = back + dx1[mine]
            total = jnp.zeros_like(rest)
            for _ in range(3):
                piece = rest.astype(bf16)
                rest = rest - piece.astype(f32)
                total = total + nt(piece, table)
            own[mine] = total


def input_back(dh, x, gains, dx1, order, after=()):
    rows, width = dx1.shape
    return call(
        input_back_kernel,
        [shaped((rows, width), f32), shaped((rows, width), bf16)],
        [dh, x, gains, dx1, order],
        us=2,
        after=after,
    )


def on_device(
    tokens,
    segment_ids,
    w_query,
    w_key,
    w_value,
    w_output,
    w_gate,
    w_up,
    w_down,
    norm_gains,
    qk_gains,
    cotangent,
):
    n = lax.axis_size("seq")
    me = lax.axis_index("seq")
    rows, width = tokens.shape
    shard = w_query.shape[0]
    qk_shard = qk_gains.shape[0]

    extra = jnp.concatenate(
        [
            norm_gains.T,
            jnp.pad(qk_gains, (0, shard - qk_shard))[:, None],
            jnp.zeros((shard, EXTRA - 5), bf16),
        ],
        axis=1,
    )
    shard_a = jnp.concatenate([w_query, w_key, w_value, extra], axis=1)
    shard_b = jnp.concatenate([w_output.T, w_gate, w_up], axis=1)
    shard_c = w_down.T

    even, odd, inner = row_table(n, shard)
    device = me ^ jnp.where(me & 1 == 0, jnp.asarray(even), jnp.asarray(odd))
    place = device * shard + inner
    order = (jnp.arange(width, dtype=jnp.int32)[:, None] == place[None, :]).astype(bf16)
    qk_place = jnp.where(inner < qk_shard, device * qk_shard + inner, -1)
    qk_order = (qk_place[:, None] == jnp.arange(2 * HD, dtype=jnp.int32)[None, :]).astype(bf16)

    padded = jnp.concatenate([jnp.full((LONGEST + rows,), -1, jnp.int32), segment_ids])
    nearby = lax.dynamic_slice_in_dim(padded, me * rows, 2 * rows + LONGEST)
    keys_segment = nearby[LONGEST:]
    ahead = (jnp.arange(2 * rows) + LONGEST)[:, None] > jnp.arange(2 * rows + LONGEST)[None, :]
    positions = jnp.sum(
        ((keys_segment[:, None] == nearby[None, :]) & ahead).astype(jnp.int32), axis=1
    )
    freqs = 10000.0 ** (-2.0 * jnp.arange(HD // 2, dtype=f32) / HD)
    angles = positions.astype(f32)[:, None] * freqs[None, :]
    cosine, sine = jnp.cos(angles), jnp.sin(angles)
    seg_q = keys_segment[rows:, None]
    seg_k = jnp.stack(
        [keys_segment[b * BLOCK : b * BLOCK + REACH] for b in range(rows // BLOCK)]
    )[:, None, :]

    tokens_before = lax.ppermute(tokens, "seq", [(i, i + 1) for i in range(n - 1)])
    shards = [shard_a, shard_b, shard_c]
    travel_a, travel_b, travel_c = call(
        tile_kernel, [shaped(travel_shape(*w.shape), bf16) for w in shards], shards, us=0.5
    )
    a_c = to_first(travel_c, n)
    (own_a,) = pack(
        far_direct(travel_a, n), *shard_a.shape, 1, n,
        after=(seg_q, seg_k, qk_order, a_c, tokens_before),
    )
    pair_c, travel_b = call(
        start_kernel,
        [shaped((2 * travel_c.shape[0], travel_c.shape[1]), bf16), shaped(travel_b.shape, bf16)],
        [travel_c, a_c, travel_b],
        us=0.2,
        after=(own_a,),
    )
    a_a, b_a = to_first(own_a, n), to_second(own_a, n)
    near_a = [own_a, a_a, b_a, to_second(a_a, n)]
    x = nn(jnp.concatenate([tokens_before, tokens], axis=0), order).astype(bf16)
    dy = nn(cotangent, order).astype(bf16)
    (own_b,) = pack(
        far_direct(travel_b, n), *shard_b.shape, 1, n, after=(x, dy, cosine, sine, *near_a[1:])
    )
    own_a, pair_c = hold(own_a, pair_c, after=(own_b,))
    weights_a = [own_a, *near_a[1:]]
    weights_a = [*weights_a, *to_core(weights_a, n)]
    hidden, q_raw, k_raw, q, k, v, probs, o, gains, qk_gain = attend(
        x, weights_a, qk_order, cosine, sine, seg_q, seg_k, after=(own_b,)
    )
    a_b, b_b = to_first(own_b, n), to_second(own_b, n)
    half_c = pack(
        far_direct(pair_c, n), *shard_c.shape, 2, n, after=(o, a_b, b_b)
    )
    a_b, own_b = hold(a_b, own_b, after=half_c)
    half_c = [*half_c, to_second(half_c[0], n)]
    weights_b = [own_b, a_b, b_b, to_second(a_b, n)]
    weights_b = [*weights_b, *to_core(weights_b, n)]
    weights_c = [*half_c, *to_core(half_c, n)]
    steps = len(far_bits(n)[0])
    a, middle, normed, product, by_gate, by_up = feed(o, weights_b, x, gains, after=())
    mixed, low, gain3, *grad_d = turn(product, weights_c, middle, dy, gains, order)
    gate_low, up_low, *grad_f = feed_back(low, weights_c, by_gate, by_up, normed)
    sum_d = core_sum_by_far(grad_d[0], grad_d[1:], n, after=(gate_low,))
    dx1, gain12, attn_low, do = middle_back(
        gate_low, up_low, weights_b, middle, a, dy, gains, after=sum_d[:1]
    )
    sum_f = core_sum(grad_f[0], grad_f[1:], n, after=(do,))
    dq_low, dkv_low, qk_grad = attend_back(
        probs, do, q, k, v, q_raw, k_raw, cosine, sine, qk_gain, after=sum_f[:1]
    )
    for step in reversed(range(1, steps)):
        sum_d = far_fold(sum_d, n, step, after=(dq_low,))
    dh, *grad_a = project_back(
        dq_low, dkv_low, qk_grad, hidden, x, o, attn_low, qk_order, gain3, gain12, weights_a,
        after=sum_d[:1],
    )
    own, before = input_back(dh, x, gains, dx1, order, after=())
    behind = lax.ppermute(before, "seq", [(i + 1, i) for i in range(n - 1)])
    sum_d = far_fold(sum_d, n, 0, after=(own,))
    sum_a = core_sum(grad_a[0], grad_a[1:], n, after=sum_d[:1])
    sum_f = near_sum_first(sum_f, n, after=sum_a[:1])
    sum_d = near_sum_first(sum_d, n, after=sum_f[:1])
    sum_a = near_sum_first(sum_a, n, after=sum_d[:1])
    sum_f = near_sum_second(sum_f, n, after=sum_a[:1])
    ff = grad_d[0].shape[1]
    (sum_d,) = near_sum_last(sum_d, n, shard, (0, ff), after=sum_f[:1])
    sum_a = near_sum_second(sum_a, n, after=(sum_d,))
    sum_f = far_sum_first(sum_f, n, after=sum_a[:1])
    input_grad = own + behind.astype(f32)
    sum_g, sum_u = far_sum_last(sum_f, n, shard, (0, ff, 2 * ff), after=sum_f[:1])
    sum_a = far_sum_first(sum_a, n, after=(sum_g,))
    sum_q, sum_k, sum_v, sum_n, sum_o = far_sum_last(
        sum_a, n, shard, (0, 1024, 1280, 1536, 1664, 2688), after=(sum_g,)
    )
    return (
        mixed,
        input_grad,
        sum_q,
        sum_k,
        sum_v,
        sum_o.T,
        sum_g,
        sum_u,
        sum_d.T,
        sum_n[:, :4].T,
        sum_n[:qk_shard, 4],
    )


def solution(mesh):
    return jax.shard_map(
        on_device,
        mesh=mesh,
        in_specs=(
            P("seq", None),
            P(),
            P("seq", None),
            P("seq", None),
            P("seq", None),
            P(None, "seq"),
            P("seq", None),
            P("seq", None),
            P(None, "seq"),
            P(None, "seq"),
            P("seq"),
            P("seq", None),
        ),
        out_specs=(
            P("seq", None),
            P("seq", None),
            P("seq", None),
            P("seq", None),
            P("seq", None),
            P(None, "seq"),
            P("seq", None),
            P("seq", None),
            P(None, "seq"),
            P(None, "seq"),
            P("seq"),
        ),
        check_vma=False,
    )
```

```python
import functools

import jax
import jax.numpy as jnp
import numpy as np
from jax import lax
from jax.experimental import pallas as pl
from jax.experimental.pallas import tpu as pltpu
from jax.sharding import PartitionSpec as P

H = 4
HD = 256
WINDOW = 512
LONGEST = 2048
EXTRA = 128
FF_CHUNK = 512
BLOCK = 128
REACH = BLOCK + WINDOW
MIB = 1024 * 1024

epsilon = 1e-06
bf16 = jnp.bfloat16
f32 = jnp.float32


def far_bits(n):
    bits = [1 << i for i in range(n.bit_length() - 1)]
    rest = [b for b in bits[1:] if b not in near_pair(n)]
    return rest, rest[::-1]


def far_slots(bits):
    slots = [0]
    for b in bits:
        slots = slots + [s | b for s in slots]
    return slots


def near_pair(n):
    return (2, 8) if n > 64 else (2, 4)


def to_partner(x, n, masks):
    return lax.ppermute(x, "seq", [(i, i ^ masks[i & 1]) for i in range(n)])


def row_table(n, shard):
    first, second = near_pair(n)
    main = whole_tiles(shard)
    count = n // 8
    inner = [(i, r) for i in range(count) for r in range(main)]
    inner += [(i, r) for i in range(count) for r in range(main, shard)]

    def offsets(a, b, bits):
        far = far_slots(bits)
        return [m ^ far[i] for m in (0, a, b, a | b) for i, _ in inner]

    even_bits, odd_bits = far_bits(n)
    even, odd = offsets(first, second, even_bits), offsets(second, first, odd_bits)
    return (
        np.array(even + [1 ^ m for m in odd], np.int32),
        np.array(odd + [1 ^ m for m in even], np.int32),
        np.array([r for _, r in inner] * 8, np.int32),
    )


def nn(left, right):
    return jnp.dot(left, right, preferred_element_type=f32)


def tn(left, right):
    return lax.dot_general(left, right, (((0,), (0,)), ((), ())), preferred_element_type=f32)


def nt(left, right):
    return lax.dot_general(left, right, (((1,), (1,)), ((), ())), preferred_element_type=f32)


def inverse_rms(values):
    return lax.rsqrt(jnp.mean(values * values, axis=-1, keepdims=True) + epsilon)


def rms_back(values, gain, grad):
    scale = inverse_rms(values)
    hat = values * scale
    inner = grad * gain
    mean = jnp.mean(inner * hat, axis=-1, keepdims=True)
    return scale * (inner - hat * mean), jnp.sum(grad * hat, axis=0, keepdims=True)


def rotate(values, cosine, sine):
    half = values.shape[-1] // 2
    a, b = values[:, :half], values[:, half:]
    return jnp.concatenate([a * cosine - b * sine, b * cosine + a * sine], axis=-1)


def rotate_back(values, cosine, sine):
    half = values.shape[-1] // 2
    a, b = values[:, :half], values[:, half:]
    return jnp.concatenate([a * cosine + b * sine, b * cosine - a * sine], axis=-1)


def call(kernel, outs, args, us, scratch=(), after=(), room=12):
    given, extra = len(args), len(after)

    def body(*refs):
        kernel(*refs[:given], *refs[given + extra :])

    return pl.pallas_call(
        body,
        in_specs=[pl.BlockSpec(memory_space=pltpu.VMEM)] * given
        + [pl.BlockSpec(memory_space=pl.ANY)] * extra,
        out_specs=[pl.BlockSpec(memory_space=pltpu.VMEM)] * len(outs),
        out_shape=outs,
        scratch_shapes=scratch,
        compiler_params=pltpu.CompilerParams(vmem_limit_bytes=room * MIB),
        cost_estimate=pl.CostEstimate(
            flops=int(us * 10**9), bytes_accessed=int(us * 10**6), transcendentals=0
        ),
    )(*args, *after)


def shaped(shape, dtype):
    return jax.ShapeDtypeStruct(shape, dtype)


def join_rows(parts, cols=slice(None)):
    return jnp.concatenate([p[:, cols] for p in parts], axis=0)


def whole_tiles(rows):
    return rows // 16 * 16


def padded(cols):
    return -(-cols // 512) * 512


def in_tiles(rows):
    return rows == 20


def travel_shape(rows, cols):
    return (16, padded(cols) * 5 // 4) if in_tiles(rows) else (rows, cols)


def to_tiles(values):
    rows, cols = values.shape
    if not in_tiles(rows):
        return values
    wide = padded(cols)
    if wide > cols:
        values = jnp.concatenate([values, jnp.zeros((rows, wide - cols), f32)], axis=1)
    quarter = wide // 4
    rest = [values[16:, k * quarter : (k + 1) * quarter] for k in range(4)]
    return jnp.concatenate([values[:16], jnp.concatenate(rest, axis=0)], axis=1)


def tile_kernel(counts, *refs):
    total = sum(counts)
    given, outs = refs[:total], refs[total : total + len(counts)]
    held, sem = refs[total + len(counts) : -1], refs[-1]
    copies = [
        pltpu.make_async_copy(source, target, sem.at[i])
        for i, (source, target) in enumerate(zip(given, held))
    ]
    for copy in copies:
        copy.start()
    for copy in copies:
        copy.wait()
    for count, out in zip(counts, outs):
        parts, held = held[:count], held[count:]
        values = jnp.concatenate([p[...].astype(f32) for p in parts], axis=1)
        out[...] = to_tiles(values).astype(bf16)


def travelling(*groups):
    counts = [len(g) for g in groups]
    given = [w for g in groups for w in g]
    outs = []
    for g in groups:
        outs.append(shaped(travel_shape(g[0].shape[0], sum(w.shape[1] for w in g)), bf16))
    return pl.pallas_call(
        functools.partial(tile_kernel, counts),
        in_specs=[pl.BlockSpec(memory_space=pltpu.HBM)] * len(given),
        out_specs=[pl.BlockSpec(memory_space=pltpu.VMEM)] * len(outs),
        out_shape=outs,
        scratch_shapes=[pltpu.VMEM(w.shape, bf16) for w in given]
        + [pltpu.SemaphoreType.DMA((len(given),))],
        compiler_params=pltpu.CompilerParams(vmem_limit_bytes=8 * MIB),
    )(*[pltpu.with_memory_space_constraint(w, pltpu.HBM) for w in given])


def stack_kernel(*refs):
    count = len(refs) // 3
    for i in range(count):
        a, b, out = refs[2 * i], refs[2 * i + 1], refs[2 * count + i]
        rows = a.shape[0]
        if rows % 16 == 0:
            out[:rows] = a[...]
            out[rows:] = b[...]
        else:
            both = [a[...].astype(f32), b[...].astype(f32)]
            out[...] = jnp.concatenate(both, axis=0).astype(bf16)


def stack(*pairs, after=()):
    outs = [shaped((2 * a.shape[0], a.shape[1]), bf16) for a, _ in pairs]
    return call(stack_kernel, outs, [x for pair in pairs for x in pair], us=0.5, after=after)


def pack_kernel(pieces, blocks, out):
    count = len(pieces)
    share, cols = out.shape[0] // blocks, out.shape[1]
    rows = share // count
    main = whole_tiles(rows)
    height, wide = travel_shape(rows, cols)
    quarter = padded(cols) // 4
    for block in range(blocks):
        at = block * share
        starts = [(ref, begin + block * height) for ref, begin in pieces]
        if main:
            for i, (ref, begin) in enumerate(starts):
                out[at + i * main : at + (i + 1) * main] = ref[begin : begin + main, :cols]
        at = at + main * count
        if in_tiles(rows):
            rest = [ref[begin : begin + 16, 4 * quarter :].astype(f32) for ref, begin in starts]
            for k in range(4):
                end = min((k + 1) * quarter, cols)
                part = jnp.concatenate([r[4 * k : 4 * k + 4] for r in rest], axis=0)
                out[at : at + 4 * count, k * quarter : end] = part[:, : end - k * quarter].astype(
                    bf16
                )
        elif rows > main:
            rest = [
                ref[...].astype(f32)[begin + main : begin + rows] for ref, begin in starts
            ]
            out[at : at + (rows - main) * count] = jnp.concatenate(rest, axis=0).astype(bf16)


def pack(arrays, rows, cols, blocks, n, parts=1, after=()):
    count = n // 8
    height = travel_shape(rows, cols)[0] * blocks
    held = count // len(arrays)
    total = rows * count * blocks

    def kernel(*refs):
        given = refs[: len(arrays)]
        pieces = [(ref, h * height) for ref in given for h in range(held)]
        if parts == 1:
            pack_kernel(pieces, blocks, refs[-1])
        else:
            for block, out in enumerate(refs[len(arrays) :]):
                shift = block * height // blocks
                pack_kernel([(ref, at + shift) for ref, at in pieces], 1, out)

    outs = [shaped((total // parts, cols), bf16)] * parts
    return call(kernel, outs, arrays, us=1.5, after=after)


def far_step(block, n, step):
    even, odd = far_bits(n)
    return to_partner(block, n, (even[step], odd[step]))


def far_direct(block, n):
    even, odd = far_bits(n)
    slots = zip(far_slots(even)[1:], far_slots(odd)[1:])
    return [block] + [to_partner(block, n, masks) for masks in slots]


def start_kernel(a, b, one, one_out, out):
    stack_kernel(a, b, out)
    one_out[...] = one[...]


def hold_kernel(*refs):
    half = len(refs) // 2
    for value, out in zip(refs[:half], refs[half:]):
        out[...] = value[...]


def hold(*values, after):
    return call(hold_kernel, [shaped(v.shape, v.dtype) for v in values], values, 0.2, after=after)


def far_gather(blocks, n, joins):
    steps = len(far_bits(n)[0])
    for k in range(steps - 1):
        got = [far_step(b, n, k) for b in blocks]
        blocks = stack(*zip(blocks, got), after=joins[k] if k < len(joins) else ())
    return [(b, far_step(b, n, steps - 1)) for b in blocks]


def to_first(x, n):
    first, second = near_pair(n)
    return to_partner(x, n, (first, second))


def to_second(x, n):
    first, second = near_pair(n)
    return to_partner(x, n, (second, first))


def near_pieces(own, n, direct=False):
    first, second = near_pair(n)
    a, b = to_first(own, n), to_second(own, n)
    return [own, a, b, to_partner(own, n, (first | second,) * 2) if direct else to_second(a, n)]


def to_core(pieces, n):
    return [to_partner(p, n, (1, 1)) for p in pieces]


def fold_kernel(count, *refs):
    given, outs = refs[:count], refs[count:]
    mine, got = given[0], given[1:]
    rows = outs[0].shape[0]
    height = got[0].shape[0]
    if rows % 16 == 0 and height % rows == 0:
        per = height // rows
        for i, out in enumerate(outs):
            other = got[i // per][(i % per) * rows : (i % per + 1) * rows]
            part = mine[i * rows : (i + 1) * rows]
            out[...] = (part.astype(f32) + other.astype(f32)).astype(bf16)
    else:
        total = mine[...].astype(f32)
        total = total + jnp.concatenate([g[...].astype(f32) for g in got], axis=0)
        for i, out in enumerate(outs):
            out[...] = total[i * rows : (i + 1) * rows].astype(bf16)


def fold(mine, got, after=(), us=0.5):
    rows, cols = mine.shape
    outs = [shaped((rows // 2, cols), bf16)] * 2
    kernel = functools.partial(fold_kernel, 1 + len(got))
    return call(kernel, outs, [mine, *got], us=us, after=after)


def wide_fold_kernel(mine, *refs):
    got, (keep, send) = refs[:-2], refs[-2:]
    rows = got[0].shape[0]
    per = keep.shape[0] // rows
    for i, other in enumerate(got):
        out = keep if i < per else send
        at = (i % per) * rows
        part = mine[i * rows : (i + 1) * rows].astype(f32)
        out[at : at + rows] = (part + other[...].astype(f32)).astype(bf16)


def core_sum(top, sends, n, after=()):
    rows, cols = top.shape
    outs = [shaped((rows // 2, cols), bf16)] * 2
    return call(wide_fold_kernel, outs, [top, *to_core(sends, n)], us=0.7, after=after)


def core_sum_by_far(top, sends, n, after=()):
    rows, cols = top.shape
    count, blocks = n // 8, len(sends)
    shard = rows // blocks // count
    main = whole_tiles(shard)
    rest, done = shard - main, main * count
    height, wide = travel_shape(shard, cols)

    def kernel(mine, *refs):
        got, (keep, send) = refs[:-2], refs[-2:]
        share = rows // blocks
        tiles = []
        for block in range(blocks):
            total = mine[block * share : (block + 1) * share].astype(f32) + got[block][...].astype(
                f32
            )
            for i in range(count):
                parts = []
                if main:
                    parts.append(total[i * main : (i + 1) * main])
                if rest:
                    parts.append(total[done + i * rest : done + (i + 1) * rest])
                tiles.append((i, block, to_tiles(jnp.concatenate(parts, axis=0))))
        tiles = [t for _, _, t in sorted(tiles, key=lambda item: item[:2])]
        half = len(tiles) // 2
        keep[...] = jnp.concatenate(tiles[:half], axis=0).astype(bf16)
        send[...] = jnp.concatenate(tiles[half:], axis=0).astype(bf16)

    outs = [shaped((count // 2 * blocks * height, wide), bf16)] * 2
    return call(kernel, outs, [top, *to_core(sends, n)], us=1.5, after=after)


def far_fold(halves, n, step, after=()):
    keep, send = halves
    return fold(keep, [far_step(send, n, step)], after)


def near_sum_last(halves, n, shard, cuts, after=()):
    keep, send = halves
    outs = [shaped((shard, e - b), f32) for b, e in zip(cuts[:-1], cuts[1:])]
    return call(
        functools.partial(far_sum_kernel, cuts), outs, [keep, to_first(send, n)], us=1, after=after
    )


def near_sum_first(halves, n, after=(), us=0.5):
    keep, send = halves
    return fold(keep, [to_second(send, n)], after, us)


def fold_both_kernel(*refs):
    given, (keep, send) = refs[:4], refs[4:]
    rows, cols = keep.shape
    cols = cols // 2
    for i in range(2):
        mine, got = given[2 * i : 2 * i + 2]
        for j, out in enumerate((keep, send)):
            part = slice(j * rows, (j + 1) * rows)
            out[:, i * cols : (i + 1) * cols] = (
                mine[part].astype(f32) + got[part].astype(f32)
            ).astype(bf16)


def near_sum_first_both(one, two, n, after=()):
    args = [x for keep, send in (one, two) for x in (keep, to_second(send, n))]
    rows, cols = one[0].shape
    outs = [shaped((rows // 2, 2 * cols), bf16)] * 2
    return call(fold_both_kernel, outs, args, us=0.5, after=after)


def split_kernel(count, mine, got, keep, send):
    total = mine[...].astype(f32) + got[...].astype(f32)
    rows = total.shape[0] // count
    main = whole_tiles(rows)
    rest, done = rows - main, main * count
    slots = []
    for i in range(count):
        parts = []
        if main:
            parts.append(total[i * main : (i + 1) * main])
        if rest:
            parts.append(total[done + i * rest : done + (i + 1) * rest])
        slots.append(to_tiles(jnp.concatenate(parts, axis=0)))
    keep[...] = jnp.concatenate(slots[: count // 2], axis=0).astype(bf16)
    send[...] = jnp.concatenate(slots[count // 2 :], axis=0).astype(bf16)


def near_sum_second(halves, n, after=()):
    keep, send = halves
    rows, cols = keep.shape
    count = n // 8
    height, wide = travel_shape(rows // count, cols)
    outs = [shaped((count // 2 * height, wide), bf16)] * 2
    return call(
        functools.partial(split_kernel, count), outs, [keep, to_first(send, n)], us=1, after=after
    )


def slots_kernel(count, mine, got, *outs):
    total = mine[...].astype(f32) + got[...].astype(f32)
    rows = total.shape[0] // count
    main = whole_tiles(rows)
    rest, done = rows - main, main * count
    for i, out in enumerate(outs):
        parts = []
        if main:
            parts.append(total[i * main : (i + 1) * main])
        if rest:
            parts.append(total[done + i * rest : done + (i + 1) * rest])
        out[...] = to_tiles(jnp.concatenate(parts, axis=0)).astype(bf16)


def near_sum_direct_far(halves, n, after=()):
    keep, send = halves
    rows, cols = keep.shape
    count = n // 8
    outs = [shaped(travel_shape(rows // count, cols), bf16)] * count
    return call(
        functools.partial(slots_kernel, count), outs, [keep, to_first(send, n)], us=1, after=after
    )


def far_sum_direct(pieces, n, shard, cuts, after=()):
    even, odd = far_bits(n)
    slots = zip(pieces[1:], far_slots(even)[1:], far_slots(odd)[1:])
    got = [to_partner(p, n, (e, o)) for p, e, o in slots]
    outs = [shaped((shard, e - b), f32) for b, e in zip(cuts[:-1], cuts[1:])]
    return call(
        functools.partial(far_sum_kernel, cuts), outs, [pieces[0], *got], us=1, after=after
    )


def far_sum_first(halves, n, after=()):
    keep, send = halves
    for k in reversed(range(1, len(far_bits(n)[0]))):
        keep, send = fold(keep, [far_step(send, n, k)], after)
        after = ()
    return keep, send


def far_sum_kernel(cuts, *refs):
    given, outs = refs[: 1 - len(cuts)], refs[1 - len(cuts) :]
    total = given[0][...].astype(f32)
    for got in given[1:]:
        total = total + got[...].astype(f32)
    rows = outs[0].shape[0]
    if in_tiles(rows):
        wide = padded(cuts[-1])
        rest = [total[4 * k : 4 * k + 4, wide:] for k in range(4)]
        total = jnp.concatenate([total[:, :wide], jnp.concatenate(rest, axis=1)], axis=0)
    for out, begin, end in zip(outs, cuts[:-1], cuts[1:]):
        out[...] = total[:, begin:end]


def far_sum_last(halves, n, shard, cuts, after=()):
    keep, send = halves
    outs = [shaped((shard, e - b), f32) for b, e in zip(cuts[:-1], cuts[1:])]
    return call(
        functools.partial(far_sum_kernel, cuts), outs, [keep, far_step(send, n, 0)], us=1,
        after=after,
    )


def table_kernel(near, near_col, freqs, place, place_col, qk_place, cosine, sine, order, qk_order):
    count = cosine.shape[0]
    ahead = near.shape[1] - count
    steps = freqs[...]
    for c in range(count // 256):
        reach = slice(c * 256, c * 256 + ahead + 256)
        here = near_col[ahead + c * 256 : ahead + (c + 1) * 256]
        i = lax.broadcasted_iota(jnp.int32, (256, ahead + 256), 0) + ahead
        j = lax.broadcasted_iota(jnp.int32, (256, ahead + 256), 1)
        same = (here == near[:, reach]) & (j < i)
        position = jnp.sum(same.astype(f32), axis=1, keepdims=True)
        angles = position * steps
        cosine[c * 256 : (c + 1) * 256] = jnp.cos(angles)
        sine[c * 256 : (c + 1) * 256] = jnp.sin(angles)
    i = lax.broadcasted_iota(jnp.int32, order.shape, 0)
    order[...] = (i == place[...]).astype(f32).astype(bf16)
    j = lax.broadcasted_iota(jnp.int32, qk_order.shape, 1)
    qk_order[...] = (qk_place[...] == j).astype(f32).astype(bf16)


def tables(near, rows, place, qk_place, width, after=()):
    freqs = np.float32(10000.0) ** (-2.0 * np.arange(HD // 2, dtype=np.float32) / np.float32(HD))
    args = [
        near[None, :], near[:, None], jnp.asarray(freqs)[None, :], place[None, :], place[:, None],
        qk_place[:, None],
    ]
    outs = [
        shaped((2 * rows, HD // 2), f32), shaped((2 * rows, HD // 2), f32),
        shaped((width, width), bf16), shaped((width, 2 * HD), bf16),
    ]
    return call(table_kernel, outs, args, us=3, after=after)


def permute_kernel(tokens_before, tokens, cotangent, order, x, dy):
    table = order[...]
    rows = tokens.shape[0]
    x[:rows] = nn(tokens_before[...], table).astype(bf16)
    x[rows:] = nn(tokens[...], table).astype(bf16)
    dy[...] = nn(cotangent[...], table).astype(bf16)


def permute(tokens_before, tokens, cotangent, order, after=()):
    rows, width = tokens.shape
    outs = [shaped((2 * rows, width), bf16), shaped((rows, width), bf16)]
    args = [tokens_before, tokens, cotangent, order]
    return call(permute_kernel, outs, args, us=2, after=after)


def attend_kernel(x, qk_order, cosine, sine, seg_q, seg_k, *refs):
    pieces = refs[:-10]
    hidden, q_raw, k_raw, q_out, k_out, v_out, probs, o, gains, qk_gain = refs[-10:]
    rows = q_raw.shape[0]
    w_q = join_rows(pieces, slice(0, 1024))
    w_kv = join_rows(pieces, slice(1024, 1536))
    gain_rows = join_rows(pieces, slice(1536, 1664)).astype(f32).T[:8]
    gains[...] = gain_rows
    gain_qk = nn(gain_rows.astype(bf16), qk_order[...])
    qk_gain[...] = gain_qk
    gain_q, gain_k = gain_qk[4:5, :HD], gain_qk[4:5, HD:]
    for c in range(2 * rows // 256):
        part = pl.ds(c * 256, 256)
        xs = x[part].astype(f32)
        hs = (xs * inverse_rms(xs) * gain_rows[0:1]).astype(bf16)
        hidden[part] = hs
        cs, sn = cosine[part], sine[part]
        kv = nn(hs, w_kv)
        raw = kv[:, :HD]
        k_raw[part] = raw
        k_out[part] = rotate(raw * inverse_rms(raw) * gain_k, cs, sn).astype(bf16)
        v_out[part] = kv[:, HD:].astype(bf16)
        if c * 256 >= rows:
            own = pl.ds(c * 256 - rows, 256)
            qs = nn(hs, w_q)
            q_raw[own] = qs
            for h in range(H):
                raw = qs[:, h * HD : (h + 1) * HD]
                q_out[own, h * HD : (h + 1) * HD] = rotate(
                    raw * inverse_rms(raw) * gain_q, cs, sn
                ).astype(bf16)
    for b in range(rows // BLOCK):
        mine = pl.ds(b * BLOCK, BLOCK)
        reach = pl.ds(b * BLOCK, REACH)
        q_rows = q_out[mine] * bf16(1.0 / 16.0)
        q_stack = jnp.concatenate([q_rows[:, h * HD : (h + 1) * HD] for h in range(H)], axis=0)
        scores = nt(q_stack, k_out[reach])
        i = lax.broadcasted_iota(jnp.int32, (BLOCK, REACH), 0)
        j = lax.broadcasted_iota(jnp.int32, (BLOCK, REACH), 1)
        allowed = (j > i) & (j <= i + WINDOW) & (seg_q[mine] == seg_k[b])
        allowed = jnp.concatenate([allowed.astype(f32)] * H, axis=0)
        weights = jnp.exp(scores) * allowed
        total = jnp.sum(weights, axis=-1, keepdims=True)
        p = (weights * (1.0 / total)).astype(bf16)
        probs[b] = p
        out = nn(p, v_out[reach])
        for h in range(H):
            o[mine, h * HD : (h + 1) * HD] = out[h * BLOCK : (h + 1) * BLOCK].astype(bf16)


def attend(x, pieces, qk_order, cosine, sine, seg_q, seg_k, after):
    rows = x.shape[0] // 2
    width = x.shape[1]
    return call(
        attend_kernel,
        [
            shaped((2 * rows, width), bf16),
            shaped((rows, H * HD), f32),
            shaped((2 * rows, HD), f32),
            shaped((rows, H * HD), bf16),
            shaped((2 * rows, HD), bf16),
            shaped((2 * rows, HD), bf16),
            shaped((rows // BLOCK, H * BLOCK, REACH), bf16),
            shaped((rows, H * HD), bf16),
            shaped((8, width), f32),
            shaped((8, 2 * HD), f32),
        ],
        [x, qk_order, cosine, sine, seg_q, seg_k, *pieces],
        us=8,
        after=after,
    )


def gelu_parts(g):
    c0, c1 = 0.7978845608028654, 0.044715
    square = g * g
    t = jnp.tanh(c0 * g * (1.0 + c1 * square))
    value = 0.5 * g * (1.0 + t)
    slope = 0.5 * (1.0 + t) + 0.5 * g * (1.0 - t * t) * c0 * (1.0 + 3.0 * c1 * square)
    return value, slope


def feed_kernel(o, x, gains, *refs):
    pieces = refs[:-6]
    a_out, middle, normed, product, by_gate, by_up = refs[-6:]
    rows, ff = product.shape
    w_o = join_rows(pieces, slice(0, H * HD))
    for c in range(rows // 256):
        part = pl.ds(c * 256, 256)
        a = nt(o[part], w_o)
        a_out[part] = a
        x1 = x[rows + c * 256 : rows + (c + 1) * 256].astype(f32) + a * inverse_rms(a) * gains[1:2]
        middle[part] = x1
        normed[part] = (x1 * inverse_rms(x1) * gains[2:3]).astype(bf16)
    for j in range(ff // FF_CHUNK):
        cols = slice(j * FF_CHUNK, (j + 1) * FF_CHUNK)
        w_g = join_rows(pieces, slice(H * HD + cols.start, H * HD + cols.stop))
        w_u = join_rows(pieces, slice(H * HD + ff + cols.start, H * HD + ff + cols.stop))
        for c in range(rows // 256):
            part = pl.ds(c * 256, 256)
            h2 = normed[part]
            g = nn(h2, w_g)
            u = nn(h2, w_u)
            value, slope = gelu_parts(g)
            product[part, cols] = (value * u).astype(bf16)
            by_gate[part, cols] = (slope * u).astype(bf16)
            by_up[part, cols] = value.astype(bf16)


def feed(o, pieces, x, gains, after):
    rows, width = o.shape[0], x.shape[1]
    ff = (pieces[0].shape[1] - H * HD) // 2
    return call(
        feed_kernel,
        [
            shaped((rows, width), f32),
            shaped((rows, width), f32),
            shaped((rows, width), bf16),
            shaped((rows, ff), bf16),
            shaped((rows, ff), bf16),
            shaped((rows, ff), bf16),
        ],
        [o, x, gains, *pieces],
        us=6,
        after=after,
    )


def put_grad(grads, cols, values):
    top, *sends = grads
    half = top.shape[0]
    top[:, cols] = values[:half]
    part = half // len(sends)
    for i, send in enumerate(sends):
        send[:, cols] = values[half + i * part : half + (i + 1) * part]


def grad_shapes(width, cols):
    return [shaped((width // 2, cols), bf16)] + [shaped((width // 8, cols), bf16)] * 4


def turn_kernel(product, middle, dy, gains, order, *refs):
    pieces, (mixed, low, gain_grad, *grads) = refs[:-8], refs[-8:]
    ff = product.shape[1]
    w_d = join_rows(pieces)
    total = jnp.zeros((1, dy.shape[1]), f32)
    for c in range(dy.shape[0] // 256):
        part = pl.ds(c * 256, 256)
        f = nt(product[part], w_d)
        grad = dy[part].astype(f32)
        y = middle[part] + f * inverse_rms(f) * gains[3:4]
        mixed[part] = nt(y.astype(bf16), order[...]).astype(bf16)
        df, dgain = rms_back(f, gains[3:4], grad)
        low[part] = df.astype(bf16)
        total = total + dgain
    gain_grad[...] = jnp.broadcast_to(total, gain_grad.shape)
    for j in range(ff // FF_CHUNK):
        cols = slice(j * FF_CHUNK, (j + 1) * FF_CHUNK)
        grad = tn(low[...], product[:, cols]).astype(bf16)
        put_grad(grads, cols, grad)


def turn(product, pieces, middle, dy, gains, order):
    rows, width = middle.shape
    return call(
        turn_kernel,
        [
            shaped((rows, width), bf16),
            shaped((rows, width), bf16),
            shaped((8, width), f32),
            *grad_shapes(width, product.shape[1]),
        ],
        [product, middle, dy, gains, order, *pieces],
        us=6,
    )


def feed_back_kernel(low, by_gate, by_up, normed, *refs):
    pieces, (gate_low, up_low, *grads) = refs[:-7], refs[-7:]
    rows, ff = gate_low.shape
    for j in range(ff // FF_CHUNK):
        cols = slice(j * FF_CHUNK, (j + 1) * FF_CHUNK)
        w_d = join_rows(pieces, cols)
        for c in range(rows // 256):
            part = pl.ds(c * 256, 256)
            dm = nn(low[part], w_d)
            gate_low[part, cols] = (dm * by_gate[part, cols].astype(f32)).astype(bf16)
            up_low[part, cols] = (dm * by_up[part, cols].astype(f32)).astype(bf16)
        put_grad(grads, cols, tn(normed[...], gate_low[:, cols]).astype(bf16))


def feed_back(low, pieces, by_gate, by_up, normed):
    rows, width = low.shape
    ff = by_gate.shape[1]
    return call(
        feed_back_kernel,
        [shaped((rows, ff), bf16)] * 2 + grad_shapes(width, ff),
        [low, by_gate, by_up, normed, *pieces],
        us=4,
    )


def middle_back_kernel(gate_low, up_low, middle, a, dy, gains, normed, o, *refs):
    pieces, (dx1, gain_grad, do, *grads) = refs[:-8], refs[-8:]
    rows, ff = gate_low.shape
    w_o = join_rows(pieces, slice(0, H * HD))
    w_g = join_rows(pieces, slice(H * HD, H * HD + ff))
    w_u = join_rows(pieces, slice(H * HD + ff, H * HD + 2 * ff))
    sum1 = jnp.zeros((1, dy.shape[1]), f32)
    sum2 = jnp.zeros((1, dy.shape[1]), f32)
    lows = []
    for c in range(rows // 256):
        part = pl.ds(c * 256, 256)
        grad = nt(gate_low[part], w_g) + nt(up_low[part], w_u)
        back, dgain2 = rms_back(middle[part], gains[2:3], grad)
        dx = dy[part].astype(f32) + back
        dx1[part] = dx
        da, dgain1 = rms_back(a[part], gains[1:2], dx)
        low = da.astype(bf16)
        lows.append(low)
        do[part] = nn(low, w_o).astype(bf16)
        sum1, sum2 = sum1 + dgain1, sum2 + dgain2
    gain_grad[...] = jnp.concatenate([sum1, sum2, jnp.zeros((6, dy.shape[1]), f32)], axis=0)
    for j in range(ff // FF_CHUNK):
        cols = slice(j * FF_CHUNK, (j + 1) * FF_CHUNK)
        put_grad(grads, cols, tn(normed[...], up_low[:, cols]).astype(bf16))
    grad = tn(jnp.concatenate(lows, axis=0), o[...]).astype(bf16)
    put_grad(grads, slice(ff, ff + H * HD), grad)


def middle_back(gate_low, up_low, pieces, middle, a, dy, gains, normed, o, after):
    rows, width = middle.shape
    return call(
        middle_back_kernel,
        [
            shaped((rows, width), f32),
            shaped((8, width), f32),
            shaped((rows, H * HD), bf16),
            *grad_shapes(width, gate_low.shape[1] + H * HD),
        ],
        [gate_low, up_low, middle, a, dy, gains, normed, o, *pieces],
        us=14,
        after=after,
        room=16,
    )


def attend_back_kernel(
    probs, do, q, k, v, q_raw, k_raw, cosine, sine, qk_gain, dq_low, dkv_before, dkv_own, qk_grad, dk, dv
):
    rows = q_raw.shape[0]
    dk[...] = jnp.zeros_like(dk)
    dv[...] = jnp.zeros_like(dv)
    gain_q, gain_k = qk_gain[4:5, :HD], qk_gain[4:5, HD:]
    sum_q = jnp.zeros((1, HD), f32)
    for b in range(rows // BLOCK):
        mine = pl.ds(b * BLOCK, BLOCK)
        reach = pl.ds(b * BLOCK, REACH)
        keys, values = k[reach], v[reach]
        do_rows, q_rows = do[mine], q[mine]
        do_stack = jnp.concatenate([do_rows[:, h * HD : (h + 1) * HD] for h in range(H)], axis=0)
        q_stack = jnp.concatenate([q_rows[:, h * HD : (h + 1) * HD] for h in range(H)], axis=0)
        p_low = probs[b]
        p = p_low.astype(f32)
        t = p * nt(do_stack, values)
        ds = (t - p * jnp.sum(t, axis=-1, keepdims=True)).astype(bf16)
        dk[reach] += tn(ds, q_stack)
        dv[reach] += tn(p_low, do_stack)
        dq = nn(ds, keys) * (1.0 / 16.0)
        own = pl.ds(rows + b * BLOCK, BLOCK)
        cs, sn = cosine[own], sine[own]
        for h in range(H):
            grad = rotate_back(dq[h * BLOCK : (h + 1) * BLOCK], cs, sn)
            back, dgain = rms_back(q_raw[mine, h * HD : (h + 1) * HD], gain_q, grad)
            dq_low[mine, h * HD : (h + 1) * HD] = back.astype(bf16)
            sum_q = sum_q + dgain
    sum_k = jnp.zeros((1, HD), f32)
    for c in range(2 * rows // 256):
        part = pl.ds(c * 256, 256)
        grad = rotate_back(dk[part] * (1.0 / 16.0), cosine[part], sine[part])
        back, dgain = rms_back(k_raw[part], gain_k, grad)
        out, at = (dkv_before, c * 256) if c * 256 < rows else (dkv_own, c * 256 - rows)
        out[at : at + 256, :HD] = back.astype(bf16)
        out[at : at + 256, HD:] = dv[part].astype(bf16)
        sum_k = sum_k + dgain
    qk_grad[...] = jnp.broadcast_to(jnp.concatenate([sum_q, sum_k], axis=1), qk_grad.shape)


def attend_back(probs, do, q, k, v, q_raw, k_raw, cosine, sine, qk_gain, after):
    rows = q.shape[0]
    return call(
        attend_back_kernel,
        [
            shaped((rows, H * HD), bf16), shaped((rows, 2 * HD), bf16),
            shaped((rows, 2 * HD), bf16), shaped((8, 2 * HD), f32),
        ],
        [probs, do, q, k, v, q_raw, k_raw, cosine, sine, qk_gain],
        us=0.3,
        scratch=[pltpu.VMEM((2 * rows, HD), f32), pltpu.VMEM((2 * rows, HD), f32)],
        after=after,
    )


def project_back_kernel(
    dq_low, dkv_before, dkv_own, qk_grad, hidden, x, qk_order, gain3, gain12, *refs
):
    pieces, (dh_before, dh, *grads) = refs[:-7], refs[-7:]
    rows = dq_low.shape[0]
    put_grad(grads, slice(0, 1024), tn(hidden[rows:], dq_low[...]).astype(bf16))
    grad = tn(hidden[:rows], dkv_before[...]) + tn(hidden[rows:], dkv_own[...])
    put_grad(grads, slice(1024, 1536), grad.astype(bf16))
    w_q = join_rows(pieces, slice(0, 1024))
    w_kv = join_rows(pieces, slice(1024, 1536))
    sum0 = jnp.zeros((1, x.shape[1]), f32)
    for c in range(rows // 256):
        part = pl.ds(c * 256, 256)
        before = x[part].astype(f32)
        grad = nt(dkv_before[part], w_kv)
        dh_before[part] = grad
        sum0 = sum0 + jnp.sum(grad * (before * inverse_rms(before)), axis=0, keepdims=True)
        own = x[rows + c * 256 : rows + (c + 1) * 256].astype(f32)
        grad = nt(dkv_own[part], w_kv) + nt(dq_low[part], w_q)
        dh[part] = grad
        sum0 = sum0 + jnp.sum(grad * (own * inverse_rms(own)), axis=0, keepdims=True)
    qk_spread = nt(qk_grad[...].astype(bf16), qk_order[...])
    rows_of = jnp.concatenate(
        [
            sum0, gain12[0:1], gain12[1:2], gain3[0:1], qk_spread[0:1],
            jnp.zeros((EXTRA - 5, x.shape[1]), f32),
        ],
        axis=0,
    )
    put_grad(grads, slice(1536, 1664), rows_of.T.astype(bf16))


def project_back(args, pieces, after):
    rows, width = args[0].shape[0], args[5].shape[1]
    return call(
        project_back_kernel,
        [shaped((rows, width), f32)] * 2 + grad_shapes(width, pieces[0].shape[1]),
        [*args, *pieces],
        us=8,
        after=after,
    )


def input_back_kernel(dh_before, dh, x, gains, dx1, order, before, own):
    rows = dx1.shape[0]
    table = order[...]
    for c in range(rows // 256):
        part = pl.ds(c * 256, 256)
        back, _ = rms_back(x[part].astype(f32), gains[0:1], dh_before[part])
        before[part] = nt(back.astype(bf16), table).astype(bf16)
        mine = x[rows + c * 256 : rows + (c + 1) * 256].astype(f32)
        back, _ = rms_back(mine, gains[0:1], dh[part])
        rest = back + dx1[part]
        total = jnp.zeros_like(rest)
        for _ in range(3):
            piece = rest.astype(bf16)
            rest = rest - piece.astype(f32)
            total = total + nt(piece, table)
        own[part] = total


def input_back(dh_before, dh, x, gains, dx1, order, after=()):
    outs = [shaped(dx1.shape, bf16), shaped(dx1.shape, f32)]
    args = [dh_before, dh, x, gains, dx1, order]
    return call(input_back_kernel, outs, args, us=0.3, after=after)


def on_device(
    tokens,
    segment_ids,
    w_query,
    w_key,
    w_value,
    w_output,
    w_gate,
    w_up,
    w_down,
    norm_gains,
    qk_gains,
    cotangent,
):
    n = lax.axis_size("seq")
    me = lax.axis_index("seq")
    rows, width = tokens.shape
    shard = w_query.shape[0]
    qk_shard = qk_gains.shape[0]

    extra = jnp.concatenate(
        [
            norm_gains.T,
            jnp.pad(qk_gains, (0, shard - qk_shard))[:, None],
            jnp.zeros((shard, EXTRA - 5), bf16),
        ],
        axis=1,
    )
    travel_a, travel_b, travel_c = travelling(
        (w_query, w_key, w_value, extra), (w_output.T, w_gate, w_up), (w_down.T,)
    )
    cols_a = w_query.shape[1] + w_key.shape[1] + w_value.shape[1] + EXTRA
    cols_b = w_output.shape[0] + w_gate.shape[1] + w_up.shape[1]
    cols_c = w_down.shape[0]

    even, odd, inner = row_table(n, shard)
    device = me ^ jnp.where(me & 1 == 0, jnp.asarray(even), jnp.asarray(odd))
    place = device * shard + inner
    qk_place = jnp.where(inner < qk_shard, device * qk_shard + inner, -1)
    padded_ids = jnp.concatenate([jnp.full((LONGEST + rows,), -1, jnp.int32), segment_ids])
    nearby = lax.dynamic_slice_in_dim(padded_ids, me * rows, 2 * rows + LONGEST)
    keys_segment = nearby[LONGEST:]
    seg_q = keys_segment[rows:, None]
    seg_k = jnp.stack(
        [keys_segment[b * BLOCK : b * BLOCK + REACH] for b in range(rows // BLOCK)]
    )[:, None, :]

    tokens_before = lax.ppermute(tokens, "seq", [(i, i + 1) for i in range(n - 1)])
    a_c = to_first(travel_c, n)
    (own_a,) = pack(far_direct(travel_a, n), shard, cols_a, 1, n, after=(a_c, tokens_before))
    travel_b, pair_c = call(
        start_kernel,
        [
            shaped(travel_b.shape, bf16),
            shaped((2 * travel_c.shape[0], travel_c.shape[1]), bf16),
        ],
        [travel_c, a_c, travel_b],
        us=0.2,
        after=(own_a,),
    )
    near_a = near_pieces(own_a, n, direct=True)
    cosine, sine, order, qk_order = tables(nearby, rows, place, qk_place, width, after=(own_a,))
    x, dy = permute(tokens_before, tokens, cotangent, order)
    (own_b,) = pack(
        far_direct(travel_b, n), shard, cols_b, 1, n, after=(x, seg_q, seg_k, *near_a[1:])
    )
    own_a, pair_c = hold(own_a, pair_c, after=(own_b,))
    weights_a = [own_a, *near_a[1:]]
    weights_a = [*weights_a, *to_core(weights_a, n)]
    hidden, q_raw, k_raw, q, k, v, probs, o, gains, qk_gain = attend(
        x, weights_a, qk_order, cosine, sine, seg_q, seg_k, after=(own_b,)
    )
    a_b, b_b = to_first(own_b, n), to_second(own_b, n)
    half_c = pack(far_direct(pair_c, n), shard, cols_c, 2, n, after=(o, a_b, b_b))
    a_b, own_b = hold(a_b, own_b, after=half_c)
    far_half = to_second(half_c[0], n)
    weights_b = [own_b, a_b, b_b, to_second(a_b, n)]
    weights_b = [*weights_b, *to_core(weights_b, n)]
    steps = len(far_bits(n)[0])
    a, middle, normed, product, by_gate, by_up = feed(o, weights_b, x, gains, after=())
    half_c = [*half_c, *hold(far_half, after=(product,))]
    weights_c = [*half_c, *to_core(half_c, n)]
    mixed, low, gain3, *grad_d = turn(product, weights_c, middle, dy, gains, order)
    gate_low, up_low, *grad_g = feed_back(low, weights_c, by_gate, by_up, normed)
    sum_d = core_sum(grad_d[0], grad_d[1:], n, after=(gate_low,))
    sum_g = core_sum(grad_g[0], grad_g[1:], n, after=sum_d[:1])
    dx1, gain12, do, *grad_u = middle_back(
        gate_low, up_low, weights_b, middle, a, dy, gains, normed, o, after=sum_g[:1]
    )
    dq_low, dkv_before, dkv_own, qk_grad = attend_back(
        probs, do, q, k, v, q_raw, k_raw, cosine, sine, qk_gain, after=()
    )
    sum_d = near_sum_first_both(sum_d, sum_g, n, after=(dq_low,))
    sum_u = core_sum(grad_u[0], grad_u[1:], n, after=sum_d[:1])
    dh_before, dh, *grad_a = project_back(
        [dq_low, dkv_before, dkv_own, qk_grad, hidden, x, qk_order, gain3, gain12],
        weights_a,
        after=sum_u[:1],
    )
    sum_a = core_sum(grad_a[0], grad_a[1:], n)
    sum_d = near_sum_second(sum_d, n, after=sum_a[:1])
    sum_u = near_sum_first(sum_u, n, after=sum_d[:1], us=4)
    before, own = input_back(dh_before, dh, x, gains, dx1, order, after=sum_u[:1])
    sum_a = near_sum_first(sum_a, n, after=(own,))
    sum_d = far_sum_first(sum_d, n, after=sum_a[:1])
    sum_u = near_sum_second(sum_u, n, after=sum_d[:1])
    sum_a = near_sum_direct_far(sum_a, n, after=sum_u[:1])
    ff = grad_d[0].shape[1]
    sum_d, sum_g = far_sum_last(sum_d, n, shard, (0, ff, 2 * ff), after=sum_a[:1])
    sum_u = far_sum_first(sum_u, n, after=(sum_d,))
    behind = lax.ppermute(before, "seq", [(i + 1, i) for i in range(n - 1)])
    sum_u, sum_o = far_sum_last(sum_u, n, shard, (0, ff, ff + 1024))
    sum_q, sum_k, sum_v, sum_n = far_sum_direct(
        sum_a, n, shard, (0, 1024, 1280, 1536, 1664), after=(sum_u,)
    )
    input_grad = own + behind.astype(f32)
    return (
        mixed,
        input_grad,
        sum_q,
        sum_k,
        sum_v,
        sum_o.T,
        sum_g,
        sum_u,
        sum_d.T,
        sum_n[:, :4].T,
        sum_n[:qk_shard, 4],
    )


def solution(mesh):
    return jax.shard_map(
        on_device,
        mesh=mesh,
        in_specs=(
            P("seq", None),
            P(),
            P("seq", None),
            P("seq", None),
            P("seq", None),
            P(None, "seq"),
            P("seq", None),
            P("seq", None),
            P(None, "seq"),
            P(None, "seq"),
            P("seq"),
            P("seq", None),
        ),
        out_specs=(
            P("seq", None),
            P("seq", None),
            P("seq", None),
            P("seq", None),
            P("seq", None),
            P(None, "seq"),
            P("seq", None),
            P("seq", None),
            P(None, "seq"),
            P(None, "seq"),
            P("seq"),
        ),
        check_vma=False,
    )
```

```python
import functools

import jax
import jax.numpy as jnp
import numpy as np
from jax import lax
from jax.experimental import pallas as pl
from jax.experimental.pallas import tpu as pltpu
from jax.sharding import PartitionSpec as P

H = 4
HD = 256
WINDOW = 512
LONGEST = 2048
EXTRA = 128
EIGHT = 8
FF_CHUNK = 512
BLOCK = 128
REACH = BLOCK + WINDOW
MIB = 1024 * 1024

epsilon = 1e-06
bf16 = jnp.bfloat16
f32 = jnp.float32


def far_bits(n):
    bits = [1 << i for i in range(n.bit_length() - 1)]
    rest = [b for b in bits[1:] if b not in near_pair(n)]
    return rest, rest[::-1]


def far_slots(bits):
    slots = [0]
    for b in bits:
        slots = slots + [s | b for s in slots]
    return slots


def near_pair(n):
    return (2, 8) if n > 64 else (2, 4)


def to_partner(x, n, masks):
    return lax.ppermute(x, "seq", [(i, i ^ masks[i & 1]) for i in range(n)])


def row_table(n, shard):
    first, second = near_pair(n)
    main = whole_tiles(shard)
    count = n // 8
    inner = [(i, r) for i in range(count) for r in range(main)]
    inner += [(i, r) for i in range(count) for r in range(main, shard)]

    def offsets(a, b, bits):
        far = far_slots(bits)
        return [m ^ far[i] for m in (0, a, b, a | b) for i, _ in inner]

    even_bits, odd_bits = far_bits(n)
    even, odd = offsets(first, second, even_bits), offsets(second, first, odd_bits)
    return (
        np.array(even + [1 ^ m for m in odd], np.int32),
        np.array(odd + [1 ^ m for m in even], np.int32),
        np.array([r for _, r in inner] * 8, np.int32),
    )


def nn(left, right):
    return jnp.dot(left, right, preferred_element_type=f32)


def tn(left, right):
    return lax.dot_general(left, right, (((0,), (0,)), ((), ())), preferred_element_type=f32)


def nt(left, right):
    return lax.dot_general(left, right, (((1,), (1,)), ((), ())), preferred_element_type=f32)


def inverse_rms(values):
    return lax.rsqrt(jnp.mean(values * values, axis=-1, keepdims=True) + epsilon)


def rms_back(values, gain, grad):
    scale = inverse_rms(values)
    hat = values * scale
    inner = grad * gain
    mean = jnp.mean(inner * hat, axis=-1, keepdims=True)
    return scale * (inner - hat * mean), jnp.sum(grad * hat, axis=0, keepdims=True)


def rotate(values, cosine, sine):
    half = values.shape[-1] // 2
    a, b = values[:, :half], values[:, half:]
    return jnp.concatenate([a * cosine - b * sine, b * cosine + a * sine], axis=-1)


def rotate_back(values, cosine, sine):
    half = values.shape[-1] // 2
    a, b = values[:, :half], values[:, half:]
    return jnp.concatenate([a * cosine + b * sine, b * cosine - a * sine], axis=-1)


def call(kernel, outs, args, us, scratch=(), after=(), room=12):
    given, extra = len(args), len(after)

    def body(*refs):
        kernel(*refs[:given], *refs[given + extra :])

    return pl.pallas_call(
        body,
        in_specs=[pl.BlockSpec(memory_space=pltpu.VMEM)] * given
        + [pl.BlockSpec(memory_space=pl.ANY)] * extra,
        out_specs=[pl.BlockSpec(memory_space=pltpu.VMEM)] * len(outs),
        out_shape=outs,
        scratch_shapes=scratch,
        compiler_params=pltpu.CompilerParams(vmem_limit_bytes=room * MIB),
        cost_estimate=pl.CostEstimate(
            flops=int(us * 10**9), bytes_accessed=int(us * 10**6), transcendentals=0
        ),
    )(*args, *after)


def shaped(shape, dtype):
    return jax.ShapeDtypeStruct(shape, dtype)


def join_rows(parts, cols=slice(None)):
    return jnp.concatenate([p[:, cols] for p in parts], axis=0)


def whole_tiles(rows):
    return rows // 16 * 16


def padded(cols):
    return -(-cols // 512) * 512


def in_tiles(rows):
    return rows == 20


def travel_shape(rows, cols):
    return (16, padded(cols) * 5 // 4) if in_tiles(rows) else (rows, cols)


def to_tiles(values):
    rows, cols = values.shape
    if not in_tiles(rows):
        return values
    wide = padded(cols)
    if wide > cols:
        values = jnp.concatenate([values, jnp.zeros((rows, wide - cols), f32)], axis=1)
    quarter = wide // 4
    rest = [values[16:, k * quarter : (k + 1) * quarter] for k in range(4)]
    return jnp.concatenate([values[:16], jnp.concatenate(rest, axis=0)], axis=1)


def tile_kernel(counts, *refs):
    total = sum(counts)
    given, outs = refs[:total], refs[total : total + len(counts)]
    held, sem = refs[total + len(counts) : -1], refs[-1]
    copies = [
        pltpu.make_async_copy(source, target, sem.at[i])
        for i, (source, target) in enumerate(zip(given, held))
    ]
    for copy in copies:
        copy.start()
    for copy in copies:
        copy.wait()
    for count, out in zip(counts, outs):
        parts, held = held[:count], held[count:]
        values = jnp.concatenate([p[...].astype(f32) for p in parts], axis=1)
        out[...] = to_tiles(values).astype(bf16)


def travelling(*groups):
    counts = [len(g) for g in groups]
    given = [w for g in groups for w in g]
    outs = []
    for g in groups:
        outs.append(shaped(travel_shape(g[0].shape[0], sum(w.shape[1] for w in g)), bf16))
    return pl.pallas_call(
        functools.partial(tile_kernel, counts),
        in_specs=[pl.BlockSpec(memory_space=pltpu.HBM)] * len(given),
        out_specs=[pl.BlockSpec(memory_space=pltpu.VMEM)] * len(outs),
        out_shape=outs,
        scratch_shapes=[pltpu.VMEM(w.shape, bf16) for w in given]
        + [pltpu.SemaphoreType.DMA((len(given),))],
        compiler_params=pltpu.CompilerParams(vmem_limit_bytes=8 * MIB),
    )(*[pltpu.with_memory_space_constraint(w, pltpu.HBM) for w in given])


def stack_kernel(*refs):
    count = len(refs) // 3
    for i in range(count):
        a, b, out = refs[2 * i], refs[2 * i + 1], refs[2 * count + i]
        rows = a.shape[0]
        if rows % 16 == 0:
            out[:rows] = a[...]
            out[rows:] = b[...]
        else:
            both = [a[...].astype(f32), b[...].astype(f32)]
            out[...] = jnp.concatenate(both, axis=0).astype(bf16)


def stack(*pairs, after=()):
    outs = [shaped((2 * a.shape[0], a.shape[1]), bf16) for a, _ in pairs]
    return call(stack_kernel, outs, [x for pair in pairs for x in pair], us=0.5, after=after)


def pack_kernel(pieces, blocks, out):
    count = len(pieces)
    share, cols = out.shape[0] // blocks, out.shape[1]
    rows = share // count
    main = whole_tiles(rows)
    height, wide = travel_shape(rows, cols)
    quarter = padded(cols) // 4
    for block in range(blocks):
        at = block * share
        starts = [(ref, begin + block * height) for ref, begin in pieces]
        if main:
            for i, (ref, begin) in enumerate(starts):
                out[at + i * main : at + (i + 1) * main] = ref[begin : begin + main, :cols]
        at = at + main * count
        if in_tiles(rows):
            rest = [ref[begin : begin + 16, 4 * quarter :].astype(f32) for ref, begin in starts]
            for k in range(4):
                end = min((k + 1) * quarter, cols)
                part = jnp.concatenate([r[4 * k : 4 * k + 4] for r in rest], axis=0)
                out[at : at + 4 * count, k * quarter : end] = part[:, : end - k * quarter].astype(
                    bf16
                )
        elif rows > main:
            rest = [
                ref[...].astype(f32)[begin + main : begin + rows] for ref, begin in starts
            ]
            out[at : at + (rows - main) * count] = jnp.concatenate(rest, axis=0).astype(bf16)


def pack(arrays, rows, cols, blocks, n, parts=1, after=()):
    count = n // 8
    height = travel_shape(rows, cols)[0] * blocks
    held = count // len(arrays)
    total = rows * count * blocks

    def kernel(*refs):
        given = refs[: len(arrays)]
        pieces = [(ref, h * height) for ref in given for h in range(held)]
        if parts == 1:
            pack_kernel(pieces, blocks, refs[-1])
        else:
            for block, out in enumerate(refs[len(arrays) :]):
                shift = block * height // blocks
                pack_kernel([(ref, at + shift) for ref, at in pieces], 1, out)

    outs = [shaped((total // parts, cols), bf16)] * parts
    return call(kernel, outs, arrays, us=1.5, after=after)


def far_step(block, n, step):
    even, odd = far_bits(n)
    return to_partner(block, n, (even[step], odd[step]))


def far_direct(block, n):
    even, odd = far_bits(n)
    slots = zip(far_slots(even)[1:], far_slots(odd)[1:])
    return [block] + [to_partner(block, n, masks) for masks in slots]


def start_kernel(a, b, one, one_out, out):
    stack_kernel(a, b, out)
    one_out[...] = one[...]


def hold_kernel(*refs):
    half = len(refs) // 2
    for value, out in zip(refs[:half], refs[half:]):
        out[...] = value[...]


def hold(*values, after):
    return call(hold_kernel, [shaped(v.shape, v.dtype) for v in values], values, 0.2, after=after)


def far_gather(blocks, n, joins):
    steps = len(far_bits(n)[0])
    for k in range(steps - 1):
        got = [far_step(b, n, k) for b in blocks]
        blocks = stack(*zip(blocks, got), after=joins[k] if k < len(joins) else ())
    return [(b, far_step(b, n, steps - 1)) for b in blocks]


def to_first(x, n):
    first, second = near_pair(n)
    return to_partner(x, n, (first, second))


def to_second(x, n):
    first, second = near_pair(n)
    return to_partner(x, n, (second, first))


def near_pieces(own, n, direct=False):
    first, second = near_pair(n)
    a, b = to_first(own, n), to_second(own, n)
    return [own, a, b, to_partner(own, n, (first | second,) * 2) if direct else to_second(a, n)]


def to_core(pieces, n):
    return [to_partner(p, n, (1, 1)) for p in pieces]


def fold_kernel(count, *refs):
    given, outs = refs[:count], refs[count:]
    mine, got = given[0], given[1:]
    rows = outs[0].shape[0]
    height = got[0].shape[0]
    if rows % 16 == 0 and height % rows == 0:
        per = height // rows
        for i, out in enumerate(outs):
            other = got[i // per][(i % per) * rows : (i % per + 1) * rows]
            part = mine[i * rows : (i + 1) * rows]
            out[...] = (part.astype(f32) + other.astype(f32)).astype(bf16)
    else:
        total = mine[...].astype(f32)
        total = total + jnp.concatenate([g[...].astype(f32) for g in got], axis=0)
        for i, out in enumerate(outs):
            out[...] = total[i * rows : (i + 1) * rows].astype(bf16)


def fold(mine, got, after=(), us=0.5):
    rows, cols = mine.shape
    outs = [shaped((rows // 2, cols), bf16)] * 2
    kernel = functools.partial(fold_kernel, 1 + len(got))
    return call(kernel, outs, [mine, *got], us=us, after=after)


def wide_fold_kernel(mine, *refs):
    got, (keep, send) = refs[:-2], refs[-2:]
    rows = got[0].shape[0]
    per = keep.shape[0] // rows
    for i, other in enumerate(got):
        out = keep if i < per else send
        at = (i % per) * rows
        part = mine[i * rows : (i + 1) * rows].astype(f32)
        out[at : at + rows] = (part + other[...].astype(f32)).astype(bf16)


def core_sum(top, sends, n, after=()):
    rows, cols = top.shape
    outs = [shaped((rows // 2, cols), bf16)] * 2
    return call(wide_fold_kernel, outs, [top, *to_core(sends, n)], us=0.7, after=after)


def core_sum_by_far(top, sends, n, after=()):
    rows, cols = top.shape
    count, blocks = n // 8, len(sends)
    shard = rows // blocks // count
    main = whole_tiles(shard)
    rest, done = shard - main, main * count
    height, wide = travel_shape(shard, cols)

    def kernel(mine, *refs):
        got, (keep, send) = refs[:-2], refs[-2:]
        share = rows // blocks
        tiles = []
        for block in range(blocks):
            total = mine[block * share : (block + 1) * share].astype(f32) + got[block][...].astype(
                f32
            )
            for i in range(count):
                parts = []
                if main:
                    parts.append(total[i * main : (i + 1) * main])
                if rest:
                    parts.append(total[done + i * rest : done + (i + 1) * rest])
                tiles.append((i, block, to_tiles(jnp.concatenate(parts, axis=0))))
        tiles = [t for _, _, t in sorted(tiles, key=lambda item: item[:2])]
        half = len(tiles) // 2
        keep[...] = jnp.concatenate(tiles[:half], axis=0).astype(bf16)
        send[...] = jnp.concatenate(tiles[half:], axis=0).astype(bf16)

    outs = [shaped((count // 2 * blocks * height, wide), bf16)] * 2
    return call(kernel, outs, [top, *to_core(sends, n)], us=1.5, after=after)


def far_fold(halves, n, step, after=()):
    keep, send = halves
    return fold(keep, [far_step(send, n, step)], after)


def near_sum_last(halves, n, shard, cuts, after=()):
    keep, send = halves
    outs = [shaped((shard, e - b), f32) for b, e in zip(cuts[:-1], cuts[1:])]
    return call(
        functools.partial(far_sum_kernel, (cuts,)), outs, [keep, to_first(send, n)], us=1, after=after
    )


def near_sum_first(halves, n, after=(), us=0.5):
    keep, send = halves
    return fold(keep, [to_second(send, n)], after, us)


def fold_both_kernel(*refs):
    given, (keep, send) = refs[:4], refs[4:]
    rows, cols = keep.shape
    cols = cols // 2
    for i in range(2):
        mine, got = given[2 * i : 2 * i + 2]
        for j, out in enumerate((keep, send)):
            part = slice(j * rows, (j + 1) * rows)
            out[:, i * cols : (i + 1) * cols] = (
                mine[part].astype(f32) + got[part].astype(f32)
            ).astype(bf16)


def near_sum_first_both(one, two, n, after=()):
    args = [x for keep, send in (one, two) for x in (keep, to_second(send, n))]
    rows, cols = one[0].shape
    outs = [shaped((rows // 2, 2 * cols), bf16)] * 2
    return call(fold_both_kernel, outs, args, us=5, after=after)


def split_kernel(count, mine, got, keep, send):
    total = mine[...].astype(f32) + got[...].astype(f32)
    rows = total.shape[0] // count
    main = whole_tiles(rows)
    rest, done = rows - main, main * count
    slots = []
    for i in range(count):
        parts = []
        if main:
            parts.append(total[i * main : (i + 1) * main])
        if rest:
            parts.append(total[done + i * rest : done + (i + 1) * rest])
        slots.append(to_tiles(jnp.concatenate(parts, axis=0)))
    keep[...] = jnp.concatenate(slots[: count // 2], axis=0).astype(bf16)
    send[...] = jnp.concatenate(slots[count // 2 :], axis=0).astype(bf16)


def near_sum_second(halves, n, after=()):
    keep, send = halves
    rows, cols = keep.shape
    count = n // 8
    height, wide = travel_shape(rows // count, cols)
    outs = [shaped((count // 2 * height, wide), bf16)] * 2
    return call(
        functools.partial(split_kernel, count), outs, [keep, to_first(send, n)], us=1, after=after
    )


def slots_kernel(groups, count, *refs):
    outs = refs[2 * groups :]
    slots = [[] for _ in range(count)]
    for g in range(groups):
        total = refs[2 * g][...].astype(f32) + refs[2 * g + 1][...].astype(f32)
        rows = total.shape[0] // count
        main = whole_tiles(rows)
        rest, done = rows - main, main * count
        for i in range(count):
            parts = []
            if main:
                parts.append(total[i * main : (i + 1) * main])
            if rest:
                parts.append(total[done + i * rest : done + (i + 1) * rest])
            slots[i].append(to_tiles(jnp.concatenate(parts, axis=0)))
    per = count // len(outs)
    for i, parts in enumerate(slots):
        values = jnp.concatenate(parts, axis=1).astype(bf16)
        height = values.shape[0]
        if per == 1:
            outs[i][...] = values
        elif height % 16 == 0:
            outs[i // per][i % per * height : (i % per + 1) * height] = values
    if per > 1 and height % 16 != 0:
        for j, out in enumerate(outs):
            values = [jnp.concatenate(p, axis=1) for p in slots[j * per : (j + 1) * per]]
            out[...] = jnp.concatenate(values, axis=0).astype(bf16)


def near_sum_far(groups, n, parts, after=()):
    count = n // 8
    args, wide = [], 0
    for keep, send in groups:
        args += [keep, to_first(send, n)]
        height, cols = travel_shape(keep.shape[0] // count, keep.shape[1])
        wide += cols
    outs = [shaped((height * count // parts, wide), bf16)] * parts
    kernel = functools.partial(slots_kernel, len(groups), count)
    return call(kernel, outs, args, us=1, after=after)


def far_sum_direct(pieces, n, shard, groups, after=()):
    even, odd = far_bits(n)
    slots = zip(pieces[1:], far_slots(even)[1:], far_slots(odd)[1:])
    got = [to_partner(p, n, (e, o)) for p, e, o in slots]
    outs = [shaped((shard, e - b), f32) for cuts in groups for b, e in zip(cuts[:-1], cuts[1:])]
    return call(
        functools.partial(far_sum_kernel, groups), outs, [pieces[0], *got], us=1, after=after
    )


def far_sum_first(halves, n, after=()):
    keep, send = halves
    for k in reversed(range(1, len(far_bits(n)[0]))):
        keep, send = fold(keep, [far_step(send, n, k)], after)
        after = ()
    return keep, send


def far_sum_kernel(groups, *refs):
    count = sum(len(cuts) - 1 for cuts in groups)
    given, outs = refs[:-count], refs[-count:]
    total = given[0][...].astype(f32)
    for got in given[1:]:
        total = total + got[...].astype(f32)
    rows = outs[0].shape[0]
    begin_at = 0
    for cuts in groups:
        wide = padded(cuts[-1]) if in_tiles(rows) else cuts[-1]
        part = total[:, begin_at : begin_at + wide]
        if in_tiles(rows):
            quarter = wide // 4
            rest = total[:, begin_at + wide : begin_at + wide + quarter]
            rest = [rest[4 * k : 4 * k + 4] for k in range(4)]
            part = jnp.concatenate([part, jnp.concatenate(rest, axis=1)], axis=0)
            begin_at += quarter
        begin_at += wide
        for begin, end in zip(cuts[:-1], cuts[1:]):
            outs[0][...] = part[:, begin:end]
            outs = outs[1:]


def far_sum_last(halves, n, shard, groups, after=()):
    keep, send = halves
    outs = [shaped((shard, e - b), f32) for cuts in groups for b, e in zip(cuts[:-1], cuts[1:])]
    return call(
        functools.partial(far_sum_kernel, groups), outs, [keep, far_step(send, n, 0)], us=1,
        after=after,
    )


def table_kernel(near, near_col, freqs, place, qk_place, first, cosine, sine, order, qk_order, first_out):
    count = cosine.shape[0]
    ahead = near.shape[1] - count
    steps = freqs[...]
    for c in range(count // 256):
        reach = slice(c * 256, c * 256 + ahead + 256)
        here = near_col[ahead + c * 256 : ahead + (c + 1) * 256]
        i = lax.broadcasted_iota(jnp.int32, (256, ahead + 256), 0) + ahead
        j = lax.broadcasted_iota(jnp.int32, (256, ahead + 256), 1)
        same = (here == near[:, reach]) & (j < i)
        position = jnp.sum(same.astype(f32), axis=1, keepdims=True)
        angles = position * steps
        cosine[c * 256 : (c + 1) * 256] = jnp.cos(angles)
        sine[c * 256 : (c + 1) * 256] = jnp.sin(angles)
    i = lax.broadcasted_iota(jnp.int32, order.shape, 0)
    order[...] = (i == place[...]).astype(f32).astype(bf16)
    j = lax.broadcasted_iota(jnp.int32, qk_order.shape, 1)
    qk_order[...] = (qk_place[...] == j).astype(f32).astype(bf16)
    first_out[...] = jnp.broadcast_to(first[...], first_out.shape)


def tables(near, rows, place, qk_place, width, first, after=()):
    freqs = np.float32(10000.0) ** (-2.0 * np.arange(HD // 2, dtype=np.float32) / np.float32(HD))
    args = [
        near[None, :], near[:, None], jnp.asarray(freqs)[None, :], place[None, :], qk_place[:, None],
        first,
    ]
    outs = [
        shaped((2 * rows, HD // 2), f32), shaped((2 * rows, HD // 2), f32),
        shaped((width, width), bf16), shaped((width, 2 * HD), bf16), shaped((8, 128), f32),
    ]
    return call(table_kernel, outs, args, us=3, after=after)


def permute_kernel(tokens_before, tokens, cotangent, order, x, dy):
    table = order[...]
    rows = tokens.shape[0]
    x[:rows] = nn(tokens_before[...], table).astype(bf16)
    x[rows:] = nn(tokens[...], table).astype(bf16)
    dy[...] = nn(cotangent[...], table).astype(bf16)


def permute(tokens_before, tokens, cotangent, order, after=()):
    rows, width = tokens.shape
    outs = [shaped((2 * rows, width), bf16), shaped((rows, width), bf16)]
    args = [tokens_before, tokens, cotangent, order]
    return call(permute_kernel, outs, args, us=2, after=after)


def attend_kernel(x, qk_order, cosine, sine, seg_q, seg_k, *refs):
    pieces = refs[:-10]
    hidden, q_raw, k_raw, q_out, k_out, v_out, probs, o, gains, qk_gain = refs[-10:]
    rows = q_raw.shape[0]
    w_q = join_rows(pieces, slice(0, 1024))
    w_kv = join_rows(pieces, slice(1024, 1536))
    gain_rows = join_rows(pieces, slice(1536, 1664)).astype(f32).T[:8]
    gains[...] = gain_rows
    gain_qk = nn(gain_rows.astype(bf16), qk_order[...])
    qk_gain[...] = gain_qk
    gain_q, gain_k = gain_qk[4:5, :HD], gain_qk[4:5, HD:]
    for c in range(2 * rows // 256):
        part = pl.ds(c * 256, 256)
        xs = x[part].astype(f32)
        hs = (xs * inverse_rms(xs) * gain_rows[0:1]).astype(bf16)
        hidden[part] = hs
        cs, sn = cosine[part], sine[part]
        kv = nn(hs, w_kv)
        raw = kv[:, :HD]
        k_raw[part] = raw
        k_out[part] = rotate(raw * inverse_rms(raw) * gain_k, cs, sn).astype(bf16)
        v_out[part] = kv[:, HD:].astype(bf16)
        if c * 256 >= rows:
            own = pl.ds(c * 256 - rows, 256)
            qs = nn(hs, w_q)
            q_raw[own] = qs
            for h in range(H):
                raw = qs[:, h * HD : (h + 1) * HD]
                q_out[own, h * HD : (h + 1) * HD] = rotate(
                    raw * inverse_rms(raw) * gain_q, cs, sn
                ).astype(bf16)
    for b in range(rows // BLOCK):
        mine = pl.ds(b * BLOCK, BLOCK)
        reach = pl.ds(b * BLOCK, REACH)
        q_rows = q_out[mine] * bf16(1.0 / 16.0)
        q_stack = jnp.concatenate([q_rows[:, h * HD : (h + 1) * HD] for h in range(H)], axis=0)
        scores = nt(q_stack, k_out[reach])
        i = lax.broadcasted_iota(jnp.int32, (BLOCK, REACH), 0)
        j = lax.broadcasted_iota(jnp.int32, (BLOCK, REACH), 1)
        allowed = (j > i) & (j <= i + WINDOW) & (seg_q[mine] == seg_k[b])
        allowed = jnp.concatenate([allowed.astype(f32)] * H, axis=0)
        weights = jnp.exp(scores) * allowed
        total = jnp.sum(weights, axis=-1, keepdims=True)
        p = (weights * (1.0 / total)).astype(bf16)
        probs[b] = p
        out = nn(p, v_out[reach])
        for h in range(H):
            o[mine, h * HD : (h + 1) * HD] = out[h * BLOCK : (h + 1) * BLOCK].astype(bf16)


def attend(x, pieces, qk_order, cosine, sine, seg_q, seg_k, after):
    rows = x.shape[0] // 2
    width = x.shape[1]
    return call(
        attend_kernel,
        [
            shaped((2 * rows, width), bf16),
            shaped((rows, H * HD), f32),
            shaped((2 * rows, HD), f32),
            shaped((rows, H * HD), bf16),
            shaped((2 * rows, HD), bf16),
            shaped((2 * rows, HD), bf16),
            shaped((rows // BLOCK, H * BLOCK, REACH), bf16),
            shaped((rows, H * HD), bf16),
            shaped((8, width), f32),
            shaped((8, 2 * HD), f32),
        ],
        [x, qk_order, cosine, sine, seg_q, seg_k, *pieces],
        us=8,
        after=after,
    )


def gelu_parts(g):
    c0, c1 = 0.7978845608028654, 0.044715
    square = g * g
    t = jnp.tanh(c0 * g * (1.0 + c1 * square))
    value = 0.5 * g * (1.0 + t)
    slope = 0.5 * (1.0 + t) + 0.5 * g * (1.0 - t * t) * c0 * (1.0 + 3.0 * c1 * square)
    return value, slope


def feed_kernel(o, x, gains, *refs):
    pieces = refs[:-6]
    a_out, middle, normed, product, by_gate, by_up = refs[-6:]
    rows, ff = product.shape
    w_o = join_rows(pieces, slice(0, H * HD))
    for c in range(rows // 256):
        part = pl.ds(c * 256, 256)
        a = nt(o[part], w_o)
        a_out[part] = a
        x1 = x[rows + c * 256 : rows + (c + 1) * 256].astype(f32) + a * inverse_rms(a) * gains[1:2]
        middle[part] = x1
        normed[part] = (x1 * inverse_rms(x1) * gains[2:3]).astype(bf16)
    for j in range(ff // FF_CHUNK):
        cols = slice(j * FF_CHUNK, (j + 1) * FF_CHUNK)
        w_g = join_rows(pieces, slice(H * HD + cols.start, H * HD + cols.stop))
        w_u = join_rows(pieces, slice(H * HD + ff + cols.start, H * HD + ff + cols.stop))
        for c in range(rows // 256):
            part = pl.ds(c * 256, 256)
            h2 = normed[part]
            g = nn(h2, w_g)
            u = nn(h2, w_u)
            value, slope = gelu_parts(g)
            product[part, cols] = (value * u).astype(bf16)
            by_gate[part, cols] = (slope * u).astype(bf16)
            by_up[part, cols] = value.astype(bf16)


def feed(o, pieces, x, gains, after):
    rows, width = o.shape[0], x.shape[1]
    ff = (pieces[0].shape[1] - H * HD) // 2
    return call(
        feed_kernel,
        [
            shaped((rows, width), f32),
            shaped((rows, width), f32),
            shaped((rows, width), bf16),
            shaped((rows, ff), bf16),
            shaped((rows, ff), bf16),
            shaped((rows, ff), bf16),
        ],
        [o, x, gains, *pieces],
        us=6,
        after=after,
    )


def put_grad(grads, cols, values):
    top, *sends = grads
    half = top.shape[0]
    top[:, cols] = values[:half]
    part = half // len(sends)
    for i, send in enumerate(sends):
        send[:, cols] = values[half + i * part : half + (i + 1) * part]


def grad_shapes(width, cols):
    return [shaped((width // 2, cols), bf16)] + [shaped((width // 4, cols), bf16)] * 2


def turn_kernel(product, middle, dy, gains, order, *refs):
    pieces, (mixed, low, gain_grad, *grads) = refs[:-6], refs[-6:]
    ff = product.shape[1]
    w_d = join_rows(pieces)
    total = jnp.zeros((1, dy.shape[1]), f32)
    for c in range(dy.shape[0] // 256):
        part = pl.ds(c * 256, 256)
        f = nt(product[part], w_d)
        grad = dy[part].astype(f32)
        y = middle[part] + f * inverse_rms(f) * gains[3:4]
        mixed[part] = nt(y.astype(bf16), order[...]).astype(bf16)
        df, dgain = rms_back(f, gains[3:4], grad)
        low[part] = df.astype(bf16)
        total = total + dgain
    gain_grad[...] = jnp.broadcast_to(total, gain_grad.shape)
    for j in range(ff // FF_CHUNK):
        cols = slice(j * FF_CHUNK, (j + 1) * FF_CHUNK)
        grad = tn(low[...], product[:, cols]).astype(bf16)
        put_grad(grads, cols, grad)


def turn(product, pieces, middle, dy, gains, order):
    rows, width = middle.shape
    return call(
        turn_kernel,
        [
            shaped((rows, width), bf16),
            shaped((rows, width), bf16),
            shaped((8, width), f32),
            *grad_shapes(width, product.shape[1]),
        ],
        [product, middle, dy, gains, order, *pieces],
        us=6,
    )


def feed_back_kernel(low, by_gate, by_up, normed, *refs):
    pieces, (gate_low, up_low, *grads) = refs[:-5], refs[-5:]
    rows, ff = gate_low.shape
    for j in range(ff // FF_CHUNK):
        cols = slice(j * FF_CHUNK, (j + 1) * FF_CHUNK)
        w_d = join_rows(pieces, cols)
        for c in range(rows // 256):
            part = pl.ds(c * 256, 256)
            dm = nn(low[part], w_d)
            gate_low[part, cols] = (dm * by_gate[part, cols].astype(f32)).astype(bf16)
            up_low[part, cols] = (dm * by_up[part, cols].astype(f32)).astype(bf16)
        put_grad(grads, cols, tn(normed[...], gate_low[:, cols]).astype(bf16))


def feed_back(low, pieces, by_gate, by_up, normed):
    rows, width = low.shape
    ff = by_gate.shape[1]
    return call(
        feed_back_kernel,
        [shaped((rows, ff), bf16)] * 2 + grad_shapes(width, ff),
        [low, by_gate, by_up, normed, *pieces],
        us=4,
    )


def middle_back_kernel(gate_low, up_low, middle, a, dy, gains, normed, o, *refs):
    pieces, (dx1, gain_grad, do, *grads) = refs[:-6], refs[-6:]
    rows, ff = gate_low.shape
    w_o = join_rows(pieces, slice(0, H * HD))
    w_g = join_rows(pieces, slice(H * HD, H * HD + ff))
    w_u = join_rows(pieces, slice(H * HD + ff, H * HD + 2 * ff))
    sum1 = jnp.zeros((1, dy.shape[1]), f32)
    sum2 = jnp.zeros((1, dy.shape[1]), f32)
    lows = []
    for c in range(rows // 256):
        part = pl.ds(c * 256, 256)
        grad = nt(gate_low[part], w_g) + nt(up_low[part], w_u)
        back, dgain2 = rms_back(middle[part], gains[2:3], grad)
        dx = dy[part].astype(f32) + back
        dx1[part] = dx
        da, dgain1 = rms_back(a[part], gains[1:2], dx)
        low = da.astype(bf16)
        lows.append(low)
        do[part] = nn(low, w_o).astype(bf16)
        sum1, sum2 = sum1 + dgain1, sum2 + dgain2
    gain_grad[...] = jnp.concatenate([sum1, sum2, jnp.zeros((6, dy.shape[1]), f32)], axis=0)
    for j in range(ff // FF_CHUNK):
        cols = slice(j * FF_CHUNK, (j + 1) * FF_CHUNK)
        put_grad(grads, cols, tn(normed[...], up_low[:, cols]).astype(bf16))
    grad = tn(jnp.concatenate(lows, axis=0), o[...]).astype(bf16)
    put_grad(grads, slice(ff, ff + H * HD), grad)


def middle_back(gate_low, up_low, pieces, middle, a, dy, gains, normed, o, after):
    rows, width = middle.shape
    return call(
        middle_back_kernel,
        [
            shaped((rows, width), f32),
            shaped((8, width), f32),
            shaped((rows, H * HD), bf16),
            *grad_shapes(width, gate_low.shape[1] + H * HD),
        ],
        [gate_low, up_low, middle, a, dy, gains, normed, o, *pieces],
        us=14,
        after=after,
        room=16,
    )


def attend_back_kernel(
    probs, do, q, k, v, q_raw, k_raw, cosine, sine, qk_gain, dq_low, dkv_before, dkv_own, qk_grad, dk, dv
):
    rows = q_raw.shape[0]
    dk[...] = jnp.zeros_like(dk)
    dv[...] = jnp.zeros_like(dv)
    gain_q, gain_k = qk_gain[4:5, :HD], qk_gain[4:5, HD:]
    sum_q = jnp.zeros((1, HD), f32)
    for b in range(rows // BLOCK):
        mine = pl.ds(b * BLOCK, BLOCK)
        reach = pl.ds(b * BLOCK, REACH)
        keys, values = k[reach], v[reach]
        do_rows, q_rows = do[mine], q[mine]
        do_stack = jnp.concatenate([do_rows[:, h * HD : (h + 1) * HD] for h in range(H)], axis=0)
        q_stack = jnp.concatenate([q_rows[:, h * HD : (h + 1) * HD] for h in range(H)], axis=0)
        p_low = probs[b]
        p = p_low.astype(f32)
        t = p * nt(do_stack, values)
        ds = (t - p * jnp.sum(t, axis=-1, keepdims=True)).astype(bf16)
        dk[reach] += tn(ds, q_stack)
        dv[reach] += tn(p_low, do_stack)
        dq = nn(ds, keys) * (1.0 / 16.0)
        own = pl.ds(rows + b * BLOCK, BLOCK)
        cs, sn = cosine[own], sine[own]
        for h in range(H):
            grad = rotate_back(dq[h * BLOCK : (h + 1) * BLOCK], cs, sn)
            back, dgain = rms_back(q_raw[mine, h * HD : (h + 1) * HD], gain_q, grad)
            dq_low[mine, h * HD : (h + 1) * HD] = back.astype(bf16)
            sum_q = sum_q + dgain
    sum_k = jnp.zeros((1, HD), f32)
    for c in range(2 * rows // 256):
        part = pl.ds(c * 256, 256)
        grad = rotate_back(dk[part] * (1.0 / 16.0), cosine[part], sine[part])
        back, dgain = rms_back(k_raw[part], gain_k, grad)
        out, at = (dkv_before, c * 256) if c * 256 < rows else (dkv_own, c * 256 - rows)
        out[at : at + 256, :HD] = back.astype(bf16)
        out[at : at + 256, HD:] = dv[part].astype(bf16)
        sum_k = sum_k + dgain
    qk_grad[...] = jnp.broadcast_to(jnp.concatenate([sum_q, sum_k], axis=1), qk_grad.shape)


def attend_back(probs, do, q, k, v, q_raw, k_raw, cosine, sine, qk_gain, after):
    rows = q.shape[0]
    return call(
        attend_back_kernel,
        [
            shaped((rows, H * HD), bf16), shaped((rows, 2 * HD), bf16),
            shaped((rows, 2 * HD), bf16), shaped((8, 2 * HD), f32),
        ],
        [probs, do, q, k, v, q_raw, k_raw, cosine, sine, qk_gain],
        us=0.3,
        scratch=[pltpu.VMEM((2 * rows, HD), f32), pltpu.VMEM((2 * rows, HD), f32)],
        after=after,
    )


def project_back_kernel(
    dq_low, dkv_before, dkv_own, qk_grad, hidden, x, qk_order, gain3, gain12, *refs
):
    pieces, (dh_before, dh, *grads) = refs[:-5], refs[-5:]
    rows = dq_low.shape[0]
    put_grad(grads, slice(0, 1024), tn(hidden[rows:], dq_low[...]).astype(bf16))
    grad = tn(hidden[:rows], dkv_before[...]) + tn(hidden[rows:], dkv_own[...])
    put_grad(grads, slice(1024, 1536), grad.astype(bf16))
    w_q = join_rows(pieces, slice(0, 1024))
    w_kv = join_rows(pieces, slice(1024, 1536))
    sum0 = jnp.zeros((1, x.shape[1]), f32)
    for c in range(rows // 256):
        part = pl.ds(c * 256, 256)
        before = x[part].astype(f32)
        grad = nt(dkv_before[part], w_kv)
        dh_before[part] = grad
        sum0 = sum0 + jnp.sum(grad * (before * inverse_rms(before)), axis=0, keepdims=True)
        own = x[rows + c * 256 : rows + (c + 1) * 256].astype(f32)
        grad = nt(dkv_own[part], w_kv) + nt(dq_low[part], w_q)
        dh[part] = grad
        sum0 = sum0 + jnp.sum(grad * (own * inverse_rms(own)), axis=0, keepdims=True)
    qk_spread = nt(qk_grad[...].astype(bf16), qk_order[...])
    rows_of = jnp.concatenate(
        [
            sum0, gain12[0:1], gain12[1:2], gain3[0:1], qk_spread[0:1],
            jnp.zeros((EXTRA - 5, x.shape[1]), f32),
        ],
        axis=0,
    )
    put_grad(grads, slice(1536, 1664), rows_of.T.astype(bf16))


def project_back(args, pieces, after):
    rows, width = args[0].shape[0], args[5].shape[1]
    return call(
        project_back_kernel,
        [shaped((rows, width), f32)] * 2 + grad_shapes(width, pieces[0].shape[1]),
        [*args, *pieces],
        us=8,
        after=after,
    )


def input_back_kernel(dh_before, dh, x, gains, dx1, order, before, own):
    rows = dx1.shape[0]
    table = order[...]
    for c in range(rows // 256):
        part = pl.ds(c * 256, 256)
        back, _ = rms_back(x[part].astype(f32), gains[0:1], dh_before[part])
        before[part] = nt(back.astype(bf16), table).astype(bf16)
        mine = x[rows + c * 256 : rows + (c + 1) * 256].astype(f32)
        back, _ = rms_back(mine, gains[0:1], dh[part])
        rest = back + dx1[part]
        total = jnp.zeros_like(rest)
        for _ in range(3):
            piece = rest.astype(bf16)
            rest = rest - piece.astype(f32)
            total = total + nt(piece, table)
        own[part] = total


def input_back(dh_before, dh, x, gains, dx1, order, after=()):
    outs = [shaped(dx1.shape, bf16), shaped(dx1.shape, f32)]
    args = [dh_before, dh, x, gains, dx1, order]
    return call(input_back_kernel, outs, args, us=0.3, after=after)


def select_kernel(first, own, other, out):
    pick = first[:1, :1] > 0.5
    out[...] = jnp.where(pick, other[...].astype(f32), own[...].astype(f32)).astype(bf16)


def to_device_before(x, n, first, after=()):
    hop = lax.ppermute(x, "seq", [(i + EIGHT, i) for i in range(0, n - EIGHT, EIGHT)])
    (out,) = call(select_kernel, [shaped(x.shape, bf16)], [first, x, hop], us=0.3, after=after)
    pairs = [(i, i - 1) for i in range(n) if i % EIGHT]
    pairs += [(i, i + EIGHT - 1) for i in range(0, n - EIGHT, EIGHT)]
    return out, lax.ppermute(out, "seq", pairs)


def join_halo_kernel(own, behind, out):
    out[...] = own[...] + behind[...].astype(f32)


def join_halo(own, behind, after=()):
    outs = [shaped(own.shape, f32)]
    return call(join_halo_kernel, outs, [own, behind], us=0.3, after=after)[0]


def on_device(
    tokens,
    segment_ids,
    w_query,
    w_key,
    w_value,
    w_output,
    w_gate,
    w_up,
    w_down,
    norm_gains,
    qk_gains,
    cotangent,
):
    n = lax.axis_size("seq")
    me = lax.axis_index("seq")
    rows, width = tokens.shape
    shard = w_query.shape[0]
    qk_shard = qk_gains.shape[0]

    extra = jnp.concatenate(
        [
            norm_gains.T,
            jnp.pad(qk_gains, (0, shard - qk_shard))[:, None],
            jnp.zeros((shard, EXTRA - 5), bf16),
        ],
        axis=1,
    )
    travel_a, travel_b, travel_c = travelling(
        (w_query, w_key, w_value, extra), (w_output.T, w_gate, w_up), (w_down.T,)
    )
    cols_a = w_query.shape[1] + w_key.shape[1] + w_value.shape[1] + EXTRA
    cols_b = w_output.shape[0] + w_gate.shape[1] + w_up.shape[1]
    cols_c = w_down.shape[0]

    even, odd, inner = row_table(n, shard)
    device = me ^ jnp.where(me & 1 == 0, jnp.asarray(even), jnp.asarray(odd))
    place = device * shard + inner
    qk_place = jnp.where(inner < qk_shard, device * qk_shard + inner, -1)
    padded_ids = jnp.concatenate([jnp.full((LONGEST + rows,), -1, jnp.int32), segment_ids])
    nearby = lax.dynamic_slice_in_dim(padded_ids, me * rows, 2 * rows + LONGEST)
    keys_segment = nearby[LONGEST:]
    seg_q = keys_segment[rows:, None]
    seg_k = jnp.stack(
        [keys_segment[b * BLOCK : b * BLOCK + REACH] for b in range(rows // BLOCK)]
    )[:, None, :]

    tokens_before = lax.ppermute(tokens, "seq", [(i, i + 1) for i in range(n - 1)])
    a_c = to_first(travel_c, n)
    (own_a,) = pack(far_direct(travel_a, n), shard, cols_a, 1, n, after=(a_c, tokens_before))
    travel_b, pair_c = call(
        start_kernel,
        [
            shaped(travel_b.shape, bf16),
            shaped((2 * travel_c.shape[0], travel_c.shape[1]), bf16),
        ],
        [travel_c, a_c, travel_b],
        us=0.2,
        after=(own_a,),
    )
    near_a = near_pieces(own_a, n, direct=True)
    first = (me % EIGHT == 0).astype(f32).reshape(1, 1)
    cosine, sine, order, qk_order, first = tables(
        nearby, rows, place, qk_place, width, first, after=(own_a,)
    )
    x, dy = permute(tokens_before, tokens, cotangent, order)
    (own_b,) = pack(
        far_direct(travel_b, n), shard, cols_b, 1, n, after=(x, seg_q, seg_k, *near_a[1:])
    )
    own_a, pair_c = hold(own_a, pair_c, after=(own_b,))
    weights_a = [own_a, *near_a[1:]]
    weights_a = [*weights_a, *to_core(weights_a, n)]
    hidden, q_raw, k_raw, q, k, v, probs, o, gains, qk_gain = attend(
        x, weights_a, qk_order, cosine, sine, seg_q, seg_k, after=(own_b,)
    )
    a_b, b_b = to_first(own_b, n), to_second(own_b, n)
    half_c = pack(far_direct(pair_c, n), shard, cols_c, 2, n, after=(o, a_b, b_b))
    a_b, own_b = hold(a_b, own_b, after=half_c)
    far_half = to_second(half_c[0], n)
    weights_b = [own_b, a_b, b_b, to_second(a_b, n)]
    weights_b = [*weights_b, *to_core(weights_b, n)]
    steps = len(far_bits(n)[0])
    a, middle, normed, product, by_gate, by_up = feed(o, weights_b, x, gains, after=())
    half_c = [*half_c, *hold(far_half, after=(product,))]
    weights_c = [*half_c, *to_core(half_c, n)]
    mixed, low, gain3, *grad_d = turn(product, weights_c, middle, dy, gains, order)
    gate_low, up_low, *grad_g = feed_back(low, weights_c, by_gate, by_up, normed)
    sum_d = core_sum(grad_d[0], grad_d[1:], n, after=(gate_low,))
    sum_g = core_sum(grad_g[0], grad_g[1:], n, after=sum_d[:1])
    dx1, gain12, do, *grad_u = middle_back(
        gate_low, up_low, weights_b, middle, a, dy, gains, normed, o, after=sum_g[:1]
    )
    dq_low, dkv_before, dkv_own, qk_grad = attend_back(
        probs, do, q, k, v, q_raw, k_raw, cosine, sine, qk_gain, after=()
    )
    sum_d = near_sum_first_both(sum_d, sum_g, n, after=(dq_low,))
    sum_u = core_sum(grad_u[0], grad_u[1:], n, after=sum_d[:1])
    dh_before, dh, *grad_a = project_back(
        [dq_low, dkv_before, dkv_own, qk_grad, hidden, x, qk_order, gain3, gain12],
        weights_a,
        after=sum_u[:1],
    )
    sum_a = core_sum(grad_a[0], grad_a[1:], n)
    before, own = input_back(dh_before, dh, x, gains, dx1, order, after=sum_a[:1])
    sum_d = near_sum_second(sum_d, n, after=(own,))
    sum_u = near_sum_first(sum_u, n, after=sum_d[:1], us=4)
    sum_a = near_sum_first(sum_a, n, after=sum_u[:1])
    sum_d = far_sum_first(sum_d, n, after=sum_a[:1])
    before, behind = to_device_before(before, n, first, after=sum_d[:1])
    sum_a = near_sum_far([sum_a, sum_u], n, 2, after=(before,))
    ff = grad_d[0].shape[1]
    sum_a = far_sum_first(sum_a, n)
    input_grad = join_halo(own, behind, after=sum_a[:1])
    sum_d, sum_g = far_sum_last(sum_d, n, shard, ((0, ff, 2 * ff),), after=(input_grad,))
    sum_q, sum_k, sum_v, sum_n, sum_u, sum_o = far_sum_last(
        sum_a, n, shard, ((0, 1024, 1280, 1536, 1664), (0, ff, ff + 1024)), after=(sum_d,)
    )
    return (
        mixed,
        input_grad,
        sum_q,
        sum_k,
        sum_v,
        sum_o.T,
        sum_g,
        sum_u,
        sum_d.T,
        sum_n[:, :4].T,
        sum_n[:qk_shard, 4],
    )


def solution(mesh):
    return jax.shard_map(
        on_device,
        mesh=mesh,
        in_specs=(
            P("seq", None),
            P(),
            P("seq", None),
            P("seq", None),
            P("seq", None),
            P(None, "seq"),
            P("seq", None),
            P("seq", None),
            P(None, "seq"),
            P(None, "seq"),
            P("seq"),
            P("seq", None),
        ),
        out_specs=(
            P("seq", None),
            P("seq", None),
            P("seq", None),
            P("seq", None),
            P("seq", None),
            P(None, "seq"),
            P("seq", None),
            P("seq", None),
            P(None, "seq"),
            P(None, "seq"),
            P("seq"),
        ),
        check_vma=False,
    )
```

```python
import functools

import jax
import jax.numpy as jnp
import numpy as np
from jax import lax
from jax.experimental import pallas as pl
from jax.experimental.pallas import tpu as pltpu
from jax.sharding import PartitionSpec as P

H = 4
HD = 256
WINDOW = 512
LONGEST = 2048
EXTRA = 128
EIGHT = 8
FF_CHUNK = 512
BLOCK = 128
REACH = BLOCK + WINDOW
MIB = 1024 * 1024

epsilon = 1e-06
bf16 = jnp.bfloat16
f32 = jnp.float32


def far_bits(n):
    bits = [1 << i for i in range(n.bit_length() - 1)]
    rest = [b for b in bits[1:] if b not in near_pair(n)]
    return rest, rest[::-1]


def far_slots(bits):
    slots = [0]
    for b in bits:
        slots = slots + [s | b for s in slots]
    return slots


def near_pair(n):
    return (2, 8) if n > 64 else (2, 4)


def to_partner(x, n, masks):
    return lax.ppermute(x, "seq", [(i, i ^ masks[i & 1]) for i in range(n)])


def row_table(n, shard):
    first, second = near_pair(n)
    main = whole_tiles(shard)
    count = n // 8
    inner = [(i, r) for i in range(count) for r in range(main)]
    inner += [(i, r) for i in range(count) for r in range(main, shard)]

    def offsets(a, b, bits):
        far = far_slots(bits)
        return [m ^ far[i] for m in (0, a, b, a | b) for i, _ in inner]

    even_bits, odd_bits = far_bits(n)
    even, odd = offsets(first, second, even_bits), offsets(second, first, odd_bits)
    return (
        np.array(even + [1 ^ m for m in odd], np.int32),
        np.array(odd + [1 ^ m for m in even], np.int32),
        np.array([r for _, r in inner] * 8, np.int32),
    )


def nn(left, right):
    return jnp.dot(left, right, preferred_element_type=f32)


def tn(left, right):
    return lax.dot_general(left, right, (((0,), (0,)), ((), ())), preferred_element_type=f32)


def nt(left, right):
    return lax.dot_general(left, right, (((1,), (1,)), ((), ())), preferred_element_type=f32)


def inverse_rms(values):
    return lax.rsqrt(jnp.mean(values * values, axis=-1, keepdims=True) + epsilon)


def rms_back(values, gain, grad):
    scale = inverse_rms(values)
    hat = values * scale
    inner = grad * gain
    mean = jnp.mean(inner * hat, axis=-1, keepdims=True)
    return scale * (inner - hat * mean), jnp.sum(grad * hat, axis=0, keepdims=True)


def rotate(values, cosine, sine):
    half = values.shape[-1] // 2
    a, b = values[:, :half], values[:, half:]
    return jnp.concatenate([a * cosine - b * sine, b * cosine + a * sine], axis=-1)


def rotate_back(values, cosine, sine):
    half = values.shape[-1] // 2
    a, b = values[:, :half], values[:, half:]
    return jnp.concatenate([a * cosine + b * sine, b * cosine - a * sine], axis=-1)


def call(kernel, outs, args, us, scratch=(), after=(), room=12, result=False):
    given, extra = len(args), len(after)

    def body(*refs):
        if result:
            *refs, token = refs
            token[...] = jnp.zeros_like(token)
        kernel(*refs[:given], *refs[given + extra :])

    if result:
        outs = [pltpu.HBM(o.shape, o.dtype) for o in outs] + [shaped((8, 128), f32)]
    return pl.pallas_call(
        body,
        in_specs=[pl.BlockSpec(memory_space=pltpu.VMEM)] * given
        + [pl.BlockSpec(memory_space=pl.ANY)] * extra,
        out_specs=[pl.BlockSpec(memory_space=pltpu.VMEM)] * len(outs),
        out_shape=outs,
        scratch_shapes=scratch,
        compiler_params=pltpu.CompilerParams(vmem_limit_bytes=room * MIB),
        cost_estimate=pl.CostEstimate(
            flops=int(us * 10**9), bytes_accessed=int(us * 10**6), transcendentals=0
        ),
    )(*args, *after)


def shaped(shape, dtype):
    return jax.ShapeDtypeStruct(shape, dtype)


def join_rows(parts, cols=slice(None)):
    return jnp.concatenate([p[:, cols] for p in parts], axis=0)


def whole_tiles(rows):
    return rows // 16 * 16


def padded(cols):
    return -(-cols // 512) * 512


def in_tiles(rows):
    return rows == 20


def travel_shape(rows, cols):
    return (16, padded(cols) * 5 // 4) if in_tiles(rows) else (rows, cols)


def to_tiles(values):
    rows, cols = values.shape
    if not in_tiles(rows):
        return values
    wide = padded(cols)
    if wide > cols:
        values = jnp.concatenate([values, jnp.zeros((rows, wide - cols), f32)], axis=1)
    quarter = wide // 4
    rest = [values[16:, k * quarter : (k + 1) * quarter] for k in range(4)]
    return jnp.concatenate([values[:16], jnp.concatenate(rest, axis=0)], axis=1)


def tile_kernel(counts, *refs):
    total = sum(counts) + 2
    given, outs = refs[:total], refs[total : total + len(counts)]
    held, sem = refs[total + len(counts) : -1], refs[-1]
    copies = [
        pltpu.make_async_copy(source, target, sem.at[i])
        for i, (source, target) in enumerate(zip(given, held))
    ]
    for copy in copies:
        copy.start()
    for copy in copies:
        copy.wait()
    *held, norm_gains, qk_gains = held
    shard = norm_gains.shape[1]
    rows = [
        jnp.concatenate([g[...].astype(f32), jnp.zeros((g.shape[0], EXTRA - g.shape[1]), f32)], axis=1)
        for g in (norm_gains, qk_gains)
    ]
    rows.append(jnp.zeros((EXTRA - 5, EXTRA), f32))
    extra = jnp.concatenate(rows, axis=0).T[:shard]
    for group, (count, out) in enumerate(zip(counts, outs)):
        parts = [p[...].astype(f32) for p in held[:count]]
        held = held[count:]
        if group == 0:
            parts.append(extra)
        out[...] = to_tiles(jnp.concatenate(parts, axis=1)).astype(bf16)


def travelling(norm_gains, qk_gains, *groups):
    counts = [len(g) for g in groups]
    given = [w for g in groups for w in g] + [norm_gains, qk_gains]
    outs = []
    for i, g in enumerate(groups):
        cols = sum(w.shape[1] for w in g) + (EXTRA if i == 0 else 0)
        outs.append(shaped(travel_shape(g[0].shape[0], cols), bf16))
    return pl.pallas_call(
        functools.partial(tile_kernel, counts),
        in_specs=[pl.BlockSpec(memory_space=pltpu.HBM)] * len(given),
        out_specs=[pl.BlockSpec(memory_space=pltpu.VMEM)] * len(outs),
        out_shape=outs,
        scratch_shapes=[pltpu.VMEM(w.shape, bf16) for w in given]
        + [pltpu.SemaphoreType.DMA((len(given),))],
        compiler_params=pltpu.CompilerParams(vmem_limit_bytes=8 * MIB),
    )(*[pltpu.with_memory_space_constraint(w, pltpu.HBM) for w in given])


def stack_kernel(*refs):
    count = len(refs) // 3
    for i in range(count):
        a, b, out = refs[2 * i], refs[2 * i + 1], refs[2 * count + i]
        rows = a.shape[0]
        if rows % 16 == 0:
            out[:rows] = a[...]
            out[rows:] = b[...]
        else:
            both = [a[...].astype(f32), b[...].astype(f32)]
            out[...] = jnp.concatenate(both, axis=0).astype(bf16)


def stack(*pairs, after=()):
    outs = [shaped((2 * a.shape[0], a.shape[1]), bf16) for a, _ in pairs]
    return call(stack_kernel, outs, [x for pair in pairs for x in pair], us=0.5, after=after)


def pack_kernel(pieces, blocks, out):
    count = len(pieces)
    share, cols = out.shape[0] // blocks, out.shape[1]
    rows = share // count
    main = whole_tiles(rows)
    height, wide = travel_shape(rows, cols)
    quarter = padded(cols) // 4
    for block in range(blocks):
        at = block * share
        starts = [(ref, begin + block * height) for ref, begin in pieces]
        if main:
            for i, (ref, begin) in enumerate(starts):
                out[at + i * main : at + (i + 1) * main] = ref[begin : begin + main, :cols]
        at = at + main * count
        if in_tiles(rows):
            rest = [ref[begin : begin + 16, 4 * quarter :].astype(f32) for ref, begin in starts]
            for k in range(4):
                end = min((k + 1) * quarter, cols)
                part = jnp.concatenate([r[4 * k : 4 * k + 4] for r in rest], axis=0)
                out[at : at + 4 * count, k * quarter : end] = part[:, : end - k * quarter].astype(
                    bf16
                )
        elif rows > main:
            rest = [
                ref[...].astype(f32)[begin + main : begin + rows] for ref, begin in starts
            ]
            out[at : at + (rows - main) * count] = jnp.concatenate(rest, axis=0).astype(bf16)


def pack(arrays, rows, cols, blocks, n, parts=1, after=()):
    count = n // 8
    height = travel_shape(rows, cols)[0] * blocks
    held = count // len(arrays)
    total = rows * count * blocks

    def kernel(*refs):
        given = refs[: len(arrays)]
        pieces = [(ref, h * height) for ref in given for h in range(held)]
        if parts == 1:
            pack_kernel(pieces, blocks, refs[-1])
        else:
            for block, out in enumerate(refs[len(arrays) :]):
                shift = block * height // blocks
                pack_kernel([(ref, at + shift) for ref, at in pieces], 1, out)

    outs = [shaped((total // parts, cols), bf16)] * parts
    return call(kernel, outs, arrays, us=1.5, after=after)


def far_step(block, n, step):
    even, odd = far_bits(n)
    return to_partner(block, n, (even[step], odd[step]))


def far_direct(block, n):
    even, odd = far_bits(n)
    slots = zip(far_slots(even)[1:], far_slots(odd)[1:])
    return [block] + [to_partner(block, n, masks) for masks in slots]


def start_kernel(a, b, one, out, one_out):
    stack_kernel(a, b, out)
    one_out[...] = one[...]


def hold_kernel(*refs):
    half = len(refs) // 2
    for value, out in zip(refs[:half], refs[half:]):
        out[...] = value[...]


def hold(*values, after):
    return call(hold_kernel, [shaped(v.shape, v.dtype) for v in values], values, 0.2, after=after)


def hold_parts_kernel(one, two, one_out, two_out, upper, lower):
    one_out[...] = one[...]
    two_out[...] = two[...]
    rows = upper.shape[0]
    upper[...] = one[:rows]
    lower[...] = one[rows:]


def hold_parts(one, two, after):
    rows, cols = one.shape
    upper = rows // 32 * 16 + (16 if rows % 32 else 0)
    outs = [shaped(one.shape, bf16), shaped(two.shape, bf16)]
    outs += [shaped((upper, cols), bf16), shaped((rows - upper, cols), bf16)]
    return call(hold_parts_kernel, outs, [one, two], us=0.2, after=after)


def far_gather(blocks, n, joins):
    steps = len(far_bits(n)[0])
    for k in range(steps - 1):
        got = [far_step(b, n, k) for b in blocks]
        blocks = stack(*zip(blocks, got), after=joins[k] if k < len(joins) else ())
    return [(b, far_step(b, n, steps - 1)) for b in blocks]


def to_first(x, n):
    first, second = near_pair(n)
    return to_partner(x, n, (first, second))


def to_second(x, n):
    first, second = near_pair(n)
    return to_partner(x, n, (second, first))


def near_pieces(own, n, direct=False):
    first, second = near_pair(n)
    a, b = to_first(own, n), to_second(own, n)
    return [own, a, b, to_partner(own, n, (first | second,) * 2) if direct else to_second(a, n)]


def to_core(pieces, n):
    return [to_partner(p, n, (1, 1)) for p in pieces]


def fold_kernel(count, *refs):
    given, outs = refs[:count], refs[count:]
    mine, got = given[0], given[1:]
    rows = outs[0].shape[0]
    height = got[0].shape[0]
    if rows % 16 == 0 and height % rows == 0:
        per = height // rows
        for i, out in enumerate(outs):
            other = got[i // per][(i % per) * rows : (i % per + 1) * rows]
            part = mine[i * rows : (i + 1) * rows]
            out[...] = (part.astype(f32) + other.astype(f32)).astype(bf16)
    else:
        total = mine[...].astype(f32)
        total = total + jnp.concatenate([g[...].astype(f32) for g in got], axis=0)
        for i, out in enumerate(outs):
            out[...] = total[i * rows : (i + 1) * rows].astype(bf16)


def fold(mine, got, after=(), us=0.5):
    rows, cols = mine.shape
    outs = [shaped((rows // 2, cols), bf16)] * 2
    kernel = functools.partial(fold_kernel, 1 + len(got))
    return call(kernel, outs, [mine, *got], us=us, after=after)


def wide_fold_kernel(mine, *refs):
    got, (keep, send) = refs[:-2], refs[-2:]
    rows = got[0].shape[0]
    per = keep.shape[0] // rows
    for i, other in enumerate(got):
        out = keep if i < per else send
        at = (i % per) * rows
        part = mine[i * rows : (i + 1) * rows].astype(f32)
        out[at : at + rows] = (part + other[...].astype(f32)).astype(bf16)


def core_sum(top, sends, n, after=()):
    rows, cols = top.shape
    outs = [shaped((rows // 2, cols), bf16)] * 2
    return call(wide_fold_kernel, outs, [top, *to_core(sends, n)], us=0.7, after=after)


def core_sum_by_far(top, sends, n, after=()):
    rows, cols = top.shape
    count, blocks = n // 8, len(sends)
    shard = rows // blocks // count
    main = whole_tiles(shard)
    rest, done = shard - main, main * count
    height, wide = travel_shape(shard, cols)

    def kernel(mine, *refs):
        got, (keep, send) = refs[:-2], refs[-2:]
        share = rows // blocks
        tiles = []
        for block in range(blocks):
            total = mine[block * share : (block + 1) * share].astype(f32) + got[block][...].astype(
                f32
            )
            for i in range(count):
                parts = []
                if main:
                    parts.append(total[i * main : (i + 1) * main])
                if rest:
                    parts.append(total[done + i * rest : done + (i + 1) * rest])
                tiles.append((i, block, to_tiles(jnp.concatenate(parts, axis=0))))
        tiles = [t for _, _, t in sorted(tiles, key=lambda item: item[:2])]
        half = len(tiles) // 2
        keep[...] = jnp.concatenate(tiles[:half], axis=0).astype(bf16)
        send[...] = jnp.concatenate(tiles[half:], axis=0).astype(bf16)

    outs = [shaped((count // 2 * blocks * height, wide), bf16)] * 2
    return call(kernel, outs, [top, *to_core(sends, n)], us=1.5, after=after)


def far_fold(halves, n, step, after=()):
    keep, send = halves
    return fold(keep, [far_step(send, n, step)], after)


def near_sum_last(halves, n, shard, cuts, after=()):
    keep, send = halves
    outs = [shaped((shard, e - b), f32) for b, e in zip(cuts[:-1], cuts[1:])]
    return call(
        functools.partial(far_sum_kernel, (cuts,)), outs, [keep, to_first(send, n)], us=1, after=after
    )


def near_sum_first(halves, n, after=(), us=0.5):
    keep, send = halves
    return fold(keep, [to_second(send, n)], after, us)


def fold_both_kernel(*refs):
    given, (keep, send) = refs[:4], refs[4:]
    rows, cols = keep.shape
    cols = cols // 2
    for i in range(2):
        mine, got = given[2 * i : 2 * i + 2]
        for j, out in enumerate((keep, send)):
            part = slice(j * rows, (j + 1) * rows)
            out[:, i * cols : (i + 1) * cols] = (
                mine[part].astype(f32) + got[part].astype(f32)
            ).astype(bf16)


def near_sum_first_both(one, two, n, after=()):
    args = [x for keep, send in (one, two) for x in (keep, to_second(send, n))]
    rows, cols = one[0].shape
    outs = [shaped((rows // 2, 2 * cols), bf16)] * 2
    return call(fold_both_kernel, outs, args, us=5, after=after)


def split_kernel(count, mine, got, keep, send):
    total = mine[...].astype(f32) + got[...].astype(f32)
    rows = total.shape[0] // count
    main = whole_tiles(rows)
    rest, done = rows - main, main * count
    slots = []
    for i in range(count):
        parts = []
        if main:
            parts.append(total[i * main : (i + 1) * main])
        if rest:
            parts.append(total[done + i * rest : done + (i + 1) * rest])
        slots.append(to_tiles(jnp.concatenate(parts, axis=0)))
    keep[...] = jnp.concatenate(slots[: count // 2], axis=0).astype(bf16)
    send[...] = jnp.concatenate(slots[count // 2 :], axis=0).astype(bf16)


def near_sum_second(halves, n, after=()):
    keep, send = halves
    rows, cols = keep.shape
    count = n // 8
    height, wide = travel_shape(rows // count, cols)
    outs = [shaped((count // 2 * height, wide), bf16)] * 2
    return call(
        functools.partial(split_kernel, count), outs, [keep, to_first(send, n)], us=1, after=after
    )


def slots_kernel(groups, count, *refs):
    outs = refs[2 * groups :]
    slots = [[] for _ in range(count)]
    for g in range(groups):
        total = refs[2 * g][...].astype(f32) + refs[2 * g + 1][...].astype(f32)
        rows = total.shape[0] // count
        main = whole_tiles(rows)
        rest, done = rows - main, main * count
        for i in range(count):
            parts = []
            if main:
                parts.append(total[i * main : (i + 1) * main])
            if rest:
                parts.append(total[done + i * rest : done + (i + 1) * rest])
            slots[i].append(to_tiles(jnp.concatenate(parts, axis=0)))
    per = count // len(outs)
    for i, parts in enumerate(slots):
        values = jnp.concatenate(parts, axis=1).astype(bf16)
        height = values.shape[0]
        if per == 1:
            outs[i][...] = values
        elif height % 16 == 0:
            outs[i // per][i % per * height : (i % per + 1) * height] = values
    if per > 1 and height % 16 != 0:
        for j, out in enumerate(outs):
            values = [jnp.concatenate(p, axis=1) for p in slots[j * per : (j + 1) * per]]
            out[...] = jnp.concatenate(values, axis=0).astype(bf16)


def near_sum_far(groups, n, parts, after=()):
    count = n // 8
    args, wide = [], 0
    for keep, send in groups:
        args += [keep, to_first(send, n)]
        height, cols = travel_shape(keep.shape[0] // count, keep.shape[1])
        wide += cols
    outs = [shaped((height * count // parts, wide), bf16)] * parts
    kernel = functools.partial(slots_kernel, len(groups), count)
    return call(kernel, outs, args, us=1, after=after)


def far_sum_direct(pieces, n, shard, groups, after=()):
    even, odd = far_bits(n)
    slots = zip(pieces[1:], far_slots(even)[1:], far_slots(odd)[1:])
    got = [to_partner(p, n, (e, o)) for p, e, o in slots]
    outs = [shaped((shard, e - b), f32) for cuts in groups for b, e in zip(cuts[:-1], cuts[1:])]
    return call(
        functools.partial(far_sum_kernel, groups), outs, [pieces[0], *got], us=1, after=after
    )


def far_sum_first(halves, n, after=()):
    keep, send = halves
    for k in reversed(range(1, len(far_bits(n)[0]))):
        keep, send = fold(keep, [far_step(send, n, k)], after)
        after = ()
    return keep, send


def far_sum_kernel(groups, *refs):
    count = sum(len(cuts) - 1 for cuts in groups)
    given, outs = refs[:-count], refs[-count:]
    total = given[0][...].astype(f32)
    for got in given[1:]:
        total = total + got[...].astype(f32)
    rows = outs[0].shape[0]
    begin_at = 0
    for cuts in groups:
        wide = padded(cuts[-1]) if in_tiles(rows) else cuts[-1]
        part = total[:, begin_at : begin_at + wide]
        if in_tiles(rows):
            quarter = wide // 4
            rest = total[:, begin_at + wide : begin_at + wide + quarter]
            rest = [rest[4 * k : 4 * k + 4] for k in range(4)]
            part = jnp.concatenate([part, jnp.concatenate(rest, axis=1)], axis=0)
            begin_at += quarter
        begin_at += wide
        for begin, end in zip(cuts[:-1], cuts[1:]):
            outs[0][...] = part[:, begin:end]
            outs = outs[1:]


def far_sum_last(halves, n, shard, groups, after=()):
    keep, send = halves
    outs = [shaped((shard, e - b), f32) for cuts in groups for b, e in zip(cuts[:-1], cuts[1:])]
    return call(
        functools.partial(far_sum_kernel, groups), outs, [keep, far_step(send, n, 0)], us=1,
        after=after, result=True,
    )


def table_kernel(near, near_col, freqs, place, qk_place, first, cosine, sine, order, qk_order, first_out):
    count = cosine.shape[0]
    ahead = near.shape[1] - count
    steps = freqs[...]
    for c in range(count // 256):
        reach = slice(c * 256, c * 256 + ahead + 256)
        here = near_col[ahead + c * 256 : ahead + (c + 1) * 256]
        i = lax.broadcasted_iota(jnp.int32, (256, ahead + 256), 0) + ahead
        j = lax.broadcasted_iota(jnp.int32, (256, ahead + 256), 1)
        same = (here == near[:, reach]) & (j < i)
        position = jnp.sum(same.astype(f32), axis=1, keepdims=True)
        angles = position * steps
        cosine[c * 256 : (c + 1) * 256] = jnp.cos(angles)
        sine[c * 256 : (c + 1) * 256] = jnp.sin(angles)
    i = lax.broadcasted_iota(jnp.int32, order.shape, 0)
    order[...] = (i == place[...]).astype(f32).astype(bf16)
    j = lax.broadcasted_iota(jnp.int32, qk_order.shape, 1)
    qk_order[...] = (qk_place[...] == j).astype(f32).astype(bf16)
    first_out[...] = jnp.broadcast_to(first[...], first_out.shape)


def tables(near, rows, place, qk_place, width, first, after=()):
    freqs = np.float32(10000.0) ** (-2.0 * np.arange(HD // 2, dtype=np.float32) / np.float32(HD))
    args = [
        near[None, :], near[:, None], jnp.asarray(freqs)[None, :], place[None, :], qk_place[:, None],
        first,
    ]
    outs = [
        shaped((2 * rows, HD // 2), f32), shaped((2 * rows, HD // 2), f32),
        shaped((width, width), bf16), shaped((width, 2 * HD), bf16), shaped((8, 128), f32),
    ]
    return call(table_kernel, outs, args, us=3, after=after)


def permute_kernel(tokens_before, tokens, cotangent, order, x, dy):
    table = order[...]
    rows = tokens.shape[0]
    x[:rows] = nn(tokens_before[...], table).astype(bf16)
    x[rows:] = nn(tokens[...], table).astype(bf16)
    dy[...] = nn(cotangent[...], table).astype(bf16)


def permute(tokens_before, tokens, cotangent, order, after=()):
    rows, width = tokens.shape
    outs = [shaped((2 * rows, width), bf16), shaped((rows, width), bf16)]
    args = [tokens_before, tokens, cotangent, order]
    return call(permute_kernel, outs, args, us=2, after=after)


def attend_kernel(x, qk_order, cosine, sine, seg_q, seg_k, *refs):
    pieces = refs[:-10]
    hidden, q_raw, k_raw, q_out, k_out, v_out, probs, o, gains, qk_gain = refs[-10:]
    rows = q_raw.shape[0]
    w_q = join_rows(pieces, slice(0, 1024))
    w_kv = join_rows(pieces, slice(1024, 1536))
    gain_rows = join_rows(pieces, slice(1536, 1664)).astype(f32).T[:8]
    gains[...] = gain_rows
    gain_qk = nn(gain_rows.astype(bf16), qk_order[...])
    qk_gain[...] = gain_qk
    gain_q, gain_k = gain_qk[4:5, :HD], gain_qk[4:5, HD:]
    for c in range(2 * rows // 256):
        part = pl.ds(c * 256, 256)
        xs = x[part].astype(f32)
        hs = (xs * inverse_rms(xs) * gain_rows[0:1]).astype(bf16)
        hidden[part] = hs
        cs, sn = cosine[part], sine[part]
        kv = nn(hs, w_kv)
        raw = kv[:, :HD]
        k_raw[part] = raw
        k_out[part] = rotate(raw * inverse_rms(raw) * gain_k, cs, sn).astype(bf16)
        v_out[part] = kv[:, HD:].astype(bf16)
        if c * 256 >= rows:
            own = pl.ds(c * 256 - rows, 256)
            qs = nn(hs, w_q)
            q_raw[own] = qs
            for h in range(H):
                raw = qs[:, h * HD : (h + 1) * HD]
                q_out[own, h * HD : (h + 1) * HD] = rotate(
                    raw * inverse_rms(raw) * gain_q, cs, sn
                ).astype(bf16)
    for b in range(rows // BLOCK):
        mine = pl.ds(b * BLOCK, BLOCK)
        reach = pl.ds(b * BLOCK, REACH)
        q_rows = q_out[mine] * bf16(1.0 / 16.0)
        q_stack = jnp.concatenate([q_rows[:, h * HD : (h + 1) * HD] for h in range(H)], axis=0)
        scores = nt(q_stack, k_out[reach])
        i = lax.broadcasted_iota(jnp.int32, (BLOCK, REACH), 0)
        j = lax.broadcasted_iota(jnp.int32, (BLOCK, REACH), 1)
        allowed = (j > i) & (j <= i + WINDOW) & (seg_q[mine] == seg_k[b])
        allowed = jnp.concatenate([allowed.astype(f32)] * H, axis=0)
        weights = jnp.exp(scores) * allowed
        total = jnp.sum(weights, axis=-1, keepdims=True)
        p = (weights * (1.0 / total)).astype(bf16)
        probs[b] = p
        out = nn(p, v_out[reach])
        for h in range(H):
            o[mine, h * HD : (h + 1) * HD] = out[h * BLOCK : (h + 1) * BLOCK].astype(bf16)


def attend(x, pieces, qk_order, cosine, sine, seg_q, seg_k, after):
    rows = x.shape[0] // 2
    width = x.shape[1]
    return call(
        attend_kernel,
        [
            shaped((2 * rows, width), bf16),
            shaped((rows, H * HD), f32),
            shaped((2 * rows, HD), f32),
            shaped((rows, H * HD), bf16),
            shaped((2 * rows, HD), bf16),
            shaped((2 * rows, HD), bf16),
            shaped((rows // BLOCK, H * BLOCK, REACH), bf16),
            shaped((rows, H * HD), bf16),
            shaped((8, width), f32),
            shaped((8, 2 * HD), f32),
        ],
        [x, qk_order, cosine, sine, seg_q, seg_k, *pieces],
        us=12,
        after=after,
    )


def gelu_parts(g):
    c0, c1 = 0.7978845608028654, 0.044715
    square = g * g
    t = jnp.tanh(c0 * g * (1.0 + c1 * square))
    value = 0.5 * g * (1.0 + t)
    slope = 0.5 * (1.0 + t) + 0.5 * g * (1.0 - t * t) * c0 * (1.0 + 3.0 * c1 * square)
    return value, slope


def join_kernel(o, x, gains, *refs):
    pieces, (a_out, middle, normed) = refs[:-3], refs[-3:]
    rows = o.shape[0]
    w_o = join_rows(pieces, slice(0, H * HD))
    for c in range(rows // 256):
        part = pl.ds(c * 256, 256)
        a = nt(o[part], w_o)
        a_out[part] = a
        x1 = x[rows + c * 256 : rows + (c + 1) * 256].astype(f32) + a * inverse_rms(a) * gains[1:2]
        middle[part] = x1
        normed[part] = (x1 * inverse_rms(x1) * gains[2:3]).astype(bf16)


def join(o, pieces, x, gains):
    rows, width = o.shape[0], x.shape[1]
    outs = [shaped((rows, width), f32), shaped((rows, width), f32), shaped((rows, width), bf16)]
    return call(join_kernel, outs, [o, x, gains, *pieces], us=2)


def feed_kernel(normed, *refs):
    pieces, (product, by_gate, by_up) = refs[:-3], refs[-3:]
    rows, ff = product.shape
    for j in range(ff // FF_CHUNK):
        cols = slice(j * FF_CHUNK, (j + 1) * FF_CHUNK)
        w_g = join_rows(pieces, slice(H * HD + cols.start, H * HD + cols.stop))
        w_u = join_rows(pieces, slice(H * HD + ff + cols.start, H * HD + ff + cols.stop))
        for c in range(rows // 256):
            part = pl.ds(c * 256, 256)
            h2 = normed[part]
            g = nn(h2, w_g)
            u = nn(h2, w_u)
            value, slope = gelu_parts(g)
            product[part, cols] = (value * u).astype(bf16)
            by_gate[part, cols] = (slope * u).astype(bf16)
            by_up[part, cols] = value.astype(bf16)


def feed(normed, pieces, after=()):
    rows = normed.shape[0]
    ff = (pieces[0].shape[1] - H * HD) // 2
    outs = [shaped((rows, ff), bf16)] * 3
    return call(feed_kernel, outs, [normed, *pieces], us=5, after=after)


def put_grad(grads, cols, values):
    top, *sends = grads
    half = top.shape[0]
    top[:, cols] = values[:half]
    part = half // len(sends)
    for i, send in enumerate(sends):
        send[:, cols] = values[half + i * part : half + (i + 1) * part]


def grad_shapes(width, cols):
    return [shaped((width // 2, cols), bf16)] + [shaped((width // 4, cols), bf16)] * 2


def turn_kernel(product, middle, dy, gains, order, *refs):
    pieces, (mixed, low, gain_grad, *grads) = refs[:-6], refs[-6:]
    ff = product.shape[1]
    w_d = join_rows(pieces)
    total = jnp.zeros((1, dy.shape[1]), f32)
    for c in range(dy.shape[0] // 256):
        part = pl.ds(c * 256, 256)
        f = nt(product[part], w_d)
        grad = dy[part].astype(f32)
        y = middle[part] + f * inverse_rms(f) * gains[3:4]
        mixed[part] = nt(y.astype(bf16), order[...]).astype(bf16)
        df, dgain = rms_back(f, gains[3:4], grad)
        low[part] = df.astype(bf16)
        total = total + dgain
    gain_grad[...] = jnp.broadcast_to(total, gain_grad.shape)
    for j in range(ff // FF_CHUNK):
        cols = slice(j * FF_CHUNK, (j + 1) * FF_CHUNK)
        grad = tn(low[...], product[:, cols]).astype(bf16)
        put_grad(grads, cols, grad)


def turn(product, pieces, middle, dy, gains, order):
    rows, width = middle.shape
    return call(
        turn_kernel,
        [
            shaped((rows, width), bf16),
            shaped((rows, width), bf16),
            shaped((8, width), f32),
            *grad_shapes(width, product.shape[1]),
        ],
        [product, middle, dy, gains, order, *pieces],
        us=6,
    )


def feed_back_kernel(low, by_gate, by_up, normed, *refs):
    pieces, (gate_low, up_low, *grads) = refs[:-5], refs[-5:]
    rows, ff = gate_low.shape
    for j in range(ff // FF_CHUNK):
        cols = slice(j * FF_CHUNK, (j + 1) * FF_CHUNK)
        w_d = join_rows(pieces, cols)
        for c in range(rows // 256):
            part = pl.ds(c * 256, 256)
            dm = nn(low[part], w_d)
            gate_low[part, cols] = (dm * by_gate[part, cols].astype(f32)).astype(bf16)
            up_low[part, cols] = (dm * by_up[part, cols].astype(f32)).astype(bf16)
        put_grad(grads, cols, tn(normed[...], gate_low[:, cols]).astype(bf16))


def feed_back(low, pieces, by_gate, by_up, normed):
    rows, width = low.shape
    ff = by_gate.shape[1]
    return call(
        feed_back_kernel,
        [shaped((rows, ff), bf16)] * 2 + grad_shapes(width, ff),
        [low, by_gate, by_up, normed, *pieces],
        us=4,
    )


def middle_back_kernel(gate_low, up_low, middle, a, dy, gains, normed, o, *refs):
    pieces, (dx1, gain_grad, do, *grads) = refs[:-6], refs[-6:]
    rows, ff = gate_low.shape
    w_o = join_rows(pieces, slice(0, H * HD))
    w_g = join_rows(pieces, slice(H * HD, H * HD + ff))
    w_u = join_rows(pieces, slice(H * HD + ff, H * HD + 2 * ff))
    sum1 = jnp.zeros((1, dy.shape[1]), f32)
    sum2 = jnp.zeros((1, dy.shape[1]), f32)
    lows = []
    for c in range(rows // 256):
        part = pl.ds(c * 256, 256)
        grad = nt(gate_low[part], w_g) + nt(up_low[part], w_u)
        back, dgain2 = rms_back(middle[part], gains[2:3], grad)
        dx = dy[part].astype(f32) + back
        dx1[part] = dx
        da, dgain1 = rms_back(a[part], gains[1:2], dx)
        low = da.astype(bf16)
        lows.append(low)
        do[part] = nn(low, w_o).astype(bf16)
        sum1, sum2 = sum1 + dgain1, sum2 + dgain2
    gain_grad[...] = jnp.concatenate([sum1, sum2, jnp.zeros((6, dy.shape[1]), f32)], axis=0)
    for j in range(ff // FF_CHUNK):
        cols = slice(j * FF_CHUNK, (j + 1) * FF_CHUNK)
        put_grad(grads, cols, tn(normed[...], up_low[:, cols]).astype(bf16))
    grad = tn(jnp.concatenate(lows, axis=0), o[...]).astype(bf16)
    put_grad(grads, slice(ff, ff + H * HD), grad)


def middle_back(gate_low, up_low, pieces, middle, a, dy, gains, normed, o, after):
    rows, width = middle.shape
    return call(
        middle_back_kernel,
        [
            shaped((rows, width), f32),
            shaped((8, width), f32),
            shaped((rows, H * HD), bf16),
            *grad_shapes(width, gate_low.shape[1] + H * HD),
        ],
        [gate_low, up_low, middle, a, dy, gains, normed, o, *pieces],
        us=14,
        after=after,
        room=16,
    )


def attend_back_kernel(
    probs, do, q, k, v, q_raw, k_raw, cosine, sine, qk_gain, dq_low, dkv_before, dkv_own, qk_grad, dk, dv
):
    rows = q_raw.shape[0]
    dk[...] = jnp.zeros_like(dk)
    dv[...] = jnp.zeros_like(dv)
    gain_q, gain_k = qk_gain[4:5, :HD], qk_gain[4:5, HD:]
    sum_q = jnp.zeros((1, HD), f32)
    for b in range(rows // BLOCK):
        mine = pl.ds(b * BLOCK, BLOCK)
        reach = pl.ds(b * BLOCK, REACH)
        keys, values = k[reach], v[reach]
        do_rows, q_rows = do[mine], q[mine]
        do_stack = jnp.concatenate([do_rows[:, h * HD : (h + 1) * HD] for h in range(H)], axis=0)
        q_stack = jnp.concatenate([q_rows[:, h * HD : (h + 1) * HD] for h in range(H)], axis=0)
        p_low = probs[b]
        p = p_low.astype(f32)
        t = p * nt(do_stack, values)
        ds = (t - p * jnp.sum(t, axis=-1, keepdims=True)).astype(bf16)
        dk[reach] += tn(ds, q_stack)
        dv[reach] += tn(p_low, do_stack)
        dq = nn(ds, keys) * (1.0 / 16.0)
        own = pl.ds(rows + b * BLOCK, BLOCK)
        cs, sn = cosine[own], sine[own]
        for h in range(H):
            grad = rotate_back(dq[h * BLOCK : (h + 1) * BLOCK], cs, sn)
            back, dgain = rms_back(q_raw[mine, h * HD : (h + 1) * HD], gain_q, grad)
            dq_low[mine, h * HD : (h + 1) * HD] = back.astype(bf16)
            sum_q = sum_q + dgain
    sum_k = jnp.zeros((1, HD), f32)
    for c in range(2 * rows // 256):
        part = pl.ds(c * 256, 256)
        grad = rotate_back(dk[part] * (1.0 / 16.0), cosine[part], sine[part])
        back, dgain = rms_back(k_raw[part], gain_k, grad)
        out, at = (dkv_before, c * 256) if c * 256 < rows else (dkv_own, c * 256 - rows)
        out[at : at + 256, :HD] = back.astype(bf16)
        out[at : at + 256, HD:] = dv[part].astype(bf16)
        sum_k = sum_k + dgain
    qk_grad[...] = jnp.broadcast_to(jnp.concatenate([sum_q, sum_k], axis=1), qk_grad.shape)


def attend_back(probs, do, q, k, v, q_raw, k_raw, cosine, sine, qk_gain, after):
    rows = q.shape[0]
    return call(
        attend_back_kernel,
        [
            shaped((rows, H * HD), bf16), shaped((rows, 2 * HD), bf16),
            shaped((rows, 2 * HD), bf16), shaped((8, 2 * HD), f32),
        ],
        [probs, do, q, k, v, q_raw, k_raw, cosine, sine, qk_gain],
        us=0.3,
        scratch=[pltpu.VMEM((2 * rows, HD), f32), pltpu.VMEM((2 * rows, HD), f32)],
        after=after,
    )


def project_back_kernel(
    dq_low, dkv_before, dkv_own, qk_grad, hidden, x, qk_order, gain3, gain12, *refs
):
    pieces, (dh_before, dh, *grads) = refs[:-5], refs[-5:]
    rows = dq_low.shape[0]
    put_grad(grads, slice(0, 1024), tn(hidden[rows:], dq_low[...]).astype(bf16))
    grad = tn(hidden[:rows], dkv_before[...]) + tn(hidden[rows:], dkv_own[...])
    put_grad(grads, slice(1024, 1536), grad.astype(bf16))
    w_q = join_rows(pieces, slice(0, 1024))
    w_kv = join_rows(pieces, slice(1024, 1536))
    sum0 = jnp.zeros((1, x.shape[1]), f32)
    for c in range(rows // 256):
        part = pl.ds(c * 256, 256)
        before = x[part].astype(f32)
        grad = nt(dkv_before[part], w_kv)
        dh_before[part] = grad
        sum0 = sum0 + jnp.sum(grad * (before * inverse_rms(before)), axis=0, keepdims=True)
        own = x[rows + c * 256 : rows + (c + 1) * 256].astype(f32)
        grad = nt(dkv_own[part], w_kv) + nt(dq_low[part], w_q)
        dh[part] = grad
        sum0 = sum0 + jnp.sum(grad * (own * inverse_rms(own)), axis=0, keepdims=True)
    qk_spread = nt(qk_grad[...].astype(bf16), qk_order[...])
    rows_of = jnp.concatenate(
        [
            sum0, gain12[0:1], gain12[1:2], gain3[0:1], qk_spread[0:1],
            jnp.zeros((EXTRA - 5, x.shape[1]), f32),
        ],
        axis=0,
    )
    put_grad(grads, slice(1536, 1664), rows_of.T.astype(bf16))


def project_back(args, pieces, after):
    rows, width = args[0].shape[0], args[5].shape[1]
    return call(
        project_back_kernel,
        [shaped((rows, width), f32)] * 2 + grad_shapes(width, pieces[0].shape[1]),
        [*args, *pieces],
        us=8,
        after=after,
    )


def input_back_kernel(dh_before, dh, x, gains, dx1, order, before, own):
    rows = dx1.shape[0]
    table = order[...]
    for c in range(rows // 256):
        part = pl.ds(c * 256, 256)
        back, _ = rms_back(x[part].astype(f32), gains[0:1], dh_before[part])
        before[part] = nt(back.astype(bf16), table).astype(bf16)
        mine = x[rows + c * 256 : rows + (c + 1) * 256].astype(f32)
        back, _ = rms_back(mine, gains[0:1], dh[part])
        rest = back + dx1[part]
        total = jnp.zeros_like(rest)
        for _ in range(3):
            piece = rest.astype(bf16)
            rest = rest - piece.astype(f32)
            total = total + nt(piece, table)
        own[part] = total


def input_back(dh_before, dh, x, gains, dx1, order, after=()):
    outs = [shaped(dx1.shape, bf16), shaped(dx1.shape, f32)]
    args = [dh_before, dh, x, gains, dx1, order]
    return call(input_back_kernel, outs, args, us=0.3, after=after)


def select_kernel(first, own, other, out):
    pick = first[:1, :1] > 0.5
    out[...] = jnp.where(pick, other[...].astype(f32), own[...].astype(f32)).astype(bf16)


def to_device_before(x, n, first, after=()):
    hop = lax.ppermute(x, "seq", [(i + EIGHT, i) for i in range(0, n - EIGHT, EIGHT)])
    (out,) = call(select_kernel, [shaped(x.shape, bf16)], [first, x, hop], us=0.3, after=after)
    pairs = [(i, i - 1) for i in range(n) if i % EIGHT]
    pairs += [(i, i + EIGHT - 1) for i in range(0, n - EIGHT, EIGHT)]
    return out, lax.ppermute(out, "seq", pairs)


def join_halo_kernel(own, behind, out):
    out[...] = own[...] + behind[...].astype(f32)


def join_halo(own, behind, after=()):
    outs = [shaped(own.shape, f32)]
    return call(join_halo_kernel, outs, [own, behind], us=0.3, after=after, result=True)


def on_device(
    tokens,
    segment_ids,
    w_query,
    w_key,
    w_value,
    w_output,
    w_gate,
    w_up,
    w_down,
    norm_gains,
    qk_gains,
    cotangent,
):
    n = lax.axis_size("seq")
    me = lax.axis_index("seq")
    rows, width = tokens.shape
    shard = w_query.shape[0]
    qk_shard = qk_gains.shape[0]

    travel_a, travel_b, travel_c = travelling(
        norm_gains, qk_gains[None, :], (w_query, w_key, w_value), (w_output.T, w_gate, w_up),
        (w_down.T,),
    )
    cols_a = w_query.shape[1] + w_key.shape[1] + w_value.shape[1] + EXTRA
    cols_b = w_output.shape[0] + w_gate.shape[1] + w_up.shape[1]
    cols_c = w_down.shape[0]

    even, odd, inner = row_table(n, shard)
    device = me ^ jnp.where(me & 1 == 0, jnp.asarray(even), jnp.asarray(odd))
    place = device * shard + inner
    qk_place = jnp.where(inner < qk_shard, device * qk_shard + inner, -1)
    padded_ids = jnp.concatenate([jnp.full((LONGEST + rows,), -1, jnp.int32), segment_ids])
    nearby = lax.dynamic_slice_in_dim(padded_ids, me * rows, 2 * rows + LONGEST)
    keys_segment = nearby[LONGEST:]
    seg_q = keys_segment[rows:, None]
    seg_k = jnp.stack(
        [keys_segment[b * BLOCK : b * BLOCK + REACH] for b in range(rows // BLOCK)]
    )[:, None, :]

    tokens_before = lax.ppermute(tokens, "seq", [(i, i + 1) for i in range(n - 1)])
    steps = len(far_bits(n)[0])
    a_c = to_first(travel_c, n)
    (own_b,) = pack(far_direct(travel_b, n), shard, cols_b, 1, n, after=(a_c,))
    a_b, b_b = to_first(own_b, n), to_second(own_b, n)
    pair_c, block_a = call(
        start_kernel,
        [
            shaped((2 * travel_c.shape[0], travel_c.shape[1]), bf16),
            shaped(travel_a.shape, bf16),
        ],
        [travel_c, a_c, travel_a],
        us=0.2,
        after=(own_b,),
    )
    for step in range(steps - 1):
        block_a, pair_c = stack(
            (block_a, far_step(block_a, n, step)), (pair_c, far_step(pair_c, n, step))
        )
    (own_a,) = pack([block_a, far_step(block_a, n, steps - 1)], shard, cols_a, 1, n)
    a_a, b_a = to_first(own_a, n), to_second(own_a, n)
    half_c = pack([pair_c, far_step(pair_c, n, steps - 1)], shard, cols_c, 2, n, after=(own_a,))
    first = (me % EIGHT == 0).astype(f32).reshape(1, 1)
    cosine, sine, order, qk_order, first = tables(
        nearby, rows, place, qk_place, width, first, after=(own_b,)
    )
    x, dy = permute(tokens_before, tokens, cotangent, order)
    a_b, own_b, *parts_b = hold_parts(
        a_b, own_b, after=(b_b, x, seg_q, seg_k, a_a, b_a, *half_c)
    )
    weights_a = [own_a, a_a, b_a, to_second(a_a, n)]
    weights_a = [*weights_a, *to_core(weights_a, n)]
    hidden, q_raw, k_raw, q, k, v, probs, o, gains, qk_gain = attend(
        x, weights_a, qk_order, cosine, sine, seg_q, seg_k, after=()
    )
    far_half = to_second(half_c[0], n)
    parts_b = [to_second(p, n) for p in parts_b]
    weights_b = [own_b, a_b, b_b, *parts_b]
    weights_b = [*weights_b, *to_core(weights_b, n)]
    a, middle, normed = join(o, weights_b, x, gains)
    half_c = [*half_c, *hold(far_half, after=(normed,))]
    weights_c = [*half_c, *to_core(half_c, n)]
    product, by_gate, by_up = feed(normed, weights_b, after=half_c[1:])
    mixed, low, gain3, *grad_d = turn(product, weights_c, middle, dy, gains, order)
    gate_low, up_low, *grad_g = feed_back(low, weights_c, by_gate, by_up, normed)
    sum_d = core_sum(grad_d[0], grad_d[1:], n, after=(gate_low,))
    sum_g = core_sum(grad_g[0], grad_g[1:], n, after=sum_d[:1])
    dx1, gain12, do, *grad_u = middle_back(
        gate_low, up_low, weights_b, middle, a, dy, gains, normed, o, after=sum_g[:1]
    )
    dq_low, dkv_before, dkv_own, qk_grad = attend_back(
        probs, do, q, k, v, q_raw, k_raw, cosine, sine, qk_gain, after=()
    )
    sum_d = near_sum_first_both(sum_d, sum_g, n, after=(dq_low,))
    sum_u = core_sum(grad_u[0], grad_u[1:], n, after=sum_d[:1])
    dh_before, dh, *grad_a = project_back(
        [dq_low, dkv_before, dkv_own, qk_grad, hidden, x, qk_order, gain3, gain12],
        weights_a,
        after=sum_u[:1],
    )
    sum_a = core_sum(grad_a[0], grad_a[1:], n)
    before, own = input_back(dh_before, dh, x, gains, dx1, order, after=sum_a[:1])
    sum_d = near_sum_second(sum_d, n, after=(own,))
    sum_u = near_sum_first(sum_u, n, after=sum_d[:1], us=4)
    sum_a = near_sum_first(sum_a, n, after=sum_u[:1])
    sum_d = far_sum_first(sum_d, n, after=sum_a[:1])
    before, behind = to_device_before(before, n, first, after=sum_d[:1])
    sum_a = near_sum_far([sum_a, sum_u], n, 2, after=(before,))
    ff = grad_d[0].shape[1]
    sum_a = far_sum_first(sum_a, n)
    input_grad, token = join_halo(own, behind, after=sum_a[:1])
    sum_d, sum_g, token = far_sum_last(sum_d, n, shard, ((0, ff, 2 * ff),), after=(token,))
    sum_q, sum_k, sum_v, sum_n, sum_u, sum_o, _ = far_sum_last(
        sum_a, n, shard, ((0, 1024, 1280, 1536, 1664), (0, ff, ff + 1024)), after=(token,)
    )
    return (
        mixed,
        input_grad,
        sum_q,
        sum_k,
        sum_v,
        sum_o.T,
        sum_g,
        sum_u,
        sum_d.T,
        sum_n[:, :4].T,
        sum_n[:qk_shard, 4],
    )


def solution(mesh):
    return jax.shard_map(
        on_device,
        mesh=mesh,
        in_specs=(
            P("seq", None),
            P(),
            P("seq", None),
            P("seq", None),
            P("seq", None),
            P(None, "seq"),
            P("seq", None),
            P("seq", None),
            P(None, "seq"),
            P(None, "seq"),
            P("seq"),
            P("seq", None),
        ),
        out_specs=(
            P("seq", None),
            P("seq", None),
            P("seq", None),
            P("seq", None),
            P("seq", None),
            P(None, "seq"),
            P("seq", None),
            P("seq", None),
            P(None, "seq"),
            P(None, "seq"),
            P("seq"),
        ),
        check_vma=False,
    )
```

```python
import functools

import jax
import jax.numpy as jnp
import numpy as np
from jax import lax
from jax.experimental import pallas as pl
from jax.experimental.pallas import tpu as pltpu
from jax.sharding import PartitionSpec as P

H = 4
HD = 256
WINDOW = 512
LONGEST = 2048
EXTRA = 128
EIGHT = 8
FF_CHUNK = 512
BLOCK = 128
REACH = BLOCK + WINDOW
MIB = 1024 * 1024

epsilon = 1e-06
bf16 = jnp.bfloat16
f32 = jnp.float32


def far_bits(n):
    bits = [1 << i for i in range(n.bit_length() - 1)]
    rest = [b for b in bits[1:] if b not in near_pair(n)]
    return rest, rest[::-1]


def far_slots(bits):
    slots = [0]
    for b in bits:
        slots = slots + [s | b for s in slots]
    return slots


def near_pair(n):
    return (2, 8) if n > 64 else (2, 4)


def to_partner(x, n, masks):
    return lax.ppermute(x, "seq", [(i, i ^ masks[i & 1]) for i in range(n)])


def row_table(n, shard):
    first, second = near_pair(n)
    main = whole_tiles(shard)
    count = n // 8
    inner = [(i, r) for i in range(count) for r in range(main)]
    inner += [(i, r) for i in range(count) for r in range(main, shard)]

    def offsets(a, b, bits):
        far = far_slots(bits)
        return [m ^ far[i] for m in (0, a, b, a | b) for i, _ in inner]

    even_bits, odd_bits = far_bits(n)
    even, odd = offsets(first, second, even_bits), offsets(second, first, odd_bits)
    return (
        np.array(even + [1 ^ m for m in odd], np.int32),
        np.array(odd + [1 ^ m for m in even], np.int32),
        np.array([r for _, r in inner] * 8, np.int32),
    )


def nn(left, right):
    return jnp.dot(left, right, preferred_element_type=f32)


def tn(left, right):
    return lax.dot_general(left, right, (((0,), (0,)), ((), ())), preferred_element_type=f32)


def nt(left, right):
    return lax.dot_general(left, right, (((1,), (1,)), ((), ())), preferred_element_type=f32)


def inverse_rms(values):
    return lax.rsqrt(jnp.mean(values * values, axis=-1, keepdims=True) + epsilon)


def rms_back(values, gain, grad):
    scale = inverse_rms(values)
    hat = values * scale
    inner = grad * gain
    mean = jnp.mean(inner * hat, axis=-1, keepdims=True)
    return scale * (inner - hat * mean), jnp.sum(grad * hat, axis=0, keepdims=True)


def rotate(values, cosine, sine):
    half = values.shape[-1] // 2
    a, b = values[:, :half], values[:, half:]
    return jnp.concatenate([a * cosine - b * sine, b * cosine + a * sine], axis=-1)


def rotate_back(values, cosine, sine):
    half = values.shape[-1] // 2
    a, b = values[:, :half], values[:, half:]
    return jnp.concatenate([a * cosine + b * sine, b * cosine - a * sine], axis=-1)


def call(kernel, outs, args, us, scratch=(), after=(), room=12, result=False):
    given, extra = len(args), len(after)

    def body(*refs):
        if result:
            *refs, token = refs
            token[...] = jnp.zeros_like(token)
        kernel(*refs[:given], *refs[given + extra :])

    if result:
        outs = [pltpu.HBM(o.shape, o.dtype) for o in outs] + [shaped((8, 128), f32)]
    return pl.pallas_call(
        body,
        in_specs=[pl.BlockSpec(memory_space=pltpu.VMEM)] * given
        + [pl.BlockSpec(memory_space=pl.ANY)] * extra,
        out_specs=[pl.BlockSpec(memory_space=pltpu.VMEM)] * len(outs),
        out_shape=outs,
        scratch_shapes=scratch,
        compiler_params=pltpu.CompilerParams(vmem_limit_bytes=room * MIB),
        cost_estimate=pl.CostEstimate(
            flops=int(us * 10**9), bytes_accessed=int(us * 10**6), transcendentals=0
        ),
    )(*args, *after)


def shaped(shape, dtype):
    return jax.ShapeDtypeStruct(shape, dtype)


def join_rows(parts, cols=slice(None)):
    return jnp.concatenate([p[:, cols] for p in parts], axis=0)


def whole_tiles(rows):
    return rows // 16 * 16


def padded(cols):
    return -(-cols // 512) * 512


def in_tiles(rows):
    return rows == 20


def travel_shape(rows, cols):
    return (16, padded(cols) * 5 // 4) if in_tiles(rows) else (rows, cols)


def to_tiles(values):
    rows, cols = values.shape
    if not in_tiles(rows):
        return values
    wide = padded(cols)
    if wide > cols:
        values = jnp.concatenate([values, jnp.zeros((rows, wide - cols), f32)], axis=1)
    quarter = wide // 4
    rest = [values[16:, k * quarter : (k + 1) * quarter] for k in range(4)]
    return jnp.concatenate([values[:16], jnp.concatenate(rest, axis=0)], axis=1)


def tile_kernel(counts, *refs):
    total = sum(counts) + 2
    given, outs = refs[:total], refs[total : total + len(counts)]
    held, sem = refs[total + len(counts) : -1], refs[-1]
    copies = [
        pltpu.make_async_copy(source, target, sem.at[i])
        for i, (source, target) in enumerate(zip(given, held))
    ]
    for copy in copies:
        copy.start()
    for copy in copies:
        copy.wait()
    *held, norm_gains, qk_gains = held
    shard = norm_gains.shape[1]
    rows = [
        jnp.concatenate([g[...].astype(f32), jnp.zeros((g.shape[0], EXTRA - g.shape[1]), f32)], axis=1)
        for g in (norm_gains, qk_gains)
    ]
    rows.append(jnp.zeros((EXTRA - 5, EXTRA), f32))
    extra = jnp.concatenate(rows, axis=0).T[:shard]
    for group, (count, out) in enumerate(zip(counts, outs)):
        parts = [p[...].astype(f32) for p in held[:count]]
        held = held[count:]
        if group == 0:
            parts.append(extra)
        out[...] = to_tiles(jnp.concatenate(parts, axis=1)).astype(bf16)


def travelling(norm_gains, qk_gains, *groups):
    counts = [len(g) for g in groups]
    given = [w for g in groups for w in g] + [norm_gains, qk_gains]
    outs = []
    for i, g in enumerate(groups):
        cols = sum(w.shape[1] for w in g) + (EXTRA if i == 0 else 0)
        outs.append(shaped(travel_shape(g[0].shape[0], cols), bf16))
    return pl.pallas_call(
        functools.partial(tile_kernel, counts),
        in_specs=[pl.BlockSpec(memory_space=pltpu.HBM)] * len(given),
        out_specs=[pl.BlockSpec(memory_space=pltpu.VMEM)] * len(outs),
        out_shape=outs,
        scratch_shapes=[pltpu.VMEM(w.shape, bf16) for w in given]
        + [pltpu.SemaphoreType.DMA((len(given),))],
        compiler_params=pltpu.CompilerParams(vmem_limit_bytes=8 * MIB),
    )(*[pltpu.with_memory_space_constraint(w, pltpu.HBM) for w in given])


def stack_kernel(*refs):
    count = len(refs) // 3
    for i in range(count):
        a, b, out = refs[2 * i], refs[2 * i + 1], refs[2 * count + i]
        rows = a.shape[0]
        if rows % 16 == 0:
            out[:rows] = a[...]
            out[rows:] = b[...]
        else:
            both = [a[...].astype(f32), b[...].astype(f32)]
            out[...] = jnp.concatenate(both, axis=0).astype(bf16)


def stack(*pairs, after=()):
    outs = [shaped((2 * a.shape[0], a.shape[1]), bf16) for a, _ in pairs]
    return call(stack_kernel, outs, [x for pair in pairs for x in pair], us=0.5, after=after)


def pack_kernel(pieces, blocks, out):
    count = len(pieces)
    share, cols = out.shape[0] // blocks, out.shape[1]
    rows = share // count
    main = whole_tiles(rows)
    height, wide = travel_shape(rows, cols)
    quarter = padded(cols) // 4
    for block in range(blocks):
        at = block * share
        starts = [(ref, begin + block * height) for ref, begin in pieces]
        if main:
            for i, (ref, begin) in enumerate(starts):
                out[at + i * main : at + (i + 1) * main] = ref[begin : begin + main, :cols]
        at = at + main * count
        if in_tiles(rows):
            rest = [ref[begin : begin + 16, 4 * quarter :].astype(f32) for ref, begin in starts]
            for k in range(4):
                end = min((k + 1) * quarter, cols)
                part = jnp.concatenate([r[4 * k : 4 * k + 4] for r in rest], axis=0)
                out[at : at + 4 * count, k * quarter : end] = part[:, : end - k * quarter].astype(
                    bf16
                )
        elif rows > main:
            rest = [
                ref[...].astype(f32)[begin + main : begin + rows] for ref, begin in starts
            ]
            out[at : at + (rows - main) * count] = jnp.concatenate(rest, axis=0).astype(bf16)


def pack(arrays, rows, cols, blocks, n, parts=1, after=()):
    count = n // 8
    height = travel_shape(rows, cols)[0] * blocks
    held = count // len(arrays)
    total = rows * count * blocks

    def kernel(*refs):
        given = refs[: len(arrays)]
        pieces = [(ref, h * height) for ref in given for h in range(held)]
        if parts == 1:
            pack_kernel(pieces, blocks, refs[-1])
        else:
            for block, out in enumerate(refs[len(arrays) :]):
                shift = block * height // blocks
                pack_kernel([(ref, at + shift) for ref, at in pieces], 1, out)

    outs = [shaped((total // parts, cols), bf16)] * parts
    return call(kernel, outs, arrays, us=1.5, after=after)


def far_step(block, n, step):
    even, odd = far_bits(n)
    return to_partner(block, n, (even[step], odd[step]))


def far_direct(block, n):
    even, odd = far_bits(n)
    slots = zip(far_slots(even)[1:], far_slots(odd)[1:])
    return [block] + [to_partner(block, n, masks) for masks in slots]


def start_kernel(a, b, one, out, one_out):
    stack_kernel(a, b, out)
    one_out[...] = one[...]


def hold_kernel(*refs):
    half = len(refs) // 2
    for value, out in zip(refs[:half], refs[half:]):
        out[...] = value[...]


def hold(*values, after):
    return call(hold_kernel, [shaped(v.shape, v.dtype) for v in values], values, 0.2, after=after)


def hold_parts_kernel(one, two, one_out, two_out, upper, lower):
    one_out[...] = one[...]
    two_out[...] = two[...]
    rows = upper.shape[0]
    upper[...] = one[:rows]
    lower[...] = one[rows:]


def hold_parts(one, two, after):
    rows, cols = one.shape
    upper = rows // 32 * 16 + (16 if rows % 32 else 0)
    outs = [shaped(one.shape, bf16), shaped(two.shape, bf16)]
    outs += [shaped((upper, cols), bf16), shaped((rows - upper, cols), bf16)]
    return call(hold_parts_kernel, outs, [one, two], us=0.2, after=after)


def far_gather(blocks, n, joins):
    steps = len(far_bits(n)[0])
    for k in range(steps - 1):
        got = [far_step(b, n, k) for b in blocks]
        blocks = stack(*zip(blocks, got), after=joins[k] if k < len(joins) else ())
    return [(b, far_step(b, n, steps - 1)) for b in blocks]


def to_first(x, n):
    first, second = near_pair(n)
    return to_partner(x, n, (first, second))


def to_second(x, n):
    first, second = near_pair(n)
    return to_partner(x, n, (second, first))


def near_pieces(own, n, direct=False):
    first, second = near_pair(n)
    a, b = to_first(own, n), to_second(own, n)
    return [own, a, b, to_partner(own, n, (first | second,) * 2) if direct else to_second(a, n)]


def to_core(pieces, n):
    return [to_partner(p, n, (1, 1)) for p in pieces]


def fold_kernel(count, *refs):
    given, outs = refs[:count], refs[count:]
    mine, got = given[0], given[1:]
    rows = outs[0].shape[0]
    height = got[0].shape[0]
    if rows % 16 == 0 and height % rows == 0:
        per = height // rows
        for i, out in enumerate(outs):
            other = got[i // per][(i % per) * rows : (i % per + 1) * rows]
            part = mine[i * rows : (i + 1) * rows]
            out[...] = (part.astype(f32) + other.astype(f32)).astype(bf16)
    else:
        total = mine[...].astype(f32)
        total = total + jnp.concatenate([g[...].astype(f32) for g in got], axis=0)
        for i, out in enumerate(outs):
            out[...] = total[i * rows : (i + 1) * rows].astype(bf16)


def fold(mine, got, after=(), us=0.5):
    rows, cols = mine.shape
    outs = [shaped((rows // 2, cols), bf16)] * 2
    kernel = functools.partial(fold_kernel, 1 + len(got))
    return call(kernel, outs, [mine, *got], us=us, after=after)


def wide_fold_kernel(mine, *refs):
    got, (keep, send) = refs[:-2], refs[-2:]
    rows = got[0].shape[0]
    per = keep.shape[0] // rows
    for i, other in enumerate(got):
        out = keep if i < per else send
        at = (i % per) * rows
        part = mine[i * rows : (i + 1) * rows].astype(f32)
        out[at : at + rows] = (part + other[...].astype(f32)).astype(bf16)


def core_sum(top, sends, n, after=()):
    rows, cols = top.shape
    outs = [shaped((rows // 2, cols), bf16)] * 2
    return call(wide_fold_kernel, outs, [top, *to_core(sends, n)], us=0.7, after=after)


def core_sum_by_far(top, sends, n, after=()):
    rows, cols = top.shape
    count, blocks = n // 8, 4
    share = rows // blocks
    shard = share // count
    main = whole_tiles(shard)
    rest, done = shard - main, main * count
    height, wide = travel_shape(shard, cols)

    def kernel(mine, *refs):
        got, (keep, send) = refs[:-2], refs[-2:]
        per = blocks // len(got)
        tiles = []
        for block in range(blocks):
            other = got[block // per][(block % per) * share : (block % per + 1) * share]
            total = mine[block * share : (block + 1) * share].astype(f32) + other.astype(f32)
            for i in range(count):
                parts = []
                if main:
                    parts.append(total[i * main : (i + 1) * main])
                if rest:
                    parts.append(total[done + i * rest : done + (i + 1) * rest])
                tiles.append((i, block, to_tiles(jnp.concatenate(parts, axis=0))))
        tiles = [t for _, _, t in sorted(tiles, key=lambda item: item[:2])]
        half = len(tiles) // 2
        keep[...] = jnp.concatenate(tiles[:half], axis=0).astype(bf16)
        send[...] = jnp.concatenate(tiles[half:], axis=0).astype(bf16)

    outs = [shaped((count // 2 * blocks * height, wide), bf16)] * 2
    return call(kernel, outs, [top, *to_core(sends, n)], us=1.5, after=after)


def far_fold(halves, n, step, after=(), us=0.5):
    keep, send = halves
    return fold(keep, [far_step(send, n, step)], after, us)


def near_sum_last(halves, n, shard, cuts, after=()):
    keep, send = halves
    outs = [shaped((shard, e - b), f32) for b, e in zip(cuts[:-1], cuts[1:])]
    return call(
        functools.partial(far_sum_kernel, (cuts,), None), outs, [keep, to_first(send, n)], us=1,
        after=after, result=True,
    )


def near_sum_first(halves, n, after=(), us=0.5):
    keep, send = halves
    return fold(keep, [to_second(send, n)], after, us)


def fold_both_kernel(*refs):
    given, (keep, send) = refs[:4], refs[4:]
    rows, cols = keep.shape
    cols = cols // 2
    for i in range(2):
        mine, got = given[2 * i : 2 * i + 2]
        for j, out in enumerate((keep, send)):
            part = slice(j * rows, (j + 1) * rows)
            out[:, i * cols : (i + 1) * cols] = (
                mine[part].astype(f32) + got[part].astype(f32)
            ).astype(bf16)


def near_sum_first_both(one, two, n, after=()):
    args = [x for keep, send in (one, two) for x in (keep, to_second(send, n))]
    rows, cols = one[0].shape
    outs = [shaped((rows // 2, 2 * cols), bf16)] * 2
    return call(fold_both_kernel, outs, args, us=5, after=after)


def split_kernel(count, mine, got, keep, send):
    total = mine[...].astype(f32) + got[...].astype(f32)
    rows = total.shape[0] // count
    main = whole_tiles(rows)
    rest, done = rows - main, main * count
    slots = []
    for i in range(count):
        parts = []
        if main:
            parts.append(total[i * main : (i + 1) * main])
        if rest:
            parts.append(total[done + i * rest : done + (i + 1) * rest])
        slots.append(to_tiles(jnp.concatenate(parts, axis=0)))
    keep[...] = jnp.concatenate(slots[: count // 2], axis=0).astype(bf16)
    send[...] = jnp.concatenate(slots[count // 2 :], axis=0).astype(bf16)


def near_sum_second(halves, n, after=()):
    keep, send = halves
    rows, cols = keep.shape
    count = n // 8
    height, wide = travel_shape(rows // count, cols)
    outs = [shaped((count // 2 * height, wide), bf16)] * 2
    return call(
        functools.partial(split_kernel, count), outs, [keep, to_first(send, n)], us=1, after=after
    )


def slots_kernel(groups, count, *refs):
    outs = refs[2 * groups :]
    slots = [[] for _ in range(count)]
    for g in range(groups):
        total = refs[2 * g][...].astype(f32) + refs[2 * g + 1][...].astype(f32)
        rows = total.shape[0] // count
        main = whole_tiles(rows)
        rest, done = rows - main, main * count
        for i in range(count):
            parts = []
            if main:
                parts.append(total[i * main : (i + 1) * main])
            if rest:
                parts.append(total[done + i * rest : done + (i + 1) * rest])
            slots[i].append(to_tiles(jnp.concatenate(parts, axis=0)))
    per = count // len(outs)
    for i, parts in enumerate(slots):
        values = jnp.concatenate(parts, axis=1).astype(bf16)
        height = values.shape[0]
        if per == 1:
            outs[i][...] = values
        elif height % 16 == 0:
            outs[i // per][i % per * height : (i % per + 1) * height] = values
    if per > 1 and height % 16 != 0:
        for j, out in enumerate(outs):
            values = [jnp.concatenate(p, axis=1) for p in slots[j * per : (j + 1) * per]]
            out[...] = jnp.concatenate(values, axis=0).astype(bf16)


def near_sum_far(groups, n, parts, after=()):
    count = n // 8
    args, wide = [], 0
    for keep, send in groups:
        args += [keep, to_first(send, n)]
        height, cols = travel_shape(keep.shape[0] // count, keep.shape[1])
        wide += cols
    outs = [shaped((height * count // parts, wide), bf16)] * parts
    kernel = functools.partial(slots_kernel, len(groups), count)
    return call(kernel, outs, args, us=1, after=after)


def far_sum_first(halves, n, after=()):
    keep, send = halves
    for k in reversed(range(1, len(far_bits(n)[0]))):
        keep, send = fold(keep, [far_step(send, n, k)], after)
        after = ()
    return keep, send


def far_sum_kernel(groups, gains_at, *refs):
    count = sum(len(cuts) - 1 for cuts in groups) + (gains_at is not None)
    given, outs = refs[:-count], refs[-count:]
    total = given[0][...].astype(f32)
    for got in given[1:]:
        total = total + got[...].astype(f32)
    rows = outs[0].shape[0]
    begin_at = 0
    for number, cuts in enumerate(groups):
        wide = padded(cuts[-1]) if in_tiles(rows) else cuts[-1]
        part = total[:, begin_at : begin_at + wide]
        if in_tiles(rows):
            quarter = wide // 4
            rest = total[:, begin_at + wide : begin_at + wide + quarter]
            rest = [rest[4 * k : 4 * k + 4] for k in range(4)]
            part = jnp.concatenate([part, jnp.concatenate(rest, axis=1)], axis=0)
            begin_at += quarter
        begin_at += wide
        for begin, end in zip(cuts[:-1], cuts[1:]):
            values = part[:, begin:end]
            if number == 0 and begin == gains_at:
                values = jnp.concatenate([values, jnp.zeros((EXTRA - rows, EXTRA), f32)], axis=0).T
                norms, qk, *outs = outs
                norms[...] = values[: norms.shape[0], :rows]
                qk[...] = values[norms.shape[0] : norms.shape[0] + 1, : qk.shape[1]]
            else:
                outs[0][...] = values
                outs = outs[1:]


def result_shapes(shard, groups, gains_at, gain_shapes):
    outs = []
    for number, cuts in enumerate(groups):
        for begin, end in zip(cuts[:-1], cuts[1:]):
            if number == 0 and begin == gains_at:
                outs += [shaped(shape, f32) for shape in gain_shapes]
            else:
                outs.append(shaped((shard, end - begin), f32))
    return outs


def far_sum_last(halves, n, shard, groups, gains_at=None, gain_shapes=(), after=()):
    keep, send = halves
    outs = result_shapes(shard, groups, gains_at, gain_shapes)
    kernel = functools.partial(far_sum_kernel, groups, gains_at)
    args = [keep, far_step(send, n, 0)]
    return call(kernel, outs, args, us=1, after=after, result=True)


def table_kernel(near, near_col, freqs, place, qk_place, first, cosine, sine, order, qk_order, first_out):
    count = cosine.shape[0]
    ahead = near.shape[1] - count
    steps = freqs[...]
    for c in range(count // 256):
        reach = slice(c * 256, c * 256 + ahead + 256)
        here = near_col[ahead + c * 256 : ahead + (c + 1) * 256]
        i = lax.broadcasted_iota(jnp.int32, (256, ahead + 256), 0) + ahead
        j = lax.broadcasted_iota(jnp.int32, (256, ahead + 256), 1)
        same = (here == near[:, reach]) & (j < i)
        position = jnp.sum(same.astype(f32), axis=1, keepdims=True)
        angles = position * steps
        cosine[c * 256 : (c + 1) * 256] = jnp.cos(angles)
        sine[c * 256 : (c + 1) * 256] = jnp.sin(angles)
    i = lax.broadcasted_iota(jnp.int32, order.shape, 0)
    order[...] = (i == place[...]).astype(f32).astype(bf16)
    j = lax.broadcasted_iota(jnp.int32, qk_order.shape, 1)
    qk_order[...] = (qk_place[...] == j).astype(f32).astype(bf16)
    first_out[...] = jnp.broadcast_to(first[...], first_out.shape)


def tables(near, rows, place, qk_place, width, first, after=()):
    freqs = np.float32(10000.0) ** (-2.0 * np.arange(HD // 2, dtype=np.float32) / np.float32(HD))
    args = [
        near[None, :], near[:, None], jnp.asarray(freqs)[None, :], place[None, :], qk_place[:, None],
        first,
    ]
    outs = [
        shaped((2 * rows, HD // 2), f32), shaped((2 * rows, HD // 2), f32),
        shaped((width, width), bf16), shaped((width, 2 * HD), bf16), shaped((8, 128), f32),
    ]
    return call(table_kernel, outs, args, us=3, after=after)


def permute_kernel(tokens_before, tokens, cotangent, order, x, dy):
    table = order[...]
    rows = tokens.shape[0]
    x[:rows] = nn(tokens_before[...], table).astype(bf16)
    x[rows:] = nn(tokens[...], table).astype(bf16)
    dy[...] = nn(cotangent[...], table).astype(bf16)


def permute(tokens_before, tokens, cotangent, order, after=()):
    rows, width = tokens.shape
    outs = [shaped((2 * rows, width), bf16), shaped((rows, width), bf16)]
    args = [tokens_before, tokens, cotangent, order]
    return call(permute_kernel, outs, args, us=2, after=after)


def attend_kernel(x, qk_order, cosine, sine, seg_q, seg_k, *refs):
    pieces = refs[:-10]
    hidden, q_raw, k_raw, q_out, k_out, v_out, probs, o, gains, qk_gain = refs[-10:]
    rows = q_raw.shape[0]
    w_q = join_rows(pieces, slice(0, 1024))
    w_kv = join_rows(pieces, slice(1024, 1536))
    gain_rows = join_rows(pieces, slice(1536, 1664)).astype(f32).T[:8]
    gains[...] = gain_rows
    gain_qk = nn(gain_rows.astype(bf16), qk_order[...])
    qk_gain[...] = gain_qk
    gain_q, gain_k = gain_qk[4:5, :HD], gain_qk[4:5, HD:]
    for c in range(2 * rows // 256):
        part = pl.ds(c * 256, 256)
        xs = x[part].astype(f32)
        hs = (xs * inverse_rms(xs) * gain_rows[0:1]).astype(bf16)
        hidden[part] = hs
        cs, sn = cosine[part], sine[part]
        kv = nn(hs, w_kv)
        raw = kv[:, :HD]
        k_raw[part] = raw
        k_out[part] = rotate(raw * inverse_rms(raw) * gain_k, cs, sn).astype(bf16)
        v_out[part] = kv[:, HD:].astype(bf16)
        if c * 256 >= rows:
            own = pl.ds(c * 256 - rows, 256)
            qs = nn(hs, w_q)
            q_raw[own] = qs
            for h in range(H):
                raw = qs[:, h * HD : (h + 1) * HD]
                q_out[own, h * HD : (h + 1) * HD] = rotate(
                    raw * inverse_rms(raw) * gain_q, cs, sn
                ).astype(bf16)
    for b in range(rows // BLOCK):
        mine = pl.ds(b * BLOCK, BLOCK)
        reach = pl.ds(b * BLOCK, REACH)
        q_rows = q_out[mine] * bf16(1.0 / 16.0)
        q_stack = jnp.concatenate([q_rows[:, h * HD : (h + 1) * HD] for h in range(H)], axis=0)
        scores = nt(q_stack, k_out[reach])
        i = lax.broadcasted_iota(jnp.int32, (BLOCK, REACH), 0)
        j = lax.broadcasted_iota(jnp.int32, (BLOCK, REACH), 1)
        allowed = (j > i) & (j <= i + WINDOW) & (seg_q[mine] == seg_k[b])
        allowed = jnp.concatenate([allowed.astype(f32)] * H, axis=0)
        weights = jnp.exp(scores) * allowed
        total = jnp.sum(weights, axis=-1, keepdims=True)
        p = (weights * (1.0 / total)).astype(bf16)
        probs[b] = p
        out = nn(p, v_out[reach])
        for h in range(H):
            o[mine, h * HD : (h + 1) * HD] = out[h * BLOCK : (h + 1) * BLOCK].astype(bf16)


def attend(x, pieces, qk_order, cosine, sine, seg_q, seg_k, after):
    rows = x.shape[0] // 2
    width = x.shape[1]
    return call(
        attend_kernel,
        [
            shaped((2 * rows, width), bf16),
            shaped((rows, H * HD), f32),
            shaped((2 * rows, HD), f32),
            shaped((rows, H * HD), bf16),
            shaped((2 * rows, HD), bf16),
            shaped((2 * rows, HD), bf16),
            shaped((rows // BLOCK, H * BLOCK, REACH), bf16),
            shaped((rows, H * HD), bf16),
            shaped((8, width), f32),
            shaped((8, 2 * HD), f32),
        ],
        [x, qk_order, cosine, sine, seg_q, seg_k, *pieces],
        us=12,
        after=after,
    )


def gelu_parts(g):
    c0, c1 = 0.7978845608028654, 0.044715
    square = g * g
    t = jnp.tanh(c0 * g * (1.0 + c1 * square))
    value = 0.5 * g * (1.0 + t)
    slope = 0.5 * (1.0 + t) + 0.5 * g * (1.0 - t * t) * c0 * (1.0 + 3.0 * c1 * square)
    return value, slope


def join_kernel(o, x, gains, *refs):
    pieces, (a_out, middle, normed) = refs[:-3], refs[-3:]
    rows = o.shape[0]
    w_o = join_rows(pieces, slice(0, H * HD))
    for c in range(rows // 256):
        part = pl.ds(c * 256, 256)
        a = nt(o[part], w_o)
        a_out[part] = a
        x1 = x[rows + c * 256 : rows + (c + 1) * 256].astype(f32) + a * inverse_rms(a) * gains[1:2]
        middle[part] = x1
        normed[part] = (x1 * inverse_rms(x1) * gains[2:3]).astype(bf16)


def join(o, pieces, x, gains):
    rows, width = o.shape[0], x.shape[1]
    outs = [shaped((rows, width), f32), shaped((rows, width), f32), shaped((rows, width), bf16)]
    return call(join_kernel, outs, [o, x, gains, *pieces], us=2)


def feed_kernel(normed, *refs):
    pieces, (product, by_gate, by_up) = refs[:-3], refs[-3:]
    rows, ff = product.shape
    for j in range(ff // FF_CHUNK):
        cols = slice(j * FF_CHUNK, (j + 1) * FF_CHUNK)
        w_g = join_rows(pieces, slice(H * HD + cols.start, H * HD + cols.stop))
        w_u = join_rows(pieces, slice(H * HD + ff + cols.start, H * HD + ff + cols.stop))
        for c in range(rows // 256):
            part = pl.ds(c * 256, 256)
            h2 = normed[part]
            g = nn(h2, w_g)
            u = nn(h2, w_u)
            value, slope = gelu_parts(g)
            product[part, cols] = (value * u).astype(bf16)
            by_gate[part, cols] = (slope * u).astype(bf16)
            by_up[part, cols] = value.astype(bf16)


def feed(normed, pieces, after=()):
    rows = normed.shape[0]
    ff = (pieces[0].shape[1] - H * HD) // 2
    outs = [shaped((rows, ff), bf16)] * 3
    return call(feed_kernel, outs, [normed, *pieces], us=5, after=after)


def put_grad(grads, cols, values):
    top, *sends = grads
    half = top.shape[0]
    top[:, cols] = values[:half]
    part = half // len(sends)
    for i, send in enumerate(sends):
        send[:, cols] = values[half + i * part : half + (i + 1) * part]


def grad_shapes(width, cols):
    return [shaped((width // 2, cols), bf16)] + [shaped((width // 4, cols), bf16)] * 2


def turn_kernel(product, middle, dy, gains, order, *refs):
    pieces, (mixed, low, gain_grad, *grads) = refs[:-6], refs[-6:]
    ff = product.shape[1]
    w_d = join_rows(pieces)
    total = jnp.zeros((1, dy.shape[1]), f32)
    for c in range(dy.shape[0] // 256):
        part = pl.ds(c * 256, 256)
        f = nt(product[part], w_d)
        grad = dy[part].astype(f32)
        y = middle[part] + f * inverse_rms(f) * gains[3:4]
        mixed[part] = nt(y.astype(bf16), order[...]).astype(bf16)
        df, dgain = rms_back(f, gains[3:4], grad)
        low[part] = df.astype(bf16)
        total = total + dgain
    gain_grad[...] = jnp.broadcast_to(total, gain_grad.shape)
    for j in range(ff // FF_CHUNK):
        cols = slice(j * FF_CHUNK, (j + 1) * FF_CHUNK)
        grad = tn(low[...], product[:, cols]).astype(bf16)
        put_grad(grads, cols, grad)


def turn(product, pieces, middle, dy, gains, order):
    rows, width = middle.shape
    return call(
        turn_kernel,
        [
            shaped((rows, width), bf16),
            shaped((rows, width), bf16),
            shaped((8, width), f32),
            *grad_shapes(width, product.shape[1]),
        ],
        [product, middle, dy, gains, order, *pieces],
        us=6,
    )


def feed_back_kernel(low, by_gate, by_up, normed, *refs):
    pieces, (gate_low, up_low, *grads) = refs[:-5], refs[-5:]
    rows, ff = gate_low.shape
    for j in range(ff // FF_CHUNK):
        cols = slice(j * FF_CHUNK, (j + 1) * FF_CHUNK)
        w_d = join_rows(pieces, cols)
        for c in range(rows // 256):
            part = pl.ds(c * 256, 256)
            dm = nn(low[part], w_d)
            gate_low[part, cols] = (dm * by_gate[part, cols].astype(f32)).astype(bf16)
            up_low[part, cols] = (dm * by_up[part, cols].astype(f32)).astype(bf16)
        put_grad(grads, cols, tn(normed[...], gate_low[:, cols]).astype(bf16))


def feed_back(low, pieces, by_gate, by_up, normed):
    rows, width = low.shape
    ff = by_gate.shape[1]
    return call(
        feed_back_kernel,
        [shaped((rows, ff), bf16)] * 2 + grad_shapes(width, ff),
        [low, by_gate, by_up, normed, *pieces],
        us=4,
    )


def middle_back_kernel(gate_low, up_low, middle, a, dy, gains, normed, o, *refs):
    pieces, (dx1, gain_grad, do, *grads) = refs[:-6], refs[-6:]
    rows, ff = gate_low.shape
    w_o = join_rows(pieces, slice(0, H * HD))
    w_g = join_rows(pieces, slice(H * HD, H * HD + ff))
    w_u = join_rows(pieces, slice(H * HD + ff, H * HD + 2 * ff))
    sum1 = jnp.zeros((1, dy.shape[1]), f32)
    sum2 = jnp.zeros((1, dy.shape[1]), f32)
    lows = []
    for c in range(rows // 256):
        part = pl.ds(c * 256, 256)
        grad = nt(gate_low[part], w_g) + nt(up_low[part], w_u)
        back, dgain2 = rms_back(middle[part], gains[2:3], grad)
        dx = dy[part].astype(f32) + back
        dx1[part] = dx
        da, dgain1 = rms_back(a[part], gains[1:2], dx)
        low = da.astype(bf16)
        lows.append(low)
        do[part] = nn(low, w_o).astype(bf16)
        sum1, sum2 = sum1 + dgain1, sum2 + dgain2
    gain_grad[...] = jnp.concatenate([sum1, sum2, jnp.zeros((6, dy.shape[1]), f32)], axis=0)
    for j in range(ff // FF_CHUNK):
        cols = slice(j * FF_CHUNK, (j + 1) * FF_CHUNK)
        put_grad(grads, cols, tn(normed[...], up_low[:, cols]).astype(bf16))
    grad = tn(jnp.concatenate(lows, axis=0), o[...]).astype(bf16)
    put_grad(grads, slice(ff, ff + H * HD), grad)


def middle_back(gate_low, up_low, pieces, middle, a, dy, gains, normed, o, after):
    rows, width = middle.shape
    return call(
        middle_back_kernel,
        [
            shaped((rows, width), f32),
            shaped((8, width), f32),
            shaped((rows, H * HD), bf16),
            *grad_shapes(width, gate_low.shape[1] + H * HD),
        ],
        [gate_low, up_low, middle, a, dy, gains, normed, o, *pieces],
        us=14,
        after=after,
        room=16,
    )


def attend_back_kernel(
    probs, do, q, k, v, q_raw, k_raw, cosine, sine, qk_gain, dq_low, dkv_before, dkv_own, qk_grad, dk, dv
):
    rows = q_raw.shape[0]
    dk[...] = jnp.zeros_like(dk)
    dv[...] = jnp.zeros_like(dv)
    gain_q, gain_k = qk_gain[4:5, :HD], qk_gain[4:5, HD:]
    sum_q = jnp.zeros((1, HD), f32)
    for b in range(rows // BLOCK):
        mine = pl.ds(b * BLOCK, BLOCK)
        reach = pl.ds(b * BLOCK, REACH)
        keys, values = k[reach], v[reach]
        do_rows, q_rows = do[mine], q[mine]
        do_stack = jnp.concatenate([do_rows[:, h * HD : (h + 1) * HD] for h in range(H)], axis=0)
        q_stack = jnp.concatenate([q_rows[:, h * HD : (h + 1) * HD] for h in range(H)], axis=0)
        p_low = probs[b]
        p = p_low.astype(f32)
        t = p * nt(do_stack, values)
        ds = (t - p * jnp.sum(t, axis=-1, keepdims=True)).astype(bf16)
        dk[reach] += tn(ds, q_stack)
        dv[reach] += tn(p_low, do_stack)
        dq = nn(ds, keys) * (1.0 / 16.0)
        own = pl.ds(rows + b * BLOCK, BLOCK)
        cs, sn = cosine[own], sine[own]
        for h in range(H):
            grad = rotate_back(dq[h * BLOCK : (h + 1) * BLOCK], cs, sn)
            back, dgain = rms_back(q_raw[mine, h * HD : (h + 1) * HD], gain_q, grad)
            dq_low[mine, h * HD : (h + 1) * HD] = back.astype(bf16)
            sum_q = sum_q + dgain
    sum_k = jnp.zeros((1, HD), f32)
    for c in range(2 * rows // 256):
        part = pl.ds(c * 256, 256)
        grad = rotate_back(dk[part] * (1.0 / 16.0), cosine[part], sine[part])
        back, dgain = rms_back(k_raw[part], gain_k, grad)
        out, at = (dkv_before, c * 256) if c * 256 < rows else (dkv_own, c * 256 - rows)
        out[at : at + 256, :HD] = back.astype(bf16)
        out[at : at + 256, HD:] = dv[part].astype(bf16)
        sum_k = sum_k + dgain
    qk_grad[...] = jnp.broadcast_to(jnp.concatenate([sum_q, sum_k], axis=1), qk_grad.shape)


def attend_back(probs, do, q, k, v, q_raw, k_raw, cosine, sine, qk_gain, after):
    rows = q.shape[0]
    return call(
        attend_back_kernel,
        [
            shaped((rows, H * HD), bf16), shaped((rows, 2 * HD), bf16),
            shaped((rows, 2 * HD), bf16), shaped((8, 2 * HD), f32),
        ],
        [probs, do, q, k, v, q_raw, k_raw, cosine, sine, qk_gain],
        us=0.3,
        scratch=[pltpu.VMEM((2 * rows, HD), f32), pltpu.VMEM((2 * rows, HD), f32)],
        after=after,
    )


def project_back_kernel(
    dq_low, dkv_before, dkv_own, qk_grad, hidden, x, qk_order, gain3, gain12, *refs
):
    pieces, (dh_before, dh, *grads) = refs[:-5], refs[-5:]
    rows = dq_low.shape[0]
    put_grad(grads, slice(0, 1024), tn(hidden[rows:], dq_low[...]).astype(bf16))
    grad = tn(hidden[:rows], dkv_before[...]) + tn(hidden[rows:], dkv_own[...])
    put_grad(grads, slice(1024, 1536), grad.astype(bf16))
    w_q = join_rows(pieces, slice(0, 1024))
    w_kv = join_rows(pieces, slice(1024, 1536))
    sum0 = jnp.zeros((1, x.shape[1]), f32)
    for c in range(rows // 256):
        part = pl.ds(c * 256, 256)
        before = x[part].astype(f32)
        grad = nt(dkv_before[part], w_kv)
        dh_before[part] = grad
        sum0 = sum0 + jnp.sum(grad * (before * inverse_rms(before)), axis=0, keepdims=True)
        own = x[rows + c * 256 : rows + (c + 1) * 256].astype(f32)
        grad = nt(dkv_own[part], w_kv) + nt(dq_low[part], w_q)
        dh[part] = grad
        sum0 = sum0 + jnp.sum(grad * (own * inverse_rms(own)), axis=0, keepdims=True)
    qk_spread = nt(qk_grad[...].astype(bf16), qk_order[...])
    rows_of = jnp.concatenate(
        [
            sum0, gain12[0:1], gain12[1:2], gain3[0:1], qk_spread[0:1],
            jnp.zeros((EXTRA - 5, x.shape[1]), f32),
        ],
        axis=0,
    )
    put_grad(grads, slice(1536, 1664), rows_of.T.astype(bf16))


def project_back(args, pieces, after):
    rows, width = args[0].shape[0], args[5].shape[1]
    return call(
        project_back_kernel,
        [shaped((rows, width), f32)] * 2 + grad_shapes(width, pieces[0].shape[1]),
        [*args, *pieces],
        us=8,
        after=after,
    )


def input_back_kernel(dh_before, dh, x, gains, dx1, order, before, own):
    rows = dx1.shape[0]
    table = order[...]
    for c in range(rows // 256):
        part = pl.ds(c * 256, 256)
        back, _ = rms_back(x[part].astype(f32), gains[0:1], dh_before[part])
        before[part] = nt(back.astype(bf16), table).astype(bf16)
        mine = x[rows + c * 256 : rows + (c + 1) * 256].astype(f32)
        back, _ = rms_back(mine, gains[0:1], dh[part])
        rest = back + dx1[part]
        total = jnp.zeros_like(rest)
        for _ in range(3):
            piece = rest.astype(bf16)
            rest = rest - piece.astype(f32)
            total = total + nt(piece, table)
        own[part] = total


def input_back(dh_before, dh, x, gains, dx1, order, after=()):
    outs = [shaped(dx1.shape, bf16), shaped(dx1.shape, f32)]
    args = [dh_before, dh, x, gains, dx1, order]
    return call(input_back_kernel, outs, args, us=0.3, after=after)


def select_kernel(first, own, other, out):
    pick = first[:1, :1] > 0.5
    out[...] = jnp.where(pick, other[...].astype(f32), own[...].astype(f32)).astype(bf16)


def to_device_before(x, n, first, after=()):
    hop = lax.ppermute(x, "seq", [(i + EIGHT, i) for i in range(0, n - EIGHT, EIGHT)])
    (out,) = call(select_kernel, [shaped(x.shape, bf16)], [first, x, hop], us=0.3, after=after)
    pairs = [(i, i - 1) for i in range(n) if i % EIGHT]
    pairs += [(i, i + EIGHT - 1) for i in range(0, n - EIGHT, EIGHT)]
    return out, lax.ppermute(out, "seq", pairs)


def join_halo_kernel(own, behind, out):
    out[...] = own[...] + behind[...].astype(f32)


def join_halo(own, behind, after=()):
    outs = [shaped(own.shape, f32)]
    return call(join_halo_kernel, outs, [own, behind], us=0.3, after=after, result=True)


def on_device(
    tokens,
    segment_ids,
    w_query,
    w_key,
    w_value,
    w_output,
    w_gate,
    w_up,
    w_down,
    norm_gains,
    qk_gains,
    cotangent,
):
    n = lax.axis_size("seq")
    me = lax.axis_index("seq")
    rows, width = tokens.shape
    shard = w_query.shape[0]
    qk_shard = qk_gains.shape[0]

    travel_a, travel_b, travel_c = travelling(
        norm_gains, qk_gains[None, :], (w_query, w_key, w_value), (w_output.T, w_gate, w_up),
        (w_down.T,),
    )
    cols_a = w_query.shape[1] + w_key.shape[1] + w_value.shape[1] + EXTRA
    cols_b = w_output.shape[0] + w_gate.shape[1] + w_up.shape[1]
    cols_c = w_down.shape[0]

    even, odd, inner = row_table(n, shard)
    device = me ^ jnp.where(me & 1 == 0, jnp.asarray(even), jnp.asarray(odd))
    place = device * shard + inner
    qk_place = jnp.where(inner < qk_shard, device * qk_shard + inner, -1)
    padded_ids = jnp.concatenate([jnp.full((LONGEST + rows,), -1, jnp.int32), segment_ids])
    nearby = lax.dynamic_slice_in_dim(padded_ids, me * rows, 2 * rows + LONGEST)
    keys_segment = nearby[LONGEST:]
    seg_q = keys_segment[rows:, None]
    seg_k = jnp.stack(
        [keys_segment[b * BLOCK : b * BLOCK + REACH] for b in range(rows // BLOCK)]
    )[:, None, :]

    tokens_before = lax.ppermute(tokens, "seq", [(i, i + 1) for i in range(n - 1)])
    steps = len(far_bits(n)[0])
    a_c = to_first(travel_c, n)
    (own_b,) = pack(far_direct(travel_b, n), shard, cols_b, 1, n, after=(a_c,))
    a_b, b_b = to_first(own_b, n), to_second(own_b, n)
    pair_c, block_a = call(
        start_kernel,
        [
            shaped((2 * travel_c.shape[0], travel_c.shape[1]), bf16),
            shaped(travel_a.shape, bf16),
        ],
        [travel_c, a_c, travel_a],
        us=0.2,
        after=(own_b,),
    )
    for step in range(steps - 1):
        block_a, pair_c = stack(
            (block_a, far_step(block_a, n, step)), (pair_c, far_step(pair_c, n, step))
        )
    (own_a,) = pack([block_a, far_step(block_a, n, steps - 1)], shard, cols_a, 1, n)
    a_a, b_a = to_first(own_a, n), to_second(own_a, n)
    half_c = pack([pair_c, far_step(pair_c, n, steps - 1)], shard, cols_c, 2, n, after=(own_a,))
    first = (me % EIGHT == 0).astype(f32).reshape(1, 1)
    cosine, sine, order, qk_order, first = tables(
        nearby, rows, place, qk_place, width, first, after=(own_b,)
    )
    x, dy = permute(tokens_before, tokens, cotangent, order)
    a_b, own_b, *parts_b = hold_parts(
        a_b, own_b, after=(b_b, x, seg_q, seg_k, a_a, b_a, *half_c)
    )
    weights_a = [own_a, a_a, b_a, to_second(a_a, n)]
    weights_a = [*weights_a, *to_core(weights_a, n)]
    hidden, q_raw, k_raw, q, k, v, probs, o, gains, qk_gain = attend(
        x, weights_a, qk_order, cosine, sine, seg_q, seg_k, after=()
    )
    far_half = to_second(half_c[0], n)
    parts_b = [to_second(p, n) for p in parts_b]
    weights_b = [own_b, a_b, b_b, *parts_b]
    weights_b = [*weights_b, *to_core(weights_b, n)]
    a, middle, normed = join(o, weights_b, x, gains)
    half_c = [*half_c, *hold(far_half, after=(normed,))]
    weights_c = [*half_c, *to_core(half_c, n)]
    product, by_gate, by_up = feed(normed, weights_b, after=half_c[1:])
    mixed, low, gain3, *grad_d = turn(product, weights_c, middle, dy, gains, order)
    gate_low, up_low, *grad_g = feed_back(low, weights_c, by_gate, by_up, normed)
    sum_d = core_sum_by_far(grad_d[0], grad_d[1:], n, after=(gate_low,))
    sum_g = core_sum(grad_g[0], grad_g[1:], n, after=sum_d[:1])
    dx1, gain12, do, *grad_u = middle_back(
        gate_low, up_low, weights_b, middle, a, dy, gains, normed, o, after=sum_g[:1]
    )
    sum_g = near_sum_first(sum_g, n, after=(do,))
    dq_low, dkv_before, dkv_own, qk_grad = attend_back(
        probs, do, q, k, v, q_raw, k_raw, cosine, sine, qk_gain, after=sum_g[:1]
    )
    sum_g = near_sum_second(sum_g, n, after=(dq_low,))
    for step in reversed(range(1, steps)):
        sum_d = far_fold(sum_d, n, step, after=sum_g[:1], us=5)
    sum_u = core_sum(grad_u[0], grad_u[1:], n, after=sum_d[:1])
    dh_before, dh, *grad_a = project_back(
        [dq_low, dkv_before, dkv_own, qk_grad, hidden, x, qk_order, gain3, gain12],
        weights_a,
        after=sum_u[:1],
    )
    sum_a = core_sum(grad_a[0], grad_a[1:], n)
    before, own = input_back(dh_before, dh, x, gains, dx1, order, after=sum_a[:1])
    sum_u = near_sum_first(sum_u, n, after=(own,), us=4)
    sum_d = far_fold(sum_d, n, 0, after=sum_u[:1])
    sum_a = near_sum_first(sum_a, n, after=sum_d[:1])
    sum_g = far_sum_first(sum_g, n, after=sum_a[:1])
    sum_d = near_sum_first(sum_d, n, after=sum_g[:1])
    before, behind = to_device_before(before, n, first, after=sum_d[:1])
    sum_a = near_sum_far([sum_a, sum_u], n, 2, after=(before,))
    ff = grad_d[0].shape[1]
    sum_a = far_sum_first(sum_a, n)
    input_grad, token = join_halo(own, behind, after=sum_a[:1])
    sum_g, token = far_sum_last(sum_g, n, shard, ((0, ff),), after=(token,))
    sum_d, token = near_sum_last(sum_d, n, shard, (0, ff), after=(token,))
    sum_q, sum_k, sum_v, norm_sums, qk_sums, sum_u, sum_o, _ = far_sum_last(
        sum_a, n, shard, ((0, 1024, 1280, 1536, 1664), (0, ff, ff + 1024)),
        gains_at=1536, gain_shapes=(norm_gains.shape, (1, qk_shard)), after=(token,),
    )
    return (
        mixed,
        input_grad,
        sum_q,
        sum_k,
        sum_v,
        sum_o.T,
        sum_g,
        sum_u,
        sum_d.T,
        norm_sums,
        qk_sums.reshape(qk_shard),
    )


def solution(mesh):
    return jax.shard_map(
        on_device,
        mesh=mesh,
        in_specs=(
            P("seq", None),
            P(),
            P("seq", None),
            P("seq", None),
            P("seq", None),
            P(None, "seq"),
            P("seq", None),
            P("seq", None),
            P(None, "seq"),
            P(None, "seq"),
            P("seq"),
            P("seq", None),
        ),
        out_specs=(
            P("seq", None),
            P("seq", None),
            P("seq", None),
            P("seq", None),
            P("seq", None),
            P(None, "seq"),
            P("seq", None),
            P("seq", None),
            P(None, "seq"),
            P(None, "seq"),
            P("seq"),
        ),
        check_vma=False,
    )
```

```python
import functools

import jax
import jax.numpy as jnp
import numpy as np
from jax import lax
from jax.experimental import pallas as pl
from jax.experimental.pallas import tpu as pltpu
from jax.sharding import PartitionSpec as P

H = 4
HD = 256
WINDOW = 512
LONGEST = 2048
EXTRA = 128
EIGHT = 8
FF_CHUNK = 512
BLOCK = 128
REACH = BLOCK + WINDOW
MIB = 1024 * 1024

epsilon = 1e-06
bf16 = jnp.bfloat16
f32 = jnp.float32


def far_bits(n):
    bits = [1 << i for i in range(n.bit_length() - 1)]
    rest = [b for b in bits[1:] if b not in near_pair(n)]
    return rest, rest[::-1]


def far_slots(bits):
    slots = [0]
    for b in bits:
        slots = slots + [s | b for s in slots]
    return slots


def near_pair(n):
    return (2, 8) if n > 64 else (2, 4)


def to_partner(x, n, masks):
    return lax.ppermute(x, "seq", [(i, i ^ masks[i & 1]) for i in range(n)])


def row_table(n, shard):
    first, second = near_pair(n)
    main = whole_tiles(shard)
    count = n // 8
    inner = [(i, r) for i in range(count) for r in range(main)]
    inner += [(i, r) for i in range(count) for r in range(main, shard)]

    def offsets(a, b, bits):
        far = far_slots(bits)
        return [m ^ far[i] for m in (0, a, b, a | b) for i, _ in inner]

    even_bits, odd_bits = far_bits(n)
    even, odd = offsets(first, second, even_bits), offsets(second, first, odd_bits)
    return (
        np.array(even + [1 ^ m for m in odd], np.int32),
        np.array(odd + [1 ^ m for m in even], np.int32),
        np.array([r for _, r in inner] * 8, np.int32),
    )


def nn(left, right):
    return jnp.dot(left, right, preferred_element_type=f32)


def tn(left, right):
    return lax.dot_general(left, right, (((0,), (0,)), ((), ())), preferred_element_type=f32)


def nt(left, right):
    return lax.dot_general(left, right, (((1,), (1,)), ((), ())), preferred_element_type=f32)


def inverse_rms(values):
    return lax.rsqrt(jnp.mean(values * values, axis=-1, keepdims=True) + epsilon)


def rms_back(values, gain, grad):
    scale = inverse_rms(values)
    hat = values * scale
    inner = grad * gain
    mean = jnp.mean(inner * hat, axis=-1, keepdims=True)
    return scale * (inner - hat * mean), jnp.sum(grad * hat, axis=0, keepdims=True)


def rotate(values, cosine, sine):
    half = values.shape[-1] // 2
    a, b = values[:, :half], values[:, half:]
    return jnp.concatenate([a * cosine - b * sine, b * cosine + a * sine], axis=-1)


def rotate_back(values, cosine, sine):
    half = values.shape[-1] // 2
    a, b = values[:, :half], values[:, half:]
    return jnp.concatenate([a * cosine + b * sine, b * cosine - a * sine], axis=-1)


def call(kernel, outs, args, us, scratch=(), after=(), room=12, result=False):
    given, extra = len(args), len(after)

    def body(*refs):
        if result:
            *refs, token = refs
            token[...] = jnp.zeros_like(token)
        kernel(*refs[:given], *refs[given + extra :])

    if result:
        outs = [pltpu.HBM(o.shape, o.dtype) for o in outs] + [shaped((8, 128), f32)]
    return pl.pallas_call(
        body,
        in_specs=[pl.BlockSpec(memory_space=pltpu.VMEM)] * given
        + [pl.BlockSpec(memory_space=pl.ANY)] * extra,
        out_specs=[pl.BlockSpec(memory_space=pltpu.VMEM)] * len(outs),
        out_shape=outs,
        scratch_shapes=scratch,
        compiler_params=pltpu.CompilerParams(vmem_limit_bytes=room * MIB),
        cost_estimate=pl.CostEstimate(
            flops=int(us * 10**9), bytes_accessed=int(us * 10**6), transcendentals=0
        ),
    )(*args, *after)


def shaped(shape, dtype):
    return jax.ShapeDtypeStruct(shape, dtype)


def join_rows(parts, cols=slice(None)):
    return jnp.concatenate([p[:, cols] for p in parts], axis=0)


def whole_tiles(rows):
    return rows // 16 * 16


def padded(cols):
    return -(-cols // 512) * 512


def in_tiles(rows):
    return rows == 20


def travel_shape(rows, cols):
    return (16, padded(cols) * 5 // 4) if in_tiles(rows) else (rows, cols)


def to_tiles(values):
    rows, cols = values.shape
    if not in_tiles(rows):
        return values
    wide = padded(cols)
    if wide > cols:
        values = jnp.concatenate([values, jnp.zeros((rows, wide - cols), f32)], axis=1)
    quarter = wide // 4
    rest = [values[16:, k * quarter : (k + 1) * quarter] for k in range(4)]
    return jnp.concatenate([values[:16], jnp.concatenate(rest, axis=0)], axis=1)


def tile_kernel(counts, *refs):
    total = sum(counts) + 2
    given, outs = refs[:total], refs[total : total + len(counts)]
    held, sem = refs[total + len(counts) : -1], refs[-1]
    copies = [
        pltpu.make_async_copy(source, target, sem.at[i])
        for i, (source, target) in enumerate(zip(given, held))
    ]
    for copy in copies:
        copy.start()
    for copy in copies:
        copy.wait()
    *held, norm_gains, qk_gains = held
    shard = norm_gains.shape[1]
    rows = [
        jnp.concatenate([g[...].astype(f32), jnp.zeros((g.shape[0], EXTRA - g.shape[1]), f32)], axis=1)
        for g in (norm_gains, qk_gains)
    ]
    rows.append(jnp.zeros((EXTRA - 5, EXTRA), f32))
    extra = jnp.concatenate(rows, axis=0).T[:shard]
    for group, (count, out) in enumerate(zip(counts, outs)):
        parts = [p[...].astype(f32) for p in held[:count]]
        held = held[count:]
        if group == 0:
            parts.append(extra)
        out[...] = to_tiles(jnp.concatenate(parts, axis=1)).astype(bf16)


def travelling(norm_gains, qk_gains, *groups):
    counts = [len(g) for g in groups]
    given = [w for g in groups for w in g] + [norm_gains, qk_gains]
    outs = []
    for i, g in enumerate(groups):
        cols = sum(w.shape[1] for w in g) + (EXTRA if i == 0 else 0)
        outs.append(shaped(travel_shape(g[0].shape[0], cols), bf16))
    return pl.pallas_call(
        functools.partial(tile_kernel, counts),
        in_specs=[pl.BlockSpec(memory_space=pltpu.HBM)] * len(given),
        out_specs=[pl.BlockSpec(memory_space=pltpu.VMEM)] * len(outs),
        out_shape=outs,
        scratch_shapes=[pltpu.VMEM(w.shape, bf16) for w in given]
        + [pltpu.SemaphoreType.DMA((len(given),))],
        compiler_params=pltpu.CompilerParams(vmem_limit_bytes=8 * MIB),
    )(*[pltpu.with_memory_space_constraint(w, pltpu.HBM) for w in given])


def stack_kernel(*refs):
    count = len(refs) // 3
    for i in range(count):
        a, b, out = refs[2 * i], refs[2 * i + 1], refs[2 * count + i]
        rows = a.shape[0]
        if rows % 16 == 0:
            out[:rows] = a[...]
            out[rows:] = b[...]
        else:
            both = [a[...].astype(f32), b[...].astype(f32)]
            out[...] = jnp.concatenate(both, axis=0).astype(bf16)


def stack(*pairs, after=()):
    outs = [shaped((2 * a.shape[0], a.shape[1]), bf16) for a, _ in pairs]
    return call(stack_kernel, outs, [x for pair in pairs for x in pair], us=0.5, after=after)


def pack_kernel(pieces, blocks, out):
    count = len(pieces)
    share, cols = out.shape[0] // blocks, out.shape[1]
    rows = share // count
    main = whole_tiles(rows)
    height, wide = travel_shape(rows, cols)
    quarter = padded(cols) // 4
    for block in range(blocks):
        at = block * share
        starts = [(ref, begin + block * height) for ref, begin in pieces]
        if main:
            for i, (ref, begin) in enumerate(starts):
                out[at + i * main : at + (i + 1) * main] = ref[begin : begin + main, :cols]
        at = at + main * count
        if in_tiles(rows):
            rest = [ref[begin : begin + 16, 4 * quarter :].astype(f32) for ref, begin in starts]
            for k in range(4):
                end = min((k + 1) * quarter, cols)
                part = jnp.concatenate([r[4 * k : 4 * k + 4] for r in rest], axis=0)
                out[at : at + 4 * count, k * quarter : end] = part[:, : end - k * quarter].astype(
                    bf16
                )
        elif rows > main:
            rest = [
                ref[...].astype(f32)[begin + main : begin + rows] for ref, begin in starts
            ]
            out[at : at + (rows - main) * count] = jnp.concatenate(rest, axis=0).astype(bf16)


def pack(arrays, rows, cols, blocks, n, parts=1, after=()):
    count = n // 8
    height = travel_shape(rows, cols)[0] * blocks
    held = count // len(arrays)
    total = rows * count * blocks

    def kernel(*refs):
        given = refs[: len(arrays)]
        pieces = [(ref, h * height) for ref in given for h in range(held)]
        if parts == 1:
            pack_kernel(pieces, blocks, refs[-1])
        else:
            for block, out in enumerate(refs[len(arrays) :]):
                shift = block * height // blocks
                pack_kernel([(ref, at + shift) for ref, at in pieces], 1, out)

    outs = [shaped((total // parts, cols), bf16)] * parts
    return call(kernel, outs, arrays, us=1.5, after=after)


def far_step(block, n, step):
    even, odd = far_bits(n)
    return to_partner(block, n, (even[step], odd[step]))


def far_direct(block, n):
    even, odd = far_bits(n)
    slots = zip(far_slots(even)[1:], far_slots(odd)[1:])
    return [block] + [to_partner(block, n, masks) for masks in slots]


def start_kernel(a, b, one, out, one_out):
    stack_kernel(a, b, out)
    one_out[...] = one[...]


def hold_kernel(*refs):
    half = len(refs) // 2
    for value, out in zip(refs[:half], refs[half:]):
        out[...] = value[...]


def hold(*values, after):
    return call(hold_kernel, [shaped(v.shape, v.dtype) for v in values], values, 0.2, after=after)


def hold_parts_kernel(one, two, one_out, two_out, upper, lower):
    one_out[...] = one[...]
    two_out[...] = two[...]
    rows = upper.shape[0]
    upper[...] = one[:rows]
    lower[...] = one[rows:]


def hold_parts(one, two, after):
    rows, cols = one.shape
    upper = rows // 32 * 16 + (16 if rows % 32 else 0)
    outs = [shaped(one.shape, bf16), shaped(two.shape, bf16)]
    outs += [shaped((upper, cols), bf16), shaped((rows - upper, cols), bf16)]
    return call(hold_parts_kernel, outs, [one, two], us=0.2, after=after)


def far_gather(blocks, n, joins):
    steps = len(far_bits(n)[0])
    for k in range(steps - 1):
        got = [far_step(b, n, k) for b in blocks]
        blocks = stack(*zip(blocks, got), after=joins[k] if k < len(joins) else ())
    return [(b, far_step(b, n, steps - 1)) for b in blocks]


def to_first(x, n):
    first, second = near_pair(n)
    return to_partner(x, n, (first, second))


def to_second(x, n):
    first, second = near_pair(n)
    return to_partner(x, n, (second, first))


def near_pieces(own, n, direct=False):
    first, second = near_pair(n)
    a, b = to_first(own, n), to_second(own, n)
    return [own, a, b, to_partner(own, n, (first | second,) * 2) if direct else to_second(a, n)]


def to_core(pieces, n):
    return [to_partner(p, n, (1, 1)) for p in pieces]


def fold_kernel(count, *refs):
    given, outs = refs[:count], refs[count:]
    mine, got = given[0], given[1:]
    rows = outs[0].shape[0]
    height = got[0].shape[0]
    if rows % 16 == 0 and height % rows == 0:
        per = height // rows
        for i, out in enumerate(outs):
            other = got[i // per][(i % per) * rows : (i % per + 1) * rows]
            part = mine[i * rows : (i + 1) * rows]
            out[...] = (part.astype(f32) + other.astype(f32)).astype(bf16)
    else:
        total = mine[...].astype(f32)
        total = total + jnp.concatenate([g[...].astype(f32) for g in got], axis=0)
        for i, out in enumerate(outs):
            out[...] = total[i * rows : (i + 1) * rows].astype(bf16)


def fold(mine, got, after=(), us=0.5):
    rows, cols = mine.shape
    outs = [shaped((rows // 2, cols), bf16)] * 2
    kernel = functools.partial(fold_kernel, 1 + len(got))
    return call(kernel, outs, [mine, *got], us=us, after=after)


def wide_fold_kernel(mine, *refs):
    got, (keep, send) = refs[:-2], refs[-2:]
    rows = got[0].shape[0]
    per = keep.shape[0] // rows
    for i, other in enumerate(got):
        out = keep if i < per else send
        at = (i % per) * rows
        part = mine[i * rows : (i + 1) * rows].astype(f32)
        out[at : at + rows] = (part + other[...].astype(f32)).astype(bf16)


def core_sum(top, sends, n, after=()):
    rows, cols = top.shape
    outs = [shaped((rows // 2, cols), bf16)] * 2
    return call(wide_fold_kernel, outs, [top, *to_core(sends, n)], us=0.7, after=after)


def core_sum_by_far(top, sends, n, after=()):
    rows, cols = top.shape
    count, blocks = n // 8, 4
    share = rows // blocks
    shard = share // count
    main = whole_tiles(shard)
    rest, done = shard - main, main * count
    height, wide = travel_shape(shard, cols)

    def kernel(mine, *refs):
        got, (keep, send) = refs[:-2], refs[-2:]
        per = blocks // len(got)
        tiles = []
        for block in range(blocks):
            other = got[block // per][(block % per) * share : (block % per + 1) * share]
            total = mine[block * share : (block + 1) * share].astype(f32) + other.astype(f32)
            for i in range(count):
                parts = []
                if main:
                    parts.append(total[i * main : (i + 1) * main])
                if rest:
                    parts.append(total[done + i * rest : done + (i + 1) * rest])
                tiles.append((i, block, to_tiles(jnp.concatenate(parts, axis=0))))
        tiles = [t for _, _, t in sorted(tiles, key=lambda item: item[:2])]
        half = len(tiles) // 2
        keep[...] = jnp.concatenate(tiles[:half], axis=0).astype(bf16)
        send[...] = jnp.concatenate(tiles[half:], axis=0).astype(bf16)

    outs = [shaped((count // 2 * blocks * height, wide), bf16)] * 2
    return call(kernel, outs, [top, *to_core(sends, n)], us=1.5, after=after)


def far_fold(halves, n, step, after=(), us=0.5):
    keep, send = halves
    return fold(keep, [far_step(send, n, step)], after, us)


def near_sum_last(halves, n, shard, cuts, after=()):
    keep, send = halves
    outs = [shaped((shard, e - b), f32) for b, e in zip(cuts[:-1], cuts[1:])]
    return call(
        functools.partial(far_sum_kernel, (cuts,), None), outs, [keep, to_first(send, n)], us=1,
        after=after, result=True,
    )


def near_sum_first(halves, n, after=(), us=0.5):
    keep, send = halves
    return fold(keep, [to_second(send, n)], after, us)


def fold_both_kernel(*refs):
    given, (keep, send) = refs[:4], refs[4:]
    rows, cols = keep.shape
    cols = cols // 2
    for i in range(2):
        mine, got = given[2 * i : 2 * i + 2]
        for j, out in enumerate((keep, send)):
            part = slice(j * rows, (j + 1) * rows)
            out[:, i * cols : (i + 1) * cols] = (
                mine[part].astype(f32) + got[part].astype(f32)
            ).astype(bf16)


def near_sum_first_both(one, two, n, after=()):
    args = [x for keep, send in (one, two) for x in (keep, to_second(send, n))]
    rows, cols = one[0].shape
    outs = [shaped((rows // 2, 2 * cols), bf16)] * 2
    return call(fold_both_kernel, outs, args, us=5, after=after)


def split_kernel(count, mine, got, keep, send):
    total = mine[...].astype(f32) + got[...].astype(f32)
    rows = total.shape[0] // count
    main = whole_tiles(rows)
    rest, done = rows - main, main * count
    slots = []
    for i in range(count):
        parts = []
        if main:
            parts.append(total[i * main : (i + 1) * main])
        if rest:
            parts.append(total[done + i * rest : done + (i + 1) * rest])
        slots.append(to_tiles(jnp.concatenate(parts, axis=0)))
    keep[...] = jnp.concatenate(slots[: count // 2], axis=0).astype(bf16)
    send[...] = jnp.concatenate(slots[count // 2 :], axis=0).astype(bf16)


def near_sum_second(halves, n, after=()):
    keep, send = halves
    rows, cols = keep.shape
    count = n // 8
    height, wide = travel_shape(rows // count, cols)
    outs = [shaped((count // 2 * height, wide), bf16)] * 2
    return call(
        functools.partial(split_kernel, count), outs, [keep, to_first(send, n)], us=1, after=after
    )


def slots_kernel(groups, count, *refs):
    outs = refs[2 * groups :]
    slots = [[] for _ in range(count)]
    for g in range(groups):
        total = refs[2 * g][...].astype(f32) + refs[2 * g + 1][...].astype(f32)
        rows = total.shape[0] // count
        main = whole_tiles(rows)
        rest, done = rows - main, main * count
        for i in range(count):
            parts = []
            if main:
                parts.append(total[i * main : (i + 1) * main])
            if rest:
                parts.append(total[done + i * rest : done + (i + 1) * rest])
            slots[i].append(to_tiles(jnp.concatenate(parts, axis=0)))
    per = count // len(outs)
    for i, parts in enumerate(slots):
        values = jnp.concatenate(parts, axis=1).astype(bf16)
        height = values.shape[0]
        if per == 1:
            outs[i][...] = values
        elif height % 16 == 0:
            outs[i // per][i % per * height : (i % per + 1) * height] = values
    if per > 1 and height % 16 != 0:
        for j, out in enumerate(outs):
            values = [jnp.concatenate(p, axis=1) for p in slots[j * per : (j + 1) * per]]
            out[...] = jnp.concatenate(values, axis=0).astype(bf16)


def near_sum_far(groups, n, parts, after=()):
    count = n // 8
    args, wide = [], 0
    for keep, send in groups:
        args += [keep, to_first(send, n)]
        height, cols = travel_shape(keep.shape[0] // count, keep.shape[1])
        wide += cols
    outs = [shaped((height * count // parts, wide), bf16)] * parts
    kernel = functools.partial(slots_kernel, len(groups), count)
    return call(kernel, outs, args, us=1, after=after)


def far_sum_first(halves, n, after=()):
    keep, send = halves
    for k in reversed(range(1, len(far_bits(n)[0]))):
        keep, send = fold(keep, [far_step(send, n, k)], after)
        after = ()
    return keep, send


def far_sum_kernel(groups, gains_at, *refs):
    count = sum(len(cuts) - 1 for cuts in groups) + (gains_at is not None)
    given, outs = refs[:-count], refs[-count:]
    total = given[0][...].astype(f32)
    for got in given[1:]:
        total = total + got[...].astype(f32)
    rows = outs[0].shape[0]
    begin_at = 0
    for number, cuts in enumerate(groups):
        wide = padded(cuts[-1]) if in_tiles(rows) else cuts[-1]
        part = total[:, begin_at : begin_at + wide]
        if in_tiles(rows):
            quarter = wide // 4
            rest = total[:, begin_at + wide : begin_at + wide + quarter]
            rest = [rest[4 * k : 4 * k + 4] for k in range(4)]
            part = jnp.concatenate([part, jnp.concatenate(rest, axis=1)], axis=0)
            begin_at += quarter
        begin_at += wide
        for begin, end in zip(cuts[:-1], cuts[1:]):
            values = part[:, begin:end]
            if number == 0 and begin == gains_at:
                values = jnp.concatenate([values, jnp.zeros((EXTRA - rows, EXTRA), f32)], axis=0).T
                norms, qk, *outs = outs
                norms[...] = values[: norms.shape[0], :rows]
                qk[...] = values[norms.shape[0] : norms.shape[0] + 1, : qk.shape[1]]
            else:
                outs[0][...] = values
                outs = outs[1:]


def result_shapes(shard, groups, gains_at, gain_shapes):
    outs = []
    for number, cuts in enumerate(groups):
        for begin, end in zip(cuts[:-1], cuts[1:]):
            if number == 0 and begin == gains_at:
                outs += [shaped(shape, f32) for shape in gain_shapes]
            else:
                outs.append(shaped((shard, end - begin), f32))
    return outs


def far_sum_last(halves, n, shard, groups, gains_at=None, gain_shapes=(), after=()):
    keep, send = halves
    outs = result_shapes(shard, groups, gains_at, gain_shapes)
    kernel = functools.partial(far_sum_kernel, groups, gains_at)
    args = [keep, far_step(send, n, 0)]
    return call(kernel, outs, args, us=1, after=after, result=True)


def table_kernel(near, near_col, freqs, place, qk_place, first, cosine, sine, order, qk_order, first_out):
    count = cosine.shape[0]
    ahead = near.shape[1] - count
    steps = freqs[...]
    for c in range(count // 256):
        reach = slice(c * 256, c * 256 + ahead + 256)
        here = near_col[ahead + c * 256 : ahead + (c + 1) * 256]
        i = lax.broadcasted_iota(jnp.int32, (256, ahead + 256), 0) + ahead
        j = lax.broadcasted_iota(jnp.int32, (256, ahead + 256), 1)
        same = (here == near[:, reach]) & (j < i)
        position = jnp.sum(same.astype(f32), axis=1, keepdims=True)
        angles = position * steps
        cosine[c * 256 : (c + 1) * 256] = jnp.cos(angles)
        sine[c * 256 : (c + 1) * 256] = jnp.sin(angles)
    i = lax.broadcasted_iota(jnp.int32, order.shape, 0)
    order[...] = (i == place[...]).astype(f32).astype(bf16)
    j = lax.broadcasted_iota(jnp.int32, qk_order.shape, 1)
    qk_order[...] = (qk_place[...] == j).astype(f32).astype(bf16)
    first_out[...] = jnp.broadcast_to(first[...], first_out.shape)


def tables(near, rows, place, qk_place, width, first, after=()):
    freqs = np.float32(10000.0) ** (-2.0 * np.arange(HD // 2, dtype=np.float32) / np.float32(HD))
    args = [
        near[None, :], near[:, None], jnp.asarray(freqs)[None, :], place[None, :], qk_place[:, None],
        first,
    ]
    outs = [
        shaped((2 * rows, HD // 2), f32), shaped((2 * rows, HD // 2), f32),
        shaped((width, width), bf16), shaped((width, 2 * HD), bf16), shaped((8, 128), f32),
    ]
    return call(table_kernel, outs, args, us=3, after=after)


def permute_kernel(tokens_before, tokens, cotangent, order, x, dy):
    table = order[...]
    rows = tokens.shape[0]
    x[:rows] = nn(tokens_before[...], table).astype(bf16)
    x[rows:] = nn(tokens[...], table).astype(bf16)
    dy[...] = nn(cotangent[...], table).astype(bf16)


def permute(tokens_before, tokens, cotangent, order, after=()):
    rows, width = tokens.shape
    outs = [shaped((2 * rows, width), bf16), shaped((rows, width), bf16)]
    args = [tokens_before, tokens, cotangent, order]
    return call(permute_kernel, outs, args, us=2, after=after)


def attend_kernel(x, qk_order, cosine, sine, seg_q, seg_k, *refs):
    pieces = refs[:-10]
    hidden, q_raw, k_raw, q_out, k_out, v_out, probs, o, gains, qk_gain = refs[-10:]
    rows = q_raw.shape[0]
    w_q = join_rows(pieces, slice(0, 1024))
    w_kv = join_rows(pieces, slice(1024, 1536))
    gain_rows = join_rows(pieces, slice(1536, 1664)).astype(f32).T[:8]
    gains[...] = gain_rows
    gain_qk = nn(gain_rows.astype(bf16), qk_order[...])
    qk_gain[...] = gain_qk
    gain_q, gain_k = gain_qk[4:5, :HD], gain_qk[4:5, HD:]
    for c in range(2 * rows // 256):
        part = pl.ds(c * 256, 256)
        xs = x[part].astype(f32)
        hs = (xs * inverse_rms(xs) * gain_rows[0:1]).astype(bf16)
        hidden[part] = hs
        cs, sn = cosine[part], sine[part]
        kv = nn(hs, w_kv)
        raw = kv[:, :HD]
        k_raw[part] = raw
        k_out[part] = rotate(raw * inverse_rms(raw) * gain_k, cs, sn).astype(bf16)
        v_out[part] = kv[:, HD:].astype(bf16)
        if c * 256 >= rows:
            own = pl.ds(c * 256 - rows, 256)
            qs = nn(hs, w_q)
            q_raw[own] = qs
            for h in range(H):
                raw = qs[:, h * HD : (h + 1) * HD]
                q_out[own, h * HD : (h + 1) * HD] = rotate(
                    raw * inverse_rms(raw) * gain_q, cs, sn
                ).astype(bf16)
    for b in range(rows // BLOCK):
        mine = pl.ds(b * BLOCK, BLOCK)
        reach = pl.ds(b * BLOCK, REACH)
        q_rows = q_out[mine] * bf16(1.0 / 16.0)
        q_stack = jnp.concatenate([q_rows[:, h * HD : (h + 1) * HD] for h in range(H)], axis=0)
        scores = nt(q_stack, k_out[reach])
        i = lax.broadcasted_iota(jnp.int32, (BLOCK, REACH), 0)
        j = lax.broadcasted_iota(jnp.int32, (BLOCK, REACH), 1)
        allowed = (j > i) & (j <= i + WINDOW) & (seg_q[mine] == seg_k[b])
        allowed = jnp.concatenate([allowed.astype(f32)] * H, axis=0)
        weights = jnp.exp(scores) * allowed
        total = jnp.sum(weights, axis=-1, keepdims=True)
        p = (weights * (1.0 / total)).astype(bf16)
        probs[b] = p
        out = nn(p, v_out[reach])
        for h in range(H):
            o[mine, h * HD : (h + 1) * HD] = out[h * BLOCK : (h + 1) * BLOCK].astype(bf16)


def attend(x, pieces, qk_order, cosine, sine, seg_q, seg_k, after):
    rows = x.shape[0] // 2
    width = x.shape[1]
    return call(
        attend_kernel,
        [
            shaped((2 * rows, width), bf16),
            shaped((rows, H * HD), f32),
            shaped((2 * rows, HD), f32),
            shaped((rows, H * HD), bf16),
            shaped((2 * rows, HD), bf16),
            shaped((2 * rows, HD), bf16),
            shaped((rows // BLOCK, H * BLOCK, REACH), bf16),
            shaped((rows, H * HD), bf16),
            shaped((8, width), f32),
            shaped((8, 2 * HD), f32),
        ],
        [x, qk_order, cosine, sine, seg_q, seg_k, *pieces],
        us=12,
        after=after,
    )


def gelu_parts(g):
    c0, c1 = 0.7978845608028654, 0.044715
    square = g * g
    t = jnp.tanh(g * (c0 + (c0 * c1) * square))
    half = 0.5 + 0.5 * t
    value = g * half
    slope = half + value * ((1.0 - t) * (c0 + (3.0 * c0 * c1) * square))
    return value, slope


def join_kernel(o, x, gains, *refs):
    pieces, (a_out, middle, normed) = refs[:-3], refs[-3:]
    rows = o.shape[0]
    w_o = join_rows(pieces, slice(0, H * HD))
    for c in range(rows // 256):
        part = pl.ds(c * 256, 256)
        a = nt(o[part], w_o)
        a_out[part] = a
        x1 = x[rows + c * 256 : rows + (c + 1) * 256].astype(f32) + a * inverse_rms(a) * gains[1:2]
        middle[part] = x1
        normed[part] = (x1 * inverse_rms(x1) * gains[2:3]).astype(bf16)


def join(o, pieces, x, gains):
    rows, width = o.shape[0], x.shape[1]
    outs = [shaped((rows, width), f32), shaped((rows, width), f32), shaped((rows, width), bf16)]
    return call(join_kernel, outs, [o, x, gains, *pieces], us=2)


def feed_kernel(normed, *refs):
    pieces, (product, by_gate, by_up) = refs[:-3], refs[-3:]
    rows, ff = product.shape
    for j in range(ff // FF_CHUNK):
        cols = slice(j * FF_CHUNK, (j + 1) * FF_CHUNK)
        w_g = join_rows(pieces, slice(H * HD + cols.start, H * HD + cols.stop))
        w_u = join_rows(pieces, slice(H * HD + ff + cols.start, H * HD + ff + cols.stop))
        for c in range(rows // 256):
            part = pl.ds(c * 256, 256)
            h2 = normed[part]
            g = nn(h2, w_g)
            u = nn(h2, w_u)
            value, slope = gelu_parts(g)
            product[part, cols] = (value * u).astype(bf16)
            by_gate[part, cols] = (slope * u).astype(bf16)
            by_up[part, cols] = value.astype(bf16)


def feed(normed, pieces, after=()):
    rows = normed.shape[0]
    ff = (pieces[0].shape[1] - H * HD) // 2
    outs = [shaped((rows, ff), bf16)] * 3
    return call(feed_kernel, outs, [normed, *pieces], us=5, after=after)


def put_grad(grads, cols, values):
    top, *sends = grads
    half = top.shape[0]
    top[:, cols] = values[:half]
    part = half // len(sends)
    for i, send in enumerate(sends):
        send[:, cols] = values[half + i * part : half + (i + 1) * part]


def grad_shapes(width, cols):
    return [shaped((width // 2, cols), bf16)] + [shaped((width // 4, cols), bf16)] * 2


def turn_kernel(product, middle, dy, gains, *refs):
    pieces, (y_low, low, gain_grad, *grads) = refs[:-6], refs[-6:]
    ff = product.shape[1]
    w_d = join_rows(pieces)
    total = jnp.zeros((1, dy.shape[1]), f32)
    for c in range(dy.shape[0] // 256):
        part = pl.ds(c * 256, 256)
        f = nt(product[part], w_d)
        grad = dy[part].astype(f32)
        y = middle[part] + f * inverse_rms(f) * gains[3:4]
        y_low[part] = y.astype(bf16)
        df, dgain = rms_back(f, gains[3:4], grad)
        low[part] = df.astype(bf16)
        total = total + dgain
    gain_grad[...] = jnp.broadcast_to(total, gain_grad.shape)
    for j in range(ff // FF_CHUNK):
        cols = slice(j * FF_CHUNK, (j + 1) * FF_CHUNK)
        grad = tn(low[...], product[:, cols]).astype(bf16)
        put_grad(grads, cols, grad)


def turn(product, pieces, middle, dy, gains):
    rows, width = middle.shape
    return call(
        turn_kernel,
        [
            shaped((rows, width), bf16),
            shaped((rows, width), bf16),
            shaped((8, width), f32),
            *grad_shapes(width, product.shape[1]),
        ],
        [product, middle, dy, gains, *pieces],
        us=6,
    )


def feed_back_kernel(low, by_gate, by_up, normed, *refs):
    pieces, (gate_low, up_low, *grads) = refs[:-5], refs[-5:]
    rows, ff = gate_low.shape
    for j in range(ff // FF_CHUNK):
        cols = slice(j * FF_CHUNK, (j + 1) * FF_CHUNK)
        w_d = join_rows(pieces, cols)
        for c in range(rows // 256):
            part = pl.ds(c * 256, 256)
            dm = nn(low[part], w_d)
            gate_low[part, cols] = (dm * by_gate[part, cols].astype(f32)).astype(bf16)
            up_low[part, cols] = (dm * by_up[part, cols].astype(f32)).astype(bf16)
        put_grad(grads, cols, tn(normed[...], gate_low[:, cols]).astype(bf16))


def feed_back(low, pieces, by_gate, by_up, normed):
    rows, width = low.shape
    ff = by_gate.shape[1]
    return call(
        feed_back_kernel,
        [shaped((rows, ff), bf16)] * 2 + grad_shapes(width, ff),
        [low, by_gate, by_up, normed, *pieces],
        us=4,
    )


def middle_back_kernel(gate_low, up_low, middle, a, dy, gains, normed, o, *refs):
    pieces, (dx1, gain_grad, do, *grads) = refs[:-6], refs[-6:]
    rows, ff = gate_low.shape
    w_g = join_rows(pieces, slice(H * HD, H * HD + ff))
    w_u = join_rows(pieces, slice(H * HD + ff, H * HD + 2 * ff))
    normed_grad = nt(gate_low[...], w_g) + nt(up_low[...], w_u)
    for j in range(ff // FF_CHUNK):
        cols = slice(j * FF_CHUNK, (j + 1) * FF_CHUNK)
        put_grad(grads, cols, tn(normed[...], up_low[:, cols]).astype(bf16))
    sum1 = jnp.zeros((1, dy.shape[1]), f32)
    sum2 = jnp.zeros((1, dy.shape[1]), f32)
    lows = []
    for c in range(rows // 256):
        part = slice(c * 256, (c + 1) * 256)
        back, dgain2 = rms_back(middle[part], gains[2:3], normed_grad[part])
        dx = dy[part].astype(f32) + back
        dx1[part] = dx
        da, dgain1 = rms_back(a[part], gains[1:2], dx)
        lows.append(da.astype(bf16))
        sum1, sum2 = sum1 + dgain1, sum2 + dgain2
    gain_grad[...] = jnp.concatenate([sum1, sum2, jnp.zeros((6, dy.shape[1]), f32)], axis=0)
    low = jnp.concatenate(lows, axis=0)
    do[...] = nn(low, join_rows(pieces, slice(0, H * HD))).astype(bf16)
    put_grad(grads, slice(ff, ff + H * HD), tn(low, o[...]).astype(bf16))


def middle_back(gate_low, up_low, pieces, middle, a, dy, gains, normed, o, after):
    rows, width = middle.shape
    return call(
        middle_back_kernel,
        [
            shaped((rows, width), f32),
            shaped((8, width), f32),
            shaped((rows, H * HD), bf16),
            *grad_shapes(width, gate_low.shape[1] + H * HD),
        ],
        [gate_low, up_low, middle, a, dy, gains, normed, o, *pieces],
        us=14,
        after=after,
        room=24,
    )


def attend_back_kernel(
    probs, do, q, k, v, q_raw, k_raw, cosine, sine, qk_gain, dq_low, dkv_before, dkv_own, qk_grad, dk, dv
):
    rows = q_raw.shape[0]
    dk[...] = jnp.zeros_like(dk)
    dv[...] = jnp.zeros_like(dv)
    gain_q, gain_k = qk_gain[4:5, :HD], qk_gain[4:5, HD:]
    sum_q = jnp.zeros((1, HD), f32)

    def stack_heads(values):
        return jnp.concatenate([values[:, h * HD : (h + 1) * HD] for h in range(H)], axis=0)

    def probs_grad(b):
        do_stack = stack_heads(do[pl.ds(b * BLOCK, BLOCK)])
        return do_stack, nt(do_stack, v[pl.ds(b * BLOCK, REACH)])

    blocks = rows // BLOCK
    ahead = probs_grad(0)
    for b in range(blocks):
        do_stack, dp = ahead
        if b + 1 < blocks:
            ahead = probs_grad(b + 1)
        mine = pl.ds(b * BLOCK, BLOCK)
        reach = pl.ds(b * BLOCK, REACH)
        p_low = probs[b]
        p = p_low.astype(f32)
        dv[reach] += tn(p_low, do_stack)
        t = p * dp
        ds = (t - p * jnp.sum(t, axis=-1, keepdims=True)).astype(bf16)
        dk[reach] += tn(ds, stack_heads(q[mine]))
        dq = nn(ds, k[reach]) * (1.0 / 16.0)
        own = pl.ds(rows + b * BLOCK, BLOCK)
        cs, sn = cosine[own], sine[own]
        for h in range(H):
            grad = rotate_back(dq[h * BLOCK : (h + 1) * BLOCK], cs, sn)
            back, dgain = rms_back(q_raw[mine, h * HD : (h + 1) * HD], gain_q, grad)
            dq_low[mine, h * HD : (h + 1) * HD] = back.astype(bf16)
            sum_q = sum_q + dgain
    sum_k = jnp.zeros((1, HD), f32)
    for c in range(2 * rows // 256):
        part = pl.ds(c * 256, 256)
        grad = rotate_back(dk[part] * (1.0 / 16.0), cosine[part], sine[part])
        back, dgain = rms_back(k_raw[part], gain_k, grad)
        out, at = (dkv_before, c * 256) if c * 256 < rows else (dkv_own, c * 256 - rows)
        out[at : at + 256, :HD] = back.astype(bf16)
        out[at : at + 256, HD:] = dv[part].astype(bf16)
        sum_k = sum_k + dgain
    qk_grad[...] = jnp.broadcast_to(jnp.concatenate([sum_q, sum_k], axis=1), qk_grad.shape)


def attend_back(probs, do, q, k, v, q_raw, k_raw, cosine, sine, qk_gain, after):
    rows = q.shape[0]
    return call(
        attend_back_kernel,
        [
            shaped((rows, H * HD), bf16), shaped((rows, 2 * HD), bf16),
            shaped((rows, 2 * HD), bf16), shaped((8, 2 * HD), f32),
        ],
        [probs, do, q, k, v, q_raw, k_raw, cosine, sine, qk_gain],
        us=0.3,
        scratch=[pltpu.VMEM((2 * rows, HD), f32), pltpu.VMEM((2 * rows, HD), f32)],
        after=after,
        room=24,
    )


def project_back_kernel(
    dq_low, dkv_before, dkv_own, qk_grad, hidden, x, qk_order, gain3, gain12, *refs
):
    pieces, (dh_before, dh, *grads) = refs[:-5], refs[-5:]
    rows = dq_low.shape[0]
    put_grad(grads, slice(0, 1024), tn(hidden[rows:], dq_low[...]).astype(bf16))
    grad = tn(hidden[:rows], dkv_before[...]) + tn(hidden[rows:], dkv_own[...])
    put_grad(grads, slice(1024, 1536), grad.astype(bf16))
    w_q = join_rows(pieces, slice(0, 1024))
    w_kv = join_rows(pieces, slice(1024, 1536))
    sum0 = jnp.zeros((1, x.shape[1]), f32)
    for c in range(rows // 256):
        part = pl.ds(c * 256, 256)
        before = x[part].astype(f32)
        grad = nt(dkv_before[part], w_kv)
        dh_before[part] = grad
        sum0 = sum0 + jnp.sum(grad * (before * inverse_rms(before)), axis=0, keepdims=True)
        own = x[rows + c * 256 : rows + (c + 1) * 256].astype(f32)
        grad = nt(dkv_own[part], w_kv) + nt(dq_low[part], w_q)
        dh[part] = grad
        sum0 = sum0 + jnp.sum(grad * (own * inverse_rms(own)), axis=0, keepdims=True)
    qk_spread = nt(qk_grad[...].astype(bf16), qk_order[...])
    rows_of = jnp.concatenate(
        [
            sum0, gain12[0:1], gain12[1:2], gain3[0:1], qk_spread[0:1],
            jnp.zeros((EXTRA - 5, x.shape[1]), f32),
        ],
        axis=0,
    )
    put_grad(grads, slice(1536, 1664), rows_of.T.astype(bf16))


def project_back(args, pieces, after):
    rows, width = args[0].shape[0], args[5].shape[1]
    return call(
        project_back_kernel,
        [shaped((rows, width), f32)] * 2 + grad_shapes(width, pieces[0].shape[1]),
        [*args, *pieces],
        us=8,
        after=after,
    )


def input_back_kernel(dh_before, dh, x, gains, dx1, order, y_low, before, own, mixed):
    rows = dx1.shape[0]
    table = order[...]
    for c in range(rows // 256):
        part = pl.ds(c * 256, 256)
        back, _ = rms_back(x[part].astype(f32), gains[0:1], dh_before[part])
        before[part] = nt(back.astype(bf16), table).astype(bf16)
        mixed[part] = nt(y_low[part], table).astype(bf16)
        mine = x[rows + c * 256 : rows + (c + 1) * 256].astype(f32)
        back, _ = rms_back(mine, gains[0:1], dh[part])
        rest = back + dx1[part]
        total = jnp.zeros_like(rest)
        for _ in range(3):
            piece = rest.astype(bf16)
            rest = rest - piece.astype(f32)
            total = total + nt(piece, table)
        own[part] = total


def input_back(dh_before, dh, x, gains, dx1, order, y_low, after=()):
    outs = [shaped(dx1.shape, bf16), shaped(dx1.shape, f32), shaped(dx1.shape, bf16)]
    args = [dh_before, dh, x, gains, dx1, order, y_low]
    return call(input_back_kernel, outs, args, us=0.3, after=after)


def select_kernel(first, own, other, out):
    pick = first[:1, :1] > 0.5
    out[...] = jnp.where(pick, other[...].astype(f32), own[...].astype(f32)).astype(bf16)


def to_device_before(x, n, first, after=()):
    hop = lax.ppermute(x, "seq", [(i + EIGHT, i) for i in range(0, n - EIGHT, EIGHT)])
    (out,) = call(select_kernel, [shaped(x.shape, bf16)], [first, x, hop], us=0.3, after=after)
    pairs = [(i, i - 1) for i in range(n) if i % EIGHT]
    pairs += [(i, i + EIGHT - 1) for i in range(0, n - EIGHT, EIGHT)]
    return out, lax.ppermute(out, "seq", pairs)


def join_halo_kernel(own, behind, out):
    out[...] = own[...] + behind[...].astype(f32)


def join_halo(own, behind, after=()):
    outs = [shaped(own.shape, f32)]
    return call(join_halo_kernel, outs, [own, behind], us=0.3, after=after, result=True)


def on_device(
    tokens,
    segment_ids,
    w_query,
    w_key,
    w_value,
    w_output,
    w_gate,
    w_up,
    w_down,
    norm_gains,
    qk_gains,
    cotangent,
):
    n = lax.axis_size("seq")
    me = lax.axis_index("seq")
    rows, width = tokens.shape
    shard = w_query.shape[0]
    qk_shard = qk_gains.shape[0]

    travel_a, travel_b, travel_c = travelling(
        norm_gains, qk_gains[None, :], (w_query, w_key, w_value), (w_output.T, w_gate, w_up),
        (w_down.T,),
    )
    cols_a = w_query.shape[1] + w_key.shape[1] + w_value.shape[1] + EXTRA
    cols_b = w_output.shape[0] + w_gate.shape[1] + w_up.shape[1]
    cols_c = w_down.shape[0]

    even, odd, inner = row_table(n, shard)
    device = me ^ jnp.where(me & 1 == 0, jnp.asarray(even), jnp.asarray(odd))
    place = device * shard + inner
    qk_place = jnp.where(inner < qk_shard, device * qk_shard + inner, -1)
    padded_ids = jnp.concatenate([jnp.full((LONGEST + rows,), -1, jnp.int32), segment_ids])
    nearby = lax.dynamic_slice_in_dim(padded_ids, me * rows, 2 * rows + LONGEST)
    keys_segment = nearby[LONGEST:]
    seg_q = keys_segment[rows:, None]
    seg_k = jnp.stack(
        [keys_segment[b * BLOCK : b * BLOCK + REACH] for b in range(rows // BLOCK)]
    )[:, None, :]

    tokens_before = lax.ppermute(tokens, "seq", [(i, i + 1) for i in range(n - 1)])
    steps = len(far_bits(n)[0])
    a_c = to_first(travel_c, n)
    (own_b,) = pack(far_direct(travel_b, n), shard, cols_b, 1, n, after=(a_c,))
    a_b, b_b = to_first(own_b, n), to_second(own_b, n)
    pair_c, block_a = call(
        start_kernel,
        [
            shaped((2 * travel_c.shape[0], travel_c.shape[1]), bf16),
            shaped(travel_a.shape, bf16),
        ],
        [travel_c, a_c, travel_a],
        us=0.2,
        after=(own_b,),
    )
    for step in range(steps - 1):
        block_a, pair_c = stack(
            (block_a, far_step(block_a, n, step)), (pair_c, far_step(pair_c, n, step))
        )
    (own_a,) = pack([block_a, far_step(block_a, n, steps - 1)], shard, cols_a, 1, n)
    a_a, b_a = to_first(own_a, n), to_second(own_a, n)
    half_c = pack([pair_c, far_step(pair_c, n, steps - 1)], shard, cols_c, 2, n, after=(own_a,))
    first = (me % EIGHT == 0).astype(f32).reshape(1, 1)
    cosine, sine, order, qk_order, first = tables(
        nearby, rows, place, qk_place, width, first, after=(own_b,)
    )
    x, dy = permute(tokens_before, tokens, cotangent, order)
    a_b, own_b, *parts_b = hold_parts(
        a_b, own_b, after=(b_b, x, seg_q, seg_k, a_a, b_a, *half_c)
    )
    weights_a = [own_a, a_a, b_a, to_second(a_a, n)]
    weights_a = [*weights_a, *to_core(weights_a, n)]
    hidden, q_raw, k_raw, q, k, v, probs, o, gains, qk_gain = attend(
        x, weights_a, qk_order, cosine, sine, seg_q, seg_k, after=()
    )
    far_half = to_second(half_c[0], n)
    parts_b = [to_second(p, n) for p in parts_b]
    weights_b = [own_b, a_b, b_b, *parts_b]
    weights_b = [*weights_b, *to_core(weights_b, n)]
    a, middle, normed = join(o, weights_b, x, gains)
    half_c = [*half_c, *hold(far_half, after=(normed,))]
    weights_c = [*half_c, *to_core(half_c, n)]
    product, by_gate, by_up = feed(normed, weights_b, after=half_c[1:])
    y_low, low, gain3, *grad_d = turn(product, weights_c, middle, dy, gains)
    gate_low, up_low, *grad_g = feed_back(low, weights_c, by_gate, by_up, normed)
    sum_d = core_sum_by_far(grad_d[0], grad_d[1:], n, after=(gate_low,))
    sum_g = core_sum(grad_g[0], grad_g[1:], n, after=sum_d[:1])
    dx1, gain12, do, *grad_u = middle_back(
        gate_low, up_low, weights_b, middle, a, dy, gains, normed, o, after=sum_g[:1]
    )
    sum_g = near_sum_first(sum_g, n, after=(do,))
    dq_low, dkv_before, dkv_own, qk_grad = attend_back(
        probs, do, q, k, v, q_raw, k_raw, cosine, sine, qk_gain, after=sum_g[:1]
    )
    sum_g = near_sum_second(sum_g, n, after=(dq_low,))
    for step in reversed(range(1, steps)):
        sum_d = far_fold(sum_d, n, step, after=sum_g[:1], us=5)
    sum_u = core_sum(grad_u[0], grad_u[1:], n, after=sum_d[:1])
    dh_before, dh, *grad_a = project_back(
        [dq_low, dkv_before, dkv_own, qk_grad, hidden, x, qk_order, gain3, gain12],
        weights_a,
        after=sum_u[:1],
    )
    sum_a = core_sum(grad_a[0], grad_a[1:], n)
    before, own, mixed = input_back(
        dh_before, dh, x, gains, dx1, order, y_low, after=sum_a[:1]
    )
    sum_u = near_sum_first(sum_u, n, after=(own,), us=4)
    sum_d = far_fold(sum_d, n, 0, after=sum_u[:1])
    sum_a = near_sum_first(sum_a, n, after=sum_d[:1])
    sum_g = far_sum_first(sum_g, n, after=sum_a[:1])
    sum_d = near_sum_first(sum_d, n, after=sum_g[:1])
    before, behind = to_device_before(before, n, first, after=sum_d[:1])
    sum_a = near_sum_far([sum_a, sum_u], n, 2, after=(before,))
    ff = grad_d[0].shape[1]
    sum_a = far_sum_first(sum_a, n)
    input_grad, token = join_halo(own, behind, after=sum_a[:1])
    sum_g, token = far_sum_last(sum_g, n, shard, ((0, ff),), after=(token,))
    sum_d, token = near_sum_last(sum_d, n, shard, (0, ff), after=(token,))
    sum_q, sum_k, sum_v, norm_sums, qk_sums, sum_u, sum_o, _ = far_sum_last(
        sum_a, n, shard, ((0, 1024, 1280, 1536, 1664), (0, ff, ff + 1024)),
        gains_at=1536, gain_shapes=(norm_gains.shape, (1, qk_shard)), after=(token,),
    )
    return (
        mixed,
        input_grad,
        sum_q,
        sum_k,
        sum_v,
        sum_o.T,
        sum_g,
        sum_u,
        sum_d.T,
        norm_sums,
        qk_sums.reshape(qk_shard),
    )


def solution(mesh):
    return jax.shard_map(
        on_device,
        mesh=mesh,
        in_specs=(
            P("seq", None),
            P(),
            P("seq", None),
            P("seq", None),
            P("seq", None),
            P(None, "seq"),
            P("seq", None),
            P("seq", None),
            P(None, "seq"),
            P(None, "seq"),
            P("seq"),
            P("seq", None),
        ),
        out_specs=(
            P("seq", None),
            P("seq", None),
            P("seq", None),
            P("seq", None),
            P("seq", None),
            P(None, "seq"),
            P("seq", None),
            P("seq", None),
            P(None, "seq"),
            P(None, "seq"),
            P("seq"),
        ),
        check_vma=False,
    )
```

```python
import functools

import jax
import jax.numpy as jnp
import numpy as np
from jax import lax
from jax.experimental import pallas as pl
from jax.experimental.pallas import tpu as pltpu
from jax.sharding import PartitionSpec as P

H = 4
HD = 256
WINDOW = 512
LONGEST = 2048
EXTRA = 128
EIGHT = 8
FF_CHUNK = 512
BLOCK = 128
REACH = BLOCK + WINDOW
MIB = 1024 * 1024

epsilon = 1e-06
bf16 = jnp.bfloat16
f32 = jnp.float32


def far_bits(n):
    bits = [1 << i for i in range(n.bit_length() - 1)]
    rest = [b for b in bits[1:] if b not in near_pair(n)]
    return rest, rest[::-1]


def far_slots(bits):
    slots = [0]
    for b in bits:
        slots = slots + [s | b for s in slots]
    return slots


def near_pair(n):
    return (2, 8) if n > 64 else (2, 4)


def to_partner(x, n, masks):
    return lax.ppermute(x, "seq", [(i, i ^ masks[i & 1]) for i in range(n)])


def row_table(n, shard):
    first, second = near_pair(n)
    main = whole_tiles(shard)
    count = n // 8
    inner = [(i, r) for i in range(count) for r in range(main)]
    inner += [(i, r) for i in range(count) for r in range(main, shard)]

    def offsets(a, b, bits):
        far = far_slots(bits)
        return [m ^ far[i] for m in (0, a, b, a | b) for i, _ in inner]

    even_bits, odd_bits = far_bits(n)
    even, odd = offsets(first, second, even_bits), offsets(second, first, odd_bits)
    return (
        np.array(even + [1 ^ m for m in odd], np.int32),
        np.array(odd + [1 ^ m for m in even], np.int32),
        np.array([r for _, r in inner] * 8, np.int32),
    )


def nn(left, right):
    return jnp.dot(left, right, preferred_element_type=f32)


def tn(left, right):
    return lax.dot_general(left, right, (((0,), (0,)), ((), ())), preferred_element_type=f32)


def nt(left, right):
    return lax.dot_general(left, right, (((1,), (1,)), ((), ())), preferred_element_type=f32)


def inverse_rms(values):
    return lax.rsqrt(jnp.mean(values * values, axis=-1, keepdims=True) + epsilon)


def rms_back(values, gain, grad):
    scale = inverse_rms(values)
    hat = values * scale
    inner = grad * gain
    mean = jnp.mean(inner * hat, axis=-1, keepdims=True)
    return scale * (inner - hat * mean), jnp.sum(grad * hat, axis=0, keepdims=True)


def rotate(values, cosine, sine):
    half = values.shape[-1] // 2
    a, b = values[:, :half], values[:, half:]
    return jnp.concatenate([a * cosine - b * sine, b * cosine + a * sine], axis=-1)


def rotate_back(values, cosine, sine):
    half = values.shape[-1] // 2
    a, b = values[:, :half], values[:, half:]
    return jnp.concatenate([a * cosine + b * sine, b * cosine - a * sine], axis=-1)


def call(kernel, outs, args, us, scratch=(), after=(), room=8, result=False):
    given, extra = len(args), len(after)

    def body(*refs):
        if result:
            *refs, token = refs
            token[...] = jnp.zeros_like(token)
        kernel(*refs[:given], *refs[given + extra :])

    if result:
        outs = [pltpu.HBM(o.shape, o.dtype) for o in outs] + [shaped((8, 128), f32)]
    return pl.pallas_call(
        body,
        in_specs=[pl.BlockSpec(memory_space=pltpu.VMEM)] * given
        + [pl.BlockSpec(memory_space=pl.ANY)] * extra,
        out_specs=[pl.BlockSpec(memory_space=pltpu.VMEM)] * len(outs),
        out_shape=outs,
        scratch_shapes=scratch,
        compiler_params=pltpu.CompilerParams(vmem_limit_bytes=room * MIB),
        cost_estimate=pl.CostEstimate(
            flops=int(us * 10**9), bytes_accessed=int(us * 10**6), transcendentals=0
        ),
    )(*args, *after)


def shaped(shape, dtype):
    return jax.ShapeDtypeStruct(shape, dtype)


def join_rows(parts, cols=slice(None)):
    return jnp.concatenate([p[:, cols] for p in parts], axis=0)


def whole_tiles(rows):
    return rows // 16 * 16


def padded(cols):
    return -(-cols // 512) * 512


def in_tiles(rows):
    return rows == 20


def travel_shape(rows, cols):
    return (16, padded(cols) * 5 // 4) if in_tiles(rows) else (rows, cols)


def to_tiles(values):
    rows, cols = values.shape
    if not in_tiles(rows):
        return values
    wide = padded(cols)
    if wide > cols:
        values = jnp.concatenate([values, jnp.zeros((rows, wide - cols), f32)], axis=1)
    quarter = wide // 4
    rest = [values[16:, k * quarter : (k + 1) * quarter] for k in range(4)]
    return jnp.concatenate([values[:16], jnp.concatenate(rest, axis=0)], axis=1)


def tile_kernel(counts, *refs):
    total = sum(counts) + 2
    given, outs = refs[:total], refs[total : total + len(counts)]
    held, sem = refs[total + len(counts) : -1], refs[-1]
    copies = [
        pltpu.make_async_copy(source, target, sem.at[i])
        for i, (source, target) in enumerate(zip(given, held))
    ]
    for copy in copies:
        copy.start()
    for copy in copies:
        copy.wait()
    *held, norm_gains, qk_gains = held
    shard = norm_gains.shape[1]
    rows = [
        jnp.concatenate([g[...].astype(f32), jnp.zeros((g.shape[0], EXTRA - g.shape[1]), f32)], axis=1)
        for g in (norm_gains, qk_gains)
    ]
    rows.append(jnp.zeros((EXTRA - 5, EXTRA), f32))
    extra = jnp.concatenate(rows, axis=0).T[:shard]
    for group, (count, out) in enumerate(zip(counts, outs)):
        parts = [p[...].astype(f32) for p in held[:count]]
        held = held[count:]
        if group == 0:
            parts.append(extra)
        out[...] = to_tiles(jnp.concatenate(parts, axis=1)).astype(bf16)


def travelling(norm_gains, qk_gains, *groups):
    counts = [len(g) for g in groups]
    given = [w for g in groups for w in g] + [norm_gains, qk_gains]
    outs = []
    for i, g in enumerate(groups):
        cols = sum(w.shape[1] for w in g) + (EXTRA if i == 0 else 0)
        outs.append(shaped(travel_shape(g[0].shape[0], cols), bf16))
    return pl.pallas_call(
        functools.partial(tile_kernel, counts),
        in_specs=[pl.BlockSpec(memory_space=pltpu.HBM)] * len(given),
        out_specs=[pl.BlockSpec(memory_space=pltpu.VMEM)] * len(outs),
        out_shape=outs,
        scratch_shapes=[pltpu.VMEM(w.shape, bf16) for w in given]
        + [pltpu.SemaphoreType.DMA((len(given),))],
        compiler_params=pltpu.CompilerParams(vmem_limit_bytes=8 * MIB),
    )(*[pltpu.with_memory_space_constraint(w, pltpu.HBM) for w in given])


def stack_kernel(*refs):
    count = len(refs) // 3
    for i in range(count):
        a, b, out = refs[2 * i], refs[2 * i + 1], refs[2 * count + i]
        rows = a.shape[0]
        if rows % 16 == 0:
            out[:rows] = a[...]
            out[rows:] = b[...]
        else:
            both = [a[...].astype(f32), b[...].astype(f32)]
            out[...] = jnp.concatenate(both, axis=0).astype(bf16)


def stack(*pairs, after=()):
    outs = [shaped((2 * a.shape[0], a.shape[1]), bf16) for a, _ in pairs]
    return call(stack_kernel, outs, [x for pair in pairs for x in pair], us=0.1, after=after)


def pack_kernel(pieces, blocks, out):
    count = len(pieces)
    share, cols = out.shape[0] // blocks, out.shape[1]
    rows = share // count
    main = whole_tiles(rows)
    height, wide = travel_shape(rows, cols)
    quarter = padded(cols) // 4
    for block in range(blocks):
        at = block * share
        starts = [(ref, begin + block * height) for ref, begin in pieces]
        if main:
            for i, (ref, begin) in enumerate(starts):
                out[at + i * main : at + (i + 1) * main] = ref[begin : begin + main, :cols]
        at = at + main * count
        if in_tiles(rows):
            rest = [ref[begin : begin + 16, 4 * quarter :].astype(f32) for ref, begin in starts]
            for k in range(4):
                end = min((k + 1) * quarter, cols)
                part = jnp.concatenate([r[4 * k : 4 * k + 4] for r in rest], axis=0)
                out[at : at + 4 * count, k * quarter : end] = part[:, : end - k * quarter].astype(
                    bf16
                )
        elif rows > main:
            rest = [
                ref[...].astype(f32)[begin + main : begin + rows] for ref, begin in starts
            ]
            out[at : at + (rows - main) * count] = jnp.concatenate(rest, axis=0).astype(bf16)


def pack(arrays, rows, cols, blocks, n, parts=1, after=()):
    count = n // 8
    height = travel_shape(rows, cols)[0] * blocks
    held = count // len(arrays)
    total = rows * count * blocks

    def kernel(*refs):
        given = refs[: len(arrays)]
        pieces = [(ref, h * height) for ref in given for h in range(held)]
        if parts == 1:
            pack_kernel(pieces, blocks, refs[-1])
        else:
            for block, out in enumerate(refs[len(arrays) :]):
                shift = block * height // blocks
                pack_kernel([(ref, at + shift) for ref, at in pieces], 1, out)

    outs = [shaped((total // parts, cols), bf16)] * parts
    return call(kernel, outs, arrays, us=0.1, after=after)


def far_step(block, n, step):
    even, odd = far_bits(n)
    return to_partner(block, n, (even[step], odd[step]))


def far_direct(block, n):
    even, odd = far_bits(n)
    slots = zip(far_slots(even)[1:], far_slots(odd)[1:])
    return [block] + [to_partner(block, n, masks) for masks in slots]


def start_kernel(a, b, one, out, one_out):
    stack_kernel(a, b, out)
    one_out[...] = one[...]


def hold_kernel(*refs):
    half = len(refs) // 2
    for value, out in zip(refs[:half], refs[half:]):
        out[...] = value[...]


def hold(*values, after):
    return call(hold_kernel, [shaped(v.shape, v.dtype) for v in values], values, 0.2, after=after)


def cut_kernel(whole, upper, lower):
    rows = upper.shape[0]
    upper[...] = whole[:rows]
    lower[...] = whole[rows:]


def cut(whole, after):
    rows, cols = whole.shape
    upper = rows // 32 * 16 + (16 if rows % 32 else 0)
    outs = [shaped((upper, cols), bf16), shaped((rows - upper, cols), bf16)]
    return call(cut_kernel, outs, [whole], us=0.1, after=after)


def far_gather(blocks, n, joins):
    steps = len(far_bits(n)[0])
    for k in range(steps - 1):
        got = [far_step(b, n, k) for b in blocks]
        blocks = stack(*zip(blocks, got), after=joins[k] if k < len(joins) else ())
    return [(b, far_step(b, n, steps - 1)) for b in blocks]


def to_first(x, n):
    first, second = near_pair(n)
    return to_partner(x, n, (first, second))


def to_second(x, n):
    first, second = near_pair(n)
    return to_partner(x, n, (second, first))


def near_pieces(own, n, direct=False):
    first, second = near_pair(n)
    a, b = to_first(own, n), to_second(own, n)
    return [own, a, b, to_partner(own, n, (first | second,) * 2) if direct else to_second(a, n)]


def to_core(pieces, n):
    return [to_partner(p, n, (1, 1)) for p in pieces]


def fold_kernel(count, *refs):
    given, outs = refs[:count], refs[count:]
    mine, got = given[0], given[1:]
    rows = outs[0].shape[0]
    height = got[0].shape[0]
    if rows % 16 == 0 and height % rows == 0:
        per = height // rows
        for i, out in enumerate(outs):
            other = got[i // per][(i % per) * rows : (i % per + 1) * rows]
            part = mine[i * rows : (i + 1) * rows]
            out[...] = (part.astype(f32) + other.astype(f32)).astype(bf16)
    else:
        total = mine[...].astype(f32)
        total = total + jnp.concatenate([g[...].astype(f32) for g in got], axis=0)
        for i, out in enumerate(outs):
            out[...] = total[i * rows : (i + 1) * rows].astype(bf16)


def fold(mine, got, after=(), us=0.5):
    rows, cols = mine.shape
    outs = [shaped((rows // 2, cols), bf16)] * 2
    kernel = functools.partial(fold_kernel, 1 + len(got))
    return call(kernel, outs, [mine, *got], us=us, after=after)


def wide_fold_kernel(mine, *refs):
    got, (keep, send) = refs[:-2], refs[-2:]
    rows = got[0].shape[0]
    per = keep.shape[0] // rows
    for i, other in enumerate(got):
        out = keep if i < per else send
        at = (i % per) * rows
        part = mine[i * rows : (i + 1) * rows].astype(f32)
        out[at : at + rows] = (part + other[...].astype(f32)).astype(bf16)


def core_sum(top, sends, n, after=()):
    rows, cols = top.shape
    outs = [shaped((rows // 2, cols), bf16)] * 2
    return call(wide_fold_kernel, outs, [top, *to_core(sends, n)], us=0.7, after=after)


def core_sum_by_far(top, sends, n, after=()):
    rows, cols = top.shape
    count, blocks = n // 8, 4
    share = rows // blocks
    shard = share // count
    main = whole_tiles(shard)
    rest, done = shard - main, main * count
    height, wide = travel_shape(shard, cols)

    def kernel(mine, *refs):
        got, (keep, send) = refs[:-2], refs[-2:]
        per = blocks // len(got)
        tiles = []
        for block in range(blocks):
            other = got[block // per][(block % per) * share : (block % per + 1) * share]
            total = mine[block * share : (block + 1) * share].astype(f32) + other.astype(f32)
            for i in range(count):
                parts = []
                if main:
                    parts.append(total[i * main : (i + 1) * main])
                if rest:
                    parts.append(total[done + i * rest : done + (i + 1) * rest])
                tiles.append((i, block, to_tiles(jnp.concatenate(parts, axis=0))))
        tiles = [t for _, _, t in sorted(tiles, key=lambda item: item[:2])]
        half = len(tiles) // 2
        keep[...] = jnp.concatenate(tiles[:half], axis=0).astype(bf16)
        send[...] = jnp.concatenate(tiles[half:], axis=0).astype(bf16)

    outs = [shaped((count // 2 * blocks * height, wide), bf16)] * 2
    return call(kernel, outs, [top, *to_core(sends, n)], us=1.5, after=after)


def far_fold(halves, n, step, after=(), us=0.5):
    keep, send = halves
    return fold(keep, [far_step(send, n, step)], after, us)


def near_sum_last(halves, n, shard, cuts, after=()):
    keep, send = halves
    outs = [shaped((shard, e - b), f32) for b, e in zip(cuts[:-1], cuts[1:])]
    return call(
        functools.partial(far_sum_kernel, (cuts,), None), outs, [keep, to_first(send, n)], us=1,
        after=after, result=True,
    )


def near_sum_first(halves, n, after=(), us=0.5):
    keep, send = halves
    return fold(keep, [to_second(send, n)], after, us)


def fold_both_kernel(*refs):
    given, (keep, send) = refs[:4], refs[4:]
    rows, cols = keep.shape
    cols = cols // 2
    for i in range(2):
        mine, got = given[2 * i : 2 * i + 2]
        for j, out in enumerate((keep, send)):
            part = slice(j * rows, (j + 1) * rows)
            out[:, i * cols : (i + 1) * cols] = (
                mine[part].astype(f32) + got[part].astype(f32)
            ).astype(bf16)


def near_sum_first_both(one, two, n, after=()):
    args = [x for keep, send in (one, two) for x in (keep, to_second(send, n))]
    rows, cols = one[0].shape
    outs = [shaped((rows // 2, 2 * cols), bf16)] * 2
    return call(fold_both_kernel, outs, args, us=5, after=after)


def split_kernel(count, mine, got, keep, send):
    total = mine[...].astype(f32) + got[...].astype(f32)
    rows = total.shape[0] // count
    main = whole_tiles(rows)
    rest, done = rows - main, main * count
    slots = []
    for i in range(count):
        parts = []
        if main:
            parts.append(total[i * main : (i + 1) * main])
        if rest:
            parts.append(total[done + i * rest : done + (i + 1) * rest])
        slots.append(to_tiles(jnp.concatenate(parts, axis=0)))
    keep[...] = jnp.concatenate(slots[: count // 2], axis=0).astype(bf16)
    send[...] = jnp.concatenate(slots[count // 2 :], axis=0).astype(bf16)


def near_sum_second(halves, n, after=()):
    keep, send = halves
    rows, cols = keep.shape
    count = n // 8
    height, wide = travel_shape(rows // count, cols)
    outs = [shaped((count // 2 * height, wide), bf16)] * 2
    return call(
        functools.partial(split_kernel, count), outs, [keep, to_first(send, n)], us=1, after=after
    )


def slots_kernel(groups, count, *refs):
    outs = refs[2 * groups :]
    slots = [[] for _ in range(count)]
    for g in range(groups):
        total = refs[2 * g][...].astype(f32) + refs[2 * g + 1][...].astype(f32)
        rows = total.shape[0] // count
        main = whole_tiles(rows)
        rest, done = rows - main, main * count
        for i in range(count):
            parts = []
            if main:
                parts.append(total[i * main : (i + 1) * main])
            if rest:
                parts.append(total[done + i * rest : done + (i + 1) * rest])
            slots[i].append(to_tiles(jnp.concatenate(parts, axis=0)))
    per = count // len(outs)
    for i, parts in enumerate(slots):
        values = jnp.concatenate(parts, axis=1).astype(bf16)
        height = values.shape[0]
        if per == 1:
            outs[i][...] = values
        elif height % 16 == 0:
            outs[i // per][i % per * height : (i % per + 1) * height] = values
    if per > 1 and height % 16 != 0:
        for j, out in enumerate(outs):
            values = [jnp.concatenate(p, axis=1) for p in slots[j * per : (j + 1) * per]]
            out[...] = jnp.concatenate(values, axis=0).astype(bf16)


def near_sum_far(groups, n, parts, after=()):
    count = n // 8
    args, wide = [], 0
    for keep, send in groups:
        args += [keep, to_first(send, n)]
        height, cols = travel_shape(keep.shape[0] // count, keep.shape[1])
        wide += cols
    outs = [shaped((height * count // parts, wide), bf16)] * parts
    kernel = functools.partial(slots_kernel, len(groups), count)
    return call(kernel, outs, args, us=1, after=after)


def far_sum_first(halves, n, after=()):
    keep, send = halves
    for k in reversed(range(1, len(far_bits(n)[0]))):
        keep, send = fold(keep, [far_step(send, n, k)], after)
        after = ()
    return keep, send


def far_sum_kernel(groups, gains_at, *refs):
    count = sum(len(cuts) - 1 for cuts in groups) + (gains_at is not None)
    given, outs = refs[:-count], refs[-count:]
    total = given[0][...].astype(f32)
    for got in given[1:]:
        total = total + got[...].astype(f32)
    rows = outs[0].shape[0]
    begin_at = 0
    for number, cuts in enumerate(groups):
        wide = padded(cuts[-1]) if in_tiles(rows) else cuts[-1]
        part = total[:, begin_at : begin_at + wide]
        if in_tiles(rows):
            quarter = wide // 4
            rest = total[:, begin_at + wide : begin_at + wide + quarter]
            rest = [rest[4 * k : 4 * k + 4] for k in range(4)]
            part = jnp.concatenate([part, jnp.concatenate(rest, axis=1)], axis=0)
            begin_at += quarter
        begin_at += wide
        for begin, end in zip(cuts[:-1], cuts[1:]):
            values = part[:, begin:end]
            if number == 0 and begin == gains_at:
                values = jnp.concatenate([values, jnp.zeros((EXTRA - rows, EXTRA), f32)], axis=0).T
                norms, qk, *outs = outs
                norms[...] = values[: norms.shape[0], :rows]
                qk[...] = values[norms.shape[0] : norms.shape[0] + 1, : qk.shape[1]]
            else:
                outs[0][...] = values
                outs = outs[1:]


def result_shapes(shard, groups, gains_at, gain_shapes):
    outs = []
    for number, cuts in enumerate(groups):
        for begin, end in zip(cuts[:-1], cuts[1:]):
            if number == 0 and begin == gains_at:
                outs += [shaped(shape, f32) for shape in gain_shapes]
            else:
                outs.append(shaped((shard, end - begin), f32))
    return outs


def far_sum_last(halves, n, shard, groups, gains_at=None, gain_shapes=(), after=()):
    keep, send = halves
    outs = result_shapes(shard, groups, gains_at, gain_shapes)
    kernel = functools.partial(far_sum_kernel, groups, gains_at)
    args = [keep, far_step(send, n, 0)]
    return call(kernel, outs, args, us=1, after=after, result=True)


def table_kernel(near, near_col, freqs, place, qk_place, first, cosine, sine, order, qk_order, first_out):
    count = cosine.shape[0]
    ahead = near.shape[1] - count
    steps = freqs[...]
    for c in range(count // 256):
        reach = slice(c * 256, c * 256 + ahead + 256)
        here = near_col[ahead + c * 256 : ahead + (c + 1) * 256]
        i = lax.broadcasted_iota(jnp.int32, (256, ahead + 256), 0) + ahead
        j = lax.broadcasted_iota(jnp.int32, (256, ahead + 256), 1)
        same = (here == near[:, reach]) & (j < i)
        position = jnp.sum(same.astype(f32), axis=1, keepdims=True)
        angles = position * steps
        cosine[c * 256 : (c + 1) * 256] = jnp.cos(angles)
        sine[c * 256 : (c + 1) * 256] = jnp.sin(angles)
    i = lax.broadcasted_iota(jnp.int32, order.shape, 0)
    order[...] = (i == place[...]).astype(f32).astype(bf16)
    j = lax.broadcasted_iota(jnp.int32, qk_order.shape, 1)
    qk_order[...] = (qk_place[...] == j).astype(f32).astype(bf16)
    first_out[...] = jnp.broadcast_to(first[...], first_out.shape)


def tables(near, rows, place, qk_place, width, first, after=()):
    freqs = np.float32(10000.0) ** (-2.0 * np.arange(HD // 2, dtype=np.float32) / np.float32(HD))
    args = [
        near[None, :], near[:, None], jnp.asarray(freqs)[None, :], place[None, :], qk_place[:, None],
        first,
    ]
    outs = [
        shaped((2 * rows, HD // 2), f32), shaped((2 * rows, HD // 2), f32),
        shaped((width, width), bf16), shaped((width, 2 * HD), bf16), shaped((8, 128), f32),
    ]
    return call(table_kernel, outs, args, us=3, after=after)


def permute_kernel(tokens_before, tokens, cotangent, order, x, dy):
    table = order[...]
    rows = tokens.shape[0]
    x[:rows] = nn(tokens_before[...], table).astype(bf16)
    x[rows:] = nn(tokens[...], table).astype(bf16)
    dy[...] = nn(cotangent[...], table).astype(bf16)


def permute(tokens_before, tokens, cotangent, order, after=()):
    rows, width = tokens.shape
    outs = [shaped((2 * rows, width), bf16), shaped((rows, width), bf16)]
    args = [tokens_before, tokens, cotangent, order]
    return call(permute_kernel, outs, args, us=2, after=after)


def attend_kernel(x, qk_order, cosine, sine, seg_q, seg_k, *refs):
    pieces = refs[:-10]
    hidden, q_raw, k_raw, q_out, k_out, v_out, probs, o, gains, qk_gain = refs[-10:]
    rows = q_raw.shape[0]
    w_q = join_rows(pieces, slice(0, 1024))
    w_kv = join_rows(pieces, slice(1024, 1536))
    gain_rows = join_rows(pieces, slice(1536, 1664)).astype(f32).T[:8]
    gains[...] = gain_rows
    gain_qk = nn(gain_rows.astype(bf16), qk_order[...])
    qk_gain[...] = gain_qk
    gain_q, gain_k = gain_qk[4:5, :HD], gain_qk[4:5, HD:]
    for c in range(2 * rows // 256):
        part = pl.ds(c * 256, 256)
        xs = x[part].astype(f32)
        hs = (xs * inverse_rms(xs) * gain_rows[0:1]).astype(bf16)
        hidden[part] = hs
        cs, sn = cosine[part], sine[part]
        kv = nn(hs, w_kv)
        raw = kv[:, :HD]
        k_raw[part] = raw
        k_out[part] = rotate(raw * inverse_rms(raw) * gain_k, cs, sn).astype(bf16)
        v_out[part] = kv[:, HD:].astype(bf16)
        if c * 256 >= rows:
            own = pl.ds(c * 256 - rows, 256)
            qs = nn(hs, w_q)
            q_raw[own] = qs
            for h in range(H):
                raw = qs[:, h * HD : (h + 1) * HD]
                q_out[own, h * HD : (h + 1) * HD] = rotate(
                    raw * inverse_rms(raw) * gain_q, cs, sn
                ).astype(bf16)
    for b in range(rows // BLOCK):
        mine = pl.ds(b * BLOCK, BLOCK)
        reach = pl.ds(b * BLOCK, REACH)
        q_rows = q_out[mine] * bf16(1.0 / 16.0)
        q_stack = jnp.concatenate([q_rows[:, h * HD : (h + 1) * HD] for h in range(H)], axis=0)
        scores = nt(q_stack, k_out[reach])
        i = lax.broadcasted_iota(jnp.int32, (BLOCK, REACH), 0)
        j = lax.broadcasted_iota(jnp.int32, (BLOCK, REACH), 1)
        allowed = (j > i) & (j <= i + WINDOW) & (seg_q[mine] == seg_k[b])
        allowed = jnp.concatenate([allowed.astype(f32)] * H, axis=0)
        weights = jnp.exp(scores) * allowed
        total = jnp.sum(weights, axis=-1, keepdims=True)
        p = (weights * (1.0 / total)).astype(bf16)
        probs[b] = p
        out = nn(p, v_out[reach])
        for h in range(H):
            o[mine, h * HD : (h + 1) * HD] = out[h * BLOCK : (h + 1) * BLOCK].astype(bf16)


def attend(x, pieces, qk_order, cosine, sine, seg_q, seg_k, after):
    rows = x.shape[0] // 2
    width = x.shape[1]
    return call(
        attend_kernel,
        [
            shaped((2 * rows, width), bf16),
            shaped((rows, H * HD), f32),
            shaped((2 * rows, HD), f32),
            shaped((rows, H * HD), bf16),
            shaped((2 * rows, HD), bf16),
            shaped((2 * rows, HD), bf16),
            shaped((rows // BLOCK, H * BLOCK, REACH), bf16),
            shaped((rows, H * HD), bf16),
            shaped((8, width), f32),
            shaped((8, 2 * HD), f32),
        ],
        [x, qk_order, cosine, sine, seg_q, seg_k, *pieces],
        us=0.1,
        after=after,
    )


def gelu_parts(g):
    c0, c1 = 0.7978845608028654, 0.044715
    square = g * g
    t = jnp.tanh(g * (c0 + (c0 * c1) * square))
    half = 0.5 + 0.5 * t
    value = g * half
    slope = half + value * ((1.0 - t) * (c0 + (3.0 * c0 * c1) * square))
    return value, slope


def join_kernel(o, x, gains, *refs):
    pieces, (a_out, middle, normed) = refs[:-3], refs[-3:]
    rows = o.shape[0]
    w_o = join_rows(pieces, slice(0, H * HD))
    for c in range(rows // 256):
        part = pl.ds(c * 256, 256)
        a = nt(o[part], w_o)
        a_out[part] = a
        x1 = x[rows + c * 256 : rows + (c + 1) * 256].astype(f32) + a * inverse_rms(a) * gains[1:2]
        middle[part] = x1
        normed[part] = (x1 * inverse_rms(x1) * gains[2:3]).astype(bf16)


def join(o, pieces, x, gains):
    rows, width = o.shape[0], x.shape[1]
    outs = [shaped((rows, width), f32), shaped((rows, width), f32), shaped((rows, width), bf16)]
    return call(join_kernel, outs, [o, x, gains, *pieces], us=1)


def feed_kernel(normed, *refs):
    pieces, (product, by_gate, by_up) = refs[:-3], refs[-3:]
    rows, ff = product.shape
    for j in range(ff // FF_CHUNK):
        cols = slice(j * FF_CHUNK, (j + 1) * FF_CHUNK)
        w_g = join_rows(pieces, slice(H * HD + cols.start, H * HD + cols.stop))
        w_u = join_rows(pieces, slice(H * HD + ff + cols.start, H * HD + ff + cols.stop))
        for c in range(rows // 256):
            part = pl.ds(c * 256, 256)
            h2 = normed[part]
            g = nn(h2, w_g)
            u = nn(h2, w_u)
            value, slope = gelu_parts(g)
            product[part, cols] = (value * u).astype(bf16)
            by_gate[part, cols] = (slope * u).astype(bf16)
            by_up[part, cols] = value.astype(bf16)


def feed(normed, pieces, after=()):
    rows = normed.shape[0]
    ff = (pieces[0].shape[1] - H * HD) // 2
    outs = [shaped((rows, ff), bf16)] * 3
    return call(feed_kernel, outs, [normed, *pieces], us=5, after=after)


def put_grad(grads, cols, values):
    top, *sends = grads
    half = top.shape[0]
    top[:, cols] = values[:half]
    part = half // len(sends)
    for i, send in enumerate(sends):
        send[:, cols] = values[half + i * part : half + (i + 1) * part]


def grad_shapes(width, cols):
    return [shaped((width // 2, cols), bf16)] + [shaped((width // 4, cols), bf16)] * 2


def turn_kernel(product, middle, dy, gains, *refs):
    pieces, (y_low, low, gain_grad, *grads) = refs[:-6], refs[-6:]
    ff = product.shape[1]
    w_d = join_rows(pieces)
    total = jnp.zeros((1, dy.shape[1]), f32)
    for c in range(dy.shape[0] // 256):
        part = pl.ds(c * 256, 256)
        f = nt(product[part], w_d)
        grad = dy[part].astype(f32)
        y = middle[part] + f * inverse_rms(f) * gains[3:4]
        y_low[part] = y.astype(bf16)
        df, dgain = rms_back(f, gains[3:4], grad)
        low[part] = df.astype(bf16)
        total = total + dgain
    gain_grad[...] = jnp.broadcast_to(total, gain_grad.shape)
    for j in range(ff // FF_CHUNK):
        cols = slice(j * FF_CHUNK, (j + 1) * FF_CHUNK)
        grad = tn(low[...], product[:, cols]).astype(bf16)
        put_grad(grads, cols, grad)


def turn(product, pieces, middle, dy, gains):
    rows, width = middle.shape
    return call(
        turn_kernel,
        [
            shaped((rows, width), bf16),
            shaped((rows, width), bf16),
            shaped((8, width), f32),
            *grad_shapes(width, product.shape[1]),
        ],
        [product, middle, dy, gains, *pieces],
        us=6,
    )


def feed_back_kernel(low, by_gate, by_up, normed, *refs):
    pieces, (gate_low, up_low, *grads) = refs[:-5], refs[-5:]
    rows, ff = gate_low.shape
    for j in range(ff // FF_CHUNK):
        cols = slice(j * FF_CHUNK, (j + 1) * FF_CHUNK)
        w_d = join_rows(pieces, cols)
        for c in range(rows // 256):
            part = pl.ds(c * 256, 256)
            dm = nn(low[part], w_d)
            gate_low[part, cols] = (dm * by_gate[part, cols].astype(f32)).astype(bf16)
            up_low[part, cols] = (dm * by_up[part, cols].astype(f32)).astype(bf16)
        put_grad(grads, cols, tn(normed[...], gate_low[:, cols]).astype(bf16))


def feed_back(low, pieces, by_gate, by_up, normed):
    rows, width = low.shape
    ff = by_gate.shape[1]
    return call(
        feed_back_kernel,
        [shaped((rows, ff), bf16)] * 2 + grad_shapes(width, ff),
        [low, by_gate, by_up, normed, *pieces],
        us=4,
    )


def middle_back_kernel(gate_low, up_low, middle, a, dy, gains, normed, o, *refs):
    pieces, (dx1, gain_grad, do, *grads) = refs[:-6], refs[-6:]
    rows, ff = gate_low.shape
    w_g = join_rows(pieces, slice(H * HD, H * HD + ff))
    w_u = join_rows(pieces, slice(H * HD + ff, H * HD + 2 * ff))
    normed_grad = nt(gate_low[...], w_g) + nt(up_low[...], w_u)
    for j in range(ff // FF_CHUNK):
        cols = slice(j * FF_CHUNK, (j + 1) * FF_CHUNK)
        put_grad(grads, cols, tn(normed[...], up_low[:, cols]).astype(bf16))
    sum1 = jnp.zeros((1, dy.shape[1]), f32)
    sum2 = jnp.zeros((1, dy.shape[1]), f32)
    lows = []
    for c in range(rows // 256):
        part = slice(c * 256, (c + 1) * 256)
        back, dgain2 = rms_back(middle[part], gains[2:3], normed_grad[part])
        dx = dy[part].astype(f32) + back
        dx1[part] = dx
        da, dgain1 = rms_back(a[part], gains[1:2], dx)
        lows.append(da.astype(bf16))
        sum1, sum2 = sum1 + dgain1, sum2 + dgain2
    gain_grad[...] = jnp.concatenate([sum1, sum2, jnp.zeros((6, dy.shape[1]), f32)], axis=0)
    low = jnp.concatenate(lows, axis=0)
    do[...] = nn(low, join_rows(pieces, slice(0, H * HD))).astype(bf16)
    put_grad(grads, slice(ff, ff + H * HD), tn(low, o[...]).astype(bf16))


def middle_back(gate_low, up_low, pieces, middle, a, dy, gains, normed, o, after):
    rows, width = middle.shape
    return call(
        middle_back_kernel,
        [
            shaped((rows, width), f32),
            shaped((8, width), f32),
            shaped((rows, H * HD), bf16),
            *grad_shapes(width, gate_low.shape[1] + H * HD),
        ],
        [gate_low, up_low, middle, a, dy, gains, normed, o, *pieces],
        us=14,
        after=after,
        room=10,
    )


def attend_back_kernel(
    probs, do, q, k, v, q_raw, k_raw, cosine, sine, qk_gain, dq_low, dkv_before, dkv_own, qk_grad, dk, dv
):
    rows = q_raw.shape[0]
    dk[...] = jnp.zeros_like(dk)
    dv[...] = jnp.zeros_like(dv)
    gain_q, gain_k = qk_gain[4:5, :HD], qk_gain[4:5, HD:]
    sum_q = jnp.zeros((1, HD), f32)

    def stack_heads(values):
        return jnp.concatenate([values[:, h * HD : (h + 1) * HD] for h in range(H)], axis=0)

    def probs_grad(b):
        do_stack = stack_heads(do[pl.ds(b * BLOCK, BLOCK)])
        return do_stack, nt(do_stack, v[pl.ds(b * BLOCK, REACH)])

    blocks = rows // BLOCK
    ahead = probs_grad(0)
    for b in range(blocks):
        do_stack, dp = ahead
        if b + 1 < blocks:
            ahead = probs_grad(b + 1)
        mine = pl.ds(b * BLOCK, BLOCK)
        reach = pl.ds(b * BLOCK, REACH)
        p_low = probs[b]
        p = p_low.astype(f32)
        dv[reach] += tn(p_low, do_stack)
        t = p * dp
        ds = (t - p * jnp.sum(t, axis=-1, keepdims=True)).astype(bf16)
        dk[reach] += tn(ds, stack_heads(q[mine]))
        dq = nn(ds, k[reach]) * (1.0 / 16.0)
        own = pl.ds(rows + b * BLOCK, BLOCK)
        cs, sn = cosine[own], sine[own]
        for h in range(H):
            grad = rotate_back(dq[h * BLOCK : (h + 1) * BLOCK], cs, sn)
            back, dgain = rms_back(q_raw[mine, h * HD : (h + 1) * HD], gain_q, grad)
            dq_low[mine, h * HD : (h + 1) * HD] = back.astype(bf16)
            sum_q = sum_q + dgain
    sum_k = jnp.zeros((1, HD), f32)
    for c in range(2 * rows // 256):
        part = pl.ds(c * 256, 256)
        grad = rotate_back(dk[part] * (1.0 / 16.0), cosine[part], sine[part])
        back, dgain = rms_back(k_raw[part], gain_k, grad)
        out, at = (dkv_before, c * 256) if c * 256 < rows else (dkv_own, c * 256 - rows)
        out[at : at + 256, :HD] = back.astype(bf16)
        out[at : at + 256, HD:] = dv[part].astype(bf16)
        sum_k = sum_k + dgain
    qk_grad[...] = jnp.broadcast_to(jnp.concatenate([sum_q, sum_k], axis=1), qk_grad.shape)


def attend_back(probs, do, q, k, v, q_raw, k_raw, cosine, sine, qk_gain, after):
    rows = q.shape[0]
    return call(
        attend_back_kernel,
        [
            shaped((rows, H * HD), bf16), shaped((rows, 2 * HD), bf16),
            shaped((rows, 2 * HD), bf16), shaped((8, 2 * HD), f32),
        ],
        [probs, do, q, k, v, q_raw, k_raw, cosine, sine, qk_gain],
        us=0.3,
        scratch=[pltpu.VMEM((2 * rows, HD), f32), pltpu.VMEM((2 * rows, HD), f32)],
        after=after,
        room=8,
    )


def project_back_kernel(
    dq_low, dkv_before, dkv_own, qk_grad, hidden, x, qk_order, gain3, gain12, *refs
):
    pieces, (dh_before, dh, *grads) = refs[:-5], refs[-5:]
    rows = dq_low.shape[0]
    put_grad(grads, slice(0, 1024), tn(hidden[rows:], dq_low[...]).astype(bf16))
    grad = tn(hidden[:rows], dkv_before[...]) + tn(hidden[rows:], dkv_own[...])
    put_grad(grads, slice(1024, 1536), grad.astype(bf16))
    w_q = join_rows(pieces, slice(0, 1024))
    w_kv = join_rows(pieces, slice(1024, 1536))
    sum0 = jnp.zeros((1, x.shape[1]), f32)
    for c in range(rows // 256):
        part = pl.ds(c * 256, 256)
        before = x[part].astype(f32)
        grad = nt(dkv_before[part], w_kv)
        dh_before[part] = grad
        sum0 = sum0 + jnp.sum(grad * (before * inverse_rms(before)), axis=0, keepdims=True)
        own = x[rows + c * 256 : rows + (c + 1) * 256].astype(f32)
        grad = nt(dkv_own[part], w_kv) + nt(dq_low[part], w_q)
        dh[part] = grad
        sum0 = sum0 + jnp.sum(grad * (own * inverse_rms(own)), axis=0, keepdims=True)
    qk_spread = nt(qk_grad[...].astype(bf16), qk_order[...])
    rows_of = jnp.concatenate(
        [
            sum0, gain12[0:1], gain12[1:2], gain3[0:1], qk_spread[0:1],
            jnp.zeros((EXTRA - 5, x.shape[1]), f32),
        ],
        axis=0,
    )
    put_grad(grads, slice(1536, 1664), rows_of.T.astype(bf16))


def project_back(args, pieces, after):
    rows, width = args[0].shape[0], args[5].shape[1]
    return call(
        project_back_kernel,
        [shaped((rows, width), f32)] * 2 + grad_shapes(width, pieces[0].shape[1]),
        [*args, *pieces],
        us=8,
        after=after,
    )


def input_back_kernel(dh_before, dh, x, gains, dx1, order, y_low, before, own, mixed):
    rows = dx1.shape[0]
    table = order[...]
    for c in range(rows // 256):
        part = pl.ds(c * 256, 256)
        back, _ = rms_back(x[part].astype(f32), gains[0:1], dh_before[part])
        before[part] = nt(back.astype(bf16), table).astype(bf16)
        mixed[part] = nt(y_low[part], table).astype(bf16)
        mine = x[rows + c * 256 : rows + (c + 1) * 256].astype(f32)
        back, _ = rms_back(mine, gains[0:1], dh[part])
        rest = back + dx1[part]
        total = jnp.zeros_like(rest)
        for _ in range(3):
            piece = rest.astype(bf16)
            rest = rest - piece.astype(f32)
            total = total + nt(piece, table)
        own[part] = total


def input_back(dh_before, dh, x, gains, dx1, order, y_low, after=()):
    outs = [shaped(dx1.shape, bf16), shaped(dx1.shape, f32), shaped(dx1.shape, bf16)]
    args = [dh_before, dh, x, gains, dx1, order, y_low]
    return call(input_back_kernel, outs, args, us=0.3, after=after)


def select_kernel(first, own, other, out):
    pick = first[:1, :1] > 0.5
    out[...] = jnp.where(pick, other[...].astype(f32), own[...].astype(f32)).astype(bf16)


def to_device_before(x, n, first, after=()):
    hop = lax.ppermute(x, "seq", [(i + EIGHT, i) for i in range(0, n - EIGHT, EIGHT)])
    (out,) = call(select_kernel, [shaped(x.shape, bf16)], [first, x, hop], us=0.3, after=after)
    pairs = [(i, i - 1) for i in range(n) if i % EIGHT]
    pairs += [(i, i + EIGHT - 1) for i in range(0, n - EIGHT, EIGHT)]
    return out, lax.ppermute(out, "seq", pairs)


def join_halo_kernel(own, behind, out):
    out[...] = own[...] + behind[...].astype(f32)


def join_halo(own, behind, after=()):
    outs = [shaped(own.shape, f32)]
    return call(join_halo_kernel, outs, [own, behind], us=0.3, after=after, result=True)


def on_device(
    tokens,
    segment_ids,
    w_query,
    w_key,
    w_value,
    w_output,
    w_gate,
    w_up,
    w_down,
    norm_gains,
    qk_gains,
    cotangent,
):
    n = lax.axis_size("seq")
    me = lax.axis_index("seq")
    rows, width = tokens.shape
    shard = w_query.shape[0]
    qk_shard = qk_gains.shape[0]

    travel_a, travel_b, travel_c = travelling(
        norm_gains, qk_gains[None, :], (w_query, w_key, w_value), (w_output.T, w_gate, w_up),
        (w_down.T,),
    )
    cols_a = w_query.shape[1] + w_key.shape[1] + w_value.shape[1] + EXTRA
    cols_b = w_output.shape[0] + w_gate.shape[1] + w_up.shape[1]
    cols_c = w_down.shape[0]

    even, odd, inner = row_table(n, shard)
    device = me ^ jnp.where(me & 1 == 0, jnp.asarray(even), jnp.asarray(odd))
    place = device * shard + inner
    qk_place = jnp.where(inner < qk_shard, device * qk_shard + inner, -1)
    padded_ids = jnp.concatenate([jnp.full((LONGEST + rows,), -1, jnp.int32), segment_ids])
    nearby = lax.dynamic_slice_in_dim(padded_ids, me * rows, 2 * rows + LONGEST)
    keys_segment = nearby[LONGEST:]
    seg_q = keys_segment[rows:, None]
    seg_k = jnp.stack(
        [keys_segment[b * BLOCK : b * BLOCK + REACH] for b in range(rows // BLOCK)]
    )[:, None, :]

    tokens_before = lax.ppermute(tokens, "seq", [(i, i + 1) for i in range(n - 1)])
    steps = len(far_bits(n)[0])
    a_c = to_first(travel_c, n)
    (own_b,) = pack(far_direct(travel_b, n), shard, cols_b, 1, n, after=(a_c,))
    a_b, b_b = to_first(own_b, n), to_second(own_b, n)
    pair_c, block_a = call(
        start_kernel,
        [
            shaped((2 * travel_c.shape[0], travel_c.shape[1]), bf16),
            shaped(travel_a.shape, bf16),
        ],
        [travel_c, a_c, travel_a],
        us=0.2,
        after=(own_b,),
    )
    for step in range(steps - 1):
        block_a, pair_c = stack(
            (block_a, far_step(block_a, n, step)), (pair_c, far_step(pair_c, n, step))
        )
    first = (me % EIGHT == 0).astype(f32).reshape(1, 1)
    cosine, sine, order, qk_order, first = tables(
        nearby, rows, place, qk_place, width, first, after=(own_b,)
    )
    x, dy = permute(tokens_before, tokens, cotangent, order)
    (own_a,) = pack([block_a, far_step(block_a, n, steps - 1)], shard, cols_a, 1, n, after=(x, seg_q, seg_k))
    a_a, b_a = to_first(own_a, n), to_second(own_a, n)
    half_c = pack([pair_c, far_step(pair_c, n, steps - 1)], shard, cols_c, 2, n, after=(own_a,))
    parts_b = cut(a_b, after=(b_b, a_a, b_a, *half_c))
    weights_a = [own_a, a_a, b_a, to_second(a_a, n)]
    weights_a = [*weights_a, *to_core(weights_a, n)]
    hidden, q_raw, k_raw, q, k, v, probs, o, gains, qk_gain = attend(
        x, weights_a, qk_order, cosine, sine, seg_q, seg_k, after=()
    )
    far_half = to_second(half_c[0], n)
    parts_b = hold(*[to_second(p, n) for p in parts_b], after=(o,))
    weights_b = [own_b, a_b, b_b, *parts_b]
    weights_b = [*weights_b, *to_core(weights_b, n)]
    a, middle, normed = join(o, weights_b, x, gains)
    half_c = [*half_c, *cut(far_half, after=(normed,))]
    weights_c = [*half_c, *to_core(half_c, n)]
    product, by_gate, by_up = feed(normed, weights_b, after=half_c[1:])
    y_low, low, gain3, *grad_d = turn(product, weights_c, middle, dy, gains)
    gate_low, up_low, *grad_g = feed_back(low, weights_c, by_gate, by_up, normed)
    sum_d = core_sum_by_far(grad_d[0], grad_d[1:], n, after=(gate_low,))
    sum_g = core_sum(grad_g[0], grad_g[1:], n, after=sum_d[:1])
    dx1, gain12, do, *grad_u = middle_back(
        gate_low, up_low, weights_b, middle, a, dy, gains, normed, o, after=sum_g[:1]
    )
    sum_g = near_sum_first(sum_g, n, after=(do,))
    dq_low, dkv_before, dkv_own, qk_grad = attend_back(
        probs, do, q, k, v, q_raw, k_raw, cosine, sine, qk_gain, after=sum_g[:1]
    )
    sum_g = near_sum_second(sum_g, n, after=(dq_low,))
    for step in reversed(range(1, steps)):
        sum_d = far_fold(sum_d, n, step, after=sum_g[:1], us=5)
    sum_u = core_sum(grad_u[0], grad_u[1:], n, after=sum_d[:1])
    dh_before, dh, *grad_a = project_back(
        [dq_low, dkv_before, dkv_own, qk_grad, hidden, x, qk_order, gain3, gain12],
        weights_a,
        after=sum_u[:1],
    )
    sum_a = core_sum(grad_a[0], grad_a[1:], n)
    before, own, mixed = input_back(
        dh_before, dh, x, gains, dx1, order, y_low, after=sum_a[:1]
    )
    sum_u = near_sum_first(sum_u, n, after=(own,), us=4)
    sum_d = far_fold(sum_d, n, 0, after=sum_u[:1])
    sum_a = near_sum_first(sum_a, n, after=sum_d[:1])
    sum_g = far_sum_first(sum_g, n, after=sum_a[:1])
    sum_d = near_sum_first(sum_d, n, after=sum_g[:1])
    before, behind = to_device_before(before, n, first, after=sum_d[:1])
    sum_a = near_sum_far([sum_a, sum_u], n, 2, after=(before,))
    ff = grad_d[0].shape[1]
    sum_a = far_sum_first(sum_a, n)
    input_grad, token = join_halo(own, behind, after=sum_a[:1])
    sum_g, token = far_sum_last(sum_g, n, shard, ((0, ff),), after=(token,))
    sum_d, token = near_sum_last(sum_d, n, shard, (0, ff), after=(token,))
    sum_q, sum_k, sum_v, norm_sums, qk_sums, sum_u, sum_o, _ = far_sum_last(
        sum_a, n, shard, ((0, 1024, 1280, 1536, 1664), (0, ff, ff + 1024)),
        gains_at=1536, gain_shapes=(norm_gains.shape, (1, qk_shard)), after=(token,),
    )
    return (
        mixed,
        input_grad,
        sum_q,
        sum_k,
        sum_v,
        sum_o.T,
        sum_g,
        sum_u,
        sum_d.T,
        norm_sums,
        qk_sums.reshape(qk_shard),
    )


def solution(mesh):
    return jax.shard_map(
        on_device,
        mesh=mesh,
        in_specs=(
            P("seq", None),
            P(),
            P("seq", None),
            P("seq", None),
            P("seq", None),
            P(None, "seq"),
            P("seq", None),
            P("seq", None),
            P(None, "seq"),
            P(None, "seq"),
            P("seq"),
            P("seq", None),
        ),
        out_specs=(
            P("seq", None),
            P("seq", None),
            P("seq", None),
            P("seq", None),
            P("seq", None),
            P(None, "seq"),
            P("seq", None),
            P("seq", None),
            P(None, "seq"),
            P(None, "seq"),
            P("seq"),
        ),
        check_vma=False,
    )
```

```python
import functools

import jax
import jax.numpy as jnp
import numpy as np
from jax import lax
from jax.experimental import pallas as pl
from jax.experimental.pallas import tpu as pltpu
from jax.sharding import PartitionSpec as P

H = 4
HD = 256
WINDOW = 512
LONGEST = 2048
EXTRA = 128
EIGHT = 8
FF_CHUNK = 512
BLOCK = 128
REACH = BLOCK + WINDOW
MIB = 1024 * 1024

epsilon = 1e-06
bf16 = jnp.bfloat16
f32 = jnp.float32


def far_bits(n):
    bits = [1 << i for i in range(n.bit_length() - 1)]
    rest = [b for b in bits[1:] if b not in near_pair(n)]
    return rest, rest[::-1]


def far_slots(bits):
    slots = [0]
    for b in bits:
        slots = slots + [s | b for s in slots]
    return slots


def near_pair(n):
    return (2, 8) if n > 64 else (2, 4)


def to_partner(x, n, masks):
    return lax.ppermute(x, "seq", [(i, i ^ masks[i & 1]) for i in range(n)])


def row_table(n, shard):
    first, second = near_pair(n)
    main = whole_tiles(shard)
    count = n // 8
    inner = [(i, r) for i in range(count) for r in range(main)]
    inner += [(i, r) for i in range(count) for r in range(main, shard)]

    def offsets(a, b, bits):
        far = far_slots(bits)
        return [m ^ far[i] for m in (0, a, b, a | b) for i, _ in inner]

    even_bits, odd_bits = far_bits(n)
    even, odd = offsets(first, second, even_bits), offsets(second, first, odd_bits)
    return (
        np.array(even + [1 ^ m for m in odd], np.int32),
        np.array(odd + [1 ^ m for m in even], np.int32),
        np.array([r for _, r in inner] * 8, np.int32),
    )


def nn(left, right):
    return jnp.dot(left, right, preferred_element_type=f32)


def tn(left, right):
    return lax.dot_general(left, right, (((0,), (0,)), ((), ())), preferred_element_type=f32)


def nt(left, right):
    return lax.dot_general(left, right, (((1,), (1,)), ((), ())), preferred_element_type=f32)


def inverse_rms(values):
    return lax.rsqrt(jnp.mean(values * values, axis=-1, keepdims=True) + epsilon)


def rms_back(values, gain, grad):
    scale = inverse_rms(values)
    hat = values * scale
    inner = grad * gain
    mean = jnp.mean(inner * hat, axis=-1, keepdims=True)
    return scale * (inner - hat * mean), jnp.sum(grad * hat, axis=0, keepdims=True)


def rotate(values, cosine, sine):
    half = values.shape[-1] // 2
    a, b = values[:, :half], values[:, half:]
    return jnp.concatenate([a * cosine - b * sine, b * cosine + a * sine], axis=-1)


def rotate_back(values, cosine, sine):
    half = values.shape[-1] // 2
    a, b = values[:, :half], values[:, half:]
    return jnp.concatenate([a * cosine + b * sine, b * cosine - a * sine], axis=-1)


def call(kernel, outs, args, us, scratch=(), after=(), room=8, result=False):
    given, extra = len(args), len(after)

    def body(*refs):
        if result:
            *refs, token = refs
            token[...] = jnp.zeros_like(token)
        kernel(*refs[:given], *refs[given + extra :])

    if result:
        outs = [pltpu.HBM(o.shape, o.dtype) for o in outs] + [shaped((8, 128), f32)]
    return pl.pallas_call(
        body,
        in_specs=[pl.BlockSpec(memory_space=pltpu.VMEM)] * given
        + [pl.BlockSpec(memory_space=pl.ANY)] * extra,
        out_specs=[pl.BlockSpec(memory_space=pltpu.VMEM)] * len(outs),
        out_shape=outs,
        scratch_shapes=scratch,
        compiler_params=pltpu.CompilerParams(vmem_limit_bytes=room * MIB),
        cost_estimate=pl.CostEstimate(
            flops=int(us * 10**9), bytes_accessed=int(us * 10**6), transcendentals=0
        ),
    )(*args, *after)


def shaped(shape, dtype):
    return jax.ShapeDtypeStruct(shape, dtype)


def join_rows(parts, cols=slice(None)):
    return jnp.concatenate([p[:, cols] for p in parts], axis=0)


def whole_tiles(rows):
    return rows // 16 * 16


def padded(cols):
    return -(-cols // 512) * 512


def in_tiles(rows):
    return rows == 20


def travel_shape(rows, cols):
    return (16, padded(cols) * 5 // 4) if in_tiles(rows) else (rows, cols)


def to_tiles(values):
    rows, cols = values.shape
    if not in_tiles(rows):
        return values
    wide = padded(cols)
    if wide > cols:
        values = jnp.concatenate([values, jnp.zeros((rows, wide - cols), f32)], axis=1)
    quarter = wide // 4
    rest = [values[16:, k * quarter : (k + 1) * quarter] for k in range(4)]
    return jnp.concatenate([values[:16], jnp.concatenate(rest, axis=0)], axis=1)


def tile_kernel(counts, *refs):
    total = sum(counts) + 2
    given, outs = refs[:total], refs[total : total + len(counts)]
    held, sem = refs[total + len(counts) : -1], refs[-1]
    copies = [
        pltpu.make_async_copy(source, target, sem.at[i])
        for i, (source, target) in enumerate(zip(given, held))
    ]
    for copy in copies:
        copy.start()
    for copy in copies:
        copy.wait()
    *held, norm_gains, qk_gains = held
    shard = norm_gains.shape[1]
    rows = [
        jnp.concatenate([g[...].astype(f32), jnp.zeros((g.shape[0], EXTRA - g.shape[1]), f32)], axis=1)
        for g in (norm_gains, qk_gains)
    ]
    rows.append(jnp.zeros((EXTRA - 5, EXTRA), f32))
    extra = jnp.concatenate(rows, axis=0).T[:shard]
    for group, (count, out) in enumerate(zip(counts, outs)):
        parts = [p[...].astype(f32) for p in held[:count]]
        held = held[count:]
        if group == 0:
            parts.append(extra)
        out[...] = to_tiles(jnp.concatenate(parts, axis=1)).astype(bf16)


def travelling(norm_gains, qk_gains, *groups):
    counts = [len(g) for g in groups]
    given = [w for g in groups for w in g] + [norm_gains, qk_gains]
    outs = []
    for i, g in enumerate(groups):
        cols = sum(w.shape[1] for w in g) + (EXTRA if i == 0 else 0)
        outs.append(shaped(travel_shape(g[0].shape[0], cols), bf16))
    return pl.pallas_call(
        functools.partial(tile_kernel, counts),
        in_specs=[pl.BlockSpec(memory_space=pltpu.HBM)] * len(given),
        out_specs=[pl.BlockSpec(memory_space=pltpu.VMEM)] * len(outs),
        out_shape=outs,
        scratch_shapes=[pltpu.VMEM(w.shape, bf16) for w in given]
        + [pltpu.SemaphoreType.DMA((len(given),))],
        compiler_params=pltpu.CompilerParams(vmem_limit_bytes=8 * MIB),
    )(*[pltpu.with_memory_space_constraint(w, pltpu.HBM) for w in given])


def stack_kernel(*refs):
    count = len(refs) // 3
    for i in range(count):
        a, b, out = refs[2 * i], refs[2 * i + 1], refs[2 * count + i]
        rows = a.shape[0]
        if rows % 16 == 0:
            out[:rows] = a[...]
            out[rows:] = b[...]
        else:
            both = [a[...].astype(f32), b[...].astype(f32)]
            out[...] = jnp.concatenate(both, axis=0).astype(bf16)


def stack(*pairs, after=()):
    outs = [shaped((2 * a.shape[0], a.shape[1]), bf16) for a, _ in pairs]
    return call(stack_kernel, outs, [x for pair in pairs for x in pair], us=0.1, after=after)


def pack_kernel(pieces, blocks, out):
    count = len(pieces)
    share, cols = out.shape[0] // blocks, out.shape[1]
    rows = share // count
    main = whole_tiles(rows)
    height, wide = travel_shape(rows, cols)
    quarter = padded(cols) // 4
    for block in range(blocks):
        at = block * share
        starts = [(ref, begin + block * height) for ref, begin in pieces]
        if main:
            for i, (ref, begin) in enumerate(starts):
                out[at + i * main : at + (i + 1) * main] = ref[begin : begin + main, :cols]
        at = at + main * count
        if in_tiles(rows):
            rest = [ref[begin : begin + 16, 4 * quarter :].astype(f32) for ref, begin in starts]
            for k in range(4):
                end = min((k + 1) * quarter, cols)
                part = jnp.concatenate([r[4 * k : 4 * k + 4] for r in rest], axis=0)
                out[at : at + 4 * count, k * quarter : end] = part[:, : end - k * quarter].astype(
                    bf16
                )
        elif rows > main:
            rest = [
                ref[...].astype(f32)[begin + main : begin + rows] for ref, begin in starts
            ]
            out[at : at + (rows - main) * count] = jnp.concatenate(rest, axis=0).astype(bf16)


def pack(arrays, rows, cols, blocks, n, parts=1, after=()):
    count = n // 8
    height = travel_shape(rows, cols)[0] * blocks
    held = count // len(arrays)
    total = rows * count * blocks

    def kernel(*refs):
        given = refs[: len(arrays)]
        pieces = [(ref, h * height) for ref in given for h in range(held)]
        if parts == 1:
            pack_kernel(pieces, blocks, refs[-1])
        else:
            for block, out in enumerate(refs[len(arrays) :]):
                shift = block * height // blocks
                pack_kernel([(ref, at + shift) for ref, at in pieces], 1, out)

    outs = [shaped((total // parts, cols), bf16)] * parts
    return call(kernel, outs, arrays, us=0.1, after=after)


def far_step(block, n, step):
    even, odd = far_bits(n)
    return to_partner(block, n, (even[step], odd[step]))


def far_direct(block, n):
    even, odd = far_bits(n)
    slots = zip(far_slots(even)[1:], far_slots(odd)[1:])
    return [block] + [to_partner(block, n, masks) for masks in slots]


def start_kernel(a, b, one, out, one_out):
    stack_kernel(a, b, out)
    one_out[...] = one[...]


def hold_kernel(*refs):
    half = len(refs) // 2
    for value, out in zip(refs[:half], refs[half:]):
        out[...] = value[...]


def hold(*values, after):
    return call(hold_kernel, [shaped(v.shape, v.dtype) for v in values], values, 0.2, after=after)


def cut_kernel(whole, upper, lower):
    rows = upper.shape[0]
    upper[...] = whole[:rows]
    lower[...] = whole[rows:]


def cut(whole, after):
    rows, cols = whole.shape
    upper = rows // 32 * 16 + (16 if rows % 32 else 0)
    outs = [shaped((upper, cols), bf16), shaped((rows - upper, cols), bf16)]
    return call(cut_kernel, outs, [whole], us=0.1, after=after)


def far_gather(blocks, n, joins):
    steps = len(far_bits(n)[0])
    for k in range(steps - 1):
        got = [far_step(b, n, k) for b in blocks]
        blocks = stack(*zip(blocks, got), after=joins[k] if k < len(joins) else ())
    return [(b, far_step(b, n, steps - 1)) for b in blocks]


def to_first(x, n):
    first, second = near_pair(n)
    return to_partner(x, n, (first, second))


def to_second(x, n):
    first, second = near_pair(n)
    return to_partner(x, n, (second, first))


def near_pieces(own, n, direct=False):
    first, second = near_pair(n)
    a, b = to_first(own, n), to_second(own, n)
    return [own, a, b, to_partner(own, n, (first | second,) * 2) if direct else to_second(a, n)]


def to_core(pieces, n):
    return [to_partner(p, n, (1, 1)) for p in pieces]


def fold_kernel(count, *refs):
    given, outs = refs[:count], refs[count:]
    mine, got = given[0], given[1:]
    rows = outs[0].shape[0]
    height = got[0].shape[0]
    if rows % 16 == 0 and height % rows == 0:
        per = height // rows
        for i, out in enumerate(outs):
            other = got[i // per][(i % per) * rows : (i % per + 1) * rows]
            part = mine[i * rows : (i + 1) * rows]
            out[...] = (part.astype(f32) + other.astype(f32)).astype(bf16)
    else:
        total = mine[...].astype(f32)
        total = total + jnp.concatenate([g[...].astype(f32) for g in got], axis=0)
        for i, out in enumerate(outs):
            out[...] = total[i * rows : (i + 1) * rows].astype(bf16)


def fold(mine, got, after=(), us=0.5):
    rows, cols = mine.shape
    outs = [shaped((rows // 2, cols), bf16)] * 2
    kernel = functools.partial(fold_kernel, 1 + len(got))
    return call(kernel, outs, [mine, *got], us=us, after=after)


def wide_fold_kernel(mine, *refs):
    got, (keep, send) = refs[:-2], refs[-2:]
    rows = got[0].shape[0]
    per = keep.shape[0] // rows
    for i, other in enumerate(got):
        out = keep if i < per else send
        at = (i % per) * rows
        part = mine[i * rows : (i + 1) * rows].astype(f32)
        out[at : at + rows] = (part + other[...].astype(f32)).astype(bf16)


def core_sum(top, sends, n, after=()):
    rows, cols = top.shape
    outs = [shaped((rows // 2, cols), bf16)] * 2
    return call(wide_fold_kernel, outs, [top, *to_core(sends, n)], us=0.7, after=after)


def core_sum_by_far(top, sends, n, after=()):
    rows, cols = top.shape
    count, blocks = n // 8, 4
    share = rows // blocks
    shard = share // count
    main = whole_tiles(shard)
    rest, done = shard - main, main * count
    height, wide = travel_shape(shard, cols)

    def kernel(mine, *refs):
        got, (keep, send) = refs[:-2], refs[-2:]
        per = blocks // len(got)
        tiles = []
        for block in range(blocks):
            other = got[block // per][(block % per) * share : (block % per + 1) * share]
            total = mine[block * share : (block + 1) * share].astype(f32) + other.astype(f32)
            for i in range(count):
                parts = []
                if main:
                    parts.append(total[i * main : (i + 1) * main])
                if rest:
                    parts.append(total[done + i * rest : done + (i + 1) * rest])
                tiles.append((i, block, to_tiles(jnp.concatenate(parts, axis=0))))
        tiles = [t for _, _, t in sorted(tiles, key=lambda item: item[:2])]
        half = len(tiles) // 2
        keep[...] = jnp.concatenate(tiles[:half], axis=0).astype(bf16)
        send[...] = jnp.concatenate(tiles[half:], axis=0).astype(bf16)

    outs = [shaped((count // 2 * blocks * height, wide), bf16)] * 2
    return call(kernel, outs, [top, *to_core(sends, n)], us=1.5, after=after)


def far_fold(halves, n, step, after=(), us=0.5):
    keep, send = halves
    return fold(keep, [far_step(send, n, step)], after, us)


def near_sum_last(halves, n, shard, cuts, after=()):
    keep, send = halves
    outs = [shaped((shard, e - b), f32) for b, e in zip(cuts[:-1], cuts[1:])]
    return call(
        functools.partial(far_sum_kernel, (cuts,), None), outs, [keep, to_first(send, n)], us=1,
        after=after, result=True,
    )


def near_sum_first(halves, n, after=(), us=0.5):
    keep, send = halves
    return fold(keep, [to_second(send, n)], after, us)


def fold_both_kernel(*refs):
    given, (keep, send) = refs[:4], refs[4:]
    rows, cols = keep.shape
    cols = cols // 2
    for i in range(2):
        mine, got = given[2 * i : 2 * i + 2]
        for j, out in enumerate((keep, send)):
            part = slice(j * rows, (j + 1) * rows)
            out[:, i * cols : (i + 1) * cols] = (
                mine[part].astype(f32) + got[part].astype(f32)
            ).astype(bf16)


def near_sum_first_both(one, two, n, after=()):
    args = [x for keep, send in (one, two) for x in (keep, to_second(send, n))]
    rows, cols = one[0].shape
    outs = [shaped((rows // 2, 2 * cols), bf16)] * 2
    return call(fold_both_kernel, outs, args, us=5, after=after)


def split_kernel(count, mine, got, keep, send):
    total = mine[...].astype(f32) + got[...].astype(f32)
    rows = total.shape[0] // count
    main = whole_tiles(rows)
    rest, done = rows - main, main * count
    slots = []
    for i in range(count):
        parts = []
        if main:
            parts.append(total[i * main : (i + 1) * main])
        if rest:
            parts.append(total[done + i * rest : done + (i + 1) * rest])
        slots.append(to_tiles(jnp.concatenate(parts, axis=0)))
    keep[...] = jnp.concatenate(slots[: count // 2], axis=0).astype(bf16)
    send[...] = jnp.concatenate(slots[count // 2 :], axis=0).astype(bf16)


def near_sum_second(halves, n, after=()):
    keep, send = halves
    rows, cols = keep.shape
    count = n // 8
    height, wide = travel_shape(rows // count, cols)
    outs = [shaped((count // 2 * height, wide), bf16)] * 2
    return call(
        functools.partial(split_kernel, count), outs, [keep, to_first(send, n)], us=1, after=after
    )


def slots_kernel(groups, count, *refs):
    outs = refs[2 * groups :]
    slots = [[] for _ in range(count)]
    for g in range(groups):
        total = refs[2 * g][...].astype(f32) + refs[2 * g + 1][...].astype(f32)
        rows = total.shape[0] // count
        main = whole_tiles(rows)
        rest, done = rows - main, main * count
        for i in range(count):
            parts = []
            if main:
                parts.append(total[i * main : (i + 1) * main])
            if rest:
                parts.append(total[done + i * rest : done + (i + 1) * rest])
            slots[i].append(to_tiles(jnp.concatenate(parts, axis=0)))
    per = count // len(outs)
    for i, parts in enumerate(slots):
        values = jnp.concatenate(parts, axis=1).astype(bf16)
        height = values.shape[0]
        if per == 1:
            outs[i][...] = values
        elif height % 16 == 0:
            outs[i // per][i % per * height : (i % per + 1) * height] = values
    if per > 1 and height % 16 != 0:
        for j, out in enumerate(outs):
            values = [jnp.concatenate(p, axis=1) for p in slots[j * per : (j + 1) * per]]
            out[...] = jnp.concatenate(values, axis=0).astype(bf16)


def near_sum_far(groups, n, parts, after=()):
    count = n // 8
    args, wide = [], 0
    for keep, send in groups:
        args += [keep, to_first(send, n)]
        height, cols = travel_shape(keep.shape[0] // count, keep.shape[1])
        wide += cols
    outs = [shaped((height * count // parts, wide), bf16)] * parts
    kernel = functools.partial(slots_kernel, len(groups), count)
    return call(kernel, outs, args, us=1, after=after)


def far_sum_first(halves, n, after=()):
    keep, send = halves
    for k in reversed(range(1, len(far_bits(n)[0]))):
        keep, send = fold(keep, [far_step(send, n, k)], after)
        after = ()
    return keep, send


def far_sum_kernel(groups, gains_at, *refs):
    count = sum(len(cuts) - 1 for cuts in groups) + (gains_at is not None)
    given, outs = refs[:-count], refs[-count:]
    total = given[0][...].astype(f32)
    for got in given[1:]:
        total = total + got[...].astype(f32)
    rows = outs[0].shape[0]
    begin_at = 0
    for number, cuts in enumerate(groups):
        wide = padded(cuts[-1]) if in_tiles(rows) else cuts[-1]
        part = total[:, begin_at : begin_at + wide]
        if in_tiles(rows):
            quarter = wide // 4
            rest = total[:, begin_at + wide : begin_at + wide + quarter]
            rest = [rest[4 * k : 4 * k + 4] for k in range(4)]
            part = jnp.concatenate([part, jnp.concatenate(rest, axis=1)], axis=0)
            begin_at += quarter
        begin_at += wide
        for begin, end in zip(cuts[:-1], cuts[1:]):
            values = part[:, begin:end]
            if number == 0 and begin == gains_at:
                values = jnp.concatenate([values, jnp.zeros((EXTRA - rows, EXTRA), f32)], axis=0).T
                norms, qk, *outs = outs
                norms[...] = values[: norms.shape[0], :rows]
                qk[...] = values[norms.shape[0] : norms.shape[0] + 1, : qk.shape[1]]
            else:
                outs[0][...] = values
                outs = outs[1:]


def result_shapes(shard, groups, gains_at, gain_shapes):
    outs = []
    for number, cuts in enumerate(groups):
        for begin, end in zip(cuts[:-1], cuts[1:]):
            if number == 0 and begin == gains_at:
                outs += [shaped(shape, f32) for shape in gain_shapes]
            else:
                outs.append(shaped((shard, end - begin), f32))
    return outs


def far_sum_last(halves, n, shard, groups, gains_at=None, gain_shapes=(), after=()):
    keep, send = halves
    outs = result_shapes(shard, groups, gains_at, gain_shapes)
    kernel = functools.partial(far_sum_kernel, groups, gains_at)
    args = [keep, far_step(send, n, 0)]
    return call(kernel, outs, args, us=1, after=after, result=True)


def table_kernel(near, near_col, freqs, place, qk_place, first, cosine, sine, order, qk_order, first_out):
    count = cosine.shape[0]
    ahead = near.shape[1] - count
    steps = freqs[...]
    for c in range(count // 256):
        reach = slice(c * 256, c * 256 + ahead + 256)
        here = near_col[ahead + c * 256 : ahead + (c + 1) * 256]
        i = lax.broadcasted_iota(jnp.int32, (256, ahead + 256), 0) + ahead
        j = lax.broadcasted_iota(jnp.int32, (256, ahead + 256), 1)
        same = (here == near[:, reach]) & (j < i)
        position = jnp.sum(same.astype(f32), axis=1, keepdims=True)
        angles = position * steps
        cosine[c * 256 : (c + 1) * 256] = jnp.cos(angles)
        sine[c * 256 : (c + 1) * 256] = jnp.sin(angles)
    i = lax.broadcasted_iota(jnp.int32, order.shape, 0)
    order[...] = (i == place[...]).astype(f32).astype(bf16)
    j = lax.broadcasted_iota(jnp.int32, qk_order.shape, 1)
    qk_order[...] = (qk_place[...] == j).astype(f32).astype(bf16)
    first_out[...] = jnp.broadcast_to(first[...], first_out.shape)


def tables(near, rows, place, qk_place, width, first, after=()):
    freqs = np.float32(10000.0) ** (-2.0 * np.arange(HD // 2, dtype=np.float32) / np.float32(HD))
    args = [
        near[None, :], near[:, None], jnp.asarray(freqs)[None, :], place[None, :], qk_place[:, None],
        first,
    ]
    outs = [
        shaped((2 * rows, HD // 2), f32), shaped((2 * rows, HD // 2), f32),
        shaped((width, width), bf16), shaped((width, 2 * HD), bf16), shaped((8, 128), f32),
    ]
    return call(table_kernel, outs, args, us=3, after=after)


def permute_kernel(tokens_before, tokens, cotangent, order, x, dy):
    table = order[...]
    rows = tokens.shape[0]
    x[:rows] = nn(tokens_before[...], table).astype(bf16)
    x[rows:] = nn(tokens[...], table).astype(bf16)
    dy[...] = nn(cotangent[...], table).astype(bf16)


def permute(tokens_before, tokens, cotangent, order, after=()):
    rows, width = tokens.shape
    outs = [shaped((2 * rows, width), bf16), shaped((rows, width), bf16)]
    args = [tokens_before, tokens, cotangent, order]
    return call(permute_kernel, outs, args, us=2, after=after)


def attend_kernel(x, qk_order, cosine, sine, seg_q, seg_k, *refs):
    pieces = refs[:-10]
    hidden, q_raw, k_raw, q_out, k_out, v_out, probs, o, gains, qk_gain = refs[-10:]
    rows = q_raw.shape[0]
    w_q = join_rows(pieces, slice(0, 1024))
    w_kv = join_rows(pieces, slice(1024, 1536))
    gain_rows = join_rows(pieces, slice(1536, 1664)).astype(f32).T[:8]
    gains[...] = gain_rows
    gain_qk = nn(gain_rows.astype(bf16), qk_order[...])
    qk_gain[...] = gain_qk
    gain_q, gain_k = gain_qk[4:5, :HD], gain_qk[4:5, HD:]
    for c in range(2 * rows // 256):
        part = pl.ds(c * 256, 256)
        xs = x[part].astype(f32)
        hs = (xs * inverse_rms(xs) * gain_rows[0:1]).astype(bf16)
        hidden[part] = hs
        cs, sn = cosine[part], sine[part]
        kv = nn(hs, w_kv)
        raw = kv[:, :HD]
        k_raw[part] = raw
        k_out[part] = rotate(raw * inverse_rms(raw) * gain_k, cs, sn).astype(bf16)
        v_out[part] = kv[:, HD:].astype(bf16)
        if c * 256 >= rows:
            own = pl.ds(c * 256 - rows, 256)
            qs = nn(hs, w_q)
            q_raw[own] = qs
            for h in range(H):
                raw = qs[:, h * HD : (h + 1) * HD]
                q_out[own, h * HD : (h + 1) * HD] = rotate(
                    raw * inverse_rms(raw) * gain_q, cs, sn
                ).astype(bf16)
    for b in range(rows // BLOCK):
        mine = pl.ds(b * BLOCK, BLOCK)
        reach = pl.ds(b * BLOCK, REACH)
        q_rows = q_out[mine] * bf16(1.0 / 16.0)
        q_stack = jnp.concatenate([q_rows[:, h * HD : (h + 1) * HD] for h in range(H)], axis=0)
        scores = nt(q_stack, k_out[reach])
        i = lax.broadcasted_iota(jnp.int32, (BLOCK, REACH), 0)
        j = lax.broadcasted_iota(jnp.int32, (BLOCK, REACH), 1)
        allowed = (j > i) & (j <= i + WINDOW) & (seg_q[mine] == seg_k[b])
        allowed = jnp.concatenate([allowed.astype(f32)] * H, axis=0)
        weights = jnp.exp(scores) * allowed
        total = jnp.sum(weights, axis=-1, keepdims=True)
        p = (weights * (1.0 / total)).astype(bf16)
        probs[b] = p
        out = nn(p, v_out[reach])
        for h in range(H):
            o[mine, h * HD : (h + 1) * HD] = out[h * BLOCK : (h + 1) * BLOCK].astype(bf16)


def attend(x, pieces, qk_order, cosine, sine, seg_q, seg_k, after):
    rows = x.shape[0] // 2
    width = x.shape[1]
    return call(
        attend_kernel,
        [
            shaped((2 * rows, width), bf16),
            shaped((rows, H * HD), f32),
            shaped((2 * rows, HD), f32),
            shaped((rows, H * HD), bf16),
            shaped((2 * rows, HD), bf16),
            shaped((2 * rows, HD), bf16),
            shaped((rows // BLOCK, H * BLOCK, REACH), bf16),
            shaped((rows, H * HD), bf16),
            shaped((8, width), f32),
            shaped((8, 2 * HD), f32),
        ],
        [x, qk_order, cosine, sine, seg_q, seg_k, *pieces],
        us=0.1,
        after=after,
    )


def gelu_parts(g):
    c0, c1 = 0.7978845608028654, 0.044715
    square = g * g
    t = jnp.tanh(g * (c0 + (c0 * c1) * square))
    half = 0.5 + 0.5 * t
    value = g * half
    slope = half + value * ((1.0 - t) * (c0 + (3.0 * c0 * c1) * square))
    return value, slope


def join_kernel(o, x, gains, *refs):
    pieces, (a_out, middle, normed) = refs[:-3], refs[-3:]
    rows = o.shape[0]
    w_o = join_rows(pieces, slice(0, H * HD))
    for c in range(rows // 256):
        part = pl.ds(c * 256, 256)
        a = nt(o[part], w_o)
        a_out[part] = a
        x1 = x[rows + c * 256 : rows + (c + 1) * 256].astype(f32) + a * inverse_rms(a) * gains[1:2]
        middle[part] = x1
        normed[part] = (x1 * inverse_rms(x1) * gains[2:3]).astype(bf16)


def join(o, pieces, x, gains):
    rows, width = o.shape[0], x.shape[1]
    outs = [shaped((rows, width), f32), shaped((rows, width), f32), shaped((rows, width), bf16)]
    return call(join_kernel, outs, [o, x, gains, *pieces], us=0.1)


def feed_kernel(normed, *refs):
    pieces, (product, by_gate, by_up) = refs[:-3], refs[-3:]
    rows, ff = product.shape
    for j in range(ff // FF_CHUNK):
        cols = slice(j * FF_CHUNK, (j + 1) * FF_CHUNK)
        w_g = join_rows(pieces, slice(H * HD + cols.start, H * HD + cols.stop))
        w_u = join_rows(pieces, slice(H * HD + ff + cols.start, H * HD + ff + cols.stop))
        for c in range(rows // 256):
            part = pl.ds(c * 256, 256)
            h2 = normed[part]
            g = nn(h2, w_g)
            u = nn(h2, w_u)
            value, slope = gelu_parts(g)
            product[part, cols] = (value * u).astype(bf16)
            by_gate[part, cols] = (slope * u).astype(bf16)
            by_up[part, cols] = value.astype(bf16)


def feed(normed, pieces, after=()):
    rows = normed.shape[0]
    ff = (pieces[0].shape[1] - H * HD) // 2
    outs = [shaped((rows, ff), bf16)] * 3
    return call(feed_kernel, outs, [normed, *pieces], us=5, after=after)


def put_grad(grads, cols, values):
    top, *sends = grads
    half = top.shape[0]
    top[:, cols] = values[:half]
    part = half // len(sends)
    for i, send in enumerate(sends):
        send[:, cols] = values[half + i * part : half + (i + 1) * part]


def grad_shapes(width, cols):
    return [shaped((width // 2, cols), bf16)] + [shaped((width // 4, cols), bf16)] * 2


def turn_kernel(product, middle, dy, gains, *refs):
    pieces, (y_low, low, gain_grad, *grads) = refs[:-6], refs[-6:]
    ff = product.shape[1]
    w_d = join_rows(pieces)
    total = jnp.zeros((1, dy.shape[1]), f32)
    for c in range(dy.shape[0] // 256):
        part = pl.ds(c * 256, 256)
        f = nt(product[part], w_d)
        grad = dy[part].astype(f32)
        y = middle[part] + f * inverse_rms(f) * gains[3:4]
        y_low[part] = y.astype(bf16)
        df, dgain = rms_back(f, gains[3:4], grad)
        low[part] = df.astype(bf16)
        total = total + dgain
    gain_grad[...] = jnp.broadcast_to(total, gain_grad.shape)
    for j in range(ff // FF_CHUNK):
        cols = slice(j * FF_CHUNK, (j + 1) * FF_CHUNK)
        grad = tn(low[...], product[:, cols]).astype(bf16)
        put_grad(grads, cols, grad)


def turn(product, pieces, middle, dy, gains):
    rows, width = middle.shape
    return call(
        turn_kernel,
        [
            shaped((rows, width), bf16),
            shaped((rows, width), bf16),
            shaped((8, width), f32),
            *grad_shapes(width, product.shape[1]),
        ],
        [product, middle, dy, gains, *pieces],
        us=6,
    )


def feed_back_kernel(low, by_gate, by_up, normed, *refs):
    pieces, (gate_low, up_low, *grads) = refs[:-5], refs[-5:]
    rows, ff = gate_low.shape
    for j in range(ff // FF_CHUNK):
        cols = slice(j * FF_CHUNK, (j + 1) * FF_CHUNK)
        w_d = join_rows(pieces, cols)
        for c in range(rows // 256):
            part = pl.ds(c * 256, 256)
            dm = nn(low[part], w_d)
            gate_low[part, cols] = (dm * by_gate[part, cols].astype(f32)).astype(bf16)
            up_low[part, cols] = (dm * by_up[part, cols].astype(f32)).astype(bf16)
        put_grad(grads, cols, tn(normed[...], gate_low[:, cols]).astype(bf16))


def feed_back(low, pieces, by_gate, by_up, normed):
    rows, width = low.shape
    ff = by_gate.shape[1]
    return call(
        feed_back_kernel,
        [shaped((rows, ff), bf16)] * 2 + grad_shapes(width, ff),
        [low, by_gate, by_up, normed, *pieces],
        us=4,
    )


def middle_back_kernel(gate_low, up_low, middle, a, dy, gains, normed, o, *refs):
    pieces, (dx1, gain_grad, do, *grads) = refs[:-6], refs[-6:]
    rows, ff = gate_low.shape
    w_g = join_rows(pieces, slice(H * HD, H * HD + ff))
    w_u = join_rows(pieces, slice(H * HD + ff, H * HD + 2 * ff))
    normed_grad = nt(gate_low[...], w_g) + nt(up_low[...], w_u)
    for j in range(ff // FF_CHUNK):
        cols = slice(j * FF_CHUNK, (j + 1) * FF_CHUNK)
        put_grad(grads, cols, tn(normed[...], up_low[:, cols]).astype(bf16))
    sum1 = jnp.zeros((1, dy.shape[1]), f32)
    sum2 = jnp.zeros((1, dy.shape[1]), f32)
    lows = []
    for c in range(rows // 256):
        part = slice(c * 256, (c + 1) * 256)
        back, dgain2 = rms_back(middle[part], gains[2:3], normed_grad[part])
        dx = dy[part].astype(f32) + back
        dx1[part] = dx
        da, dgain1 = rms_back(a[part], gains[1:2], dx)
        lows.append(da.astype(bf16))
        sum1, sum2 = sum1 + dgain1, sum2 + dgain2
    gain_grad[...] = jnp.concatenate([sum1, sum2, jnp.zeros((6, dy.shape[1]), f32)], axis=0)
    low = jnp.concatenate(lows, axis=0)
    do[...] = nn(low, join_rows(pieces, slice(0, H * HD))).astype(bf16)
    put_grad(grads, slice(ff, ff + H * HD), tn(low, o[...]).astype(bf16))


def middle_back(gate_low, up_low, pieces, middle, a, dy, gains, normed, o, after):
    rows, width = middle.shape
    return call(
        middle_back_kernel,
        [
            shaped((rows, width), f32),
            shaped((8, width), f32),
            shaped((rows, H * HD), bf16),
            *grad_shapes(width, gate_low.shape[1] + H * HD),
        ],
        [gate_low, up_low, middle, a, dy, gains, normed, o, *pieces],
        us=14,
        after=after,
        room=10,
    )


def attend_back_kernel(
    probs, do, q, k, v, q_raw, k_raw, cosine, sine, qk_gain, dq_low, dkv_before, dkv_own, qk_grad, dk, dv
):
    rows = q_raw.shape[0]
    dk[...] = jnp.zeros_like(dk)
    dv[...] = jnp.zeros_like(dv)
    gain_q, gain_k = qk_gain[4:5, :HD], qk_gain[4:5, HD:]
    sum_q = jnp.zeros((1, HD), f32)

    def stack_heads(values):
        return jnp.concatenate([values[:, h * HD : (h + 1) * HD] for h in range(H)], axis=0)

    def probs_grad(b):
        do_stack = stack_heads(do[pl.ds(b * BLOCK, BLOCK)])
        return do_stack, nt(do_stack, v[pl.ds(b * BLOCK, REACH)])

    blocks = rows // BLOCK
    ahead = probs_grad(0)
    for b in range(blocks):
        do_stack, dp = ahead
        if b + 1 < blocks:
            ahead = probs_grad(b + 1)
        mine = pl.ds(b * BLOCK, BLOCK)
        reach = pl.ds(b * BLOCK, REACH)
        p_low = probs[b]
        p = p_low.astype(f32)
        dv[reach] += tn(p_low, do_stack)
        t = p * dp
        ds = (t - p * jnp.sum(t, axis=-1, keepdims=True)).astype(bf16)
        dk[reach] += tn(ds, stack_heads(q[mine]))
        dq = nn(ds, k[reach]) * (1.0 / 16.0)
        own = pl.ds(rows + b * BLOCK, BLOCK)
        cs, sn = cosine[own], sine[own]
        for h in range(H):
            grad = rotate_back(dq[h * BLOCK : (h + 1) * BLOCK], cs, sn)
            back, dgain = rms_back(q_raw[mine, h * HD : (h + 1) * HD], gain_q, grad)
            dq_low[mine, h * HD : (h + 1) * HD] = back.astype(bf16)
            sum_q = sum_q + dgain
    sum_k = jnp.zeros((1, HD), f32)
    for c in range(2 * rows // 256):
        part = pl.ds(c * 256, 256)
        grad = rotate_back(dk[part] * (1.0 / 16.0), cosine[part], sine[part])
        back, dgain = rms_back(k_raw[part], gain_k, grad)
        out, at = (dkv_before, c * 256) if c * 256 < rows else (dkv_own, c * 256 - rows)
        out[at : at + 256, :HD] = back.astype(bf16)
        out[at : at + 256, HD:] = dv[part].astype(bf16)
        sum_k = sum_k + dgain
    qk_grad[...] = jnp.broadcast_to(jnp.concatenate([sum_q, sum_k], axis=1), qk_grad.shape)


def attend_back(probs, do, q, k, v, q_raw, k_raw, cosine, sine, qk_gain, after):
    rows = q.shape[0]
    return call(
        attend_back_kernel,
        [
            shaped((rows, H * HD), bf16), shaped((rows, 2 * HD), bf16),
            shaped((rows, 2 * HD), bf16), shaped((8, 2 * HD), f32),
        ],
        [probs, do, q, k, v, q_raw, k_raw, cosine, sine, qk_gain],
        us=0.3,
        scratch=[pltpu.VMEM((2 * rows, HD), f32), pltpu.VMEM((2 * rows, HD), f32)],
        after=after,
        room=8,
    )


def project_back_kernel(
    dq_low, dkv_before, dkv_own, qk_grad, hidden, x, qk_order, gain3, gain12, *refs
):
    pieces, (dh_before, dh, *grads) = refs[:-5], refs[-5:]
    rows = dq_low.shape[0]
    put_grad(grads, slice(0, 1024), tn(hidden[rows:], dq_low[...]).astype(bf16))
    grad = tn(hidden[:rows], dkv_before[...]) + tn(hidden[rows:], dkv_own[...])
    put_grad(grads, slice(1024, 1536), grad.astype(bf16))
    w_q = join_rows(pieces, slice(0, 1024))
    w_kv = join_rows(pieces, slice(1024, 1536))
    sum0 = jnp.zeros((1, x.shape[1]), f32)
    for c in range(rows // 256):
        part = pl.ds(c * 256, 256)
        before = x[part].astype(f32)
        grad = nt(dkv_before[part], w_kv)
        dh_before[part] = grad
        sum0 = sum0 + jnp.sum(grad * (before * inverse_rms(before)), axis=0, keepdims=True)
        own = x[rows + c * 256 : rows + (c + 1) * 256].astype(f32)
        grad = nt(dkv_own[part], w_kv) + nt(dq_low[part], w_q)
        dh[part] = grad
        sum0 = sum0 + jnp.sum(grad * (own * inverse_rms(own)), axis=0, keepdims=True)
    qk_spread = nt(qk_grad[...].astype(bf16), qk_order[...])
    rows_of = jnp.concatenate(
        [
            sum0, gain12[0:1], gain12[1:2], gain3[0:1], qk_spread[0:1],
            jnp.zeros((EXTRA - 5, x.shape[1]), f32),
        ],
        axis=0,
    )
    put_grad(grads, slice(1536, 1664), rows_of.T.astype(bf16))


def project_back(args, pieces, after):
    rows, width = args[0].shape[0], args[5].shape[1]
    return call(
        project_back_kernel,
        [shaped((rows, width), f32)] * 2 + grad_shapes(width, pieces[0].shape[1]),
        [*args, *pieces],
        us=8,
        after=after,
    )


def input_back_kernel(dh_before, dh, x, gains, dx1, order, y_low, before, own, mixed):
    rows = dx1.shape[0]
    table = order[...]
    for c in range(rows // 256):
        part = pl.ds(c * 256, 256)
        back, _ = rms_back(x[part].astype(f32), gains[0:1], dh_before[part])
        before[part] = nt(back.astype(bf16), table).astype(bf16)
        mixed[part] = nt(y_low[part], table).astype(bf16)
        mine = x[rows + c * 256 : rows + (c + 1) * 256].astype(f32)
        back, _ = rms_back(mine, gains[0:1], dh[part])
        rest = back + dx1[part]
        total = jnp.zeros_like(rest)
        for _ in range(3):
            piece = rest.astype(bf16)
            rest = rest - piece.astype(f32)
            total = total + nt(piece, table)
        own[part] = total


def input_back(dh_before, dh, x, gains, dx1, order, y_low, after=()):
    outs = [shaped(dx1.shape, bf16), shaped(dx1.shape, f32), shaped(dx1.shape, bf16)]
    args = [dh_before, dh, x, gains, dx1, order, y_low]
    return call(input_back_kernel, outs, args, us=0.3, after=after)


def select_kernel(first, own, other, out):
    pick = first[:1, :1] > 0.5
    out[...] = jnp.where(pick, other[...].astype(f32), own[...].astype(f32)).astype(bf16)


def to_device_before(x, n, first, after=()):
    hop = lax.ppermute(x, "seq", [(i + EIGHT, i) for i in range(0, n - EIGHT, EIGHT)])
    (out,) = call(select_kernel, [shaped(x.shape, bf16)], [first, x, hop], us=0.3, after=after)
    pairs = [(i, i - 1) for i in range(n) if i % EIGHT]
    pairs += [(i, i + EIGHT - 1) for i in range(0, n - EIGHT, EIGHT)]
    return out, lax.ppermute(out, "seq", pairs)


def join_halo_kernel(own, behind, out):
    out[...] = own[...] + behind[...].astype(f32)


def join_halo(own, behind, after=()):
    outs = [shaped(own.shape, f32)]
    return call(join_halo_kernel, outs, [own, behind], us=0.3, after=after, result=True)


def on_device(
    tokens,
    segment_ids,
    w_query,
    w_key,
    w_value,
    w_output,
    w_gate,
    w_up,
    w_down,
    norm_gains,
    qk_gains,
    cotangent,
):
    n = lax.axis_size("seq")
    me = lax.axis_index("seq")
    rows, width = tokens.shape
    shard = w_query.shape[0]
    qk_shard = qk_gains.shape[0]

    travel_a, travel_b, travel_c = travelling(
        norm_gains, qk_gains[None, :], (w_query, w_key, w_value), (w_output.T, w_gate, w_up),
        (w_down.T,),
    )
    cols_a = w_query.shape[1] + w_key.shape[1] + w_value.shape[1] + EXTRA
    cols_b = w_output.shape[0] + w_gate.shape[1] + w_up.shape[1]
    cols_c = w_down.shape[0]

    even, odd, inner = row_table(n, shard)
    device = me ^ jnp.where(me & 1 == 0, jnp.asarray(even), jnp.asarray(odd))
    place = device * shard + inner
    qk_place = jnp.where(inner < qk_shard, device * qk_shard + inner, -1)
    padded_ids = jnp.concatenate([jnp.full((LONGEST + rows,), -1, jnp.int32), segment_ids])
    nearby = lax.dynamic_slice_in_dim(padded_ids, me * rows, 2 * rows + LONGEST)
    keys_segment = nearby[LONGEST:]
    seg_q = keys_segment[rows:, None]
    seg_k = jnp.stack(
        [keys_segment[b * BLOCK : b * BLOCK + REACH] for b in range(rows // BLOCK)]
    )[:, None, :]

    tokens_before = lax.ppermute(tokens, "seq", [(i, i + 1) for i in range(n - 1)])
    steps = len(far_bits(n)[0])
    a_c = to_first(travel_c, n)
    (own_b,) = pack(far_direct(travel_b, n), shard, cols_b, 1, n, after=(a_c,))
    a_b, b_b = to_first(own_b, n), to_second(own_b, n)
    pair_c, block_a = call(
        start_kernel,
        [
            shaped((2 * travel_c.shape[0], travel_c.shape[1]), bf16),
            shaped(travel_a.shape, bf16),
        ],
        [travel_c, a_c, travel_a],
        us=0.2,
        after=(own_b,),
    )
    for step in range(steps - 1):
        block_a, pair_c = stack(
            (block_a, far_step(block_a, n, step)), (pair_c, far_step(pair_c, n, step))
        )
    first = (me % EIGHT == 0).astype(f32).reshape(1, 1)
    cosine, sine, order, qk_order, first = tables(
        nearby, rows, place, qk_place, width, first, after=(own_b,)
    )
    x, dy = permute(tokens_before, tokens, cotangent, order)
    (own_a,) = pack([block_a, far_step(block_a, n, steps - 1)], shard, cols_a, 1, n, after=(x, seg_q, seg_k))
    a_a, b_a = to_first(own_a, n), to_second(own_a, n)
    half_c = pack([pair_c, far_step(pair_c, n, steps - 1)], shard, cols_c, 2, n, after=(own_a,))
    parts_b = cut(a_b, after=(b_b, a_a, b_a, *half_c))
    weights_a = [own_a, a_a, b_a, to_second(a_a, n)]
    weights_a = [*weights_a, *to_core(weights_a, n)]
    hidden, q_raw, k_raw, q, k, v, probs, o, gains, qk_gain = attend(
        x, weights_a, qk_order, cosine, sine, seg_q, seg_k, after=()
    )
    far_half = to_second(half_c[0], n)
    parts_b = hold(*[to_second(p, n) for p in parts_b], after=(o,))
    weights_b = [own_b, a_b, b_b, *parts_b]
    weights_b = [*weights_b, *to_core(weights_b, n)]
    a, middle, normed = join(o, weights_b, x, gains)
    half_c = [*half_c, *cut(far_half, after=(o,))]
    weights_c = [*half_c, *to_core(half_c, n)]
    product, by_gate, by_up = feed(normed, weights_b, after=half_c[1:])
    y_low, low, gain3, *grad_d = turn(product, weights_c, middle, dy, gains)
    gate_low, up_low, *grad_g = feed_back(low, weights_c, by_gate, by_up, normed)
    sum_d = core_sum_by_far(grad_d[0], grad_d[1:], n, after=(gate_low,))
    sum_g = core_sum(grad_g[0], grad_g[1:], n, after=sum_d[:1])
    dx1, gain12, do, *grad_u = middle_back(
        gate_low, up_low, weights_b, middle, a, dy, gains, normed, o, after=sum_g[:1]
    )
    sum_g = near_sum_first(sum_g, n, after=(do,))
    dq_low, dkv_before, dkv_own, qk_grad = attend_back(
        probs, do, q, k, v, q_raw, k_raw, cosine, sine, qk_gain, after=sum_g[:1]
    )
    sum_g = near_sum_second(sum_g, n, after=(dq_low,))
    for step in reversed(range(1, steps)):
        sum_d = far_fold(sum_d, n, step, after=sum_g[:1], us=5)
    sum_u = core_sum(grad_u[0], grad_u[1:], n, after=sum_d[:1])
    dh_before, dh, *grad_a = project_back(
        [dq_low, dkv_before, dkv_own, qk_grad, hidden, x, qk_order, gain3, gain12],
        weights_a,
        after=sum_u[:1],
    )
    sum_a = core_sum(grad_a[0], grad_a[1:], n)
    before, own, mixed = input_back(
        dh_before, dh, x, gains, dx1, order, y_low, after=sum_a[:1]
    )
    sum_u = near_sum_first(sum_u, n, after=(own,), us=4)
    sum_d = far_fold(sum_d, n, 0, after=sum_u[:1])
    sum_a = near_sum_first(sum_a, n, after=sum_d[:1])
    sum_g = far_sum_first(sum_g, n, after=sum_a[:1])
    sum_d = near_sum_first(sum_d, n, after=sum_g[:1])
    before, behind = to_device_before(before, n, first, after=sum_d[:1])
    sum_a = near_sum_far([sum_a, sum_u], n, 2, after=(before,))
    ff = grad_d[0].shape[1]
    sum_a = far_sum_first(sum_a, n)
    input_grad, token = join_halo(own, behind, after=sum_a[:1])
    sum_g, token = far_sum_last(sum_g, n, shard, ((0, ff),), after=(token,))
    sum_d, token = near_sum_last(sum_d, n, shard, (0, ff), after=(token,))
    sum_q, sum_k, sum_v, norm_sums, qk_sums, sum_u, sum_o, _ = far_sum_last(
        sum_a, n, shard, ((0, 1024, 1280, 1536, 1664), (0, ff, ff + 1024)),
        gains_at=1536, gain_shapes=(norm_gains.shape, (1, qk_shard)), after=(token,),
    )
    return (
        mixed,
        input_grad,
        sum_q,
        sum_k,
        sum_v,
        sum_o.T,
        sum_g,
        sum_u,
        sum_d.T,
        norm_sums,
        qk_sums.reshape(qk_shard),
    )


def solution(mesh):
    return jax.shard_map(
        on_device,
        mesh=mesh,
        in_specs=(
            P("seq", None),
            P(),
            P("seq", None),
            P("seq", None),
            P("seq", None),
            P(None, "seq"),
            P("seq", None),
            P("seq", None),
            P(None, "seq"),
            P(None, "seq"),
            P("seq"),
            P("seq", None),
        ),
        out_specs=(
            P("seq", None),
            P("seq", None),
            P("seq", None),
            P("seq", None),
            P("seq", None),
            P(None, "seq"),
            P("seq", None),
            P("seq", None),
            P(None, "seq"),
            P(None, "seq"),
            P("seq"),
        ),
        check_vma=False,
    )
```
